32 devices in a mesh: ctx: 16 (over z, x, core), head: 2 (over y).
Axes of the slice: x: 2, y: 2, z: 4, core: 2. Of those that a mesh axis runs over, the one named last changes fastest.
Arguments:
- hidden_in: bfloat16 [16384, 2048], P('ctx', 'head'), may hold values from -6 to 6
- proj_weight: bfloat16 [2048, 3584], P(None, 'head'), may hold values from -0.125 to 0.125
- conv_weight: float32 [3, 1024], P(None, 'head'), may hold values from -3 to 3
- norm_gain: float32 [1024], P('head'), may hold values from 0.1 to 1.9
- out_weight: bfloat16 [1024, 2048], P('head'), may hold values from -0.25 to 0.25
Outputs:
- layer_out: bfloat16 [16384, 2048], P('ctx', 'head')
The draws below stay inside these ranges and needn't reach their ends.
All inputs are finite; a program needn't handle non-finite values.
Results may differ from the reference program's by a relative error of at most 0.014.
Values may be sent and summed in bfloat16 or wider, within the bound.
No kernel may reach another device: no remote copies, remote signals or barrier semaphores. Data moves between devices by JAX's collectives and lax.ppermute only.
A program may use at most 128 MiB of HBM per device.

```python
import jax
import jax.numpy as jnp
from jax import lax

D = 2048
HEADS = 16
DV = 64
FQK = 16
WIN = 64
CONV = 3
TOK_DEV = 1024
TOKENS = 16384
N_HEAD = 2


def with_spikes(values, key, source, target, parts, factor):
    def block_of(axis_at):
        return (jnp.arange(values.shape[axis_at]) // (values.shape[axis_at] // parts)).reshape((-1,) + (1,) * (values.ndim - 1 - axis_at))

    first = jax.random.permutation(key, parts)[block_of(target)]
    far = (block_of(target) + parts // 2) % parts
    return jnp.where((block_of(source) == first) | (block_of(source) == far), factor * values, values)


def level_of(own_key, dims, split, least, high):
    factor_of, own = 1.0, jax.random.fold_in(own_key, 6)
    for dim, parts in split:
        draws = jnp.exp(jax.random.uniform(jax.random.fold_in(own, dim), (parts,), jnp.float32, least / len(split), high / len(split)))
        factor_of = factor_of * jnp.repeat(draws, dims[dim] // parts).reshape([-1 if axis == dim else 1 for axis in range(len(dims))])
    return factor_of


def gaussian(own_key, shape, spread, most, cuts=(), held_as=jnp.bfloat16):
    entries = spread * jax.random.normal(own_key, shape, jnp.float32)
    if cuts:
        entries = entries * level_of(own_key, shape, cuts, -0.22, 0.18)
    return jnp.clip(entries, -most, most).astype(held_as)


def noise_with(stream_key, extent, width, most, split, heavy, kind=jnp.bfloat16):
    result = width * jax.random.normal(stream_key, extent, jnp.float32)
    if split:
        result = result * level_of(stream_key, extent, split, -0.22, 0.18)
    return jnp.clip(with_spikes(result, jax.random.fold_in(stream_key, 3), *heavy), -most, most).astype(kind)


def setup_inputs(seed: int = 0) -> dict:
    seeds = jax.random.split(jax.random.key(seed), 6)
    return {
        "hidden_in": gaussian(seeds[0], (TOKENS, D), 1.0, 6.0, ((0, 16), (1, 2))),
        "proj_weight": gaussian(seeds[1], (D, HEADS * (2 * FQK + 3 * DV)), D ** -0.5, 0.125, ((1, 2),)),
        "conv_weight": gaussian(seeds[2], (CONV, HEADS * DV), 0.6, 3.0, ((1, 2),), jnp.float32),
        "norm_gain": jnp.clip(1.0 + 0.18 * jax.random.normal(seeds[3], (HEADS * DV,), jnp.float32), 0.1, 1.9),
        "out_weight": noise_with(seeds[4], (HEADS * DV, D), (HEADS * DV) ** -0.5, 0.25, ((0, 2),), (0, 1, 2, 2.0)),
    }


def features(vector):
    vec_len = vector.shape[-1]
    square = (vector[..., :, None] * vector[..., None, :]).reshape(vector.shape[:-1] + (vec_len * vec_len,))
    constant = jnp.ones(vector.shape[:-1] + (1,), vector.dtype)
    return jnp.concatenate([constant, vector / vec_len ** 0.25, square / (2.0 * vec_len) ** 0.5], axis=-1)

def normalize(block_in):
    values = block_in.astype(jnp.float32)
    return (values * lax.rsqrt(lax.optimization_barrier(jnp.mean(values * values, axis=-1, keepdims=True)) + 1e-06)).astype(jnp.bfloat16)

def convolve(extended, conv_weight, count):
    tap_count = conv_weight.shape[0]
    total = jnp.zeros((count, extended.shape[1]), jnp.float32)
    for tap_id in range(tap_count):
        offset = tap_count - 1 - tap_id
        total = total + conv_weight[tap_id] * extended[offset:offset + count].astype(jnp.float32)
    return total.astype(jnp.bfloat16)

def reference(hidden_in, proj_weight, conv_weight, norm_gain, out_weight):
    highest = lax.Precision.HIGHEST
    per_head = 2 * FQK + 3 * DV
    reach_rows = WIN - 1
    projected = jnp.dot(hidden_in, proj_weight, preferred_element_type=jnp.float32).astype(jnp.bfloat16)
    projected = projected.reshape(TOKENS, HEADS, per_head)
    lin_query = projected[:, :, :FQK]
    lin_key = projected[:, :, FQK:2 * FQK]
    raw_values = projected[:, :, 2 * FQK:2 * FQK + DV].reshape(TOKENS, HEADS * DV)
    win_query = projected[:, :, 2 * FQK + DV:2 * FQK + 2 * DV]
    win_key = projected[:, :, 2 * FQK + 2 * DV:]
    padded_raw = jnp.concatenate([jnp.zeros((CONV - 1, HEADS * DV), jnp.bfloat16), raw_values], 0)
    conv_values = convolve(padded_raw, conv_weight, TOKENS).reshape(TOKENS, HEADS, DV)
    q_hat = normalize(win_query)
    k_hat = normalize(win_key)
    pad_keys = jnp.concatenate([jnp.zeros((reach_rows, HEADS, DV), jnp.bfloat16), k_hat], 0)
    pad_values = jnp.concatenate([jnp.zeros((reach_rows, HEADS, DV), jnp.bfloat16), conv_values], 0)
    block_count = TOKENS // TOK_DEV
    causal = jnp.arange(TOK_DEV)[None, :] <= jnp.arange(TOK_DEV)[:, None]
    shift_ids = jnp.arange(TOK_DEV + reach_rows)[None, :] - jnp.arange(TOK_DEV)[:, None]
    band = (shift_ids >= 0) & (shift_ids <= reach_rows)
    gain_grid = norm_gain.reshape(HEADS, DV)

    def split_rows(array):
        return array.reshape((block_count, TOK_DEV) + array.shape[1:])

    def step(prior, inputs):
        query_blk, key_blk, value_blk, qhat_blk, block_id = inputs
        offset = block_id * TOK_DEV
        query_feat = features(query_blk.astype(jnp.float32))
        key_feat = features(key_blk.astype(jnp.float32))
        value_full = value_blk.astype(jnp.float32)
        carried = jnp.einsum('thf,hfd->thd', query_feat, prior, precision=highest)
        products = jnp.einsum('thf,shf->hts', query_blk.astype(jnp.float32), key_blk.astype(jnp.float32), precision=highest)
        scaled = products / FQK ** 0.5
        kernel = jnp.where(causal[None], 1.0 + scaled + 0.5 * scaled * scaled, 0.0).astype(jnp.bfloat16)
        own_part = jnp.einsum('hts,shd->thd', kernel.astype(jnp.float32), value_full, precision=highest)
        lin = carried + own_part
        new_prior = prior + jnp.einsum('thf,thd->hfd', key_feat, value_full, precision=highest)
        keys = lax.dynamic_slice_in_dim(pad_keys, offset, TOK_DEV + reach_rows, 0)
        key_values = lax.dynamic_slice_in_dim(pad_values, offset, TOK_DEV + reach_rows, 0)
        scores = jnp.einsum('thd,shd->hts', qhat_blk.astype(jnp.float32), keys.astype(jnp.float32), precision=highest) / DV ** 0.5
        position = offset + jnp.arange(TOK_DEV + reach_rows).astype(jnp.int32) - reach_rows
        allowed = band & (position >= 0)[None, :]
        expo = jnp.where(allowed[None], jnp.exp(scores), 0.0)
        weights = (expo / lax.optimization_barrier(jnp.sum(expo, axis=-1, keepdims=True))).astype(jnp.bfloat16)
        window = jnp.einsum('hts,shd->thd', weights.astype(jnp.float32), key_values.astype(jnp.float32), precision=highest)
        mean_sq = lax.optimization_barrier(jnp.mean(lin * lin, axis=-1, keepdims=True))
        mixed_heads = (lin * lax.rsqrt(mean_sq + 1e-05) * gain_grid + window).astype(jnp.bfloat16)
        return (new_prior, mixed_heads.reshape(TOK_DEV, HEADS * DV))
    block_ids = jnp.arange(block_count).astype(jnp.int32)
    start_state = jnp.zeros((HEADS, 1 + FQK + FQK * FQK, DV), jnp.float32)
    final_state, mixed = lax.scan(step, start_state, (split_rows(lin_query), split_rows(lin_key), split_rows(conv_values), split_rows(q_hat), block_ids))
    mixed = mixed.reshape(TOKENS, HEADS * DV)
    group_rows = HEADS * DV // N_HEAD
    total = jnp.zeros((TOKENS, D), jnp.float32)
    for group in range(N_HEAD):
        part_sum = jnp.dot(mixed[:, group * group_rows:(group + 1) * group_rows], out_weight[group * group_rows:(group + 1) * group_rows], preferred_element_type=jnp.float32)
        rounded = lax.optimization_barrier(part_sum.astype(jnp.bfloat16))
        total = total + rounded.astype(jnp.float32)
    return total.astype(jnp.bfloat16)
```

```python
import functools

import jax
import jax.numpy as jnp
import numpy as np
from jax import lax
from jax.experimental import pallas as pl
from jax.experimental.pallas import tpu as pltpu
from jax.sharding import PartitionSpec as P

DV = 64
FQK = 16
WIN = 64
CONV = 3
LANES = 128
FEATS = 160
QFEATS = 256
TAIL = 128
CHUNKS = 4
F32 = jnp.float32
BF16 = jnp.bfloat16


def call(body, out_shape, *, flops=0, moved=0, vmem=48 << 20, **kwargs):
    return pl.pallas_call(
        body,
        out_shape=out_shape,
        compiler_params=pltpu.CompilerParams(vmem_limit_bytes=vmem),
        cost_estimate=pl.CostEstimate(flops=flops, bytes_accessed=moved, transcendentals=0),
        **kwargs,
    )


def feature_tables(heads):
    first = [FQK] + [FQK] * FQK
    second = [FQK] + list(range(FQK))
    weight = [1.0] + [1.0 / FQK**0.5] * FQK
    for i in range(FQK):
        for j in range(i, FQK):
            first.append(i)
            second.append(j)
            weight.append((1.0 if i == j else 2.0) / (2.0 * FQK))
    sel_a = np.zeros((heads, QFEATS, LANES), np.float32)
    sel_b = np.zeros((heads, QFEATS, LANES), np.float32)
    sel_w = np.zeros((heads, QFEATS, LANES), np.float32)
    for h in range(heads):
        for f, (i, j, w) in enumerate(zip(first, second, weight)):
            sel_a[h, f, (h * FQK + i) % LANES] = 1.0
            sel_b[h, f, (h * FQK + j) % LANES] = 1.0
            sel_w[h, f, (h * FQK + i) % LANES] = w
    return tuple(jnp.asarray(t, BF16) for t in (sel_a, sel_b, sel_w))


def mean_table():
    block = np.kron(np.eye(LANES // DV), np.ones((DV, DV))) / DV
    return jnp.asarray(np.concatenate([block, block], 0), BF16)


def head_mean(values, table):
    high = values.astype(BF16)
    low = (values - high.astype(F32)).astype(BF16)
    return jnp.dot(jnp.concatenate([high, low], 1), table, preferred_element_type=F32)


def nt_dot(a, b):
    return lax.dot_general(a, b, (((1,), (1,)), ((), ())), preferred_element_type=F32)


def arrange_kernel(w_ref, o_ref, *, heads):
    per_head = 2 * FQK + 3 * DV
    w = w_ref[...]
    at = 0
    for begin, width in ((0, FQK), (FQK, FQK), (2 * FQK, DV), (2 * FQK + DV, DV), (2 * FQK + 2 * DV, DV)):
        parts = [w[:, h * per_head + begin : h * per_head + begin + width] for h in range(heads)]
        total = heads * width
        padded = -(-total // LANES) * LANES
        if padded > total:
            parts.append(jnp.zeros((w.shape[0], padded - total), w.dtype))
        o_ref[:, at : at + padded] = jnp.concatenate(parts, 1)
        at += padded


def project_kernel(j_ref, mean_ref, w_ref, *refs, n):
    xs, (q_ref, k_ref, v_ref, wq_ref, wk_ref) = refs[:n], refs[n:]
    depth = xs[0].shape[1]
    me = j_ref[0]

    def project(begin, width):
        total = None
        for r in range(n):
            src = lax.rem(me - r + n, n)
            rows = pl.ds(pl.multiple_of(src * depth, depth), depth)
            part = jnp.dot(xs[r][...], w_ref[rows, begin : begin + width], preferred_element_type=F32)
            total = part if total is None else total + part
        return total.astype(BF16)

    at = 0
    for ref in (q_ref, k_ref, v_ref, wq_ref, wk_ref):
        width = ref.shape[1]
        got = project(at, width)
        at += width
        if ref is wq_ref or ref is wk_ref:
            for p in range(width // LANES):
                cols = slice(p * LANES, (p + 1) * LANES)
                x = got[:, cols].astype(F32)
                x = x * lax.rsqrt(head_mean(x * x, mean_ref[...]) + 1e-6)
                hat = x.astype(BF16)
                if ref is wq_ref:
                    hat = hat * jnp.asarray(1.0 / DV**0.5, BF16)
                ref[:, cols] = hat
        else:
            ref[...] = got


def convolve(conv_ref, ext_ref, begin, count):
    total = jnp.zeros((count, ext_ref.shape[1]), F32)
    for tap in range(CONV):
        total = total + conv_ref[tap : tap + 1, :] * ext_ref[begin - tap : begin - tap + count, :]
    return total.astype(BF16)


def state_kernel(conv_ref, sel_w_ref, sel_b_ref, prev_ref, raw_ref, k_ref, v_ref, s_ref, ext_ref, *, heads):
    rows = raw_ref.shape[0]
    ext_ref[0:16, :] = prev_ref[TAIL - 16 : TAIL, :].astype(F32)
    ext_ref[16 : 16 + rows, :] = raw_ref[...].astype(F32)
    v_ref[...] = convolve(conv_ref, ext_ref, 16, rows)
    lane = lax.broadcasted_iota(jnp.int32, (rows, LANES), 1)
    k = k_ref[...].astype(F32)
    low_half = lax.broadcasted_iota(jnp.int32, (FEATS, LANES), 1) < DV
    for p in range(heads * DV // LANES):
        cols = slice(p * LANES, (p + 1) * LANES)
        v = v_ref[:, cols]
        both = []
        for h in (2 * p, 2 * p + 1):
            one_lane = ((h + 1) * FQK) % LANES
            own = jnp.where(lane == one_lane, 1.0, k).astype(BF16)
            phi = nt_dot(sel_w_ref[h, 0:FEATS, :], own) * nt_dot(sel_b_ref[h, 0:FEATS, :], own)
            both.append(jnp.dot(phi.astype(BF16), v, preferred_element_type=F32))
        s_ref[:, cols] = jnp.where(low_half, both[0], both[1])


def attend_kernel(
    lo_ref, conv_ref, prev_raw_ref, prev_wk_ref, q_ref, k_ref, v_ref, wq_ref, wk_ref, lin_ref, win_ref,
    ext_ref, vext_ref, kext_ref, *, heads
):
    rows = q_ref.shape[0]
    tile = 128
    span = tile + WIN
    ext_ref[...] = prev_raw_ref[TAIL - WIN - 16 : TAIL, :].astype(F32)
    vext_ref[0:WIN, :] = convolve(conv_ref, ext_ref, 16, WIN)
    vext_ref[WIN : WIN + rows, :] = v_ref[...]
    kext_ref[0:WIN, :] = prev_wk_ref[TAIL - WIN : TAIL, :]
    kext_ref[WIN : WIN + rows, :] = wk_ref[...]
    lane = lax.broadcasted_iota(jnp.int32, (rows, LANES), 1)
    low_half = lane < DV
    causal = lax.broadcasted_iota(jnp.int32, (rows, rows), 1) <= lax.broadcasted_iota(jnp.int32, (rows, rows), 0)
    col = lax.broadcasted_iota(jnp.int32, (tile, span), 1)
    ahead = col - lax.broadcasted_iota(jnp.int32, (tile, span), 0)
    band = (ahead >= 1) & (ahead <= WIN)
    first_band = band & (col >= lo_ref[0])
    q = q_ref[...]
    k = k_ref[...]
    for p in range(heads * DV // LANES):
        cols = slice(p * LANES, (p + 1) * LANES)
        v = v_ref[:, cols]
        both = []
        for h in (2 * p, 2 * p + 1):
            own = jnp.where((lane >= h * FQK) & (lane < (h + 1) * FQK), q, jnp.zeros_like(q))
            t = nt_dot(own, k) * (1.0 / FQK**0.5) + 1.0
            kernel = jnp.where(causal, 0.5 * (t * t) + 0.5, 0.0).astype(BF16)
            both.append(jnp.dot(kernel, v, preferred_element_type=F32))
        lin_ref[:, cols] = jnp.where(low_half, both[0], both[1])
        for i in range(rows // tile):
            here = slice(i * tile, (i + 1) * tile)
            wq = wq_ref[here, cols]
            keys = kext_ref[i * tile : i * tile + span, cols]
            values = vext_ref[i * tile : i * tile + span, cols]
            both = []
            for half in range(2):
                keep = low_half[0:tile] if half == 0 else ~low_half[0:tile]
                scores = nt_dot(jnp.where(keep, wq, jnp.zeros_like(wq)), keys)
                expo = jnp.where(first_band if i == 0 else band, jnp.exp(scores), 0.0)
                weights = expo * (1.0 / jnp.sum(expo, axis=1, keepdims=True))
                both.append(jnp.dot(weights.astype(BF16), values, preferred_element_type=F32))
            win_ref[here, cols] = jnp.where(low_half[0:tile], both[0], both[1])


def finish_kernel(mean_ref, gain_ref, sel_a_ref, sel_b_ref, prior_ref, *refs, heads, before):
    states, (q_ref, lin_ref, win_ref, mix_ref) = refs[:before], refs[before:]
    rows = q_ref.shape[0]
    state = prior_ref[...]
    for ref in states:
        state = state + ref[...]
    state = state.astype(BF16)
    state = jnp.concatenate([state, jnp.zeros((QFEATS - FEATS, state.shape[1]), BF16)], 0)
    lane = lax.broadcasted_iota(jnp.int32, (rows, LANES), 1)
    q = q_ref[...].astype(F32)
    for p in range(heads * DV // LANES):
        cols = slice(p * LANES, (p + 1) * LANES)
        both = []
        for h in (2 * p, 2 * p + 1):
            one_lane = ((h + 1) * FQK) % LANES
            own = jnp.where(lane == one_lane, 1.0, q).astype(BF16)
            phi = nt_dot(own, sel_a_ref[h]) * nt_dot(own, sel_b_ref[h])
            both.append(jnp.dot(phi.astype(BF16), state[:, cols], preferred_element_type=F32))
        lin = lin_ref[:, cols] + jnp.where(lane < DV, both[0], both[1])
        scale = lax.rsqrt(head_mean(lin * lin, mean_ref[...]) + 1e-5)
        mix_ref[:, cols] = (lin * scale * gain_ref[:, cols] + win_ref[:, cols]).astype(BF16)


def output_kernel(*refs, n):
    mixed, weights, o_ref = refs[:n], refs[n : 2 * n], refs[-1]
    total = None
    for m_ref, w_ref in zip(mixed, weights):
        part = jnp.dot(m_ref[...], w_ref[...], preferred_element_type=F32).astype(BF16).astype(F32)
        total = part if total is None else total + part
    o_ref[...] = total.astype(BF16)


def per_device(hidden_in, proj_weight, conv_weight, norm_gain, out_weight):
    n = lax.axis_size("head")
    ctx = lax.axis_size("ctx")
    me = lax.axis_index("head")
    position = lax.axis_index("ctx")
    row_count, depth = hidden_in.shape
    model = proj_weight.shape[0]
    heads = out_weight.shape[0] // DV
    width = heads * DV
    rows = row_count // CHUNKS
    sel_a, sel_b, sel_w = feature_tables(heads)
    means = mean_table()
    gain = norm_gain.reshape(1, width)
    me_arr = me.astype(jnp.int32).reshape(1)
    whole = pl.BlockSpec(memory_space=pltpu.VMEM)
    scalar = pl.BlockSpec(memory_space=pltpu.SMEM)

    def from_head(value, by):
        return lax.ppermute(value, "head", [(i, (i + by) % n) for i in range(n)])

    order = [CHUNKS - 1] + list(range(CHUNKS - 1))
    pieces = {}
    for c in order:
        own = hidden_in[c * rows : (c + 1) * rows]
        pieces[c] = [own] + [from_head(own, r) for r in range(1, n)]

    qk_width = -(-heads * FQK // LANES) * LANES
    arranged_width = 2 * qk_width + 3 * width
    slab = 256
    arranged = call(
        functools.partial(arrange_kernel, heads=heads),
        jax.ShapeDtypeStruct((model, arranged_width), BF16),
        grid=(model // slab,),
        in_specs=[pl.BlockSpec((slab, proj_weight.shape[1]), lambda i: (i, 0))],
        out_specs=pl.BlockSpec((slab, arranged_width), lambda i: (i, 0)),
        moved=4 * model * arranged_width,
        vmem=32 << 20,
    )(proj_weight)

    def project(c):
        return call(
            functools.partial(project_kernel, n=n),
            [jax.ShapeDtypeStruct((rows, w), BF16) for w in (qk_width, qk_width, width, width, width)],
            in_specs=[scalar] + [whole] * (2 + n),
            out_specs=[whole] * 5,
            flops=2 * rows * model * arranged_width,
            moved=2 * model * arranged_width,
            vmem=32 << 20,
        )(me_arr, means, arranged, *pieces[c])

    def block_state(c, prev):
        q, k, raw, wq, wk = parts[c]
        return call(
            functools.partial(state_kernel, heads=heads),
            [jax.ShapeDtypeStruct((rows, width), BF16), jax.ShapeDtypeStruct((FEATS, width), F32)],
            in_specs=[whole] * 6,
            out_specs=[whole] * 2,
            scratch_shapes=[pltpu.VMEM((16 + rows, width), F32)],
            flops=6 * rows * FEATS * LANES * heads,
            moved=8 * rows * width,
            vmem=16 << 20,
        )(conv_weight, sel_w, sel_b, prev[0], raw, k)

    def attend(c, prev, lo):
        q, k, raw, wq, wk = parts[c]
        return call(
            functools.partial(attend_kernel, heads=heads),
            [jax.ShapeDtypeStruct((rows, width), F32)] * 2,
            in_specs=[scalar] + [whole] * 8,
            out_specs=[whole] * 2,
            scratch_shapes=[
                pltpu.VMEM((16 + WIN, width), F32),
                pltpu.VMEM((WIN + rows, width), BF16),
                pltpu.VMEM((WIN + rows, width), BF16),
            ],
            flops=heads * rows * 2048 * 256,
            moved=16 * rows * width,
            vmem=16 << 20,
        )(lo, conv_weight, prev[0], prev[1], q, k, values[c], wq, wk)

    def tail(c):
        return parts[c][2][rows - TAIL :], parts[c][4][rows - TAIL :]

    parts, values, states, lins, wins = {}, {}, {}, {}, {}
    inside = jnp.zeros((1,), jnp.int32)
    at_start = jnp.where(position == 0, WIN, 0).astype(jnp.int32).reshape(1)
    parts[CHUNKS - 1] = project(CHUNKS - 1)
    halo = lax.ppermute(
        jnp.concatenate(tail(CHUNKS - 1), 1), "ctx", [(i, i + 1) for i in range(ctx - 1)]
    )
    prev = {0: (halo[:, :width], halo[:, width:])}
    for c in range(CHUNKS - 1):
        parts[c] = project(c)
        prev[c + 1] = tail(c)
        values[c], states[c] = block_state(c, prev[c])
        if c < CHUNKS - 2:
            lins[c], wins[c] = attend(c, prev[c], at_start if c == 0 else inside)
    last = CHUNKS - 1
    values[last], states[last] = block_state(last, prev[last])

    total = states[0]
    for c in range(1, CHUNKS):
        total = total + states[c]
    prior = jnp.zeros_like(total)
    bit = 1
    while bit < ctx:
        got = lax.ppermute(total.astype(BF16), "ctx", [(i, i ^ bit) for i in range(ctx)]).astype(F32)
        prior = prior + jnp.where((position & bit) != 0, got, 0.0)
        total = total + got
        bit *= 2

    cols = out_weight.shape[1] // n
    out_rows = [lax.dynamic_slice_in_dim(out_weight, me * cols, cols, 1)]
    for r in range(1, n):
        block = lax.dynamic_slice_in_dim(out_weight, lax.rem(me + r, n) * cols, cols, 1)
        block, _ = lax.optimization_barrier((block, parts[CHUNKS - 2][0]))
        out_rows.append(from_head(block, r))

    for c in (CHUNKS - 2, CHUNKS - 1):
        lins[c], wins[c] = attend(c, prev[c], inside)

    result = None
    for c in range(CHUNKS):
        mixed = call(
            functools.partial(finish_kernel, heads=heads, before=c),
            jax.ShapeDtypeStruct((rows, width), BF16),
            in_specs=[whole] * (5 + c + 3),
            out_specs=whole,
            flops=6 * rows * QFEATS * LANES * heads,
            moved=12 * rows * width,
            vmem=16 << 20,
        )(means, gain, sel_a, sel_b, prior, *[states[b] for b in range(c)], parts[c][0], lins[c], wins[c])
        mixes = [mixed] + [from_head(mixed, r) for r in range(1, n)]
        operands = mixes + out_rows
        specs = [pl.BlockSpec(a.shape, lambda i: (0, 0)) for a in operands]
        aliases = {}
        if result is not None:
            aliases = {len(operands): 0}
            operands = operands + [result]
            specs = specs + [pl.BlockSpec(memory_space=pl.ANY)]
        result = call(
            functools.partial(output_kernel, n=n),
            jax.ShapeDtypeStruct((row_count, cols), BF16),
            grid=(1,),
            in_specs=specs,
            out_specs=pl.BlockSpec((rows, cols), functools.partial(lambda i, c: (c, 0), c=c)),
            input_output_aliases=aliases,
            flops=2 * rows * n * width * cols,
            moved=2 * n * width * cols,
            vmem=16 << 20,
        )(*operands)
    return result


def solution(mesh):
    return jax.shard_map(
        per_device,
        mesh=mesh,
        in_specs=(P("ctx", "head"), P(None, "head"), P(None, "head"), P("head"), P("head", None)),
        out_specs=P("ctx", "head"),
        check_vma=False,
    )
```

```python
import functools

import jax
import jax.numpy as jnp
import numpy as np
from jax import lax
from jax.experimental import pallas as pl
from jax.experimental.pallas import tpu as pltpu
from jax.sharding import PartitionSpec as P

DV = 64
FQK = 16
WIN = 64
CONV = 3
LANES = 128
FEATS = 160
QFEATS = 256
EDGE = 16
HALO = EDGE + 2 * WIN
PLANE = 4
F32 = jnp.float32
BF16 = jnp.bfloat16


def call(body, out_shape, *, flops=0, moved=0, vmem=48 << 20, **kwargs):
    return pl.pallas_call(
        body,
        out_shape=out_shape,
        compiler_params=pltpu.CompilerParams(vmem_limit_bytes=vmem),
        cost_estimate=pl.CostEstimate(flops=flops, bytes_accessed=moved, transcendentals=0),
        **kwargs,
    )


def feature_tables(heads):
    first = [FQK] + [FQK] * FQK
    second = [FQK] + list(range(FQK))
    weight = [1.0] + [1.0 / FQK**0.5] * FQK
    for i in range(FQK):
        for j in range(i, FQK):
            first.append(i)
            second.append(j)
            weight.append((1.0 if i == j else 2.0) / (2.0 * FQK))
    sel_a = np.zeros((heads, QFEATS, LANES), np.float32)
    sel_b = np.zeros((heads, QFEATS, LANES), np.float32)
    sel_w = np.zeros((heads, QFEATS, LANES), np.float32)
    for h in range(heads):
        for f, (i, j, w) in enumerate(zip(first, second, weight)):
            sel_a[h, f, (h * FQK + i) % LANES] = 1.0
            sel_b[h, f, (h * FQK + j) % LANES] = 1.0
            sel_w[h, f, (h * FQK + i) % LANES] = w
    return tuple(jnp.asarray(t, BF16) for t in (sel_a, sel_b, sel_w))


def mean_table():
    block = np.kron(np.eye(LANES // DV), np.ones((DV, DV))) / DV
    return jnp.asarray(np.concatenate([block, block], 0), BF16)


def head_mean(values, table):
    high = values.astype(BF16)
    low = (values - high.astype(F32)).astype(BF16)
    return jnp.dot(jnp.concatenate([high, low], 1), table, preferred_element_type=F32)


def nt_dot(a, b):
    return lax.dot_general(a, b, (((1,), (1,)), ((), ())), preferred_element_type=F32)


def with_one(vectors, lane, h):
    return jnp.where(lane == ((h + 1) * FQK) % LANES, 1.0, vectors).astype(BF16)


def arrange_kernel(w_ref, o_ref, *, heads):
    per_head = 2 * FQK + 3 * DV
    w = w_ref[...]
    at = 0
    for begin, width in ((0, FQK), (FQK, FQK), (2 * FQK, DV), (2 * FQK + DV, DV), (2 * FQK + 2 * DV, DV)):
        parts = [w[:, h * per_head + begin : h * per_head + begin + width] for h in range(heads)]
        total = heads * width
        padded = -(-total // LANES) * LANES
        if padded > total:
            parts.append(jnp.zeros((w.shape[0], padded - total), w.dtype))
        o_ref[:, at : at + padded] = jnp.concatenate(parts, 1)
        at += padded


def block_kernel(j_ref, mean_ref, conv_ref, sel_w_ref, sel_b_ref, w_ref, *refs, n, heads, extra, others, sends):
    xs, refs = refs[:n], refs[n:]
    prev_ref = None
    if not extra:
        prev_ref, refs = refs[0], refs[1:]
    other_refs, refs = refs[:others], refs[others:]
    q_ref, k_ref, v_ref, wq_ref, wk_ref, halo_ref, s_ref = refs[:7]
    send_refs, (ext_ref,) = refs[7 : 7 + sends], refs[7 + sends :]
    rows, depth = v_ref.shape[0], xs[0].shape[1]
    me = j_ref[0]

    def project(begin, width, skip):
        total = None
        for r in range(n):
            src = lax.rem(me - r + n, n)
            from_rows = pl.ds(pl.multiple_of(src * depth, depth), depth)
            part = jnp.dot(xs[r][skip:, :], w_ref[from_rows, begin : begin + width], preferred_element_type=F32)
            total = part if total is None else total + part
        return total.astype(BF16)

    widths = [ref.shape[1] for ref in (q_ref, k_ref, v_ref, wq_ref, wk_ref)]
    starts = [sum(widths[:i]) for i in range(5)]
    k_ref[...] = project(starts[1], widths[1], extra)
    raw = project(starts[2], widths[2], 0)
    if extra:
        ext_ref[...] = raw.astype(F32)
    else:
        ext_ref[0:EDGE, :] = prev_ref[0:EDGE, :].astype(F32)
        ext_ref[EDGE:, :] = raw.astype(F32)
    halo_ref[0:EDGE, :] = raw[raw.shape[0] - EDGE :]
    total = jnp.zeros((rows, widths[2]), F32)
    for tap in range(CONV):
        total = total + conv_ref[tap : tap + 1, :] * ext_ref[EDGE - tap : EDGE - tap + rows, :]
    v_ref[...] = total.astype(BF16)
    halo_ref[EDGE : EDGE + WIN, :] = v_ref[rows - WIN : rows, :]

    lane = lax.broadcasted_iota(jnp.int32, (rows, LANES), 1)
    low_half = lax.broadcasted_iota(jnp.int32, (FEATS, LANES), 1) < DV
    k = k_ref[...].astype(F32)
    for p in range(heads * DV // LANES):
        v = v_ref[:, p * LANES : (p + 1) * LANES]
        both = []
        for h in (2 * p, 2 * p + 1):
            own = with_one(k, lane, h)
            phi = nt_dot(sel_w_ref[h, 0:FEATS, :], own) * nt_dot(sel_b_ref[h, 0:FEATS, :], own)
            both.append(jnp.dot(phi.astype(BF16), v, preferred_element_type=F32))
        s_ref[p] = jnp.where(low_half, both[0], both[1])
    for r in range(sends):
        pair = jnp.bitwise_xor(j_ref[1], r)
        total = s_ref[pair]
        for ref in other_refs:
            total = total + ref[pair]
        send_refs[r][...] = total.astype(BF16)

    q_ref[...] = project(starts[0], widths[0], extra)
    for ref, start, width, scale in (
        (wk_ref, starts[4], widths[4], 1.0),
        (wq_ref, starts[3], widths[3], 1.0 / DV**0.5),
    ):
        got = project(start, width, extra)
        for p in range(width // LANES):
            cols = slice(p * LANES, (p + 1) * LANES)
            x = got[:, cols].astype(F32)
            x = x * lax.rsqrt(head_mean(x * x, mean_ref[...]) + 1e-6)
            ref[:, cols] = x.astype(BF16) * jnp.asarray(scale, BF16)
    halo_ref[EDGE + WIN : HALO, :] = wk_ref[rows - WIN : rows, :]


def attend_kernel(
    lo_ref, sel_a_ref, sel_b_ref, prev_ref, q_ref, k_ref, v_ref, wq_ref, wk_ref, phi_ref, lin_ref, win_ref,
    vext_ref, kext_ref, *, heads
):
    rows = q_ref.shape[0]
    tile = 128
    span = tile + WIN
    vext_ref[0:WIN, :] = prev_ref[EDGE : EDGE + WIN, :]
    vext_ref[WIN : WIN + rows, :] = v_ref[...]
    kext_ref[0:WIN, :] = prev_ref[EDGE + WIN : HALO, :]
    kext_ref[WIN : WIN + rows, :] = wk_ref[...]
    lane = lax.broadcasted_iota(jnp.int32, (rows, LANES), 1)
    low_half = lane < DV
    causal = lax.broadcasted_iota(jnp.int32, (rows, rows), 1) <= lax.broadcasted_iota(jnp.int32, (rows, rows), 0)
    col = lax.broadcasted_iota(jnp.int32, (tile, span), 1)
    ahead = col - lax.broadcasted_iota(jnp.int32, (tile, span), 0)
    band = (ahead >= 1) & (ahead <= WIN)
    first_band = band & (col >= lo_ref[0])
    q = q_ref[...]
    q_full = q.astype(F32)
    k = k_ref[...]
    for p in range(heads * DV // LANES):
        cols = slice(p * LANES, (p + 1) * LANES)
        v = v_ref[:, cols]
        both = []
        for h in (2 * p, 2 * p + 1):
            own = with_one(q_full, lane, h)
            phi = nt_dot(own, sel_a_ref[h]) * nt_dot(own, sel_b_ref[h])
            phi_ref[:, h * QFEATS : (h + 1) * QFEATS] = phi.astype(BF16)
            own = jnp.where((lane >= h * FQK) & (lane < (h + 1) * FQK), q, jnp.zeros_like(q))
            t = nt_dot(own, k) * (1.0 / FQK**0.5) + 1.0
            kernel = jnp.where(causal, 0.5 * (t * t) + 0.5, 0.0).astype(BF16)
            both.append(jnp.dot(kernel, v, preferred_element_type=F32))
        lin_ref[:, cols] = jnp.where(low_half, both[0], both[1])
        for i in range(rows // tile):
            here = slice(i * tile, (i + 1) * tile)
            wq = wq_ref[here, cols]
            keys = kext_ref[i * tile : i * tile + span, cols]
            values = vext_ref[i * tile : i * tile + span, cols]
            both = []
            for half in range(2):
                keep = low_half[0:tile] if half == 0 else ~low_half[0:tile]
                scores = nt_dot(jnp.where(keep, wq, jnp.zeros_like(wq)), keys)
                expo = jnp.where(first_band if i == 0 else band, jnp.exp(scores), 0.0)
                weights = expo * (1.0 / jnp.sum(expo, axis=1, keepdims=True))
                both.append(jnp.dot(weights.astype(BF16), values, preferred_element_type=F32))
            win_ref[here, cols] = jnp.where(low_half[0:tile], both[0], both[1])


def finish_kernel(a_ref, mean_ref, gain_ref, *refs, heads, before):
    pairs = heads * DV // LANES
    prior_refs, refs = refs[:pairs], refs[pairs:]
    states, (phi_ref, lin_ref, win_ref, mix_ref, held_ref) = refs[:before], refs[before:]
    rows = phi_ref.shape[0]
    for r in range(pairs):
        held_ref[r] = prior_refs[r][...].astype(F32)
    low_half = lax.broadcasted_iota(jnp.int32, (rows, LANES), 1) < DV
    for p in range(pairs):
        cols = slice(p * LANES, (p + 1) * LANES)
        state = held_ref[jnp.bitwise_xor(a_ref[1], p)]
        for ref in states:
            state = state + ref[p]
        state = jnp.concatenate([state.astype(BF16), jnp.zeros((QFEATS - FEATS, LANES), BF16)], 0)
        both = [
            jnp.dot(phi_ref[:, h * QFEATS : (h + 1) * QFEATS], state, preferred_element_type=F32)
            for h in (2 * p, 2 * p + 1)
        ]
        lin = lin_ref[:, cols] + jnp.where(low_half, both[0], both[1])
        scale = lax.rsqrt(head_mean(lin * lin, mean_ref[...]) + 1e-5)
        mix_ref[:, cols] = (lin * scale * gain_ref[:, cols] + win_ref[:, cols]).astype(BF16)


def output_kernel(*refs, n, offset):
    mixed, weights, (o_ref, held_ref, sem) = refs[:n], refs[n : 2 * n], refs[-3:]
    total = None
    for m_ref, w_ref in zip(mixed, weights):
        part = jnp.dot(m_ref[...], w_ref[...], preferred_element_type=F32).astype(BF16).astype(F32)
        total = part if total is None else total + part
    held_ref[...] = total.astype(BF16)
    copy = pltpu.make_async_copy(held_ref, o_ref.at[pl.ds(offset, held_ref.shape[0]), :], sem)
    copy.start()
    copy.wait()


def exchange(value, axis, flip):
    count = lax.axis_size(axis)
    return lax.ppermute(value, axis, [(i, i ^ flip) for i in range(count)])


def prior_in_planes(own, position):
    ctx = lax.axis_size("ctx")
    place = position % PLANE
    held = [own[0].astype(F32)]
    held += [exchange(own[r], "ctx", r).astype(F32) for r in range(1, PLANE)]
    plane = held[0] + held[1] + held[2] + held[3]
    ahead = []
    for r in range(PLANE):
        ahead.append(sum(jnp.where((place ^ s) < (place ^ r), held[s], 0.0) for s in range(PLANE)))
    sent = plane.astype(BF16)
    earlier = 0.0
    for d in range(1, ctx // PLANE):
        pairs = [(i, i + d * PLANE) for i in range(ctx - d * PLANE)]
        earlier = earlier + lax.ppermute(sent, "ctx", pairs).astype(F32)
    back = [(a + earlier).astype(BF16) for a in ahead]
    return [back[0]] + [exchange(back[r], "ctx", r) for r in range(1, PLANE)]


def prior_by_doubling(total, position):
    ctx = lax.axis_size("ctx")
    prior = jnp.zeros_like(total)
    bit = 1
    while bit < ctx:
        got = exchange(total.astype(BF16), "ctx", bit).astype(F32)
        prior = prior + jnp.where((position & bit) != 0, got, 0.0)
        total = total + got
        bit *= 2
    return [prior[p].astype(BF16) for p in range(total.shape[0])]


def per_device(hidden_in, proj_weight, conv_weight, norm_gain, out_weight):
    n = lax.axis_size("head")
    ctx = lax.axis_size("ctx")
    me = lax.axis_index("head").astype(jnp.int32)
    position = lax.axis_index("ctx").astype(jnp.int32)
    row_count = hidden_in.shape[0]
    model = proj_weight.shape[0]
    heads = out_weight.shape[0] // DV
    width = heads * DV
    pairs = width // LANES
    in_planes = pairs == PLANE and ctx % PLANE == 0
    place = position % PLANE if in_planes else jnp.zeros_like(position)
    step = row_count // 8
    blocks = [(0, 2 * step), (2 * step, 2 * step), (4 * step, step), (5 * step, step), (6 * step, 2 * step)]
    last = len(blocks) - 1
    sel_a, sel_b, sel_w = feature_tables(heads)
    means = mean_table()
    gain = norm_gain.reshape(1, width)
    places = jnp.stack([me, place])
    whole = pl.BlockSpec(memory_space=pltpu.VMEM)
    scalar = pl.BlockSpec(memory_space=pltpu.SMEM)

    def from_head(value, by):
        return lax.ppermute(value, "head", [(i, (i + by) % n) for i in range(n)])

    pieces = {}
    for b in [last] + list(range(last)):
        at, rows = blocks[b]
        extra = EDGE if b == last else 0
        own = hidden_in[at - extra : at + rows]
        pieces[b] = [own] + [from_head(own, r) for r in range(1, n)]

    cols = out_weight.shape[1] // n
    half = width // 2
    side = position % 2
    out_rows = [lax.dynamic_slice_in_dim(out_weight, me * cols, cols, 1)]
    fetched = []
    for r in range(1, n):
        block = lax.dynamic_slice(out_weight, (side * half, lax.rem(me + r, n) * cols), (half, cols))
        block, _ = lax.optimization_barrier((block, pieces[0][1]))
        fetched.append(from_head(block, r))

    qk_width = -(-heads * FQK // LANES) * LANES
    arranged_width = 2 * qk_width + 3 * width
    slab = 256
    arranged = call(
        functools.partial(arrange_kernel, heads=heads),
        jax.ShapeDtypeStruct((model, arranged_width), BF16),
        grid=(model // slab,),
        in_specs=[pl.BlockSpec((slab, proj_weight.shape[1]), lambda i: (i, 0))],
        out_specs=pl.BlockSpec((slab, arranged_width), lambda i: (i, 0)),
        moved=4 * model * arranged_width,
        vmem=32 << 20,
    )(proj_weight)

    def do_block(b, prev, after, others=()):
        rows = blocks[b][1]
        extra = EDGE if prev is None else 0
        sends = PLANE if in_planes and others else 0
        tokens = places
        if after is not None:
            tokens, _ = lax.optimization_barrier((places, after))
        shapes = [jax.ShapeDtypeStruct((rows, w), BF16) for w in (qk_width, qk_width, width, width, width)]
        shapes.append(jax.ShapeDtypeStruct((HALO, width), BF16))
        shapes.append(jax.ShapeDtypeStruct((pairs, FEATS, LANES), F32))
        shapes += [jax.ShapeDtypeStruct((FEATS, LANES), BF16)] * sends
        operands = [tokens, means, conv_weight, sel_w, sel_b, arranged, *pieces[b]]
        if prev is not None:
            operands.append(prev)
        operands += others
        return call(
            functools.partial(
                block_kernel, n=n, heads=heads, extra=extra, others=len(others), sends=sends
            ),
            shapes,
            in_specs=[scalar] + [whole] * (len(operands) - 1),
            out_specs=[whole] * len(shapes),
            scratch_shapes=[pltpu.VMEM((EDGE + rows, width), F32)],
            flops=2 * rows * model * arranged_width + 6 * rows * FEATS * LANES * heads,
            moved=2 * model * arranged_width,
            vmem=32 << 20,
        )(*operands)

    def attend(b, prev, lo):
        rows = blocks[b][1]
        q, k, v, wq, wk = done[b][:5]
        return call(
            functools.partial(attend_kernel, heads=heads),
            [jax.ShapeDtypeStruct((rows, heads * QFEATS), BF16)] + [jax.ShapeDtypeStruct((rows, width), F32)] * 2,
            in_specs=[scalar] + [whole] * 8,
            out_specs=[whole] * 3,
            scratch_shapes=[pltpu.VMEM((WIN + rows, width), BF16)] * 2,
            flops=heads * rows * 4096 * 256,
            moved=16 * rows * width,
            vmem=16 << 20,
        )(lo, sel_a, sel_b, prev, q, k, v, wq, wk)

    inside = jnp.zeros((1,), jnp.int32)
    at_start = jnp.where(position == 0, WIN, 0).astype(jnp.int32).reshape(1)
    done, attended = {}, {}
    done[last] = do_block(last, None, None)
    halo = lax.ppermute(done[last][5], "ctx", [(i, i + 1) for i in range(ctx - 1)])
    for b in range(last):
        prev = halo if b == 0 else done[b - 1][5]
        others = [done[c][6] for c in [last] + list(range(b))] if b == last - 1 else ()
        done[b] = do_block(b, prev, attended[b - 1][1] if b else None, others)
        if b < last - 1:
            attended[b] = attend(b, prev, at_start if b == 0 else inside)

    if in_planes:
        priors = prior_in_planes(done[last - 1][7:], position)
    else:
        priors = prior_by_doubling(sum(done[b][6] for b in range(last + 1)), position)
    for b in (last - 1, last):
        attended[b] = attend(b, done[b - 1][5], inside)

    for got in fetched:
        swapped = exchange(got, "ctx", 1)
        out_rows.append(
            jnp.concatenate([jnp.where(side == 0, got, swapped), jnp.where(side == 0, swapped, got)], 0)
        )

    result = None
    for b in (2, 0, 1, 4, 3):
        at, rows = blocks[b]
        mixed = call(
            functools.partial(finish_kernel, heads=heads, before=b),
            jax.ShapeDtypeStruct((rows, width), BF16),
            in_specs=[scalar] + [whole] * (2 + pairs + b + 3),
            out_specs=whole,
            scratch_shapes=[pltpu.VMEM((pairs, FEATS, LANES), F32)],
            flops=6 * rows * QFEATS * LANES * heads,
            moved=12 * rows * width,
            vmem=16 << 20,
        )(places, means, gain, *priors, *[done[c][6] for c in range(b)], *attended[b])
        operands = [mixed] + [from_head(mixed, r) for r in range(1, n)] + out_rows
        specs = [whole] * len(operands)
        aliases = {}
        if result is not None:
            aliases = {len(operands): 0}
            operands.append(result)
            specs.append(pl.BlockSpec(memory_space=pl.ANY))
        result = call(
            functools.partial(output_kernel, n=n, offset=at),
            jax.ShapeDtypeStruct((row_count, cols), BF16),
            in_specs=specs,
            out_specs=pl.BlockSpec(memory_space=pl.ANY),
            scratch_shapes=[pltpu.VMEM((rows, cols), BF16), pltpu.SemaphoreType.DMA],
            input_output_aliases=aliases,
            flops=2 * rows * n * width * cols,
            moved=2 * n * width * cols,
            vmem=16 << 20,
        )(*operands)
    return result


def solution(mesh):
    return jax.shard_map(
        per_device,
        mesh=mesh,
        in_specs=(P("ctx", "head"), P(None, "head"), P(None, "head"), P("head"), P("head", None)),
        out_specs=P("ctx", "head"),
        check_vma=False,
    )
```

```python
import functools

import jax
import jax.numpy as jnp
import numpy as np
from jax import lax
from jax.experimental import pallas as pl
from jax.experimental.pallas import tpu as pltpu
from jax.sharding import PartitionSpec as P

DV = 64
FQK = 16
WIN = 64
CONV = 3
LANES = 128
FEATS = 160
QFEATS = 256
EDGE = 16
HALO = EDGE + 2 * WIN
PLANE = 4
F32 = jnp.float32
BF16 = jnp.bfloat16


def call(body, out_shape, *, flops=0, moved=0, vmem=48 << 20, **kwargs):
    return pl.pallas_call(
        body,
        out_shape=out_shape,
        compiler_params=pltpu.CompilerParams(vmem_limit_bytes=vmem),
        cost_estimate=pl.CostEstimate(flops=flops, bytes_accessed=moved, transcendentals=0),
        **kwargs,
    )


def feature_tables(heads):
    first = [FQK] + [FQK] * FQK
    second = [FQK] + list(range(FQK))
    weight = [1.0] + [1.0 / FQK**0.5] * FQK
    for i in range(FQK):
        for j in range(i, FQK):
            first.append(i)
            second.append(j)
            weight.append((1.0 if i == j else 2.0) / (2.0 * FQK))
    sel_a = np.zeros((heads, QFEATS, LANES), np.float32)
    sel_b = np.zeros((heads, QFEATS, LANES), np.float32)
    sel_w = np.zeros((heads, QFEATS, LANES), np.float32)
    for h in range(heads):
        for f, (i, j, w) in enumerate(zip(first, second, weight)):
            sel_a[h, f, (h * FQK + i) % LANES] = 1.0
            sel_b[h, f, (h * FQK + j) % LANES] = 1.0
            sel_w[h, f, (h * FQK + i) % LANES] = w
    return tuple(jnp.asarray(t, BF16) for t in (sel_a, sel_b, sel_w))


def mean_table():
    block = np.kron(np.eye(LANES // DV), np.ones((DV, DV))) / DV
    return jnp.asarray(np.concatenate([block, block], 0), BF16)


def head_mean(values, table):
    high = values.astype(BF16)
    low = (values - high.astype(F32)).astype(BF16)
    return jnp.dot(jnp.concatenate([high, low], 1), table, preferred_element_type=F32)


def nt_dot(a, b):
    return lax.dot_general(a, b, (((1,), (1,)), ((), ())), preferred_element_type=F32)


def with_one(vectors, lane, h):
    return jnp.where(lane == ((h + 1) * FQK) % LANES, 1.0, vectors).astype(BF16)


def arrange_kernel(w_ref, o_ref, *, heads):
    per_head = 2 * FQK + 3 * DV
    w = w_ref[...]
    at = 0
    for begin, width in ((0, FQK), (FQK, FQK), (2 * FQK, DV), (2 * FQK + DV, DV), (2 * FQK + 2 * DV, DV)):
        parts = [w[:, h * per_head + begin : h * per_head + begin + width] for h in range(heads)]
        total = heads * width
        padded = -(-total // LANES) * LANES
        if padded > total:
            parts.append(jnp.zeros((w.shape[0], padded - total), w.dtype))
        o_ref[:, at : at + padded] = jnp.concatenate(parts, 1)
        at += padded


def block_kernel(j_ref, mean_ref, conv_ref, sel_w_ref, sel_b_ref, w_ref, *refs, n, heads, extra, others, sends):
    xs, refs = refs[:n], refs[n:]
    prev_ref = None
    if not extra:
        prev_ref, refs = refs[0], refs[1:]
    other_refs, refs = refs[:others], refs[others:]
    q_ref, k_ref, v_ref, wq_ref, wk_ref, halo_ref, s_ref = refs[:7]
    send_refs, (ext_ref,) = refs[7 : 7 + sends], refs[7 + sends :]
    rows, depth = v_ref.shape[0], xs[0].shape[1]
    me = j_ref[0]

    def project(begin, width, skip):
        total = None
        for r in range(n):
            src = lax.rem(me - r + n, n)
            from_rows = pl.ds(pl.multiple_of(src * depth, depth), depth)
            part = jnp.dot(xs[r][skip:, :], w_ref[from_rows, begin : begin + width], preferred_element_type=F32)
            total = part if total is None else total + part
        return total.astype(BF16)

    widths = [ref.shape[1] for ref in (q_ref, k_ref, v_ref, wq_ref, wk_ref)]
    starts = [sum(widths[:i]) for i in range(5)]
    k_ref[...] = project(starts[1], widths[1], extra)
    raw = project(starts[2], widths[2], 0)
    if extra:
        ext_ref[...] = raw.astype(F32)
    else:
        ext_ref[0:EDGE, :] = prev_ref[0:EDGE, :].astype(F32)
        ext_ref[EDGE:, :] = raw.astype(F32)
    halo_ref[0:EDGE, :] = raw[raw.shape[0] - EDGE :]
    total = jnp.zeros((rows, widths[2]), F32)
    for tap in range(CONV):
        total = total + conv_ref[tap : tap + 1, :] * ext_ref[EDGE - tap : EDGE - tap + rows, :]
    v_ref[...] = total.astype(BF16)
    halo_ref[EDGE : EDGE + WIN, :] = v_ref[rows - WIN : rows, :]

    lane = lax.broadcasted_iota(jnp.int32, (rows, LANES), 1)
    low_half = lax.broadcasted_iota(jnp.int32, (FEATS, LANES), 1) < DV
    k = k_ref[...].astype(F32)
    for p in range(heads * DV // LANES):
        v = v_ref[:, p * LANES : (p + 1) * LANES]
        both = []
        for h in (2 * p, 2 * p + 1):
            own = with_one(k, lane, h)
            phi = nt_dot(sel_w_ref[h, 0:FEATS, :], own) * nt_dot(sel_b_ref[h, 0:FEATS, :], own)
            both.append(jnp.dot(phi.astype(BF16), v, preferred_element_type=F32))
        s_ref[p] = jnp.where(low_half, both[0], both[1])
    for r in range(sends):
        pair = jnp.bitwise_xor(j_ref[1], r)
        total = s_ref[pair]
        for ref in other_refs:
            total = total + ref[pair]
        send_refs[r][...] = total.astype(BF16)

    q_ref[...] = project(starts[0], widths[0], extra)
    for ref, start, width, scale in (
        (wk_ref, starts[4], widths[4], 1.0),
        (wq_ref, starts[3], widths[3], 1.0 / DV**0.5),
    ):
        got = project(start, width, extra)
        for p in range(width // LANES):
            cols = slice(p * LANES, (p + 1) * LANES)
            x = got[:, cols].astype(F32)
            x = x * lax.rsqrt(head_mean(x * x, mean_ref[...]) + 1e-6)
            ref[:, cols] = x.astype(BF16) * jnp.asarray(scale, BF16)
    halo_ref[EDGE + WIN : HALO, :] = wk_ref[rows - WIN : rows, :]


def attend_kernel(
    a_ref, sel_a_ref, sel_b_ref, prev_ref, q_ref, k_ref, v_ref, wq_ref, wk_ref, phi_ref, lin_ref, win_ref,
    vext_ref, kext_ref, *, heads, first
):
    rows = q_ref.shape[0]
    tile = 128
    span = tile + WIN
    vext_ref[0:WIN, :] = prev_ref[EDGE : EDGE + WIN, :]
    vext_ref[WIN : WIN + rows, :] = v_ref[...]
    kext_ref[0:WIN, :] = prev_ref[EDGE + WIN : HALO, :]
    kext_ref[WIN : WIN + rows, :] = wk_ref[...]
    lane = lax.broadcasted_iota(jnp.int32, (rows, LANES), 1)
    low_half = lane < DV
    causal = lax.broadcasted_iota(jnp.int32, (rows, rows), 1) <= lax.broadcasted_iota(jnp.int32, (rows, rows), 0)
    col = lax.broadcasted_iota(jnp.int32, (tile, span), 1)
    ahead = col - lax.broadcasted_iota(jnp.int32, (tile, span), 0)
    band = (ahead >= 1) & (ahead <= WIN)
    first_band = band
    if first:
        first_band = band & (col >= jnp.where(a_ref[2] == 0, WIN, 0))
    q = q_ref[...]
    q_full = q.astype(F32)
    k = k_ref[...]
    for p in range(heads * DV // LANES):
        cols = slice(p * LANES, (p + 1) * LANES)
        v = v_ref[:, cols]
        both = []
        for h in (2 * p, 2 * p + 1):
            own = with_one(q_full, lane, h)
            phi = nt_dot(own, sel_a_ref[h]) * nt_dot(own, sel_b_ref[h])
            phi_ref[:, h * QFEATS : (h + 1) * QFEATS] = phi.astype(BF16)
            own = jnp.where((lane >= h * FQK) & (lane < (h + 1) * FQK), q, jnp.zeros_like(q))
            t = nt_dot(own, k) * (1.0 / FQK**0.5) + 1.0
            kernel = jnp.where(causal, 0.5 * (t * t) + 0.5, 0.0).astype(BF16)
            both.append(jnp.dot(kernel, v, preferred_element_type=F32))
        lin_ref[:, cols] = jnp.where(low_half, both[0], both[1])
        for i in range(rows // tile):
            here = slice(i * tile, (i + 1) * tile)
            wq = wq_ref[here, cols]
            keys = kext_ref[i * tile : i * tile + span, cols]
            values = vext_ref[i * tile : i * tile + span, cols]
            both = []
            for half in range(2):
                keep = low_half[0:tile] if half == 0 else ~low_half[0:tile]
                scores = nt_dot(jnp.where(keep, wq, jnp.zeros_like(wq)), keys)
                expo = jnp.where(first_band if i == 0 else band, jnp.exp(scores), 0.0)
                weights = expo * (1.0 / jnp.sum(expo, axis=1, keepdims=True))
                both.append(jnp.dot(weights.astype(BF16), values, preferred_element_type=F32))
            win_ref[here, cols] = jnp.where(low_half[0:tile], both[0], both[1])


def finish_kernel(a_ref, mean_ref, gain_ref, *refs, heads, before):
    pairs = heads * DV // LANES
    prior_refs, refs = refs[:pairs], refs[pairs:]
    states, (phi_ref, lin_ref, win_ref, mix_ref, held_ref) = refs[:before], refs[before:]
    rows = phi_ref.shape[0]
    for r in range(pairs):
        held_ref[r] = prior_refs[r][...].astype(F32)
    low_half = lax.broadcasted_iota(jnp.int32, (rows, LANES), 1) < DV
    for p in range(pairs):
        cols = slice(p * LANES, (p + 1) * LANES)
        state = held_ref[jnp.bitwise_xor(a_ref[1], p)]
        for ref in states:
            state = state + ref[p]
        state = jnp.concatenate([state.astype(BF16), jnp.zeros((QFEATS - FEATS, LANES), BF16)], 0)
        both = [
            jnp.dot(phi_ref[:, h * QFEATS : (h + 1) * QFEATS], state, preferred_element_type=F32)
            for h in (2 * p, 2 * p + 1)
        ]
        lin = lin_ref[:, cols] + jnp.where(low_half, both[0], both[1])
        scale = lax.rsqrt(head_mean(lin * lin, mean_ref[...]) + 1e-5)
        mix_ref[:, cols] = (lin * scale * gain_ref[:, cols] + win_ref[:, cols]).astype(BF16)


def output_kernel(a_ref, own_ref, w_ref, *refs, n, offset, parts):
    others, weights, (o_ref, held_ref, sem) = refs[: n - 1], refs[n - 1 : n - 1 + parts * (n - 1)], refs[-3:]
    cols = held_ref.shape[1]
    mine = pl.ds(pl.multiple_of(a_ref[0] * cols, cols), cols)
    total = jnp.dot(own_ref[...], w_ref[:, mine], preferred_element_type=F32).astype(BF16).astype(F32)
    for r, m_ref in enumerate(others):
        part = None
        for i in range(parts):
            ref = weights[r * parts + i]
            depth = ref.shape[0]
            at = depth * (jnp.bitwise_xor(a_ref[2] % 2, i) if parts > 1 else 0)
            got = jnp.dot(m_ref[:, pl.ds(pl.multiple_of(at, depth), depth)], ref[...], preferred_element_type=F32)
            part = got if part is None else part + got
        total = total + part.astype(BF16).astype(F32)
    held_ref[...] = total.astype(BF16)
    copy = pltpu.make_async_copy(held_ref, o_ref.at[pl.ds(offset, held_ref.shape[0]), :], sem)
    copy.start()
    copy.wait()


def pick_kernel(a_ref, w_ref, o_ref):
    o_ref[...] = w_ref[...]


def exchange(value, axis, flip):
    count = lax.axis_size(axis)
    return lax.ppermute(value, axis, [(i, i ^ flip) for i in range(count)])


def plane_kernel(a_ref, *refs):
    helds, plane_ref, ahead_refs = refs[:PLANE], refs[PLANE], refs[PLANE + 1 :]
    place = a_ref[1]
    held = [ref[...].astype(F32) for ref in helds]
    plane_ref[...] = (held[0] + held[1] + held[2] + held[3]).astype(BF16)
    for r in range(PLANE):
        total = jnp.zeros_like(held[0])
        for s in range(PLANE):
            before = jnp.bitwise_xor(place, s) < jnp.bitwise_xor(place, r)
            total = total + held[s] * before.astype(F32)
        ahead_refs[r][...] = total


def earlier_kernel(_, *refs, planes):
    ahead_refs, earlier_refs, back_refs = refs[:PLANE], refs[PLANE : PLANE + planes], refs[PLANE + planes :]
    earlier = jnp.zeros(ahead_refs[0].shape, F32)
    for ref in earlier_refs:
        earlier = earlier + ref[...].astype(F32)
    for r in range(PLANE):
        back_refs[r][...] = (ahead_refs[r][...] + earlier).astype(BF16)


def after(value, earlier):
    return lax.optimization_barrier((value, earlier))[0]


def prior_in_planes(own, places, beside):
    ctx = lax.axis_size("ctx")
    whole = pl.BlockSpec(memory_space=pltpu.VMEM)
    scalar = pl.BlockSpec(memory_space=pltpu.SMEM)
    narrow = jax.ShapeDtypeStruct((FEATS, LANES), BF16)
    wide = jax.ShapeDtypeStruct((FEATS, LANES), F32)
    held = [own[0]] + [exchange(own[r], "ctx", r) for r in range(1, PLANE)]
    plane, *ahead = call(
        plane_kernel,
        [narrow] + [wide] * PLANE,
        in_specs=[scalar] + [whole] * PLANE,
        out_specs=[whole] * (1 + PLANE),
        moved=24 * FEATS * LANES,
        vmem=4 << 20,
    )(after(places, beside[0]), *held)
    earlier = []
    for d in range(1, ctx // PLANE):
        pairs = [(i, i + d * PLANE) for i in range(ctx - d * PLANE)]
        earlier.append(lax.ppermute(plane, "ctx", pairs))
    back = call(
        functools.partial(earlier_kernel, planes=len(earlier)),
        [narrow] * PLANE,
        in_specs=[scalar] + [whole] * (PLANE + len(earlier)),
        out_specs=[whole] * PLANE,
        moved=24 * FEATS * LANES,
        vmem=4 << 20,
    )(after(places, beside[1]), *ahead, *earlier)
    return back[0], [back[0]] + [exchange(back[r], "ctx", r) for r in range(1, PLANE)]


def prior_by_doubling(total, position):
    ctx = lax.axis_size("ctx")
    prior = jnp.zeros_like(total)
    bit = 1
    while bit < ctx:
        got = exchange(total.astype(BF16), "ctx", bit).astype(F32)
        prior = prior + jnp.where((position & bit) != 0, got, 0.0)
        total = total + got
        bit *= 2
    return [prior[p].astype(BF16) for p in range(total.shape[0])]


def per_device(hidden_in, proj_weight, conv_weight, norm_gain, out_weight):
    n = lax.axis_size("head")
    ctx = lax.axis_size("ctx")
    me = lax.axis_index("head").astype(jnp.int32)
    position = lax.axis_index("ctx").astype(jnp.int32)
    row_count = hidden_in.shape[0]
    model = proj_weight.shape[0]
    heads = out_weight.shape[0] // DV
    width = heads * DV
    pairs = width // LANES
    in_planes = pairs == PLANE and ctx % PLANE == 0
    places = jnp.stack([me, position % PLANE if in_planes else jnp.zeros_like(position), position])
    hidden_in, places = lax.optimization_barrier((hidden_in, places))
    step = row_count // 8
    blocks = [(0, 2 * step), (2 * step, 2 * step), (4 * step, 2 * step), (6 * step, step), (7 * step, step)]
    last = len(blocks) - 1
    sel_a, sel_b, sel_w = feature_tables(heads)
    means = mean_table()
    gain = norm_gain.reshape(1, width)
    whole = pl.BlockSpec(memory_space=pltpu.VMEM)
    scalar = pl.BlockSpec(memory_space=pltpu.SMEM)

    def from_head(value, by):
        return lax.ppermute(value, "head", [(i, (i + by) % n) for i in range(n)])

    pieces = {}
    for b in [last] + list(range(last)):
        at, rows = blocks[b]
        extra = EDGE if b == last else 0
        own = hidden_in[at - extra : at + rows]
        pieces[b] = [own] + [from_head(own, r) for r in range(1, n)]

    cols = out_weight.shape[1] // n
    out_parts = 2 if width // 2 % LANES == 0 and ctx % 2 == 0 else 1
    share = width // out_parts
    fetched = []
    for r in range(1, n):
        block = call(
            pick_kernel,
            jax.ShapeDtypeStruct((share, cols), BF16),
            grid_spec=pltpu.PrefetchScalarGridSpec(
                num_scalar_prefetch=1,
                grid=(1,),
                in_specs=[
                    pl.BlockSpec((share, cols), functools.partial(lambda i, a, r: (a[2] % out_parts, (a[0] + r) % n), r=r))
                ],
                out_specs=pl.BlockSpec((share, cols), lambda i, a: (0, 0)),
            ),
            moved=4 * share * cols,
            vmem=8 << 20,
        )(places, out_weight)
        fetched.append(from_head(after(block, pieces[0][1]), r))

    qk_width = -(-heads * FQK // LANES) * LANES
    arranged_width = 2 * qk_width + 3 * width
    slab = 256
    arranged = call(
        functools.partial(arrange_kernel, heads=heads),
        jax.ShapeDtypeStruct((model, arranged_width), BF16),
        grid=(model // slab,),
        in_specs=[pl.BlockSpec((slab, proj_weight.shape[1]), lambda i: (i, 0))],
        out_specs=pl.BlockSpec((slab, arranged_width), lambda i: (i, 0)),
        moved=4 * model * arranged_width,
        vmem=32 << 20,
    )(proj_weight)

    def do_block(b, prev, behind, others=()):
        rows = blocks[b][1]
        extra = EDGE if prev is None else 0
        sends = PLANE if in_planes and others else 0
        tokens = places if behind is None else after(places, behind)
        shapes = [jax.ShapeDtypeStruct((rows, w), BF16) for w in (qk_width, qk_width, width, width, width)]
        shapes.append(jax.ShapeDtypeStruct((HALO, width), BF16))
        shapes.append(jax.ShapeDtypeStruct((pairs, FEATS, LANES), F32))
        shapes += [jax.ShapeDtypeStruct((FEATS, LANES), BF16)] * sends
        operands = [tokens, means, conv_weight, sel_w, sel_b, arranged, *pieces[b]]
        if prev is not None:
            operands.append(prev)
        operands += others
        return call(
            functools.partial(
                block_kernel, n=n, heads=heads, extra=extra, others=len(others), sends=sends
            ),
            shapes,
            in_specs=[scalar] + [whole] * (len(operands) - 1),
            out_specs=[whole] * len(shapes),
            scratch_shapes=[pltpu.VMEM((EDGE + rows, width), F32)],
            flops=2 * rows * model * arranged_width + 6 * rows * FEATS * LANES * heads,
            moved=2 * model * arranged_width,
            vmem=32 << 20,
        )(*operands)

    def attend(b, prev):
        rows = blocks[b][1]
        q, k, v, wq, wk = done[b][:5]
        return call(
            functools.partial(attend_kernel, heads=heads, first=b == 0),
            [jax.ShapeDtypeStruct((rows, heads * QFEATS), BF16)] + [jax.ShapeDtypeStruct((rows, width), F32)] * 2,
            in_specs=[scalar] + [whole] * 8,
            out_specs=[whole] * 3,
            scratch_shapes=[pltpu.VMEM((WIN + rows, width), BF16)] * 2,
            flops=heads * rows * 4096 * 256,
            moved=16 * rows * width,
            vmem=16 << 20,
        )(places, sel_a, sel_b, prev, q, k, v, wq, wk)

    done, attended = {}, {}
    done[last] = do_block(last, None, None)
    halo = lax.ppermute(done[last][5], "ctx", [(i, i + 1) for i in range(ctx - 1)])
    for b in range(last):
        prev = halo if b == 0 else done[b - 1][5]
        others = [done[c][6] for c in [last] + list(range(b))] if b == last - 1 else ()
        done[b] = do_block(b, prev, attended[b - 1][1] if b else None, others)
        if b < last - 1:
            attended[b] = attend(b, prev)

    for b in (last - 1, last):
        attended[b] = attend(b, done[b - 1][5])
    if in_planes:
        beside = [attended[b][1] for b in (last - 1, last)]
        mark, priors = prior_in_planes(done[last - 1][7:], places, beside)
    else:
        mark = sum(done[b][6] for b in range(last + 1))
        priors = prior_by_doubling(mark, position)

    out_rows = []
    for got in fetched:
        out_rows += [got] + ([exchange(after(got, mark), "ctx", 1)] if out_parts > 1 else [])

    result = mixed = None
    for b in (3, 0, 1, 2, 4):
        at, rows = blocks[b]
        mixed = call(
            functools.partial(finish_kernel, heads=heads, before=b),
            jax.ShapeDtypeStruct((rows, width), BF16),
            in_specs=[scalar] + [whole] * (2 + pairs + b + 3),
            out_specs=whole,
            scratch_shapes=[pltpu.VMEM((pairs, FEATS, LANES), F32)],
            flops=6 * rows * QFEATS * LANES * heads,
            moved=12 * rows * width,
            vmem=16 << 20,
        )(places if mixed is None else after(places, mixed), means, gain, *priors, *[done[c][6] for c in range(b)], *attended[b])
        operands = [places, mixed, out_weight] + [from_head(mixed, r) for r in range(1, n)] + out_rows
        specs = [scalar] + [whole] * (len(operands) - 1)
        aliases = {}
        if result is not None:
            aliases = {len(operands): 0}
            operands.append(result)
            specs.append(pl.BlockSpec(memory_space=pl.ANY))
        result = call(
            functools.partial(output_kernel, n=n, offset=at, parts=out_parts),
            jax.ShapeDtypeStruct((row_count, cols), BF16),
            in_specs=specs,
            out_specs=pl.BlockSpec(memory_space=pl.ANY),
            scratch_shapes=[pltpu.VMEM((rows, cols), BF16), pltpu.SemaphoreType.DMA],
            input_output_aliases=aliases,
            flops=2 * rows * n * width * cols,
            moved=2 * n * width * cols,
            vmem=16 << 20,
        )(*operands)
    return result


def solution(mesh):
    return jax.shard_map(
        per_device,
        mesh=mesh,
        in_specs=(P("ctx", "head"), P(None, "head"), P(None, "head"), P("head"), P("head", None)),
        out_specs=P("ctx", "head"),
        check_vma=False,
    )
```

```python
import functools

import jax
import jax.numpy as jnp
import numpy as np
from jax import lax
from jax.experimental import pallas as pl
from jax.experimental.pallas import tpu as pltpu
from jax.sharding import PartitionSpec as P

DV = 64
FQK = 16
WIN = 64
CONV = 3
LANES = 128
FEATS = 160
QFEATS = 256
EDGE = 16
HALO = EDGE + 2 * WIN
PLANE = 4
F32 = jnp.float32
BF16 = jnp.bfloat16


def call(body, out_shape, *, flops=0, moved=0, vmem=48 << 20, **kwargs):
    return pl.pallas_call(
        body,
        out_shape=out_shape,
        compiler_params=pltpu.CompilerParams(vmem_limit_bytes=vmem),
        cost_estimate=pl.CostEstimate(flops=1, bytes_accessed=1, transcendentals=0),
        **kwargs,
    )


def feature_tables(heads):
    first = [FQK] + [FQK] * FQK
    second = [FQK] + list(range(FQK))
    weight = [1.0] + [1.0 / FQK**0.5] * FQK
    for i in range(FQK):
        for j in range(i, FQK):
            first.append(i)
            second.append(j)
            weight.append((1.0 if i == j else 2.0) / (2.0 * FQK))
    sel_a = np.zeros((heads, QFEATS, LANES), np.float32)
    sel_b = np.zeros((heads, QFEATS, LANES), np.float32)
    sel_w = np.zeros((heads, QFEATS, LANES), np.float32)
    for h in range(heads):
        for f, (i, j, w) in enumerate(zip(first, second, weight)):
            sel_a[h, f, (h * FQK + i) % LANES] = 1.0
            sel_b[h, f, (h * FQK + j) % LANES] = 1.0
            sel_w[h, f, (h * FQK + i) % LANES] = w
    return tuple(jnp.asarray(t, BF16) for t in (sel_a, sel_b, sel_w))


def mean_table():
    block = np.kron(np.eye(LANES // DV), np.ones((DV, DV))) / DV
    return jnp.asarray(np.concatenate([block, block], 0), BF16)


def head_mean(values, table):
    high = values.astype(BF16)
    low = (values - high.astype(F32)).astype(BF16)
    return jnp.dot(jnp.concatenate([high, low], 1), table, preferred_element_type=F32)


def nt_dot(a, b):
    return lax.dot_general(a, b, (((1,), (1,)), ((), ())), preferred_element_type=F32)


def with_one(vectors, lane, h):
    return jnp.where(lane == ((h + 1) * FQK) % LANES, 1.0, vectors).astype(BF16)


def arrange_kernel(w_ref, o_ref, *, heads):
    per_head = 2 * FQK + 3 * DV
    w = w_ref[...]
    at = 0
    for begin, width in ((0, FQK), (FQK, FQK), (2 * FQK, DV), (2 * FQK + DV, DV), (2 * FQK + 2 * DV, DV)):
        parts = [w[:, h * per_head + begin : h * per_head + begin + width] for h in range(heads)]
        total = heads * width
        padded = -(-total // LANES) * LANES
        if padded > total:
            parts.append(jnp.zeros((w.shape[0], padded - total), w.dtype))
        o_ref[:, at : at + padded] = jnp.concatenate(parts, 1)
        at += padded


def block_kernel(j_ref, mean_ref, conv_ref, sel_w_ref, sel_b_ref, w_ref, *refs, n, heads, extra, others, sends):
    xs, refs = refs[:n], refs[n:]
    prev_ref = None
    if not extra:
        prev_ref, refs = refs[0], refs[1:]
    other_refs, refs = refs[:others], refs[others:]
    q_ref, k_ref, v_ref, wq_ref, wk_ref, halo_ref, s_ref = refs[:7]
    send_refs, (ext_ref,) = refs[7 : 7 + sends], refs[7 + sends :]
    rows, depth = v_ref.shape[0], xs[0].shape[1]
    me = j_ref[0]

    def project(begin, width, skip):
        total = None
        for r in range(n):
            src = lax.rem(me - r + n, n)
            from_rows = pl.ds(pl.multiple_of(src * depth, depth), depth)
            part = jnp.dot(xs[r][skip:, :], w_ref[from_rows, begin : begin + width], preferred_element_type=F32)
            total = part if total is None else total + part
        return total.astype(BF16)

    widths = [ref.shape[1] for ref in (q_ref, k_ref, v_ref, wq_ref, wk_ref)]
    starts = [sum(widths[:i]) for i in range(5)]
    k_ref[...] = project(starts[1], widths[1], extra)
    raw = project(starts[2], widths[2], 0)
    if extra:
        ext_ref[...] = raw.astype(F32)
    else:
        ext_ref[0:EDGE, :] = prev_ref[0:EDGE, :].astype(F32)
        ext_ref[EDGE:, :] = raw.astype(F32)
    halo_ref[0:EDGE, :] = raw[raw.shape[0] - EDGE :]
    total = jnp.zeros((rows, widths[2]), F32)
    for tap in range(CONV):
        total = total + conv_ref[tap : tap + 1, :] * ext_ref[EDGE - tap : EDGE - tap + rows, :]
    v_ref[...] = total.astype(BF16)
    halo_ref[EDGE : EDGE + WIN, :] = v_ref[rows - WIN : rows, :]

    lane = lax.broadcasted_iota(jnp.int32, (rows, LANES), 1)
    low_half = lax.broadcasted_iota(jnp.int32, (FEATS, LANES), 1) < DV
    k = k_ref[...].astype(F32)
    for p in range(heads * DV // LANES):
        v = v_ref[:, p * LANES : (p + 1) * LANES]
        both = []
        for h in (2 * p, 2 * p + 1):
            own = with_one(k, lane, h)
            phi = nt_dot(sel_w_ref[h, 0:FEATS, :], own) * nt_dot(sel_b_ref[h, 0:FEATS, :], own)
            both.append(jnp.dot(phi.astype(BF16), v, preferred_element_type=F32))
        s_ref[p] = jnp.where(low_half, both[0], both[1])
    for r in range(sends):
        pair = jnp.bitwise_xor(j_ref[1], r)
        total = s_ref[pair]
        for ref in other_refs:
            total = total + ref[pair]
        send_refs[r][...] = total.astype(BF16)

    q_ref[...] = project(starts[0], widths[0], extra)
    for ref, start, width, scale in (
        (wk_ref, starts[4], widths[4], 1.0),
        (wq_ref, starts[3], widths[3], 1.0 / DV**0.5),
    ):
        got = project(start, width, extra)
        for p in range(width // LANES):
            cols = slice(p * LANES, (p + 1) * LANES)
            x = got[:, cols].astype(F32)
            x = x * lax.rsqrt(head_mean(x * x, mean_ref[...]) + 1e-6)
            ref[:, cols] = x.astype(BF16) * jnp.asarray(scale, BF16)
    halo_ref[EDGE + WIN : HALO, :] = wk_ref[rows - WIN : rows, :]


def attend_kernel(
    a_ref, sel_a_ref, sel_b_ref, prev_ref, q_ref, k_ref, v_ref, wq_ref, wk_ref, phi_ref, lin_ref, win_ref,
    vext_ref, kext_ref, *, heads, first
):
    rows = q_ref.shape[0]
    tile = 128
    span = tile + WIN
    vext_ref[0:WIN, :] = prev_ref[EDGE : EDGE + WIN, :]
    vext_ref[WIN : WIN + rows, :] = v_ref[...]
    kext_ref[0:WIN, :] = prev_ref[EDGE + WIN : HALO, :]
    kext_ref[WIN : WIN + rows, :] = wk_ref[...]
    lane = lax.broadcasted_iota(jnp.int32, (rows, LANES), 1)
    low_half = lane < DV
    causal = lax.broadcasted_iota(jnp.int32, (rows, rows), 1) <= lax.broadcasted_iota(jnp.int32, (rows, rows), 0)
    col = lax.broadcasted_iota(jnp.int32, (tile, span), 1)
    ahead = col - lax.broadcasted_iota(jnp.int32, (tile, span), 0)
    band = (ahead >= 1) & (ahead <= WIN)
    first_band = band
    if first:
        first_band = band & (col >= jnp.where(a_ref[2] == 0, WIN, 0))
    q = q_ref[...]
    q_full = q.astype(F32)
    k = k_ref[...]
    for p in range(heads * DV // LANES):
        cols = slice(p * LANES, (p + 1) * LANES)
        v = v_ref[:, cols]
        both = []
        for h in (2 * p, 2 * p + 1):
            own = with_one(q_full, lane, h)
            phi = nt_dot(own, sel_a_ref[h]) * nt_dot(own, sel_b_ref[h])
            phi_ref[:, h * QFEATS : (h + 1) * QFEATS] = phi.astype(BF16)
            own = jnp.where((lane >= h * FQK) & (lane < (h + 1) * FQK), q, jnp.zeros_like(q))
            t = nt_dot(own, k) * (1.0 / FQK**0.5) + 1.0
            kernel = jnp.where(causal, 0.5 * (t * t) + 0.5, 0.0).astype(BF16)
            both.append(jnp.dot(kernel, v, preferred_element_type=F32))
        lin_ref[:, cols] = jnp.where(low_half, both[0], both[1])
        for i in range(rows // tile):
            here = slice(i * tile, (i + 1) * tile)
            wq = wq_ref[here, cols]
            keys = kext_ref[i * tile : i * tile + span, cols]
            values = vext_ref[i * tile : i * tile + span, cols]
            both = []
            for half in range(2):
                keep = low_half[0:tile] if half == 0 else ~low_half[0:tile]
                scores = nt_dot(jnp.where(keep, wq, jnp.zeros_like(wq)), keys)
                expo = jnp.where(first_band if i == 0 else band, jnp.exp(scores), 0.0)
                weights = expo * (1.0 / jnp.sum(expo, axis=1, keepdims=True))
                both.append(jnp.dot(weights.astype(BF16), values, preferred_element_type=F32))
            win_ref[here, cols] = jnp.where(low_half[0:tile], both[0], both[1])


def finish_kernel(a_ref, mean_ref, gain_ref, *refs, heads, before):
    pairs = heads * DV // LANES
    prior_refs, refs = refs[:pairs], refs[pairs:]
    states, (phi_ref, lin_ref, win_ref, mix_ref, held_ref) = refs[:before], refs[before:]
    rows = phi_ref.shape[0]
    for r in range(pairs):
        held_ref[r] = prior_refs[r][...].astype(F32)
    low_half = lax.broadcasted_iota(jnp.int32, (rows, LANES), 1) < DV
    for p in range(pairs):
        cols = slice(p * LANES, (p + 1) * LANES)
        state = held_ref[jnp.bitwise_xor(a_ref[1], p)]
        for ref in states:
            state = state + ref[p]
        state = jnp.concatenate([state.astype(BF16), jnp.zeros((QFEATS - FEATS, LANES), BF16)], 0)
        both = [
            jnp.dot(phi_ref[:, h * QFEATS : (h + 1) * QFEATS], state, preferred_element_type=F32)
            for h in (2 * p, 2 * p + 1)
        ]
        lin = lin_ref[:, cols] + jnp.where(low_half, both[0], both[1])
        scale = lax.rsqrt(head_mean(lin * lin, mean_ref[...]) + 1e-5)
        mix_ref[:, cols] = (lin * scale * gain_ref[:, cols] + win_ref[:, cols]).astype(BF16)


def output_kernel(a_ref, own_ref, w_ref, *refs, n, offset, parts):
    others, weights, (o_ref, held_ref, sem) = refs[: n - 1], refs[n - 1 : n - 1 + parts * (n - 1)], refs[-3:]
    cols = held_ref.shape[1]
    mine = pl.ds(pl.multiple_of(a_ref[0] * cols, cols), cols)
    total = jnp.dot(own_ref[...], w_ref[:, mine], preferred_element_type=F32).astype(BF16).astype(F32)
    for r, m_ref in enumerate(others):
        part = None
        for i in range(parts):
            ref = weights[r * parts + i]
            depth = ref.shape[0]
            at = depth * (jnp.bitwise_xor(a_ref[2] % 2, i) if parts > 1 else 0)
            got = jnp.dot(m_ref[:, pl.ds(pl.multiple_of(at, depth), depth)], ref[...], preferred_element_type=F32)
            part = got if part is None else part + got
        total = total + part.astype(BF16).astype(F32)
    held_ref[...] = total.astype(BF16)
    copy = pltpu.make_async_copy(held_ref, o_ref.at[pl.ds(offset, held_ref.shape[0]), :], sem)
    copy.start()
    copy.wait()


def pick_kernel(a_ref, w_ref, o_ref):
    o_ref[...] = w_ref[...]


def exchange(value, axis, flip):
    count = lax.axis_size(axis)
    return lax.ppermute(value, axis, [(i, i ^ flip) for i in range(count)])


def plane_kernel(a_ref, *refs):
    helds, plane_ref, ahead_refs = refs[:PLANE], refs[PLANE], refs[PLANE + 1 :]
    place = a_ref[1]
    held = [ref[...].astype(F32) for ref in helds]
    plane_ref[...] = (held[0] + held[1] + held[2] + held[3]).astype(BF16)
    for r in range(PLANE):
        total = jnp.zeros_like(held[0])
        for s in range(PLANE):
            before = jnp.bitwise_xor(place, s) < jnp.bitwise_xor(place, r)
            total = total + held[s] * before.astype(F32)
        ahead_refs[r][...] = total


def earlier_kernel(_, *refs, planes):
    ahead_refs, earlier_refs, back_refs = refs[:PLANE], refs[PLANE : PLANE + planes], refs[PLANE + planes :]
    earlier = jnp.zeros(ahead_refs[0].shape, F32)
    for ref in earlier_refs:
        earlier = earlier + ref[...].astype(F32)
    for r in range(PLANE):
        back_refs[r][...] = (ahead_refs[r][...] + earlier).astype(BF16)


def after(value, earlier):
    return lax.optimization_barrier((value, earlier))[0]


def prior_in_planes(own, places, beside):
    ctx = lax.axis_size("ctx")
    whole = pl.BlockSpec(memory_space=pltpu.VMEM)
    scalar = pl.BlockSpec(memory_space=pltpu.SMEM)
    narrow = jax.ShapeDtypeStruct((FEATS, LANES), BF16)
    wide = jax.ShapeDtypeStruct((FEATS, LANES), F32)
    held = [own[0]] + [exchange(own[r], "ctx", r) for r in range(1, PLANE)]
    plane, *ahead = call(
        plane_kernel,
        [narrow] + [wide] * PLANE,
        in_specs=[scalar] + [whole] * PLANE,
        out_specs=[whole] * (1 + PLANE),
        moved=24 * FEATS * LANES,
        vmem=4 << 20,
    )(after(places, beside[0]), *held)
    earlier = []
    for d in range(1, ctx // PLANE):
        pairs = [(i, i + d * PLANE) for i in range(ctx - d * PLANE)]
        earlier.append(lax.ppermute(plane, "ctx", pairs))
    back = call(
        functools.partial(earlier_kernel, planes=len(earlier)),
        [narrow] * PLANE,
        in_specs=[scalar] + [whole] * (PLANE + len(earlier)),
        out_specs=[whole] * PLANE,
        moved=24 * FEATS * LANES,
        vmem=4 << 20,
    )(after(places, beside[1]), *ahead, *earlier)
    return back[0], [back[0]] + [exchange(back[r], "ctx", r) for r in range(1, PLANE)]


def prior_by_doubling(total, position):
    ctx = lax.axis_size("ctx")
    prior = jnp.zeros_like(total)
    bit = 1
    while bit < ctx:
        got = exchange(total.astype(BF16), "ctx", bit).astype(F32)
        prior = prior + jnp.where((position & bit) != 0, got, 0.0)
        total = total + got
        bit *= 2
    return [prior[p].astype(BF16) for p in range(total.shape[0])]


def per_device(hidden_in, proj_weight, conv_weight, norm_gain, out_weight):
    n = lax.axis_size("head")
    ctx = lax.axis_size("ctx")
    me = lax.axis_index("head").astype(jnp.int32)
    position = lax.axis_index("ctx").astype(jnp.int32)
    row_count = hidden_in.shape[0]
    model = proj_weight.shape[0]
    heads = out_weight.shape[0] // DV
    width = heads * DV
    pairs = width // LANES
    in_planes = pairs == PLANE and ctx % PLANE == 0
    places = jnp.stack([me, position % PLANE if in_planes else jnp.zeros_like(position), position])
    hidden_in, places = lax.optimization_barrier((hidden_in, places))
    step = row_count // 8
    blocks = [(0, 2 * step), (2 * step, 2 * step), (4 * step, 2 * step), (6 * step, step), (7 * step, step)]
    last = len(blocks) - 1
    sel_a, sel_b, sel_w = feature_tables(heads)
    means = mean_table()
    gain = norm_gain.reshape(1, width)
    whole = pl.BlockSpec(memory_space=pltpu.VMEM)
    scalar = pl.BlockSpec(memory_space=pltpu.SMEM)

    def from_head(value, by):
        return lax.ppermute(value, "head", [(i, (i + by) % n) for i in range(n)])

    pieces = {}

    def send_block(b, behind=None):
        at, rows = blocks[b]
        extra = EDGE if b == last else 0
        own = hidden_in[at - extra : at + rows]
        if behind is not None:
            own = after(own, behind)
        pieces[b] = [own] + [from_head(own, r) for r in range(1, n)]

    send_block(last)
    send_block(0, pieces[last][0])
    for b in range(1, last):
        send_block(b, pieces[last][0])

    cols = out_weight.shape[1] // n
    out_parts = 2 if width // 2 % LANES == 0 and ctx % 2 == 0 else 1
    share = width // out_parts
    fetched = []
    for r in range(1, n):
        block = call(
            pick_kernel,
            jax.ShapeDtypeStruct((share, cols), BF16),
            grid_spec=pltpu.PrefetchScalarGridSpec(
                num_scalar_prefetch=1,
                grid=(1,),
                in_specs=[
                    pl.BlockSpec((share, cols), functools.partial(lambda i, a, r: (a[2] % out_parts, (a[0] + r) % n), r=r))
                ],
                out_specs=pl.BlockSpec((share, cols), lambda i, a: (0, 0)),
            ),
            moved=4 * share * cols,
            vmem=8 << 20,
        )(places, out_weight)
        fetched.append(from_head(after(block, pieces[1][-1]), r))

    qk_width = -(-heads * FQK // LANES) * LANES
    arranged_width = 2 * qk_width + 3 * width
    slab = 256
    arranged = call(
        functools.partial(arrange_kernel, heads=heads),
        jax.ShapeDtypeStruct((model, arranged_width), BF16),
        grid=(model // slab,),
        in_specs=[pl.BlockSpec((slab, proj_weight.shape[1]), lambda i: (i, 0))],
        out_specs=pl.BlockSpec((slab, arranged_width), lambda i: (i, 0)),
        moved=4 * model * arranged_width,
        vmem=32 << 20,
    )(proj_weight)

    def do_block(b, prev, behind, others=()):
        rows = blocks[b][1]
        extra = EDGE if prev is None else 0
        sends = PLANE if in_planes and others else 0
        tokens = places if behind is None else after(places, behind)
        shapes = [jax.ShapeDtypeStruct((rows, w), BF16) for w in (qk_width, qk_width, width, width, width)]
        shapes.append(jax.ShapeDtypeStruct((HALO, width), BF16))
        shapes.append(jax.ShapeDtypeStruct((pairs, FEATS, LANES), F32))
        shapes += [jax.ShapeDtypeStruct((FEATS, LANES), BF16)] * sends
        operands = [tokens, means, conv_weight, sel_w, sel_b, arranged, *pieces[b]]
        if prev is not None:
            operands.append(prev)
        operands += others
        return call(
            functools.partial(
                block_kernel, n=n, heads=heads, extra=extra, others=len(others), sends=sends
            ),
            shapes,
            in_specs=[scalar] + [whole] * (len(operands) - 1),
            out_specs=[whole] * len(shapes),
            scratch_shapes=[pltpu.VMEM((EDGE + rows, width), F32)],
            flops=2 * rows * model * arranged_width + 6 * rows * FEATS * LANES * heads,
            moved=2 * model * arranged_width,
            vmem=32 << 20,
        )(*operands)

    def attend(b, prev):
        rows = blocks[b][1]
        q, k, v, wq, wk = done[b][:5]
        return call(
            functools.partial(attend_kernel, heads=heads, first=b == 0),
            [jax.ShapeDtypeStruct((rows, heads * QFEATS), BF16)] + [jax.ShapeDtypeStruct((rows, width), F32)] * 2,
            in_specs=[scalar] + [whole] * 8,
            out_specs=[whole] * 3,
            scratch_shapes=[pltpu.VMEM((WIN + rows, width), BF16)] * 2,
            flops=heads * rows * 4096 * 256,
            moved=16 * rows * width,
            vmem=16 << 20,
        )(places, sel_a, sel_b, prev, q, k, v, wq, wk)

    done, attended = {}, {}
    done[last] = do_block(last, None, None)
    halo = lax.ppermute(done[last][5], "ctx", [(i, i + 1) for i in range(ctx - 1)])
    for b in range(last):
        prev = halo if b == 0 else done[b - 1][5]
        others = [done[c][6] for c in [last] + list(range(b))] if b == last - 1 else ()
        done[b] = do_block(b, prev, attended[b - 1][1] if b - 1 in attended else None, others)
        if b < last - 2:
            attended[b] = attend(b, prev)

    for b in range(last - 2, last + 1):
        attended[b] = attend(b, done[b - 1][5])
    if in_planes:
        beside = [attended[b][1] for b in (last - 2, last - 1)]
        mark, priors = prior_in_planes(done[last - 1][7:], places, beside)
    else:
        mark = sum(done[b][6] for b in range(last + 1))
        priors = prior_by_doubling(mark, position)

    out_rows = []
    for got in fetched:
        out_rows += [got] + ([exchange(after(got, mark), "ctx", 1)] if out_parts > 1 else [])

    result = None
    arrived = []
    for i, b in enumerate((3, 0, 1, 2, 4)):
        at, rows = blocks[b]
        behind = after(places, arrived[i - 2] if i >= 2 else attended[last][1])
        mixed = call(
            functools.partial(finish_kernel, heads=heads, before=b),
            jax.ShapeDtypeStruct((rows, width), BF16),
            in_specs=[scalar] + [whole] * (2 + pairs + b + 3),
            out_specs=whole,
            scratch_shapes=[pltpu.VMEM((pairs, FEATS, LANES), F32)],
            flops=6 * rows * QFEATS * LANES * heads,
            moved=12 * rows * width,
            vmem=16 << 20,
        )(behind, means, gain, *priors, *[done[c][6] for c in range(b)], *attended[b])
        others = [from_head(mixed, r) for r in range(1, n)]
        arrived.append(others[-1])
        operands = [places, mixed, out_weight] + others + out_rows
        specs = [scalar] + [whole] * (len(operands) - 1)
        aliases = {}
        if result is not None:
            aliases = {len(operands): 0}
            operands.append(result)
            specs.append(pl.BlockSpec(memory_space=pl.ANY))
        result = call(
            functools.partial(output_kernel, n=n, offset=at, parts=out_parts),
            jax.ShapeDtypeStruct((row_count, cols), BF16),
            in_specs=specs,
            out_specs=pl.BlockSpec(memory_space=pl.ANY),
            scratch_shapes=[pltpu.VMEM((rows, cols), BF16), pltpu.SemaphoreType.DMA],
            input_output_aliases=aliases,
            flops=2 * rows * n * width * cols,
            moved=2 * n * width * cols,
            vmem=16 << 20,
        )(*operands)
    return result


def solution(mesh):
    return jax.shard_map(
        per_device,
        mesh=mesh,
        in_specs=(P("ctx", "head"), P(None, "head"), P(None, "head"), P("head"), P("head", None)),
        out_specs=P("ctx", "head"),
        check_vma=False,
    )
```

```python
import functools

import jax
import jax.numpy as jnp
import numpy as np
from jax import lax
from jax.experimental import pallas as pl
from jax.experimental.pallas import tpu as pltpu
from jax.sharding import PartitionSpec as P

DV = 64
FQK = 16
WIN = 64
CONV = 3
LANES = 128
FEATS = 160
QFEATS = 256
EDGE = 16
HALO = EDGE + 2 * WIN
PLANE = 4
F32 = jnp.float32
BF16 = jnp.bfloat16


def call(body, out_shape, *, flops=0, moved=0, vmem=48 << 20, **kwargs):
    return pl.pallas_call(
        body,
        out_shape=out_shape,
        compiler_params=pltpu.CompilerParams(vmem_limit_bytes=vmem),
        cost_estimate=pl.CostEstimate(flops=1, bytes_accessed=1, transcendentals=0),
        **kwargs,
    )


def feature_tables(heads):
    first = [FQK] + [FQK] * FQK
    second = [FQK] + list(range(FQK))
    weight = [1.0] + [1.0 / FQK**0.5] * FQK
    for i in range(FQK):
        for j in range(i, FQK):
            first.append(i)
            second.append(j)
            weight.append((1.0 if i == j else 2.0) / (2.0 * FQK))
    sel_a = np.zeros((heads, QFEATS, LANES), np.float32)
    sel_b = np.zeros((heads, QFEATS, LANES), np.float32)
    sel_w = np.zeros((heads, QFEATS, LANES), np.float32)
    for h in range(heads):
        for f, (i, j, w) in enumerate(zip(first, second, weight)):
            sel_a[h, f, (h * FQK + i) % LANES] = 1.0
            sel_b[h, f, (h * FQK + j) % LANES] = 1.0
            sel_w[h, f, (h * FQK + i) % LANES] = w
    return tuple(jnp.asarray(t, BF16) for t in (sel_a, sel_b, sel_w))


def mean_table():
    block = np.kron(np.eye(LANES // DV), np.ones((DV, DV))) / DV
    return jnp.asarray(np.concatenate([block, block], 0), BF16)


def head_mean(values, table):
    high = values.astype(BF16)
    low = (values - high.astype(F32)).astype(BF16)
    return jnp.dot(jnp.concatenate([high, low], 1), table, preferred_element_type=F32)


def nt_dot(a, b):
    return lax.dot_general(a, b, (((1,), (1,)), ((), ())), preferred_element_type=F32)


def with_one(vectors, lane, h):
    return jnp.where(lane == ((h + 1) * FQK) % LANES, 1.0, vectors).astype(BF16)


def arrange_kernel(w_ref, o_ref, *, heads):
    per_head = 2 * FQK + 3 * DV
    w = w_ref[...]
    at = 0
    for begin, width in ((0, FQK), (FQK, FQK), (2 * FQK, DV), (2 * FQK + DV, DV), (2 * FQK + 2 * DV, DV)):
        parts = [w[:, h * per_head + begin : h * per_head + begin + width] for h in range(heads)]
        total = heads * width
        padded = -(-total // LANES) * LANES
        if padded > total:
            parts.append(jnp.zeros((w.shape[0], padded - total), w.dtype))
        o_ref[:, at : at + padded] = jnp.concatenate(parts, 1)
        at += padded


def block_kernel(j_ref, mean_ref, conv_ref, sel_w_ref, sel_b_ref, w_ref, *refs, n, heads, extra, others, sends):
    xs, refs = refs[:n], refs[n:]
    prev_ref = None
    if not extra:
        prev_ref, refs = refs[0], refs[1:]
    other_refs, refs = refs[:others], refs[others:]
    q_ref, k_ref, v_ref, wq_ref, wk_ref, halo_ref, s_ref = refs[:7]
    send_refs, (ext_ref,) = refs[7 : 7 + sends], refs[7 + sends :]
    rows, depth = v_ref.shape[0], xs[0].shape[1]
    me = j_ref[0]

    def project(begin, width, skip):
        total = None
        for r in range(n):
            src = lax.rem(me - r + n, n)
            from_rows = pl.ds(pl.multiple_of(src * depth, depth), depth)
            part = jnp.dot(xs[r][skip:, :], w_ref[from_rows, begin : begin + width], preferred_element_type=F32)
            total = part if total is None else total + part
        return total.astype(BF16)

    widths = [ref.shape[1] for ref in (q_ref, k_ref, v_ref, wq_ref, wk_ref)]
    starts = [sum(widths[:i]) for i in range(5)]
    k_ref[...] = project(starts[1], widths[1], extra)
    raw = project(starts[2], widths[2], 0)
    if extra:
        ext_ref[...] = raw.astype(F32)
    else:
        ext_ref[0:EDGE, :] = prev_ref[0:EDGE, :].astype(F32)
        ext_ref[EDGE:, :] = raw.astype(F32)
    halo_ref[0:EDGE, :] = raw[raw.shape[0] - EDGE :]
    total = jnp.zeros((rows, widths[2]), F32)
    for tap in range(CONV):
        total = total + conv_ref[tap : tap + 1, :] * ext_ref[EDGE - tap : EDGE - tap + rows, :]
    v_ref[...] = total.astype(BF16)
    halo_ref[EDGE : EDGE + WIN, :] = v_ref[rows - WIN : rows, :]

    lane = lax.broadcasted_iota(jnp.int32, (rows, LANES), 1)
    low_half = lax.broadcasted_iota(jnp.int32, (FEATS, LANES), 1) < DV
    k = k_ref[...].astype(F32)
    for p in range(heads * DV // LANES):
        v = v_ref[:, p * LANES : (p + 1) * LANES]
        both = []
        for h in (2 * p, 2 * p + 1):
            own = with_one(k, lane, h)
            phi = nt_dot(sel_w_ref[h, 0:FEATS, :], own) * nt_dot(sel_b_ref[h, 0:FEATS, :], own)
            both.append(jnp.dot(phi.astype(BF16), v, preferred_element_type=F32))
        s_ref[p] = jnp.where(low_half, both[0], both[1])
    for r in range(sends):
        pair = jnp.bitwise_xor(j_ref[1], r)
        total = s_ref[pair]
        for ref in other_refs:
            total = total + ref[pair]
        send_refs[r][...] = total.astype(BF16)

    q_ref[...] = project(starts[0], widths[0], extra)
    for ref, start, width, scale in (
        (wk_ref, starts[4], widths[4], 1.0),
        (wq_ref, starts[3], widths[3], 1.0 / DV**0.5),
    ):
        got = project(start, width, extra)
        for p in range(width // LANES):
            cols = slice(p * LANES, (p + 1) * LANES)
            x = got[:, cols].astype(F32)
            x = x * lax.rsqrt(head_mean(x * x, mean_ref[...]) + 1e-6)
            ref[:, cols] = x.astype(BF16) * jnp.asarray(scale, BF16)
    halo_ref[EDGE + WIN : HALO, :] = wk_ref[rows - WIN : rows, :]


def attend_kernel(
    a_ref, sel_a_ref, sel_b_ref, prev_ref, q_ref, k_ref, v_ref, wq_ref, wk_ref, phi_ref, lin_ref, win_ref,
    vext_ref, kext_ref, *, heads, first
):
    rows = q_ref.shape[0]
    tile = 128
    span = tile + WIN
    vext_ref[0:WIN, :] = prev_ref[EDGE : EDGE + WIN, :]
    vext_ref[WIN : WIN + rows, :] = v_ref[...]
    kext_ref[0:WIN, :] = prev_ref[EDGE + WIN : HALO, :]
    kext_ref[WIN : WIN + rows, :] = wk_ref[...]
    lane = lax.broadcasted_iota(jnp.int32, (rows, LANES), 1)
    low_half = lane < DV
    causal = lax.broadcasted_iota(jnp.int32, (rows, rows), 1) <= lax.broadcasted_iota(jnp.int32, (rows, rows), 0)
    col = lax.broadcasted_iota(jnp.int32, (tile, span), 1)
    ahead = col - lax.broadcasted_iota(jnp.int32, (tile, span), 0)
    band = (ahead >= 1) & (ahead <= WIN)
    first_band = band
    if first:
        first_band = band & (col >= jnp.where(a_ref[2] == 0, WIN, 0))
    q = q_ref[...]
    q_full = q.astype(F32)
    k = k_ref[...]
    for p in range(heads * DV // LANES):
        cols = slice(p * LANES, (p + 1) * LANES)
        v = v_ref[:, cols]
        both = []
        for h in (2 * p, 2 * p + 1):
            own = with_one(q_full, lane, h)
            phi = nt_dot(own, sel_a_ref[h]) * nt_dot(own, sel_b_ref[h])
            phi_ref[:, h * QFEATS : (h + 1) * QFEATS] = phi.astype(BF16)
            own = jnp.where((lane >= h * FQK) & (lane < (h + 1) * FQK), q, jnp.zeros_like(q))
            t = nt_dot(own, k) * (1.0 / FQK**0.5) + 1.0
            kernel = jnp.where(causal, 0.5 * (t * t) + 0.5, 0.0).astype(BF16)
            both.append(jnp.dot(kernel, v, preferred_element_type=F32))
        lin_ref[:, cols] = jnp.where(low_half, both[0], both[1])
        for i in range(rows // tile):
            here = slice(i * tile, (i + 1) * tile)
            wq = wq_ref[here, cols]
            keys = kext_ref[i * tile : i * tile + span, cols]
            values = vext_ref[i * tile : i * tile + span, cols]
            both = []
            for half in range(2):
                keep = low_half[0:tile] if half == 0 else ~low_half[0:tile]
                scores = nt_dot(jnp.where(keep, wq, jnp.zeros_like(wq)), keys)
                expo = jnp.where(first_band if i == 0 else band, jnp.exp(scores), 0.0)
                weights = expo * (1.0 / jnp.sum(expo, axis=1, keepdims=True))
                both.append(jnp.dot(weights.astype(BF16), values, preferred_element_type=F32))
            win_ref[here, cols] = jnp.where(low_half[0:tile], both[0], both[1])


def finish_kernel(a_ref, mean_ref, gain_ref, *refs, heads, before):
    pairs = heads * DV // LANES
    prior_refs, refs = refs[:pairs], refs[pairs:]
    states, (phi_ref, lin_ref, win_ref, mix_ref, held_ref) = refs[:before], refs[before:]
    rows = phi_ref.shape[0]
    for r in range(pairs):
        held_ref[r] = prior_refs[r][...].astype(F32)
    low_half = lax.broadcasted_iota(jnp.int32, (rows, LANES), 1) < DV
    for p in range(pairs):
        cols = slice(p * LANES, (p + 1) * LANES)
        state = held_ref[jnp.bitwise_xor(a_ref[1], p)]
        for ref in states:
            state = state + ref[p]
        state = jnp.concatenate([state.astype(BF16), jnp.zeros((QFEATS - FEATS, LANES), BF16)], 0)
        both = [
            jnp.dot(phi_ref[:, h * QFEATS : (h + 1) * QFEATS], state, preferred_element_type=F32)
            for h in (2 * p, 2 * p + 1)
        ]
        lin = lin_ref[:, cols] + jnp.where(low_half, both[0], both[1])
        scale = lax.rsqrt(head_mean(lin * lin, mean_ref[...]) + 1e-5)
        mix_ref[:, cols] = (lin * scale * gain_ref[:, cols] + win_ref[:, cols]).astype(BF16)


def output_kernel(a_ref, own_ref, w_ref, *refs, n, offset, parts):
    others, weights, (o_ref, held_ref, sem) = refs[: n - 1], refs[n - 1 : n - 1 + parts * (n - 1)], refs[-3:]
    cols = held_ref.shape[1]
    mine = pl.ds(pl.multiple_of(a_ref[0] * cols, cols), cols)
    total = jnp.dot(own_ref[...], w_ref[:, mine], preferred_element_type=F32).astype(BF16).astype(F32)
    for r, m_ref in enumerate(others):
        part = None
        for i in range(parts):
            ref = weights[r * parts + i]
            depth = ref.shape[0]
            at = depth * (jnp.bitwise_xor(a_ref[2] % 2, i) if parts > 1 else 0)
            got = jnp.dot(m_ref[:, pl.ds(pl.multiple_of(at, depth), depth)], ref[...], preferred_element_type=F32)
            part = got if part is None else part + got
        total = total + part.astype(BF16).astype(F32)
    held_ref[...] = total.astype(BF16)
    copy = pltpu.make_async_copy(held_ref, o_ref.at[pl.ds(offset, held_ref.shape[0]), :], sem)
    copy.start()
    copy.wait()


def pick_kernel(a_ref, w_ref, o_ref):
    o_ref[...] = w_ref[...]


def exchange(value, axis, flip):
    count = lax.axis_size(axis)
    return lax.ppermute(value, axis, [(i, i ^ flip) for i in range(count)])


def plane_kernel(a_ref, *refs):
    helds, plane_ref, ahead_refs = refs[:PLANE], refs[PLANE], refs[PLANE + 1 :]
    place = a_ref[1]
    held = [ref[...].astype(F32) for ref in helds]
    plane_ref[...] = (held[0] + held[1] + held[2] + held[3]).astype(BF16)
    for r in range(PLANE):
        total = jnp.zeros_like(held[0])
        for s in range(PLANE):
            before = jnp.bitwise_xor(place, s) < jnp.bitwise_xor(place, r)
            total = total + held[s] * before.astype(F32)
        ahead_refs[r][...] = total


def earlier_kernel(_, *refs, planes):
    ahead_refs, earlier_refs, back_refs = refs[:PLANE], refs[PLANE : PLANE + planes], refs[PLANE + planes :]
    earlier = jnp.zeros(ahead_refs[0].shape, F32)
    for ref in earlier_refs:
        earlier = earlier + ref[...].astype(F32)
    for r in range(PLANE):
        back_refs[r][...] = (ahead_refs[r][...] + earlier).astype(BF16)


def after(value, earlier):
    return lax.optimization_barrier((value, earlier))[0]


def prior_in_planes(own, places, beside):
    ctx = lax.axis_size("ctx")
    whole = pl.BlockSpec(memory_space=pltpu.VMEM)
    scalar = pl.BlockSpec(memory_space=pltpu.SMEM)
    narrow = jax.ShapeDtypeStruct((FEATS, LANES), BF16)
    wide = jax.ShapeDtypeStruct((FEATS, LANES), F32)
    held = [own[0]] + [exchange(own[r], "ctx", r) for r in range(1, PLANE)]
    plane, *ahead = call(
        plane_kernel,
        [narrow] + [wide] * PLANE,
        in_specs=[scalar] + [whole] * PLANE,
        out_specs=[whole] * (1 + PLANE),
        moved=24 * FEATS * LANES,
        vmem=4 << 20,
    )(after(places, beside[0]), *held)
    earlier = []
    for d in range(1, ctx // PLANE):
        pairs = [(i, i + d * PLANE) for i in range(ctx - d * PLANE)]
        earlier.append(lax.ppermute(plane, "ctx", pairs))
    back = call(
        functools.partial(earlier_kernel, planes=len(earlier)),
        [narrow] * PLANE,
        in_specs=[scalar] + [whole] * (PLANE + len(earlier)),
        out_specs=[whole] * PLANE,
        moved=24 * FEATS * LANES,
        vmem=4 << 20,
    )(after(places, beside[1]), *ahead, *earlier)
    return back[0], [back[0]] + [exchange(back[r], "ctx", r) for r in range(1, PLANE)]


def prior_by_doubling(total, position):
    ctx = lax.axis_size("ctx")
    prior = jnp.zeros_like(total)
    bit = 1
    while bit < ctx:
        got = exchange(total.astype(BF16), "ctx", bit).astype(F32)
        prior = prior + jnp.where((position & bit) != 0, got, 0.0)
        total = total + got
        bit *= 2
    return [prior[p].astype(BF16) for p in range(total.shape[0])]


def per_device(hidden_in, proj_weight, conv_weight, norm_gain, out_weight):
    n = lax.axis_size("head")
    ctx = lax.axis_size("ctx")
    me = lax.axis_index("head").astype(jnp.int32)
    position = lax.axis_index("ctx").astype(jnp.int32)
    row_count = hidden_in.shape[0]
    model = proj_weight.shape[0]
    heads = out_weight.shape[0] // DV
    width = heads * DV
    pairs = width // LANES
    in_planes = pairs == PLANE and ctx % PLANE == 0
    places = jnp.stack([me, position % PLANE if in_planes else jnp.zeros_like(position), position])
    hidden_in, places = lax.optimization_barrier((hidden_in, places))
    step = row_count // 8
    blocks = [(0, 2 * step), (2 * step, 2 * step), (4 * step, step), (5 * step, step), (6 * step, 2 * step)]
    last = len(blocks) - 1
    sel_a, sel_b, sel_w = feature_tables(heads)
    means = mean_table()
    gain = norm_gain.reshape(1, width)
    whole = pl.BlockSpec(memory_space=pltpu.VMEM)
    scalar = pl.BlockSpec(memory_space=pltpu.SMEM)

    def from_head(value, by):
        return lax.ppermute(value, "head", [(i, (i + by) % n) for i in range(n)])

    pieces = {}

    def send_block(b, behind=None):
        at, rows = blocks[b]
        extra = EDGE if b == last else 0
        own = hidden_in[at - extra : at + rows]
        if behind is not None:
            own = after(own, behind)
        pieces[b] = [own] + [from_head(own, r) for r in range(1, n)]

    send_block(last)
    send_block(0, pieces[last][0])
    for b in range(1, last):
        send_block(b, pieces[last][0])

    cols = out_weight.shape[1] // n
    out_parts = 2 if width // 2 % LANES == 0 and ctx % 2 == 0 else 1
    share = width // out_parts
    picked = []
    for r in range(1, n):
        block = call(
            pick_kernel,
            jax.ShapeDtypeStruct((share, cols), BF16),
            grid_spec=pltpu.PrefetchScalarGridSpec(
                num_scalar_prefetch=1,
                grid=(1,),
                in_specs=[
                    pl.BlockSpec((share, cols), functools.partial(lambda i, a, r: (a[2] % out_parts, (a[0] + r) % n), r=r))
                ],
                out_specs=pl.BlockSpec((share, cols), lambda i, a: (0, 0)),
            ),
            moved=4 * share * cols,
            vmem=8 << 20,
        )(places, out_weight)
        picked.append(block)

    qk_width = -(-heads * FQK // LANES) * LANES
    arranged_width = 2 * qk_width + 3 * width
    slab = 256
    arranged = call(
        functools.partial(arrange_kernel, heads=heads),
        jax.ShapeDtypeStruct((model, arranged_width), BF16),
        grid=(model // slab,),
        in_specs=[pl.BlockSpec((slab, proj_weight.shape[1]), lambda i: (i, 0))],
        out_specs=pl.BlockSpec((slab, arranged_width), lambda i: (i, 0)),
        moved=4 * model * arranged_width,
        vmem=32 << 20,
    )(proj_weight)

    def do_block(b, prev, behind, others=()):
        rows = blocks[b][1]
        extra = EDGE if prev is None else 0
        sends = PLANE if in_planes and others else 0
        tokens = places if behind is None else after(places, behind)
        shapes = [jax.ShapeDtypeStruct((rows, w), BF16) for w in (qk_width, qk_width, width, width, width)]
        shapes.append(jax.ShapeDtypeStruct((HALO, width), BF16))
        shapes.append(jax.ShapeDtypeStruct((pairs, FEATS, LANES), F32))
        shapes += [jax.ShapeDtypeStruct((FEATS, LANES), BF16)] * sends
        operands = [tokens, means, conv_weight, sel_w, sel_b, arranged, *pieces[b]]
        if prev is not None:
            operands.append(prev)
        operands += others
        return call(
            functools.partial(
                block_kernel, n=n, heads=heads, extra=extra, others=len(others), sends=sends
            ),
            shapes,
            in_specs=[scalar] + [whole] * (len(operands) - 1),
            out_specs=[whole] * len(shapes),
            scratch_shapes=[pltpu.VMEM((EDGE + rows, width), F32)],
            flops=2 * rows * model * arranged_width + 6 * rows * FEATS * LANES * heads,
            moved=2 * model * arranged_width,
            vmem=32 << 20,
        )(*operands)

    def attend(b, prev):
        rows = blocks[b][1]
        q, k, v, wq, wk = done[b][:5]
        return call(
            functools.partial(attend_kernel, heads=heads, first=b == 0),
            [jax.ShapeDtypeStruct((rows, heads * QFEATS), BF16)] + [jax.ShapeDtypeStruct((rows, width), F32)] * 2,
            in_specs=[scalar] + [whole] * 8,
            out_specs=[whole] * 3,
            scratch_shapes=[pltpu.VMEM((WIN + rows, width), BF16)] * 2,
            flops=heads * rows * 4096 * 256,
            moved=16 * rows * width,
            vmem=16 << 20,
        )(places, sel_a, sel_b, prev, q, k, v, wq, wk)

    done, attended = {}, {}
    done[last] = do_block(last, None, None)
    halo = lax.ppermute(done[last][5], "ctx", [(i, i + 1) for i in range(ctx - 1)])
    for b in range(last):
        prev = halo if b == 0 else done[b - 1][5]
        others = [done[c][6] for c in [last] + list(range(b))] if b == last - 1 else ()
        done[b] = do_block(b, prev, attended[b - 1][1] if b - 1 in attended else None, others)
        if b < last - 2:
            attended[b] = attend(b, prev)

    fetched = [from_head(after(block, done[last - 1][5]), r) for r, block in enumerate(picked, 1)]

    for b in range(last - 2, last + 1):
        attended[b] = attend(b, done[b - 1][5])
    if in_planes:
        beside = [attended[b][1] for b in (last - 2, last - 1)]
        mark, priors = prior_in_planes(done[last - 1][7:], places, beside)
    else:
        mark = sum(done[b][6] for b in range(last + 1))
        priors = prior_by_doubling(mark, position)

    out_rows = []
    for got in fetched:
        out_rows += [got] + ([exchange(after(got, mark), "ctx", 1)] if out_parts > 1 else [])

    result = None
    arrived = []
    for i, b in enumerate((3, 0, 1, 4, 2)):
        at, rows = blocks[b]
        behind = after(places, arrived[i - 2] if i >= 2 else attended[last][1])
        mixed = call(
            functools.partial(finish_kernel, heads=heads, before=b),
            jax.ShapeDtypeStruct((rows, width), BF16),
            in_specs=[scalar] + [whole] * (2 + pairs + b + 3),
            out_specs=whole,
            scratch_shapes=[pltpu.VMEM((pairs, FEATS, LANES), F32)],
            flops=6 * rows * QFEATS * LANES * heads,
            moved=12 * rows * width,
            vmem=16 << 20,
        )(behind, means, gain, *priors, *[done[c][6] for c in range(b)], *attended[b])
        others = [from_head(mixed, r) for r in range(1, n)]
        arrived.append(others[-1])
        operands = [places, mixed, out_weight] + others + out_rows
        specs = [scalar] + [whole] * (len(operands) - 1)
        aliases = {}
        if result is not None:
            aliases = {len(operands): 0}
            operands.append(result)
            specs.append(pl.BlockSpec(memory_space=pl.ANY))
        result = call(
            functools.partial(output_kernel, n=n, offset=at, parts=out_parts),
            jax.ShapeDtypeStruct((row_count, cols), BF16),
            in_specs=specs,
            out_specs=pl.BlockSpec(memory_space=pl.ANY),
            scratch_shapes=[pltpu.VMEM((rows, cols), BF16), pltpu.SemaphoreType.DMA],
            input_output_aliases=aliases,
            flops=2 * rows * n * width * cols,
            moved=2 * n * width * cols,
            vmem=16 << 20,
        )(*operands)
    return result


def solution(mesh):
    return jax.shard_map(
        per_device,
        mesh=mesh,
        in_specs=(P("ctx", "head"), P(None, "head"), P(None, "head"), P("head"), P("head", None)),
        out_specs=P("ctx", "head"),
        check_vma=False,
    )
```

```python
import functools

import jax
import jax.numpy as jnp
import numpy as np
from jax import lax
from jax.experimental import pallas as pl
from jax.experimental.pallas import tpu as pltpu
from jax.sharding import PartitionSpec as P

DV = 64
FQK = 16
WIN = 64
CONV = 3
LANES = 128
FEATS = 160
QFEATS = 256
EDGE = 16
HALO = EDGE + 2 * WIN
PLANE = 4
F32 = jnp.float32
BF16 = jnp.bfloat16


def call(body, out_shape, *, flops=0, moved=0, vmem=48 << 20, **kwargs):
    return pl.pallas_call(
        body,
        out_shape=out_shape,
        compiler_params=pltpu.CompilerParams(vmem_limit_bytes=vmem),
        cost_estimate=pl.CostEstimate(flops=1, bytes_accessed=1, transcendentals=0),
        **kwargs,
    )


def feature_tables(heads):
    first = [FQK] + [FQK] * FQK
    second = [FQK] + list(range(FQK))
    weight = [1.0] + [1.0 / FQK**0.5] * FQK
    for i in range(FQK):
        for j in range(i, FQK):
            first.append(i)
            second.append(j)
            weight.append((1.0 if i == j else 2.0) / (2.0 * FQK))
    sel_a = np.zeros((heads, QFEATS, LANES), np.float32)
    sel_b = np.zeros((heads, QFEATS, LANES), np.float32)
    sel_w = np.zeros((heads, QFEATS, LANES), np.float32)
    for h in range(heads):
        for f, (i, j, w) in enumerate(zip(first, second, weight)):
            sel_a[h, f, (h * FQK + i) % LANES] = 1.0
            sel_b[h, f, (h * FQK + j) % LANES] = 1.0
            sel_w[h, f, (h * FQK + i) % LANES] = w
    return tuple(jnp.asarray(t, BF16) for t in (sel_a, sel_b, sel_w))


def mean_table():
    block = np.kron(np.eye(LANES // DV), np.ones((DV, DV))) / DV
    return jnp.asarray(np.concatenate([block, block], 0), BF16)


def head_mean(values, table):
    high = values.astype(BF16)
    low = (values - high.astype(F32)).astype(BF16)
    return jnp.dot(jnp.concatenate([high, low], 1), table, preferred_element_type=F32)


def nt_dot(a, b):
    return lax.dot_general(a, b, (((1,), (1,)), ((), ())), preferred_element_type=F32)


def with_one(vectors, lane, h):
    return jnp.where(lane == ((h + 1) * FQK) % LANES, 1.0, vectors).astype(BF16)


def arrange_kernel(w_ref, o_ref, *, heads):
    per_head = 2 * FQK + 3 * DV
    w = w_ref[...]
    at = 0
    for begin, width in ((0, FQK), (FQK, FQK), (2 * FQK, DV), (2 * FQK + DV, DV), (2 * FQK + 2 * DV, DV)):
        parts = [w[:, h * per_head + begin : h * per_head + begin + width] for h in range(heads)]
        total = heads * width
        padded = -(-total // LANES) * LANES
        if padded > total:
            parts.append(jnp.zeros((w.shape[0], padded - total), w.dtype))
        o_ref[:, at : at + padded] = jnp.concatenate(parts, 1)
        at += padded


def block_kernel(j_ref, mean_ref, conv_ref, sel_w_ref, sel_b_ref, w_ref, *refs, n, heads, extra, others, sends):
    xs, refs = refs[:n], refs[n:]
    prev_ref = None
    if not extra:
        prev_ref, refs = refs[0], refs[1:]
    other_refs, refs = refs[:others], refs[others:]
    q_ref, k_ref, v_ref, wq_ref, wk_ref, halo_ref, s_ref = refs[:7]
    send_refs, (ext_ref,) = refs[7 : 7 + sends], refs[7 + sends :]
    rows, depth = v_ref.shape[0], xs[0].shape[1]
    me = j_ref[0]

    def project(begin, width, skip):
        total = None
        for r in range(n):
            src = lax.rem(me - r + n, n)
            from_rows = pl.ds(pl.multiple_of(src * depth, depth), depth)
            part = jnp.dot(xs[r][skip:, :], w_ref[from_rows, begin : begin + width], preferred_element_type=F32)
            total = part if total is None else total + part
        return total.astype(BF16)

    widths = [ref.shape[1] for ref in (q_ref, k_ref, v_ref, wq_ref, wk_ref)]
    starts = [sum(widths[:i]) for i in range(5)]
    k_ref[...] = project(starts[1], widths[1], extra)
    raw = project(starts[2], widths[2], 0)
    if extra:
        ext_ref[...] = raw.astype(F32)
    else:
        ext_ref[0:EDGE, :] = prev_ref[0:EDGE, :].astype(F32)
        ext_ref[EDGE:, :] = raw.astype(F32)
    halo_ref[0:EDGE, :] = raw[raw.shape[0] - EDGE :]
    total = jnp.zeros((rows, widths[2]), F32)
    for tap in range(CONV):
        total = total + conv_ref[tap : tap + 1, :] * ext_ref[EDGE - tap : EDGE - tap + rows, :]
    v_ref[...] = total.astype(BF16)
    halo_ref[EDGE : EDGE + WIN, :] = v_ref[rows - WIN : rows, :]

    lane = lax.broadcasted_iota(jnp.int32, (rows, LANES), 1)
    low_half = lax.broadcasted_iota(jnp.int32, (FEATS, LANES), 1) < DV
    k = k_ref[...].astype(F32)
    for p in range(heads * DV // LANES):
        v = v_ref[:, p * LANES : (p + 1) * LANES]
        both = []
        for h in (2 * p, 2 * p + 1):
            own = with_one(k, lane, h)
            phi = nt_dot(sel_w_ref[h, 0:FEATS, :], own) * nt_dot(sel_b_ref[h, 0:FEATS, :], own)
            both.append(jnp.dot(phi.astype(BF16), v, preferred_element_type=F32))
        s_ref[p] = jnp.where(low_half, both[0], both[1])
    for r in range(sends):
        pair = jnp.bitwise_xor(j_ref[1], r)
        total = s_ref[pair]
        for ref in other_refs:
            total = total + ref[pair]
        send_refs[r][...] = total.astype(BF16)

    q_ref[...] = project(starts[0], widths[0], extra)
    for ref, start, width, scale in (
        (wk_ref, starts[4], widths[4], 1.0),
        (wq_ref, starts[3], widths[3], 1.0 / DV**0.5),
    ):
        got = project(start, width, extra)
        for p in range(width // LANES):
            cols = slice(p * LANES, (p + 1) * LANES)
            x = got[:, cols].astype(F32)
            x = x * lax.rsqrt(head_mean(x * x, mean_ref[...]) + 1e-6)
            ref[:, cols] = x.astype(BF16) * jnp.asarray(scale, BF16)
    halo_ref[EDGE + WIN : HALO, :] = wk_ref[rows - WIN : rows, :]


def attend_kernel(
    a_ref, sel_a_ref, sel_b_ref, prev_ref, q_ref, k_ref, v_ref, wq_ref, wk_ref, phi_ref, lin_ref, win_ref,
    vext_ref, kext_ref, *, heads, first
):
    rows = q_ref.shape[0]
    tile = 128
    span = tile + WIN
    vext_ref[0:WIN, :] = prev_ref[EDGE : EDGE + WIN, :]
    vext_ref[WIN : WIN + rows, :] = v_ref[...]
    kext_ref[0:WIN, :] = prev_ref[EDGE + WIN : HALO, :]
    kext_ref[WIN : WIN + rows, :] = wk_ref[...]
    lane = lax.broadcasted_iota(jnp.int32, (rows, LANES), 1)
    low_half = lane < DV
    causal = lax.broadcasted_iota(jnp.int32, (rows, rows), 1) <= lax.broadcasted_iota(jnp.int32, (rows, rows), 0)
    col = lax.broadcasted_iota(jnp.int32, (tile, span), 1)
    ahead = col - lax.broadcasted_iota(jnp.int32, (tile, span), 0)
    band = (ahead >= 1) & (ahead <= WIN)
    first_band = band
    if first:
        first_band = band & (col >= jnp.where(a_ref[2] == 0, WIN, 0))
    q = q_ref[...]
    q_full = q.astype(F32)
    k = k_ref[...]
    for p in range(heads * DV // LANES):
        cols = slice(p * LANES, (p + 1) * LANES)
        v = v_ref[:, cols]
        both = []
        for h in (2 * p, 2 * p + 1):
            own = with_one(q_full, lane, h)
            phi = nt_dot(own, sel_a_ref[h]) * nt_dot(own, sel_b_ref[h])
            phi_ref[:, h * QFEATS : (h + 1) * QFEATS] = phi.astype(BF16)
            own = jnp.where((lane >= h * FQK) & (lane < (h + 1) * FQK), q, jnp.zeros_like(q))
            t = nt_dot(own, k) * (1.0 / FQK**0.5) + 1.0
            kernel = jnp.where(causal, 0.5 * (t * t) + 0.5, 0.0).astype(BF16)
            both.append(jnp.dot(kernel, v, preferred_element_type=F32))
        lin_ref[:, cols] = jnp.where(low_half, both[0], both[1])
        for i in range(rows // tile):
            here = slice(i * tile, (i + 1) * tile)
            wq = wq_ref[here, cols]
            keys = kext_ref[i * tile : i * tile + span, cols]
            values = vext_ref[i * tile : i * tile + span, cols]
            both = []
            for half in range(2):
                keep = low_half[0:tile] if half == 0 else ~low_half[0:tile]
                scores = nt_dot(jnp.where(keep, wq, jnp.zeros_like(wq)), keys)
                expo = jnp.where(first_band if i == 0 else band, jnp.exp(scores), 0.0)
                weights = expo * (1.0 / jnp.sum(expo, axis=1, keepdims=True))
                both.append(jnp.dot(weights.astype(BF16), values, preferred_element_type=F32))
            win_ref[here, cols] = jnp.where(low_half[0:tile], both[0], both[1])


def finish_kernel(a_ref, mean_ref, gain_ref, *refs, heads, before):
    pairs = heads * DV // LANES
    prior_refs, refs = refs[:pairs], refs[pairs:]
    states, (phi_ref, lin_ref, win_ref, mix_ref, held_ref) = refs[:before], refs[before:]
    rows = phi_ref.shape[0]
    for r in range(pairs):
        held_ref[r] = prior_refs[r][...].astype(F32)
    low_half = lax.broadcasted_iota(jnp.int32, (rows, LANES), 1) < DV
    for p in range(pairs):
        cols = slice(p * LANES, (p + 1) * LANES)
        state = held_ref[jnp.bitwise_xor(a_ref[1], p)]
        for ref in states:
            state = state + ref[p]
        state = jnp.concatenate([state.astype(BF16), jnp.zeros((QFEATS - FEATS, LANES), BF16)], 0)
        both = [
            jnp.dot(phi_ref[:, h * QFEATS : (h + 1) * QFEATS], state, preferred_element_type=F32)
            for h in (2 * p, 2 * p + 1)
        ]
        lin = lin_ref[:, cols] + jnp.where(low_half, both[0], both[1])
        scale = lax.rsqrt(head_mean(lin * lin, mean_ref[...]) + 1e-5)
        mix_ref[:, cols] = (lin * scale * gain_ref[:, cols] + win_ref[:, cols]).astype(BF16)


def output_kernel(a_ref, own_ref, w_ref, *refs, n, offset, parts):
    others, weights, (o_ref, held_ref, sem) = refs[: n - 1], refs[n - 1 : n - 1 + parts * (n - 1)], refs[-3:]
    cols = held_ref.shape[1]
    mine = pl.ds(pl.multiple_of(a_ref[0] * cols, cols), cols)
    total = jnp.dot(own_ref[...], w_ref[:, mine], preferred_element_type=F32).astype(BF16).astype(F32)
    for r, m_ref in enumerate(others):
        part = None
        for i in range(parts):
            ref = weights[r * parts + i]
            depth = ref.shape[0]
            at = depth * (jnp.bitwise_xor(a_ref[2] % 2, i) if parts > 1 else 0)
            got = jnp.dot(m_ref[:, pl.ds(pl.multiple_of(at, depth), depth)], ref[...], preferred_element_type=F32)
            part = got if part is None else part + got
        total = total + part.astype(BF16).astype(F32)
    held_ref[...] = total.astype(BF16)
    copy = pltpu.make_async_copy(held_ref, o_ref.at[pl.ds(offset, held_ref.shape[0]), :], sem)
    copy.start()
    copy.wait()


def pick_kernel(a_ref, w_ref, o_ref):
    o_ref[...] = w_ref[...]


def exchange(value, axis, flip):
    count = lax.axis_size(axis)
    return lax.ppermute(value, axis, [(i, i ^ flip) for i in range(count)])


def plane_kernel(a_ref, *refs):
    helds, plane_ref, ahead_refs = refs[:PLANE], refs[PLANE], refs[PLANE + 1 :]
    place = a_ref[1]
    held = [ref[...].astype(F32) for ref in helds]
    plane_ref[...] = (held[0] + held[1] + held[2] + held[3]).astype(BF16)
    for r in range(PLANE):
        total = jnp.zeros_like(held[0])
        for s in range(PLANE):
            before = jnp.bitwise_xor(place, s) < jnp.bitwise_xor(place, r)
            total = total + held[s] * before.astype(F32)
        ahead_refs[r][...] = total


def earlier_kernel(a_ref, *refs, planes):
    ahead_refs, plane_refs, back_refs = refs[:PLANE], refs[PLANE : PLANE + planes], refs[PLANE + planes :]
    mine = a_ref[2] // PLANE
    earlier = jnp.zeros(ahead_refs[0].shape, F32)
    for d, ref in enumerate(plane_refs, 1):
        before = jnp.bitwise_xor(mine, d) < mine
        earlier = earlier + ref[...].astype(F32) * before.astype(F32)
    for r in range(PLANE):
        back_refs[r][...] = (ahead_refs[r][...] + earlier).astype(BF16)


def after(value, earlier):
    return lax.optimization_barrier((value, earlier))[0]


def prior_in_planes(own, places, beside):
    ctx = lax.axis_size("ctx")
    whole = pl.BlockSpec(memory_space=pltpu.VMEM)
    scalar = pl.BlockSpec(memory_space=pltpu.SMEM)
    narrow = jax.ShapeDtypeStruct((FEATS, LANES), BF16)
    wide = jax.ShapeDtypeStruct((FEATS, LANES), F32)
    held = [own[0]] + [exchange(own[r], "ctx", r) for r in range(1, PLANE)]
    plane, *ahead = call(
        plane_kernel,
        [narrow] + [wide] * PLANE,
        in_specs=[scalar] + [whole] * PLANE,
        out_specs=[whole] * (1 + PLANE),
        moved=24 * FEATS * LANES,
        vmem=4 << 20,
    )(after(places, beside[0]), *held)
    earlier = []
    for d in range(1, ctx // PLANE):
        earlier.append(exchange(plane, "ctx", d * PLANE))
    back = call(
        functools.partial(earlier_kernel, planes=len(earlier)),
        [narrow] * PLANE,
        in_specs=[scalar] + [whole] * (PLANE + len(earlier)),
        out_specs=[whole] * PLANE,
        moved=24 * FEATS * LANES,
        vmem=4 << 20,
    )(after(places, beside[1]), *ahead, *earlier)
    return back[0], [back[0]] + [exchange(back[r], "ctx", r) for r in range(1, PLANE)]


def prior_by_doubling(total, position):
    ctx = lax.axis_size("ctx")
    prior = jnp.zeros_like(total)
    bit = 1
    while bit < ctx:
        got = exchange(total.astype(BF16), "ctx", bit).astype(F32)
        prior = prior + jnp.where((position & bit) != 0, got, 0.0)
        total = total + got
        bit *= 2
    return [prior[p].astype(BF16) for p in range(total.shape[0])]


def per_device(hidden_in, proj_weight, conv_weight, norm_gain, out_weight):
    n = lax.axis_size("head")
    ctx = lax.axis_size("ctx")
    me = lax.axis_index("head").astype(jnp.int32)
    position = lax.axis_index("ctx").astype(jnp.int32)
    row_count = hidden_in.shape[0]
    model = proj_weight.shape[0]
    heads = out_weight.shape[0] // DV
    width = heads * DV
    pairs = width // LANES
    in_planes = pairs == PLANE and ctx % PLANE == 0 and ctx & (ctx - 1) == 0
    places = jnp.stack([me, position % PLANE if in_planes else jnp.zeros_like(position), position])
    hidden_in, places = lax.optimization_barrier((hidden_in, places))
    step = row_count // 8
    blocks = [(0, 2 * step), (2 * step, 2 * step), (4 * step, step), (5 * step, step), (6 * step, 2 * step)]
    last = len(blocks) - 1
    sel_a, sel_b, sel_w = feature_tables(heads)
    means = mean_table()
    gain = norm_gain.reshape(1, width)
    whole = pl.BlockSpec(memory_space=pltpu.VMEM)
    scalar = pl.BlockSpec(memory_space=pltpu.SMEM)

    def from_head(value, by):
        return lax.ppermute(value, "head", [(i, (i + by) % n) for i in range(n)])

    pieces = {}

    def send_block(b, behind=None):
        at, rows = blocks[b]
        extra = EDGE if b == last else 0
        own = hidden_in[at - extra : at + rows]
        if behind is not None:
            own = after(own, behind)
        pieces[b] = [own] + [from_head(own, r) for r in range(1, n)]

    send_block(last)
    send_block(0, pieces[last][0])
    for b in range(1, last):
        send_block(b, pieces[last][0])

    cols = out_weight.shape[1] // n
    out_parts = 2 if width // 2 % LANES == 0 and ctx % 2 == 0 else 1
    share = width // out_parts
    picked = []
    for r in range(1, n):
        block = call(
            pick_kernel,
            jax.ShapeDtypeStruct((share, cols), BF16),
            grid_spec=pltpu.PrefetchScalarGridSpec(
                num_scalar_prefetch=1,
                grid=(1,),
                in_specs=[
                    pl.BlockSpec((share, cols), functools.partial(lambda i, a, r: (a[2] % out_parts, (a[0] + r) % n), r=r))
                ],
                out_specs=pl.BlockSpec((share, cols), lambda i, a: (0, 0)),
            ),
            moved=4 * share * cols,
            vmem=8 << 20,
        )(places, out_weight)
        picked.append(block)

    qk_width = -(-heads * FQK // LANES) * LANES
    arranged_width = 2 * qk_width + 3 * width
    slab = 256
    arranged = call(
        functools.partial(arrange_kernel, heads=heads),
        jax.ShapeDtypeStruct((model, arranged_width), BF16),
        grid=(model // slab,),
        in_specs=[pl.BlockSpec((slab, proj_weight.shape[1]), lambda i: (i, 0))],
        out_specs=pl.BlockSpec((slab, arranged_width), lambda i: (i, 0)),
        moved=4 * model * arranged_width,
        vmem=32 << 20,
    )(proj_weight)

    def do_block(b, prev, behind, others=()):
        rows = blocks[b][1]
        extra = EDGE if prev is None else 0
        sends = PLANE if in_planes and others else 0
        tokens = places if behind is None else after(places, behind)
        shapes = [jax.ShapeDtypeStruct((rows, w), BF16) for w in (qk_width, qk_width, width, width, width)]
        shapes.append(jax.ShapeDtypeStruct((HALO, width), BF16))
        shapes.append(jax.ShapeDtypeStruct((pairs, FEATS, LANES), F32))
        shapes += [jax.ShapeDtypeStruct((FEATS, LANES), BF16)] * sends
        operands = [tokens, means, conv_weight, sel_w, sel_b, arranged, *pieces[b]]
        if prev is not None:
            operands.append(prev)
        operands += others
        return call(
            functools.partial(
                block_kernel, n=n, heads=heads, extra=extra, others=len(others), sends=sends
            ),
            shapes,
            in_specs=[scalar] + [whole] * (len(operands) - 1),
            out_specs=[whole] * len(shapes),
            scratch_shapes=[pltpu.VMEM((EDGE + rows, width), F32)],
            flops=2 * rows * model * arranged_width + 6 * rows * FEATS * LANES * heads,
            moved=2 * model * arranged_width,
            vmem=32 << 20,
        )(*operands)

    def attend(b, prev):
        rows = blocks[b][1]
        q, k, v, wq, wk = done[b][:5]
        return call(
            functools.partial(attend_kernel, heads=heads, first=b == 0),
            [jax.ShapeDtypeStruct((rows, heads * QFEATS), BF16)] + [jax.ShapeDtypeStruct((rows, width), F32)] * 2,
            in_specs=[scalar] + [whole] * 8,
            out_specs=[whole] * 3,
            scratch_shapes=[pltpu.VMEM((WIN + rows, width), BF16)] * 2,
            flops=heads * rows * 4096 * 256,
            moved=16 * rows * width,
            vmem=16 << 20,
        )(places, sel_a, sel_b, prev, q, k, v, wq, wk)

    done, attended = {}, {}
    done[last] = do_block(last, None, None)
    halo = lax.ppermute(done[last][5], "ctx", [(i, i + 1) for i in range(ctx - 1)])
    for b in range(last):
        prev = halo if b == 0 else done[b - 1][5]
        others = [done[c][6] for c in [last] + list(range(b))] if b == last - 1 else ()
        done[b] = do_block(b, prev, attended[b - 1][1] if b - 1 in attended else None, others)
        if b < last - 2:
            attended[b] = attend(b, prev)

    fetched = [from_head(after(block, done[last - 1][5]), r) for r, block in enumerate(picked, 1)]

    for b in range(last - 2, last + 1):
        attended[b] = attend(b, done[b - 1][5])
    if in_planes:
        beside = [attended[b][1] for b in (last - 2, last - 1)]
        mark, priors = prior_in_planes(done[last - 1][7:], places, beside)
    else:
        mark = sum(done[b][6] for b in range(last + 1))
        priors = prior_by_doubling(mark, position)

    out_rows = []
    for got in fetched:
        out_rows += [got] + ([exchange(after(got, mark), "ctx", 1)] if out_parts > 1 else [])

    result = None
    mixed = attended[last][1]
    for b in (0, 1, 4, 2, 3):
        at, rows = blocks[b]
        mixed = call(
            functools.partial(finish_kernel, heads=heads, before=b),
            jax.ShapeDtypeStruct((rows, width), BF16),
            in_specs=[scalar] + [whole] * (2 + pairs + b + 3),
            out_specs=whole,
            scratch_shapes=[pltpu.VMEM((pairs, FEATS, LANES), F32)],
            flops=6 * rows * QFEATS * LANES * heads,
            moved=12 * rows * width,
            vmem=16 << 20,
        )(after(places, mixed), means, gain, *priors, *[done[c][6] for c in range(b)], *attended[b])
        others = [from_head(mixed, r) for r in range(1, n)]
        operands = [places, mixed, out_weight] + others + out_rows
        specs = [scalar] + [whole] * (len(operands) - 1)
        aliases = {}
        if result is not None:
            aliases = {len(operands): 0}
            operands.append(result)
            specs.append(pl.BlockSpec(memory_space=pl.ANY))
        result = call(
            functools.partial(output_kernel, n=n, offset=at, parts=out_parts),
            jax.ShapeDtypeStruct((row_count, cols), BF16),
            in_specs=specs,
            out_specs=pl.BlockSpec(memory_space=pl.ANY),
            scratch_shapes=[pltpu.VMEM((rows, cols), BF16), pltpu.SemaphoreType.DMA],
            input_output_aliases=aliases,
            flops=2 * rows * n * width * cols,
            moved=2 * n * width * cols,
            vmem=16 << 20,
        )(*operands)
    return result


def solution(mesh):
    return jax.shard_map(
        per_device,
        mesh=mesh,
        in_specs=(P("ctx", "head"), P(None, "head"), P(None, "head"), P("head"), P("head", None)),
        out_specs=P("ctx", "head"),
        check_vma=False,
    )
```

```python
import functools

import jax
import jax.numpy as jnp
import numpy as np
from jax import lax
from jax.experimental import pallas as pl
from jax.experimental.pallas import tpu as pltpu
from jax.sharding import PartitionSpec as P

DV = 64
FQK = 16
WIN = 64
CONV = 3
LANES = 128
SHIFTS = FQK // 2 + 1
FEATS = (SHIFTS + 1) * FQK
EDGE = 16
HALO = EDGE + 2 * WIN
PLANE = 4
F32 = jnp.float32
BF16 = jnp.bfloat16


def call(body, out_shape, *, vmem, **kwargs):
    return pl.pallas_call(
        body,
        out_shape=out_shape,
        compiler_params=pltpu.CompilerParams(vmem_limit_bytes=vmem),
        cost_estimate=pl.CostEstimate(flops=1, bytes_accessed=1, transcendentals=0),
        **kwargs,
    )


def feature_layout(heads):
    in_group = min(heads, 4)
    lanes = in_group * FQK
    per_tile = LANES // lanes
    return in_group, lanes, -(-(SHIFTS + 1) // per_tile) * per_tile


def feature_tables(heads):
    in_group, lanes, slots = feature_layout(heads)
    groups = heads // in_group
    turn = np.zeros((LANES, groups, slots, in_group, FQK), np.float32)
    for g in range(groups):
        for s in range(SHIFTS):
            for h in range(in_group):
                for i in range(FQK if s < SHIFTS - 1 else FQK // 2):
                    turn[g * lanes + h * FQK + (i + s) % FQK, g, s, h, i] = 1.0
    weight = np.zeros((SHIFTS + 1, FQK, LANES), np.float32)
    weight[0] = 1.0 / (2.0 * FQK)
    weight[1:SHIFTS] = 2.0 / (2.0 * FQK)
    weight[SHIFTS - 1, FQK // 2] = 1.0
    weight[SHIFTS] = 1.0 / FQK**0.5
    turn = turn.reshape(LANES, -1)
    by_rows = np.concatenate([turn.T, np.eye(LANES, dtype=np.float32)], 0)
    return jnp.asarray(turn, BF16), jnp.asarray(by_rows, BF16), jnp.asarray(weight.reshape(FEATS, LANES))


def mean_table():
    block = np.kron(np.eye(LANES // DV), np.ones((DV, DV))) / DV
    return jnp.asarray(np.concatenate([block, block], 0), BF16)


def head_mean(values, table):
    high = values.astype(BF16)
    low = (values - high.astype(F32)).astype(BF16)
    return jnp.dot(jnp.concatenate([high, low], 1), table, preferred_element_type=F32)


def nt_dot(a, b):
    return lax.dot_general(a, b, (((1,), (1,)), ((), ())), preferred_element_type=F32)


def arrange_kernel(w_ref, o_ref, *, heads):
    per_head = 2 * FQK + 3 * DV
    w = w_ref[...]
    at = 0
    for begin, width in ((0, FQK), (FQK, FQK), (2 * FQK, DV), (2 * FQK + DV, DV), (2 * FQK + 2 * DV, DV)):
        parts = [w[:, h * per_head + begin : h * per_head + begin + width] for h in range(heads)]
        total = heads * width
        padded = -(-total // LANES) * LANES
        if padded > total:
            parts.append(jnp.zeros((w.shape[0], padded - total), w.dtype))
        o_ref[:, at : at + padded] = jnp.concatenate(parts, 1)
        at += padded


def block_kernel(j_ref, mean_ref, conv_ref, turn_ref, weight_ref, w_ref, *refs, n, heads, extra, others, sends):
    xs, refs = refs[:n], refs[n:]
    prev_ref = None
    if not extra:
        prev_ref, refs = refs[0], refs[1:]
    other_refs, refs = refs[:others], refs[others:]
    q_ref, k_ref, v_ref, wq_ref, wk_ref, halo_ref, s_ref = refs[:7]
    send_refs, (ext_ref,) = refs[7 : 7 + sends], refs[7 + sends :]
    rows, depth = v_ref.shape[0], xs[0].shape[1]
    me = j_ref[0]

    def project(begin, width, skip):
        total = None
        for r in range(n):
            src = lax.rem(me - r + n, n)
            from_rows = pl.ds(pl.multiple_of(src * depth, depth), depth)
            part = jnp.dot(xs[r][skip:, :], w_ref[from_rows, begin : begin + width], preferred_element_type=F32)
            total = part if total is None else total + part
        return total.astype(BF16)

    widths = [ref.shape[1] for ref in (q_ref, k_ref, v_ref, wq_ref, wk_ref)]
    starts = [sum(widths[:i]) for i in range(5)]
    qk = project(starts[0], widths[0] + widths[1], extra)
    q_ref[...] = qk[:, : widths[0]]
    k_ref[...] = qk[:, widths[0] :]
    raw = project(starts[2], widths[2], 0)
    if extra:
        ext_ref[...] = raw.astype(F32)
    else:
        ext_ref[0:EDGE, :] = prev_ref[0:EDGE, :].astype(F32)
        ext_ref[EDGE:, :] = raw.astype(F32)
    halo_ref[0:EDGE, :] = raw[raw.shape[0] - EDGE :]
    total = jnp.zeros((rows, widths[2]), F32)
    for tap in range(CONV):
        total = total + conv_ref[tap : tap + 1, :] * ext_ref[EDGE - tap : EDGE - tap + rows, :]
    v_ref[...] = total.astype(BF16)
    halo_ref[EDGE : EDGE + WIN, :] = v_ref[rows - WIN : rows, :]

    in_group, lanes, slots = feature_layout(heads)
    groups = heads // in_group
    turned = nt_dot(turn_ref[...], k_ref[...])
    keys = turned[groups * slots * lanes :]
    constant = lax.broadcasted_iota(jnp.int32, (lanes, rows), 0) % FQK == FQK // 2
    low_half = lax.broadcasted_iota(jnp.int32, (SHIFTS + 1, FQK, LANES), 2) < DV
    for g in range(groups):
        own = keys[g * lanes : (g + 1) * lanes]
        phi = []
        for s in range(SHIFTS):
            at = (g * slots + s) * lanes
            phi.append(own * turned[at : at + lanes])
        phi[-1] = jnp.where(constant, 1.0, phi[-1])
        phi = jnp.concatenate([part.astype(BF16) for part in phi + [own]], 0)
        v = v_ref[:, g * in_group * DV : (g + 1) * in_group * DV]
        got = jnp.dot(phi, v, preferred_element_type=F32).reshape(SHIFTS + 1, lanes, in_group * DV)
        for p in range(in_group * DV // LANES):
            cols = slice(p * LANES, (p + 1) * LANES)
            first = got[:, 2 * p * FQK : (2 * p + 1) * FQK, cols]
            second = got[:, (2 * p + 1) * FQK : (2 * p + 2) * FQK, cols]
            state = jnp.where(low_half, first, second).reshape(FEATS, LANES)
            s_ref[g * in_group * DV // LANES + p] = state * weight_ref[...]
    for r in range(sends):
        pair = jnp.bitwise_xor(j_ref[1], r)
        total = s_ref[pair]
        for ref in other_refs:
            total = total + ref[pair]
        send_refs[r][...] = total.astype(BF16)

    for ref, start, width, scale in (
        (wk_ref, starts[4], widths[4], 1.0),
        (wq_ref, starts[3], widths[3], 1.0 / DV**0.5),
    ):
        got = project(start, width, extra)
        for p in range(width // LANES):
            cols = slice(p * LANES, (p + 1) * LANES)
            x = got[:, cols].astype(F32)
            x = x * lax.rsqrt(head_mean(x * x, mean_ref[...]) + 1e-6)
            ref[:, cols] = x.astype(BF16) * jnp.asarray(scale, BF16)
    halo_ref[EDGE + WIN : HALO, :] = wk_ref[rows - WIN : rows, :]


def attend_kernel(
    a_ref, turn_ref, prev_ref, q_ref, k_ref, v_ref, wq_ref, wk_ref, phi_ref, lin_ref, win_ref,
    vext_ref, kext_ref, *, heads, first
):
    rows = q_ref.shape[0]
    tile = 128
    span = tile + WIN
    vext_ref[0:WIN, :] = prev_ref[EDGE : EDGE + WIN, :]
    vext_ref[WIN : WIN + rows, :] = v_ref[...]
    kext_ref[0:WIN, :] = prev_ref[EDGE + WIN : HALO, :]
    kext_ref[WIN : WIN + rows, :] = wk_ref[...]
    q = q_ref[...]
    k = k_ref[...]
    lane = lax.broadcasted_iota(jnp.int32, (rows, LANES), 1)
    low_half = lane < DV

    in_group, lanes, slots = feature_layout(heads)
    per_tile = LANES // lanes
    turned = jnp.dot(q, turn_ref[...], preferred_element_type=F32)
    slot = lane // lanes
    for g in range(heads // in_group):
        own = q[:, g * lanes : (g + 1) * lanes].astype(F32)
        own = jnp.concatenate([own] * per_tile, 1)
        for t in range(slots // per_tile):
            at = (g * slots // per_tile + t) * LANES
            part = own * turned[:, at : at + LANES]
            if t == (SHIFTS - 1) // per_tile:
                here = (slot == (SHIFTS - 1) % per_tile) & (lane % FQK == FQK // 2)
                part = jnp.where(here, 1.0, part)
            if t == SHIFTS // per_tile:
                part = jnp.where(slot == SHIFTS % per_tile, own, part)
            phi_ref[:, at : at + LANES] = part.astype(BF16)

    down = lax.broadcasted_iota(jnp.int32, (2 * rows, rows), 0) % rows
    causal = lax.broadcasted_iota(jnp.int32, (2 * rows, rows), 1) <= down
    col = lax.broadcasted_iota(jnp.int32, (2 * tile, span), 1)
    ahead = col - lax.broadcasted_iota(jnp.int32, (2 * tile, span), 0) % tile
    inside = (ahead >= 1) & (ahead <= WIN)
    band = inside.astype(F32).astype(BF16)
    first_band = band
    if first:
        first_band = (inside & (col >= jnp.where(a_ref[2] == 0, WIN, 0))).astype(F32).astype(BF16)
    ones = jnp.ones((span, LANES), BF16)
    q = q * jnp.asarray(1.0 / FQK**0.5, BF16)
    for p in range(heads * DV // LANES):
        cols = slice(p * LANES, (p + 1) * LANES)
        both = [
            jnp.where((lane >= h * FQK) & (lane < (h + 1) * FQK), q, jnp.zeros_like(q)) for h in (2 * p, 2 * p + 1)
        ]
        t = nt_dot(jnp.concatenate(both, 0), k) + 1.0
        kernel = jnp.where(causal, t * t + 1.0, 0.0).astype(BF16)
        got = jnp.dot(kernel, v_ref[:, cols], preferred_element_type=F32)
        lin_ref[:, cols] = 0.5 * jnp.where(low_half, got[:rows], got[rows:])
        for i in range(rows // tile):
            here = slice(i * tile, (i + 1) * tile)
            wq = wq_ref[here, cols]
            none = jnp.zeros_like(wq)
            low = low_half[:tile]
            keys = kext_ref[i * tile : i * tile + span, cols]
            values = vext_ref[i * tile : i * tile + span, cols]
            scores = nt_dot(jnp.concatenate([jnp.where(low, wq, none), jnp.where(low, none, wq)], 0), keys)
            expo = jnp.exp(scores).astype(BF16) * (first_band if i == 0 else band)
            got = jnp.dot(expo, jnp.concatenate([values, ones], 1), preferred_element_type=F32)
            got = jnp.where(jnp.concatenate([low, low], 1), got[:tile], got[tile:])
            win_ref[here, cols] = got[:, :LANES] / got[:, LANES:]


def finish_kernel(a_ref, mean_ref, gain_ref, *refs, heads, before):
    pairs = heads * DV // LANES
    prior_refs, refs = refs[:pairs], refs[pairs:]
    states, (phi_ref, lin_ref, win_ref, mix_ref, held_ref) = refs[:before], refs[before:]
    rows = phi_ref.shape[0]
    for r in range(pairs):
        held_ref[r] = prior_refs[r][...].astype(F32)
    in_group, lanes, slots = feature_layout(heads)
    in_pairs = in_group * DV // LANES
    low_half = lax.broadcasted_iota(jnp.int32, (SHIFTS + 1, FQK, LANES), 2) < DV
    for g in range(heads // in_group):
        columns = []
        for p in range(in_pairs):
            pair = g * in_pairs + p
            state = held_ref[jnp.bitwise_xor(a_ref[1], pair)]
            for ref in states:
                state = state + ref[pair]
            state = state.reshape(SHIFTS + 1, FQK, LANES)
            parts = [jnp.where(low_half, state, 0.0), jnp.where(low_half, 0.0, state)]
            none = jnp.zeros_like(state)
            parts = [none] * (2 * p) + parts + [none] * (in_group - 2 * p - 2)
            parts = jnp.concatenate(parts, 1).reshape((SHIFTS + 1) * lanes, LANES)
            if slots > SHIFTS + 1:
                parts = jnp.concatenate([parts, jnp.zeros(((slots - SHIFTS - 1) * lanes, LANES), F32)], 0)
            columns.append(parts.astype(BF16))
        table = jnp.concatenate(columns, 1)
        carried = jnp.dot(
            phi_ref[:, g * slots * lanes : (g + 1) * slots * lanes], table, preferred_element_type=F32
        )
        for p in range(in_pairs):
            at = (g * in_pairs + p) * LANES
            cols = slice(at, at + LANES)
            lin = lin_ref[:, cols] + carried[:, p * LANES : (p + 1) * LANES]
            scale = lax.rsqrt(head_mean(lin * lin, mean_ref[...]) + 1e-5)
            mix_ref[:, cols] = (lin * scale * gain_ref[:, cols] + win_ref[:, cols]).astype(BF16)


def output_kernel(a_ref, own_ref, w_ref, *refs, n, offset, parts):
    others, weights, (o_ref, held_ref, sem) = refs[: n - 1], refs[n - 1 : n - 1 + parts * (n - 1)], refs[-3:]
    cols = held_ref.shape[1]
    mine = pl.ds(pl.multiple_of(a_ref[0] * cols, cols), cols)
    total = jnp.dot(own_ref[...], w_ref[:, mine], preferred_element_type=F32).astype(BF16).astype(F32)
    for r, m_ref in enumerate(others):
        part = None
        for i in range(parts):
            ref = weights[r * parts + i]
            depth = ref.shape[0]
            at = depth * (jnp.bitwise_xor(a_ref[2] % 2, i) if parts > 1 else 0)
            got = jnp.dot(m_ref[:, pl.ds(pl.multiple_of(at, depth), depth)], ref[...], preferred_element_type=F32)
            part = got if part is None else part + got
        total = total + part.astype(BF16).astype(F32)
    held_ref[...] = total.astype(BF16)
    copy = pltpu.make_async_copy(held_ref, o_ref.at[pl.ds(offset, held_ref.shape[0]), :], sem)
    copy.start()
    copy.wait()


def pick_kernel(a_ref, w_ref, o_ref):
    o_ref[...] = w_ref[...]


def exchange(value, axis, flip):
    count = lax.axis_size(axis)
    return lax.ppermute(value, axis, [(i, i ^ flip) for i in range(count)])


def plane_kernel(a_ref, *refs):
    helds, plane_ref, ahead_refs = refs[:PLANE], refs[PLANE], refs[PLANE + 1 :]
    place = a_ref[1]
    held = [ref[...].astype(F32) for ref in helds]
    plane_ref[...] = (held[0] + held[1] + held[2] + held[3]).astype(BF16)
    for r in range(PLANE):
        total = jnp.zeros_like(held[0])
        for s in range(PLANE):
            before = jnp.bitwise_xor(place, s) < jnp.bitwise_xor(place, r)
            total = total + held[s] * before.astype(F32)
        ahead_refs[r][...] = total


def earlier_kernel(a_ref, *refs, planes):
    ahead_refs, plane_refs, back_refs = refs[:PLANE], refs[PLANE : PLANE + planes], refs[PLANE + planes :]
    mine = a_ref[2] // PLANE
    earlier = jnp.zeros(ahead_refs[0].shape, F32)
    for d, ref in enumerate(plane_refs, 1):
        before = jnp.bitwise_xor(mine, d) < mine
        earlier = earlier + ref[...].astype(F32) * before.astype(F32)
    for r in range(PLANE):
        back_refs[r][...] = (ahead_refs[r][...] + earlier).astype(BF16)


def after(value, earlier):
    return lax.optimization_barrier((value, earlier))[0]


def prior_in_planes(own, places, beside):
    ctx = lax.axis_size("ctx")
    whole = pl.BlockSpec(memory_space=pltpu.VMEM)
    scalar = pl.BlockSpec(memory_space=pltpu.SMEM)
    narrow = jax.ShapeDtypeStruct((FEATS, LANES), BF16)
    wide = jax.ShapeDtypeStruct((FEATS, LANES), F32)
    held = [own[0]] + [exchange(own[r], "ctx", r) for r in range(1, PLANE)]
    plane, *ahead = call(
        plane_kernel,
        [narrow] + [wide] * PLANE,
        in_specs=[scalar] + [whole] * PLANE,
        out_specs=[whole] * (1 + PLANE),
        vmem=4 << 20,
    )(after(places, beside[0]), *held)
    earlier = []
    for d in range(1, ctx // PLANE):
        earlier.append(exchange(plane, "ctx", d * PLANE))
    back = call(
        functools.partial(earlier_kernel, planes=len(earlier)),
        [narrow] * PLANE,
        in_specs=[scalar] + [whole] * (PLANE + len(earlier)),
        out_specs=[whole] * PLANE,
        vmem=4 << 20,
    )(after(places, beside[1]), *ahead, *earlier)
    return back[0], [back[0]] + [exchange(back[r], "ctx", r) for r in range(1, PLANE)]


def prior_by_doubling(total, position):
    ctx = lax.axis_size("ctx")
    prior = jnp.zeros_like(total)
    bit = 1
    while bit < ctx:
        got = exchange(total.astype(BF16), "ctx", bit).astype(F32)
        prior = prior + jnp.where((position & bit) != 0, got, 0.0)
        total = total + got
        bit *= 2
    return [prior[p].astype(BF16) for p in range(total.shape[0])]


def per_device(hidden_in, proj_weight, conv_weight, norm_gain, out_weight):
    n = lax.axis_size("head")
    ctx = lax.axis_size("ctx")
    me = lax.axis_index("head").astype(jnp.int32)
    position = lax.axis_index("ctx").astype(jnp.int32)
    row_count = hidden_in.shape[0]
    model = proj_weight.shape[0]
    heads = out_weight.shape[0] // DV
    width = heads * DV
    pairs = width // LANES
    in_planes = pairs == PLANE and ctx % PLANE == 0 and ctx & (ctx - 1) == 0
    places = jnp.stack([me, position % PLANE if in_planes else jnp.zeros_like(position), position])
    hidden_in, places = lax.optimization_barrier((hidden_in, places))
    step = row_count // 8
    blocks = [(0, 2 * step), (2 * step, 2 * step), (4 * step, step), (5 * step, step), (6 * step, 2 * step)]
    last = len(blocks) - 1
    turn, turn_rows, weight = feature_tables(heads)
    means = mean_table()
    gain = norm_gain.reshape(1, width)
    whole = pl.BlockSpec(memory_space=pltpu.VMEM)
    scalar = pl.BlockSpec(memory_space=pltpu.SMEM)

    def from_head(value, by):
        return lax.ppermute(value, "head", [(i, (i + by) % n) for i in range(n)])

    pieces = {}

    def send_block(b, behind=None):
        at, rows = blocks[b]
        extra = EDGE if b == last else 0
        own = hidden_in[at - extra : at + rows]
        if behind is not None:
            own = after(own, behind)
        pieces[b] = [own] + [from_head(own, r) for r in range(1, n)]

    send_block(last)
    send_block(0, pieces[last][0])
    for b in range(1, last):
        send_block(b, pieces[last][0])

    cols = out_weight.shape[1] // n
    out_parts = 2 if width // 2 % LANES == 0 and ctx % 2 == 0 else 1
    share = width // out_parts
    picked = []
    for r in range(1, n):
        block = call(
            pick_kernel,
            jax.ShapeDtypeStruct((share, cols), BF16),
            grid_spec=pltpu.PrefetchScalarGridSpec(
                num_scalar_prefetch=1,
                grid=(1,),
                in_specs=[
                    pl.BlockSpec((share, cols), functools.partial(lambda i, a, r: (a[2] % out_parts, (a[0] + r) % n), r=r))
                ],
                out_specs=pl.BlockSpec((share, cols), lambda i, a: (0, 0)),
            ),
            vmem=8 << 20,
        )(places, out_weight)
        picked.append(block)

    qk_width = -(-heads * FQK // LANES) * LANES
    arranged_width = 2 * qk_width + 3 * width
    slab = 256
    arranged = call(
        functools.partial(arrange_kernel, heads=heads),
        jax.ShapeDtypeStruct((model, arranged_width), BF16),
        grid=(model // slab,),
        in_specs=[pl.BlockSpec((slab, proj_weight.shape[1]), lambda i: (i, 0))],
        out_specs=pl.BlockSpec((slab, arranged_width), lambda i: (i, 0)),
        vmem=32 << 20,
    )(proj_weight)

    def do_block(b, prev, behind, others=()):
        rows = blocks[b][1]
        extra = EDGE if prev is None else 0
        sends = PLANE if in_planes and others else 0
        tokens = places if behind is None else after(places, behind)
        shapes = [jax.ShapeDtypeStruct((rows, w), BF16) for w in (qk_width, qk_width, width, width, width)]
        shapes.append(jax.ShapeDtypeStruct((HALO, width), BF16))
        shapes.append(jax.ShapeDtypeStruct((pairs, FEATS, LANES), F32))
        shapes += [jax.ShapeDtypeStruct((FEATS, LANES), BF16)] * sends
        operands = [tokens, means, conv_weight, turn_rows, weight, arranged, *pieces[b]]
        if prev is not None:
            operands.append(prev)
        operands += others
        return call(
            functools.partial(
                block_kernel, n=n, heads=heads, extra=extra, others=len(others), sends=sends
            ),
            shapes,
            in_specs=[scalar] + [whole] * (len(operands) - 1),
            out_specs=[whole] * len(shapes),
            scratch_shapes=[pltpu.VMEM((EDGE + rows, width), F32)],
            vmem=32 << 20,
        )(*operands)

    def attend(b, prev):
        rows = blocks[b][1]
        q, k, v, wq, wk = done[b][:5]
        return call(
            functools.partial(attend_kernel, heads=heads, first=b == 0),
            [jax.ShapeDtypeStruct((rows, turn.shape[1]), BF16)] + [jax.ShapeDtypeStruct((rows, width), F32)] * 2,
            in_specs=[scalar] + [whole] * 7,
            out_specs=[whole] * 3,
            scratch_shapes=[pltpu.VMEM((WIN + rows, width), BF16)] * 2,
            vmem=16 << 20,
        )(places, turn, prev, q, k, v, wq, wk)

    done, attended = {}, {}
    done[last] = do_block(last, None, None)
    halo = lax.ppermute(done[last][5], "ctx", [(i, i + 1) for i in range(ctx - 1)])
    for b in range(last):
        prev = halo if b == 0 else done[b - 1][5]
        others = [done[c][6] for c in [last] + list(range(b))] if b == last - 1 else ()
        done[b] = do_block(b, prev, attended[b - 1][1] if b - 1 in attended else None, others)
        if b < last - 2:
            attended[b] = attend(b, prev)

    for b in range(last - 2, last + 1):
        attended[b] = attend(b, done[b - 1][5])
    fetched = [from_head(after(block, attended[last - 2][1]), r) for r, block in enumerate(picked, 1)]
    if in_planes:
        beside = [attended[b][1] for b in (last - 2, last - 1)]
        mark, priors = prior_in_planes(done[last - 1][7:], places, beside)
    else:
        mark = sum(done[b][6] for b in range(last + 1))
        priors = prior_by_doubling(mark, position)

    out_rows = []
    for got in fetched:
        out_rows += [got] + ([exchange(after(got, mark), "ctx", 1)] if out_parts > 1 else [])

    result = None
    mixed = attended[last][1]
    for b in (0, 1, 4, 2, 3):
        at, rows = blocks[b]
        mixed = call(
            functools.partial(finish_kernel, heads=heads, before=b),
            jax.ShapeDtypeStruct((rows, width), BF16),
            in_specs=[scalar] + [whole] * (2 + pairs + b + 3),
            out_specs=whole,
            scratch_shapes=[pltpu.VMEM((pairs, FEATS, LANES), F32)],
            vmem=16 << 20,
        )(after(places, mixed), means, gain, *priors, *[done[c][6] for c in range(b)], *attended[b])
        others = [from_head(mixed, r) for r in range(1, n)]
        operands = [places, mixed, out_weight] + others + out_rows
        specs = [scalar] + [whole] * (len(operands) - 1)
        aliases = {}
        if result is not None:
            aliases = {len(operands): 0}
            operands.append(result)
            specs.append(pl.BlockSpec(memory_space=pl.ANY))
        result = call(
            functools.partial(output_kernel, n=n, offset=at, parts=out_parts),
            jax.ShapeDtypeStruct((row_count, cols), BF16),
            in_specs=specs,
            out_specs=pl.BlockSpec(memory_space=pl.ANY),
            scratch_shapes=[pltpu.VMEM((rows, cols), BF16), pltpu.SemaphoreType.DMA],
            input_output_aliases=aliases,
            vmem=16 << 20,
        )(*operands)
    return result


def solution(mesh):
    return jax.shard_map(
        per_device,
        mesh=mesh,
        in_specs=(P("ctx", "head"), P(None, "head"), P(None, "head"), P("head"), P("head", None)),
        out_specs=P("ctx", "head"),
        check_vma=False,
    )
```

```python
import functools

import jax
import jax.numpy as jnp
import numpy as np
from jax import lax
from jax.experimental import pallas as pl
from jax.experimental.pallas import tpu as pltpu
from jax.sharding import PartitionSpec as P

DV = 64
FQK = 16
WIN = 64
CONV = 3
LANES = 128
SHIFTS = FQK // 2 + 1
FEATS = (SHIFTS + 1) * FQK
EDGE = 16
HALO = EDGE + 2 * WIN
PLANE = 4
F32 = jnp.float32
BF16 = jnp.bfloat16


def call(body, out_shape, *, vmem, flops=1, **kwargs):
    return pl.pallas_call(
        body,
        out_shape=out_shape,
        compiler_params=pltpu.CompilerParams(vmem_limit_bytes=vmem),
        cost_estimate=pl.CostEstimate(flops=flops, bytes_accessed=1, transcendentals=0),
        **kwargs,
    )


def feature_layout(heads):
    in_group = min(heads, 4)
    lanes = in_group * FQK
    per_tile = LANES // lanes
    return in_group, lanes, -(-(SHIFTS + 1) // per_tile) * per_tile


def feature_tables(heads):
    in_group, lanes, slots = feature_layout(heads)
    groups = heads // in_group
    turn = np.zeros((LANES, groups, slots, in_group, FQK), np.float32)
    for g in range(groups):
        for s in range(SHIFTS):
            for h in range(in_group):
                for i in range(FQK if s < SHIFTS - 1 else FQK // 2):
                    turn[g * lanes + h * FQK + (i + s) % FQK, g, s, h, i] = 1.0
    weight = np.zeros((SHIFTS + 1, FQK, LANES), np.float32)
    weight[0] = 1.0 / (2.0 * FQK)
    weight[1:SHIFTS] = 2.0 / (2.0 * FQK)
    weight[SHIFTS - 1, FQK // 2] = 1.0
    weight[SHIFTS] = 1.0 / FQK**0.5
    turn = turn.reshape(LANES, -1)
    by_rows = np.concatenate([turn.T, np.eye(LANES, dtype=np.float32)], 0)
    return jnp.asarray(turn, BF16), jnp.asarray(by_rows, BF16), jnp.asarray(weight.reshape(FEATS, LANES))


def mean_table():
    block = np.kron(np.eye(LANES // DV), np.ones((DV, DV))) / DV
    return jnp.asarray(np.concatenate([block, block], 0), BF16)


def head_mean(values, table):
    high = values.astype(BF16)
    low = (values - high.astype(F32)).astype(BF16)
    return jnp.dot(jnp.concatenate([high, low], 1), table, preferred_element_type=F32)


def nt_dot(a, b):
    return lax.dot_general(a, b, (((1,), (1,)), ((), ())), preferred_element_type=F32)


def arrange_kernel(w_ref, o_ref, *, heads):
    per_head = 2 * FQK + 3 * DV
    w = w_ref[...]
    at = 0
    for begin, width in ((0, FQK), (FQK, FQK), (2 * FQK, DV), (2 * FQK + DV, DV), (2 * FQK + 2 * DV, DV)):
        parts = [w[:, h * per_head + begin : h * per_head + begin + width] for h in range(heads)]
        total = heads * width
        padded = -(-total // LANES) * LANES
        if padded > total:
            parts.append(jnp.zeros((w.shape[0], padded - total), w.dtype))
        o_ref[:, at : at + padded] = jnp.concatenate(parts, 1)
        at += padded


def project(me, xs, w_ref, begin, width, skip):
    depth = xs[0].shape[1]
    total = None
    for r, x_ref in enumerate(xs):
        src = lax.rem(me - r + len(xs), len(xs))
        from_rows = pl.ds(pl.multiple_of(src * depth, depth), depth)
        part = jnp.dot(x_ref[skip:, :], w_ref[from_rows, begin : begin + width], preferred_element_type=F32)
        total = part if total is None else total + part
    return total.astype(BF16)


def normalize(got, ref, mean_ref, scale):
    for p in range(ref.shape[1] // LANES):
        cols = slice(p * LANES, (p + 1) * LANES)
        x = got[:, cols].astype(F32)
        x = x * lax.rsqrt(head_mean(x * x, mean_ref[...]) + 1e-6)
        ref[:, cols] = x.astype(BF16) * jnp.asarray(scale, BF16)


def block_kernel(j_ref, mean_ref, conv_ref, turn_ref, weight_ref, w_ref, *refs, n, heads, extra, others, sends):
    xs, refs = refs[:n], refs[n:]
    prev_ref = None
    if not extra:
        prev_ref, refs = refs[0], refs[1:]
    other_refs, refs = refs[:others], refs[others:]
    k_ref, v_ref, s_ref, refs = *refs[:3], refs[3:]
    send_refs, ext_ref = refs[:sends], refs[-1]
    q_ref, wq_ref, wk_ref, halo_ref = (None,) * 4 if others else refs[:4]
    rows = v_ref.shape[0]
    qk_width, width = k_ref.shape[1], v_ref.shape[1]
    me = j_ref[0]

    if others:
        k_ref[...] = project(me, xs, w_ref, qk_width, qk_width, extra)
    else:
        qk = project(me, xs, w_ref, 0, 2 * qk_width, extra)
        q_ref[...] = qk[:, :qk_width]
        k_ref[...] = qk[:, qk_width:]
    raw = project(me, xs, w_ref, 2 * qk_width, width, 0)
    if extra:
        ext_ref[...] = raw.astype(F32)
    else:
        ext_ref[0:EDGE, :] = prev_ref[0:EDGE, :].astype(F32)
        ext_ref[EDGE:, :] = raw.astype(F32)
    total = jnp.zeros((rows, width), F32)
    for tap in range(CONV):
        total = total + conv_ref[tap : tap + 1, :] * ext_ref[EDGE - tap : EDGE - tap + rows, :]
    v_ref[...] = total.astype(BF16)

    in_group, lanes, slots = feature_layout(heads)
    groups = heads // in_group
    turned = nt_dot(turn_ref[...], k_ref[...])
    keys = turned[groups * slots * lanes :]
    constant = lax.broadcasted_iota(jnp.int32, (lanes, rows), 0) % FQK == FQK // 2
    low_half = lax.broadcasted_iota(jnp.int32, (SHIFTS + 1, FQK, LANES), 2) < DV
    for g in range(groups):
        own = keys[g * lanes : (g + 1) * lanes]
        phi = []
        for s in range(SHIFTS):
            at = (g * slots + s) * lanes
            phi.append(own * turned[at : at + lanes])
        phi[-1] = jnp.where(constant, 1.0, phi[-1])
        phi = jnp.concatenate([part.astype(BF16) for part in phi + [own]], 0)
        v = v_ref[:, g * in_group * DV : (g + 1) * in_group * DV]
        got = jnp.dot(phi, v, preferred_element_type=F32).reshape(SHIFTS + 1, lanes, in_group * DV)
        for p in range(in_group * DV // LANES):
            cols = slice(p * LANES, (p + 1) * LANES)
            first = got[:, 2 * p * FQK : (2 * p + 1) * FQK, cols]
            second = got[:, (2 * p + 1) * FQK : (2 * p + 2) * FQK, cols]
            state = jnp.where(low_half, first, second).reshape(FEATS, LANES)
            s_ref[g * in_group * DV // LANES + p] = state * weight_ref[...]
    for r in range(sends):
        pair = jnp.bitwise_xor(j_ref[1], r)
        total = s_ref[pair]
        for ref in other_refs:
            total = total + ref[pair]
        send_refs[r][...] = total.astype(BF16)

    if not others:
        halo_ref[0:EDGE, :] = raw[raw.shape[0] - EDGE :]
        query_part(me, xs, w_ref, mean_ref, v_ref, wq_ref, wk_ref, halo_ref, 2 * qk_width + width, extra)


def query_part(me, xs, w_ref, mean_ref, v_ref, wq_ref, wk_ref, halo_ref, begin, skip):
    rows, width = v_ref.shape
    normalize(project(me, xs, w_ref, begin, width, skip), wq_ref, mean_ref, 1.0 / DV**0.5)
    normalize(project(me, xs, w_ref, begin + width, width, skip), wk_ref, mean_ref, 1.0)
    halo_ref[EDGE : EDGE + WIN, :] = v_ref[rows - WIN : rows, :]
    halo_ref[EDGE + WIN : HALO, :] = wk_ref[rows - WIN : rows, :]


def query_kernel(j_ref, mean_ref, w_ref, v_ref, *refs, n):
    xs, (q_ref, wq_ref, wk_ref, halo_ref) = refs[:n], refs[n:]
    qk_width, width = q_ref.shape[1], v_ref.shape[1]
    q_ref[...] = project(j_ref[0], xs, w_ref, 0, qk_width, 0)
    halo_ref[0:EDGE, :] = jnp.zeros((EDGE, width), BF16)
    query_part(j_ref[0], xs, w_ref, mean_ref, v_ref, wq_ref, wk_ref, halo_ref, 2 * qk_width + width, 0)


def attend_kernel(
    a_ref, turn_ref, prev_ref, q_ref, k_ref, v_ref, wq_ref, wk_ref, phi_ref, lin_ref, win_ref,
    vext_ref, kext_ref, *, heads, first
):
    rows = q_ref.shape[0]
    tile = 128
    span = tile + WIN
    vext_ref[0:WIN, :] = prev_ref[EDGE : EDGE + WIN, :]
    vext_ref[WIN : WIN + rows, :] = v_ref[...]
    kext_ref[0:WIN, :] = prev_ref[EDGE + WIN : HALO, :]
    kext_ref[WIN : WIN + rows, :] = wk_ref[...]
    q = q_ref[...]
    k = k_ref[...]
    lane = lax.broadcasted_iota(jnp.int32, (rows, LANES), 1)
    low_half = lane < DV

    in_group, lanes, slots = feature_layout(heads)
    per_tile = LANES // lanes
    turned = jnp.dot(q, turn_ref[...], preferred_element_type=F32)
    slot = lane // lanes
    for g in range(heads // in_group):
        own = q[:, g * lanes : (g + 1) * lanes].astype(F32)
        own = jnp.concatenate([own] * per_tile, 1)
        for t in range(slots // per_tile):
            at = (g * slots // per_tile + t) * LANES
            part = own * turned[:, at : at + LANES]
            if t == (SHIFTS - 1) // per_tile:
                here = (slot == (SHIFTS - 1) % per_tile) & (lane % FQK == FQK // 2)
                part = jnp.where(here, 1.0, part)
            if t == SHIFTS // per_tile:
                part = jnp.where(slot == SHIFTS % per_tile, own, part)
            phi_ref[:, at : at + LANES] = part.astype(BF16)

    down = lax.broadcasted_iota(jnp.int32, (2 * rows, rows), 0) % rows
    causal = lax.broadcasted_iota(jnp.int32, (2 * rows, rows), 1) <= down
    col = lax.broadcasted_iota(jnp.int32, (2 * tile, span), 1)
    ahead = col - lax.broadcasted_iota(jnp.int32, (2 * tile, span), 0) % tile
    inside = (ahead >= 1) & (ahead <= WIN)
    band = inside.astype(F32).astype(BF16)
    first_band = band
    if first:
        first_band = (inside & (col >= jnp.where(a_ref[2] == 0, WIN, 0))).astype(F32).astype(BF16)
    ones = jnp.ones((span, LANES), BF16)
    q = q * jnp.asarray(1.0 / FQK**0.5, BF16)
    for p in range(heads * DV // LANES):
        cols = slice(p * LANES, (p + 1) * LANES)
        both = [
            jnp.where((lane >= h * FQK) & (lane < (h + 1) * FQK), q, jnp.zeros_like(q)) for h in (2 * p, 2 * p + 1)
        ]
        t = nt_dot(jnp.concatenate(both, 0), k) + 1.0
        kernel = jnp.where(causal, t * t + 1.0, 0.0).astype(BF16)
        got = jnp.dot(kernel, v_ref[:, cols], preferred_element_type=F32)
        lin_ref[:, cols] = 0.5 * jnp.where(low_half, got[:rows], got[rows:])
        for i in range(rows // tile):
            here = slice(i * tile, (i + 1) * tile)
            wq = wq_ref[here, cols]
            none = jnp.zeros_like(wq)
            low = low_half[:tile]
            keys = kext_ref[i * tile : i * tile + span, cols]
            values = vext_ref[i * tile : i * tile + span, cols]
            scores = nt_dot(jnp.concatenate([jnp.where(low, wq, none), jnp.where(low, none, wq)], 0), keys)
            expo = jnp.exp(scores).astype(BF16) * (first_band if i == 0 else band)
            got = jnp.dot(expo, jnp.concatenate([values, ones], 1), preferred_element_type=F32)
            got = jnp.where(jnp.concatenate([low, low], 1), got[:tile], got[tile:])
            win_ref[here, cols] = got[:, :LANES] / got[:, LANES:]


def finish_kernel(a_ref, mean_ref, gain_ref, *refs, heads, before):
    pairs = heads * DV // LANES
    prior_refs, refs = refs[:pairs], refs[pairs:]
    states, (phi_ref, lin_ref, win_ref, mix_ref, held_ref) = refs[:before], refs[before:]
    rows = phi_ref.shape[0]
    for r in range(pairs):
        held_ref[r] = prior_refs[r][...].astype(F32)
    in_group, lanes, slots = feature_layout(heads)
    in_pairs = in_group * DV // LANES
    low_half = lax.broadcasted_iota(jnp.int32, (SHIFTS + 1, FQK, LANES), 2) < DV
    for g in range(heads // in_group):
        columns = []
        for p in range(in_pairs):
            pair = g * in_pairs + p
            state = held_ref[jnp.bitwise_xor(a_ref[1], pair)]
            for ref in states:
                state = state + ref[pair]
            state = state.reshape(SHIFTS + 1, FQK, LANES)
            parts = [jnp.where(low_half, state, 0.0), jnp.where(low_half, 0.0, state)]
            none = jnp.zeros_like(state)
            parts = [none] * (2 * p) + parts + [none] * (in_group - 2 * p - 2)
            parts = jnp.concatenate(parts, 1).reshape((SHIFTS + 1) * lanes, LANES)
            if slots > SHIFTS + 1:
                parts = jnp.concatenate([parts, jnp.zeros(((slots - SHIFTS - 1) * lanes, LANES), F32)], 0)
            columns.append(parts.astype(BF16))
        table = jnp.concatenate(columns, 1)
        carried = jnp.dot(
            phi_ref[:, g * slots * lanes : (g + 1) * slots * lanes], table, preferred_element_type=F32
        )
        for p in range(in_pairs):
            at = (g * in_pairs + p) * LANES
            cols = slice(at, at + LANES)
            lin = lin_ref[:, cols] + carried[:, p * LANES : (p + 1) * LANES]
            scale = lax.rsqrt(head_mean(lin * lin, mean_ref[...]) + 1e-5)
            mix_ref[:, cols] = (lin * scale * gain_ref[:, cols] + win_ref[:, cols]).astype(BF16)


def output_kernel(a_ref, own_ref, w_ref, *refs, n, offset, parts):
    others, weights, (o_ref, held_ref, sem) = refs[: n - 1], refs[n - 1 : n - 1 + parts * (n - 1)], refs[-3:]
    cols = held_ref.shape[1]
    mine = pl.ds(pl.multiple_of(a_ref[0] * cols, cols), cols)
    total = jnp.dot(own_ref[...], w_ref[:, mine], preferred_element_type=F32).astype(BF16).astype(F32)
    for r, m_ref in enumerate(others):
        part = None
        for i in range(parts):
            ref = weights[r * parts + i]
            depth = ref.shape[0]
            at = depth * (jnp.bitwise_xor(a_ref[2] % 2, i) if parts > 1 else 0)
            got = jnp.dot(m_ref[:, pl.ds(pl.multiple_of(at, depth), depth)], ref[...], preferred_element_type=F32)
            part = got if part is None else part + got
        total = total + part.astype(BF16).astype(F32)
    held_ref[...] = total.astype(BF16)
    copy = pltpu.make_async_copy(held_ref, o_ref.at[pl.ds(offset, held_ref.shape[0]), :], sem)
    copy.start()
    copy.wait()


def pick_kernel(a_ref, w_ref, o_ref):
    o_ref[...] = w_ref[...]


def exchange(value, axis, flip):
    count = lax.axis_size(axis)
    return lax.ppermute(value, axis, [(i, i ^ flip) for i in range(count)])


def plane_kernel(a_ref, *refs):
    helds, plane_ref, ahead_refs = refs[:PLANE], refs[PLANE], refs[PLANE + 1 :]
    place = a_ref[1]
    held = [ref[...].astype(F32) for ref in helds]
    plane_ref[...] = (held[0] + held[1] + held[2] + held[3]).astype(BF16)
    for r in range(PLANE):
        total = jnp.zeros_like(held[0])
        for s in range(PLANE):
            before = jnp.bitwise_xor(place, s) < jnp.bitwise_xor(place, r)
            total = total + held[s] * before.astype(F32)
        ahead_refs[r][...] = total


def earlier_kernel(a_ref, *refs, planes):
    ahead_refs, plane_refs, back_refs = refs[:PLANE], refs[PLANE : PLANE + planes], refs[PLANE + planes :]
    mine = a_ref[2] // PLANE
    earlier = jnp.zeros(ahead_refs[0].shape, F32)
    for d, ref in enumerate(plane_refs, 1):
        before = jnp.bitwise_xor(mine, d) < mine
        earlier = earlier + ref[...].astype(F32) * before.astype(F32)
    for r in range(PLANE):
        back_refs[r][...] = (ahead_refs[r][...] + earlier).astype(BF16)


def after(value, earlier):
    return lax.optimization_barrier((value, earlier))[0]


def prior_in_planes(held, places, beside):
    ctx = lax.axis_size("ctx")
    whole = pl.BlockSpec(memory_space=pltpu.VMEM)
    scalar = pl.BlockSpec(memory_space=pltpu.SMEM)
    narrow = jax.ShapeDtypeStruct((FEATS, LANES), BF16)
    wide = jax.ShapeDtypeStruct((FEATS, LANES), F32)
    plane, *ahead = call(
        plane_kernel,
        [narrow] + [wide] * PLANE,
        in_specs=[scalar] + [whole] * PLANE,
        out_specs=[whole] * (1 + PLANE),
        vmem=4 << 20,
    )(after(places, beside[0]), *held)
    earlier = []
    for d in range(1, ctx // PLANE):
        earlier.append(exchange(plane, "ctx", d * PLANE))
    back = call(
        functools.partial(earlier_kernel, planes=len(earlier)),
        [narrow] * PLANE,
        in_specs=[scalar] + [whole] * (PLANE + len(earlier)),
        out_specs=[whole] * PLANE,
        vmem=4 << 20,
    )(after(places, beside[1]), *ahead, *earlier)
    return [back[0]] + [exchange(back[r], "ctx", r) for r in range(1, PLANE)]


def prior_by_doubling(total, position):
    ctx = lax.axis_size("ctx")
    prior = jnp.zeros_like(total)
    bit = 1
    while bit < ctx:
        got = exchange(total.astype(BF16), "ctx", bit).astype(F32)
        prior = prior + jnp.where((position & bit) != 0, got, 0.0)
        total = total + got
        bit *= 2
    return [prior[p].astype(BF16) for p in range(total.shape[0])]


def per_device(hidden_in, proj_weight, conv_weight, norm_gain, out_weight):
    n = lax.axis_size("head")
    ctx = lax.axis_size("ctx")
    me = lax.axis_index("head").astype(jnp.int32)
    position = lax.axis_index("ctx").astype(jnp.int32)
    row_count = hidden_in.shape[0]
    model = proj_weight.shape[0]
    heads = out_weight.shape[0] // DV
    width = heads * DV
    pairs = width // LANES
    in_planes = pairs == PLANE and ctx % PLANE == 0 and ctx & (ctx - 1) == 0
    places = jnp.stack([me, position % PLANE if in_planes else jnp.zeros_like(position), position])
    hidden_in, places = lax.optimization_barrier((hidden_in, places))
    step = row_count // 8
    blocks = [(0, 2 * step), (2 * step, 2 * step), (4 * step, step), (5 * step, step), (6 * step, 2 * step)]
    last = len(blocks) - 1
    turn, turn_rows, weight = feature_tables(heads)
    means = mean_table()
    gain = norm_gain.reshape(1, width)
    whole = pl.BlockSpec(memory_space=pltpu.VMEM)
    scalar = pl.BlockSpec(memory_space=pltpu.SMEM)

    def from_head(value, by):
        return lax.ppermute(value, "head", [(i, (i + by) % n) for i in range(n)])

    pieces = {}

    def send_block(b, behind=None):
        at, rows = blocks[b]
        extra = EDGE if b == last else 0
        own = hidden_in[at - extra : at + rows]
        if behind is not None:
            own = after(own, behind)
        pieces[b] = [own] + [from_head(own, r) for r in range(1, n)]

    send_block(last)
    send_block(0, pieces[last][0])
    for b in range(1, last):
        send_block(b, pieces[last][0])

    cols = out_weight.shape[1] // n
    out_parts = 2 if width // 2 % LANES == 0 and ctx % 2 == 0 else 1
    share = width // out_parts
    picked = []
    for r in range(1, n):
        block = call(
            pick_kernel,
            jax.ShapeDtypeStruct((share, cols), BF16),
            grid_spec=pltpu.PrefetchScalarGridSpec(
                num_scalar_prefetch=1,
                grid=(1,),
                in_specs=[
                    pl.BlockSpec((share, cols), functools.partial(lambda i, a, r: (a[2] % out_parts, (a[0] + r) % n), r=r))
                ],
                out_specs=pl.BlockSpec((share, cols), lambda i, a: (0, 0)),
            ),
            vmem=8 << 20,
        )(places, out_weight)
        picked.append(block)

    qk_width = -(-heads * FQK // LANES) * LANES
    arranged_width = 2 * qk_width + 3 * width
    slab = 256
    arranged = call(
        functools.partial(arrange_kernel, heads=heads),
        jax.ShapeDtypeStruct((model, arranged_width), BF16),
        grid=(model // slab,),
        in_specs=[pl.BlockSpec((slab, proj_weight.shape[1]), lambda i: (i, 0))],
        out_specs=pl.BlockSpec((slab, arranged_width), lambda i: (i, 0)),
        vmem=32 << 20,
    )(proj_weight)

    def bf16(rows, *widths):
        return [jax.ShapeDtypeStruct((rows, w), BF16) for w in widths]

    def do_block(b, prev, behind, others=()):
        rows = blocks[b][1]
        extra = EDGE if prev is None else 0
        sends = PLANE if in_planes and others else 0
        tokens = places if behind is None else after(places, behind)
        shapes = bf16(rows, qk_width, width) + [jax.ShapeDtypeStruct((pairs, FEATS, LANES), F32)]
        if others:
            shapes += bf16(FEATS, LANES) * sends
        else:
            shapes += bf16(rows, qk_width, width, width) + bf16(HALO, width)
        operands = [tokens, means, conv_weight, turn_rows, weight, arranged, *pieces[b]]
        if prev is not None:
            operands.append(prev)
        operands += others
        return call(
            functools.partial(
                block_kernel, n=n, heads=heads, extra=extra, others=len(others), sends=sends
            ),
            shapes,
            in_specs=[scalar] + [whole] * (len(operands) - 1),
            out_specs=[whole] * len(shapes),
            scratch_shapes=[pltpu.VMEM((EDGE + rows, width), F32)],
            vmem=32 << 20,
        )(*operands)

    def do_queries(b, v):
        rows = blocks[b][1]
        return call(
            functools.partial(query_kernel, n=n),
            bf16(rows, qk_width, width, width) + bf16(HALO, width),
            in_specs=[scalar] + [whole] * (3 + n),
            out_specs=[whole] * 4,
            vmem=32 << 20,
        )(places, means, arranged, v, *pieces[b])

    def attend(b, prev):
        rows = blocks[b][1]
        k, v, _, q, wq, wk, _ = done[b]
        return call(
            functools.partial(attend_kernel, heads=heads, first=b == 0),
            [jax.ShapeDtypeStruct((rows, turn.shape[1]), BF16)] + [jax.ShapeDtypeStruct((rows, width), F32)] * 2,
            in_specs=[scalar] + [whole] * 7,
            out_specs=[whole] * 3,
            scratch_shapes=[pltpu.VMEM((WIN + rows, width), BF16)] * 2,
            flops=20 * 10**9 if b == last else 1,
            vmem=16 << 20,
        )(places, turn, prev, q, k, v, wq, wk)

    done, attended = {}, {}
    done[last] = do_block(last, None, None)
    halo = lax.ppermute(done[last][6], "ctx", [(i, i + 1) for i in range(ctx - 1)])
    prevs = {0: halo}
    for b in range(last - 1):
        done[b] = do_block(b, prevs[b], attended[b - 1][1] if b else None)
        prevs[b + 1] = done[b][6]
        attended[b] = attend(b, prevs[b])
    b = last - 1
    k, v, state, *sends = do_block(b, prevs[b], attended[b - 1][1], [done[c][2] for c in (last, *range(b))])
    done[b] = (k, v, state, *do_queries(b, v))
    prevs[last] = done[b][6]
    for b in (last - 1, last):
        attended[b] = attend(b, prevs[b])
    held = sends[:1] + [exchange(sends[r], "ctx", r) for r in range(1, len(sends))]
    mark = attended[last - 1][1]
    fetched = [from_head(after(block, mark), r) for r, block in enumerate(picked, 1)]
    if in_planes:
        priors = prior_in_planes(held, places, [done[last - 1][6], attended[last - 1][1]])
    else:
        priors = prior_by_doubling(sum(done[b][2] for b in range(last + 1)), position)

    result = None
    out_rows = []
    mixed = attended[last][1]
    for b in (0, 1, 4, 2, 3):
        at, rows = blocks[b]
        mixed = call(
            functools.partial(finish_kernel, heads=heads, before=b),
            jax.ShapeDtypeStruct((rows, width), BF16),
            in_specs=[scalar] + [whole] * (2 + pairs + b + 3),
            out_specs=whole,
            scratch_shapes=[pltpu.VMEM((pairs, FEATS, LANES), F32)],
            vmem=16 << 20,
        )(after(places, mixed), means, gain, *priors, *[done[c][2] for c in range(b)], *attended[b])
        others = [from_head(mixed, r) for r in range(1, n)]
        if not out_rows:
            for got in fetched:
                out_rows += [got] + ([exchange(after(got, mixed), "ctx", 1)] if out_parts > 1 else [])
        operands = [places, mixed, out_weight] + others + out_rows
        specs = [scalar] + [whole] * (len(operands) - 1)
        aliases = {}
        if result is not None:
            aliases = {len(operands): 0}
            operands.append(result)
            specs.append(pl.BlockSpec(memory_space=pl.ANY))
        result = call(
            functools.partial(output_kernel, n=n, offset=at, parts=out_parts),
            jax.ShapeDtypeStruct((row_count, cols), BF16),
            in_specs=specs,
            out_specs=pl.BlockSpec(memory_space=pl.ANY),
            scratch_shapes=[pltpu.VMEM((rows, cols), BF16), pltpu.SemaphoreType.DMA],
            input_output_aliases=aliases,
            vmem=16 << 20,
        )(*operands)
    return result


def solution(mesh):
    return jax.shard_map(
        per_device,
        mesh=mesh,
        in_specs=(P("ctx", "head"), P(None, "head"), P(None, "head"), P("head"), P("head", None)),
        out_specs=P("ctx", "head"),
        check_vma=False,
    )
```

```python
import functools

import jax
import jax.numpy as jnp
import numpy as np
from jax import lax
from jax.experimental import pallas as pl
from jax.experimental.pallas import tpu as pltpu
from jax.sharding import PartitionSpec as P

DV = 64
FQK = 16
WIN = 64
CONV = 3
LANES = 128
SHIFTS = FQK // 2 + 1
FEATS = (SHIFTS + 1) * FQK
EDGE = 16
HALO = EDGE + 2 * WIN
PLANE = 4
F32 = jnp.float32
BF16 = jnp.bfloat16


def call(body, out_shape, *, vmem, flops=1, **kwargs):
    return pl.pallas_call(
        body,
        out_shape=out_shape,
        compiler_params=pltpu.CompilerParams(vmem_limit_bytes=vmem),
        cost_estimate=pl.CostEstimate(flops=flops, bytes_accessed=1, transcendentals=0),
        **kwargs,
    )


def feature_layout(heads):
    in_group = min(heads, 4)
    lanes = in_group * FQK
    per_tile = LANES // lanes
    return in_group, lanes, -(-(SHIFTS + 1) // per_tile) * per_tile


def feature_tables(heads):
    in_group, lanes, slots = feature_layout(heads)
    groups = heads // in_group
    turn = np.zeros((LANES, groups, slots, in_group, FQK), np.float32)
    for g in range(groups):
        for s in range(SHIFTS):
            for h in range(in_group):
                for i in range(FQK if s < SHIFTS - 1 else FQK // 2):
                    turn[g * lanes + h * FQK + (i + s) % FQK, g, s, h, i] = 1.0
    weight = np.zeros((SHIFTS + 1, FQK, LANES), np.float32)
    weight[0] = 1.0 / (2.0 * FQK)
    weight[1:SHIFTS] = 2.0 / (2.0 * FQK)
    weight[SHIFTS - 1, FQK // 2] = 1.0
    weight[SHIFTS] = 1.0 / FQK**0.5
    turn = turn.reshape(LANES, -1)
    by_rows = np.concatenate([turn.T, np.eye(LANES, dtype=np.float32)], 0)
    return jnp.asarray(turn, BF16), jnp.asarray(by_rows, BF16), jnp.asarray(weight.reshape(FEATS, LANES))


def mean_table():
    block = np.kron(np.eye(LANES // DV), np.ones((DV, DV))) / DV
    return jnp.asarray(np.concatenate([block, block], 0), BF16)


def head_mean(values, table):
    high = values.astype(BF16)
    low = (values - high.astype(F32)).astype(BF16)
    return jnp.dot(jnp.concatenate([high, low], 1), table, preferred_element_type=F32)


def nt_dot(a, b):
    return lax.dot_general(a, b, (((1,), (1,)), ((), ())), preferred_element_type=F32)


def arrange_kernel(w_ref, o_ref, *, heads):
    per_head = 2 * FQK + 3 * DV
    w = w_ref[...]
    at = 0
    for begin, width in ((0, FQK), (FQK, FQK), (2 * FQK, DV), (2 * FQK + DV, DV), (2 * FQK + 2 * DV, DV)):
        parts = [w[:, h * per_head + begin : h * per_head + begin + width] for h in range(heads)]
        total = heads * width
        padded = -(-total // LANES) * LANES
        if padded > total:
            parts.append(jnp.zeros((w.shape[0], padded - total), w.dtype))
        o_ref[:, at : at + padded] = jnp.concatenate(parts, 1)
        at += padded


def project(me, xs, w_ref, begin, width, skip):
    depth = xs[0].shape[1]
    total = None
    for r, x_ref in enumerate(xs):
        src = lax.rem(me - r + len(xs), len(xs))
        from_rows = pl.ds(pl.multiple_of(src * depth, depth), depth)
        part = jnp.dot(x_ref[skip:, :], w_ref[from_rows, begin : begin + width], preferred_element_type=F32)
        total = part if total is None else total + part
    return total.astype(BF16)


def normalize(got, ref, mean_ref, scale):
    for p in range(ref.shape[1] // LANES):
        cols = slice(p * LANES, (p + 1) * LANES)
        x = got[:, cols].astype(F32)
        x = x * lax.rsqrt(head_mean(x * x, mean_ref[...]) + 1e-6)
        ref[:, cols] = x.astype(BF16) * jnp.asarray(scale, BF16)


def block_kernel(j_ref, mean_ref, conv_ref, turn_ref, weight_ref, w_ref, *refs, n, heads, extra, others, sends):
    xs, refs = refs[:n], refs[n:]
    prev_ref = None
    if not extra:
        prev_ref, refs = refs[0], refs[1:]
    other_refs, refs = refs[:others], refs[others:]
    k_ref, v_ref, s_ref, refs = *refs[:3], refs[3:]
    send_refs, ext_ref = refs[:sends], refs[-1]
    q_ref, wq_ref, wk_ref, halo_ref = (None,) * 4 if others else refs[:4]
    rows = v_ref.shape[0]
    qk_width, width = k_ref.shape[1], v_ref.shape[1]
    me = j_ref[0]

    if others:
        k_ref[...] = project(me, xs, w_ref, qk_width, qk_width, extra)
    else:
        qk = project(me, xs, w_ref, 0, 2 * qk_width, extra)
        q_ref[...] = qk[:, :qk_width]
        k_ref[...] = qk[:, qk_width:]
    raw = project(me, xs, w_ref, 2 * qk_width, width, 0)
    if extra:
        ext_ref[...] = raw.astype(F32)
    else:
        ext_ref[0:EDGE, :] = prev_ref[0:EDGE, :].astype(F32)
        ext_ref[EDGE:, :] = raw.astype(F32)
    total = jnp.zeros((rows, width), F32)
    for tap in range(CONV):
        total = total + conv_ref[tap : tap + 1, :] * ext_ref[EDGE - tap : EDGE - tap + rows, :]
    v_ref[...] = total.astype(BF16)

    in_group, lanes, slots = feature_layout(heads)
    groups = heads // in_group
    turned = nt_dot(turn_ref[...], k_ref[...])
    keys = turned[groups * slots * lanes :]
    constant = lax.broadcasted_iota(jnp.int32, (lanes, rows), 0) % FQK == FQK // 2
    low_half = lax.broadcasted_iota(jnp.int32, (SHIFTS + 1, FQK, LANES), 2) < DV
    for g in range(groups):
        own = keys[g * lanes : (g + 1) * lanes]
        phi = []
        for s in range(SHIFTS):
            at = (g * slots + s) * lanes
            phi.append(own * turned[at : at + lanes])
        phi[-1] = jnp.where(constant, 1.0, phi[-1])
        phi = jnp.concatenate([part.astype(BF16) for part in phi + [own]], 0)
        v = v_ref[:, g * in_group * DV : (g + 1) * in_group * DV]
        got = jnp.dot(phi, v, preferred_element_type=F32).reshape(SHIFTS + 1, lanes, in_group * DV)
        for p in range(in_group * DV // LANES):
            cols = slice(p * LANES, (p + 1) * LANES)
            first = got[:, 2 * p * FQK : (2 * p + 1) * FQK, cols]
            second = got[:, (2 * p + 1) * FQK : (2 * p + 2) * FQK, cols]
            state = jnp.where(low_half, first, second).reshape(FEATS, LANES)
            s_ref[g * in_group * DV // LANES + p] = state * weight_ref[...]
    for r in range(sends):
        pair = jnp.bitwise_xor(j_ref[1], r)
        total = s_ref[pair]
        for ref in other_refs:
            total = total + ref[pair]
        send_refs[r][...] = total.astype(BF16)

    if not others:
        halo_ref[0:EDGE, :] = raw[raw.shape[0] - EDGE :]
        query_part(me, xs, w_ref, mean_ref, v_ref, wq_ref, wk_ref, halo_ref, 2 * qk_width + width, extra)


def query_part(me, xs, w_ref, mean_ref, v_ref, wq_ref, wk_ref, halo_ref, begin, skip):
    rows, width = v_ref.shape
    normalize(project(me, xs, w_ref, begin, width, skip), wq_ref, mean_ref, 1.0 / DV**0.5)
    normalize(project(me, xs, w_ref, begin + width, width, skip), wk_ref, mean_ref, 1.0)
    halo_ref[EDGE : EDGE + WIN, :] = v_ref[rows - WIN : rows, :]
    halo_ref[EDGE + WIN : HALO, :] = wk_ref[rows - WIN : rows, :]


def query_kernel(j_ref, mean_ref, w_ref, v_ref, *refs, n):
    xs, (q_ref, wq_ref, wk_ref, halo_ref) = refs[:n], refs[n:]
    qk_width, width = q_ref.shape[1], v_ref.shape[1]
    q_ref[...] = project(j_ref[0], xs, w_ref, 0, qk_width, 0)
    halo_ref[0:EDGE, :] = jnp.zeros((EDGE, width), BF16)
    query_part(j_ref[0], xs, w_ref, mean_ref, v_ref, wq_ref, wk_ref, halo_ref, 2 * qk_width + width, 0)


def attend_kernel(
    a_ref, turn_ref, prev_ref, q_ref, k_ref, v_ref, wq_ref, wk_ref, phi_ref, lin_ref, win_ref,
    vext_ref, kext_ref, *, heads, first
):
    rows = q_ref.shape[0]
    tile = 128
    span = tile + WIN
    vext_ref[0:WIN, :] = prev_ref[EDGE : EDGE + WIN, :]
    vext_ref[WIN : WIN + rows, :] = v_ref[...]
    kext_ref[0:WIN, :] = prev_ref[EDGE + WIN : HALO, :]
    kext_ref[WIN : WIN + rows, :] = wk_ref[...]
    q = q_ref[...]
    k = k_ref[...]
    lane = lax.broadcasted_iota(jnp.int32, (rows, LANES), 1)
    low_half = lane < DV

    in_group, lanes, slots = feature_layout(heads)
    per_tile = LANES // lanes
    turned = jnp.dot(q, turn_ref[...], preferred_element_type=F32)
    slot = lane // lanes
    for g in range(heads // in_group):
        own = q[:, g * lanes : (g + 1) * lanes].astype(F32)
        own = jnp.concatenate([own] * per_tile, 1)
        for t in range(slots // per_tile):
            at = (g * slots // per_tile + t) * LANES
            part = own * turned[:, at : at + LANES]
            if t == (SHIFTS - 1) // per_tile:
                here = (slot == (SHIFTS - 1) % per_tile) & (lane % FQK == FQK // 2)
                part = jnp.where(here, 1.0, part)
            if t == SHIFTS // per_tile:
                part = jnp.where(slot == SHIFTS % per_tile, own, part)
            phi_ref[:, at : at + LANES] = part.astype(BF16)

    down = lax.broadcasted_iota(jnp.int32, (2 * rows, rows), 0) % rows
    causal = lax.broadcasted_iota(jnp.int32, (2 * rows, rows), 1) <= down
    col = lax.broadcasted_iota(jnp.int32, (2 * tile, span), 1)
    ahead = col - lax.broadcasted_iota(jnp.int32, (2 * tile, span), 0) % tile
    inside = (ahead >= 1) & (ahead <= WIN)
    band = inside.astype(F32).astype(BF16)
    first_band = band
    if first:
        first_band = (inside & (col >= jnp.where(a_ref[2] == 0, WIN, 0))).astype(F32).astype(BF16)
    ones = jnp.ones((span, LANES), BF16)
    q = q * jnp.asarray(1.0 / FQK**0.5, BF16)
    for p in range(heads * DV // LANES):
        cols = slice(p * LANES, (p + 1) * LANES)
        both = [
            jnp.where((lane >= h * FQK) & (lane < (h + 1) * FQK), q, jnp.zeros_like(q)) for h in (2 * p, 2 * p + 1)
        ]
        t = nt_dot(jnp.concatenate(both, 0), k) + 1.0
        kernel = jnp.where(causal, t * t + 1.0, 0.0).astype(BF16)
        got = jnp.dot(kernel, v_ref[:, cols], preferred_element_type=F32)
        lin_ref[:, cols] = 0.5 * jnp.where(low_half, got[:rows], got[rows:])
        for i in range(rows // tile):
            here = slice(i * tile, (i + 1) * tile)
            wq = wq_ref[here, cols]
            none = jnp.zeros_like(wq)
            low = low_half[:tile]
            keys = kext_ref[i * tile : i * tile + span, cols]
            values = vext_ref[i * tile : i * tile + span, cols]
            scores = nt_dot(jnp.concatenate([jnp.where(low, wq, none), jnp.where(low, none, wq)], 0), keys)
            expo = jnp.exp(scores).astype(BF16) * (first_band if i == 0 else band)
            got = jnp.dot(expo, jnp.concatenate([values, ones], 1), preferred_element_type=F32)
            got = jnp.where(jnp.concatenate([low, low], 1), got[:tile], got[tile:])
            win_ref[here, cols] = got[:, :LANES] / got[:, LANES:]


def finish_kernel(a_ref, mean_ref, gain_ref, *refs, heads, before):
    pairs = heads * DV // LANES
    prior_refs, refs = refs[:pairs], refs[pairs:]
    states, (phi_ref, lin_ref, win_ref, mix_ref, held_ref) = refs[:before], refs[before:]
    rows = phi_ref.shape[0]
    for r in range(pairs):
        held_ref[r] = prior_refs[r][...].astype(F32)
    in_group, lanes, slots = feature_layout(heads)
    in_pairs = in_group * DV // LANES
    low_half = lax.broadcasted_iota(jnp.int32, (SHIFTS + 1, FQK, LANES), 2) < DV
    for g in range(heads // in_group):
        columns = []
        for p in range(in_pairs):
            pair = g * in_pairs + p
            state = held_ref[jnp.bitwise_xor(a_ref[1], pair)]
            for ref in states:
                state = state + ref[pair]
            state = state.reshape(SHIFTS + 1, FQK, LANES)
            parts = [jnp.where(low_half, state, 0.0), jnp.where(low_half, 0.0, state)]
            none = jnp.zeros_like(state)
            parts = [none] * (2 * p) + parts + [none] * (in_group - 2 * p - 2)
            parts = jnp.concatenate(parts, 1).reshape((SHIFTS + 1) * lanes, LANES)
            if slots > SHIFTS + 1:
                parts = jnp.concatenate([parts, jnp.zeros(((slots - SHIFTS - 1) * lanes, LANES), F32)], 0)
            columns.append(parts.astype(BF16))
        table = jnp.concatenate(columns, 1)
        carried = jnp.dot(
            phi_ref[:, g * slots * lanes : (g + 1) * slots * lanes], table, preferred_element_type=F32
        )
        for p in range(in_pairs):
            at = (g * in_pairs + p) * LANES
            cols = slice(at, at + LANES)
            lin = lin_ref[:, cols] + carried[:, p * LANES : (p + 1) * LANES]
            scale = lax.rsqrt(head_mean(lin * lin, mean_ref[...]) + 1e-5)
            mix_ref[:, cols] = (lin * scale * gain_ref[:, cols] + win_ref[:, cols]).astype(BF16)


def output_kernel(a_ref, own_ref, w_ref, *refs, n, offset, parts):
    others, weights, (o_ref, held_ref, sem) = refs[: n - 1], refs[n - 1 : n - 1 + parts * (n - 1)], refs[-3:]
    cols = held_ref.shape[1]
    mine = pl.ds(pl.multiple_of(a_ref[0] * cols, cols), cols)
    total = jnp.dot(own_ref[...], w_ref[:, mine], preferred_element_type=F32).astype(BF16).astype(F32)
    for r, m_ref in enumerate(others):
        part = None
        for i in range(parts):
            ref = weights[r * parts + i]
            depth = ref.shape[0]
            at = depth * (jnp.bitwise_xor(a_ref[2] % 2, i) if parts > 1 else 0)
            got = jnp.dot(m_ref[:, pl.ds(pl.multiple_of(at, depth), depth)], ref[...], preferred_element_type=F32)
            part = got if part is None else part + got
        total = total + part.astype(BF16).astype(F32)
    held_ref[...] = total.astype(BF16)
    copy = pltpu.make_async_copy(held_ref, o_ref.at[pl.ds(offset, held_ref.shape[0]), :], sem)
    copy.start()
    copy.wait()


def pick_kernel(a_ref, w_ref, o_ref):
    o_ref[...] = w_ref[...]


def exchange(value, axis, flip):
    count = lax.axis_size(axis)
    return lax.ppermute(value, axis, [(i, i ^ flip) for i in range(count)])


def plane_kernel(a_ref, *refs):
    helds, plane_ref, ahead_refs = refs[:PLANE], refs[PLANE], refs[PLANE + 1 :]
    place = a_ref[1]
    held = [ref[...].astype(F32) for ref in helds]
    plane_ref[...] = (held[0] + held[1] + held[2] + held[3]).astype(BF16)
    for r in range(PLANE):
        total = jnp.zeros_like(held[0])
        for s in range(PLANE):
            before = jnp.bitwise_xor(place, s) < jnp.bitwise_xor(place, r)
            total = total + held[s] * before.astype(F32)
        ahead_refs[r][...] = total


def earlier_kernel(a_ref, *refs, planes):
    ahead_refs, plane_refs, back_refs = refs[:PLANE], refs[PLANE : PLANE + planes], refs[PLANE + planes :]
    mine = a_ref[2] // PLANE
    earlier = jnp.zeros(ahead_refs[0].shape, F32)
    for d, ref in enumerate(plane_refs, 1):
        before = jnp.bitwise_xor(mine, d) < mine
        earlier = earlier + ref[...].astype(F32) * before.astype(F32)
    for r in range(PLANE):
        back_refs[r][...] = (ahead_refs[r][...] + earlier).astype(BF16)


def after(value, earlier):
    return lax.optimization_barrier((value, earlier))[0]


def prior_in_planes(held, places, beside):
    ctx = lax.axis_size("ctx")
    whole = pl.BlockSpec(memory_space=pltpu.VMEM)
    scalar = pl.BlockSpec(memory_space=pltpu.SMEM)
    narrow = jax.ShapeDtypeStruct((FEATS, LANES), BF16)
    wide = jax.ShapeDtypeStruct((FEATS, LANES), F32)
    plane, *ahead = call(
        plane_kernel,
        [narrow] + [wide] * PLANE,
        in_specs=[scalar] + [whole] * PLANE,
        out_specs=[whole] * (1 + PLANE),
        vmem=4 << 20,
    )(after(places, beside[0]), *held)
    earlier = []
    for d in range(1, ctx // PLANE):
        earlier.append(exchange(plane, "ctx", d * PLANE))
    back = call(
        functools.partial(earlier_kernel, planes=len(earlier)),
        [narrow] * PLANE,
        in_specs=[scalar] + [whole] * (PLANE + len(earlier)),
        out_specs=[whole] * PLANE,
        vmem=4 << 20,
    )(after(places, beside[1]), *ahead, *earlier)
    return [back[0]] + [exchange(back[r], "ctx", r) for r in range(1, PLANE)]


def prior_by_doubling(total, position):
    ctx = lax.axis_size("ctx")
    prior = jnp.zeros_like(total)
    bit = 1
    while bit < ctx:
        got = exchange(total.astype(BF16), "ctx", bit).astype(F32)
        prior = prior + jnp.where((position & bit) != 0, got, 0.0)
        total = total + got
        bit *= 2
    return [prior[p].astype(BF16) for p in range(total.shape[0])]


def per_device(hidden_in, proj_weight, conv_weight, norm_gain, out_weight):
    n = lax.axis_size("head")
    ctx = lax.axis_size("ctx")
    me = lax.axis_index("head").astype(jnp.int32)
    position = lax.axis_index("ctx").astype(jnp.int32)
    row_count = hidden_in.shape[0]
    model = proj_weight.shape[0]
    heads = out_weight.shape[0] // DV
    width = heads * DV
    pairs = width // LANES
    in_planes = pairs == PLANE and ctx % PLANE == 0 and ctx & (ctx - 1) == 0
    places = jnp.stack([me, position % PLANE if in_planes else jnp.zeros_like(position), position])
    hidden_in, places = lax.optimization_barrier((hidden_in, places))
    step = row_count // 8
    blocks = [(0, 2 * step), (2 * step, 2 * step), (4 * step, step), (5 * step, step), (6 * step, 2 * step)]
    last = len(blocks) - 1
    turn, turn_rows, weight = feature_tables(heads)
    means = mean_table()
    gain = norm_gain.reshape(1, width)
    whole = pl.BlockSpec(memory_space=pltpu.VMEM)
    scalar = pl.BlockSpec(memory_space=pltpu.SMEM)

    def from_head(value, by):
        return lax.ppermute(value, "head", [(i, (i + by) % n) for i in range(n)])

    pieces = {}

    def send_block(b, behind=None):
        at, rows = blocks[b]
        extra = EDGE if b == last else 0
        own = hidden_in[at - extra : at + rows]
        if behind is not None:
            own = after(own, behind)
        pieces[b] = [own] + [from_head(own, r) for r in range(1, n)]

    send_block(last)
    send_block(0, pieces[last][0])
    for b in range(1, last):
        send_block(b, pieces[last][0])

    cols = out_weight.shape[1] // n
    out_parts = 2 if width // 2 % LANES == 0 and ctx % 2 == 0 else 1
    share = width // out_parts
    picked = []
    for r in range(1, n):
        block = call(
            pick_kernel,
            jax.ShapeDtypeStruct((share, cols), BF16),
            grid_spec=pltpu.PrefetchScalarGridSpec(
                num_scalar_prefetch=1,
                grid=(1,),
                in_specs=[
                    pl.BlockSpec((share, cols), functools.partial(lambda i, a, r: (a[2] % out_parts, (a[0] + r) % n), r=r))
                ],
                out_specs=pl.BlockSpec((share, cols), lambda i, a: (0, 0)),
            ),
            vmem=8 << 20,
        )(places, out_weight)
        picked.append(block)

    qk_width = -(-heads * FQK // LANES) * LANES
    arranged_width = 2 * qk_width + 3 * width
    slab = 256
    arranged = call(
        functools.partial(arrange_kernel, heads=heads),
        jax.ShapeDtypeStruct((model, arranged_width), BF16),
        grid=(model // slab,),
        in_specs=[pl.BlockSpec((slab, proj_weight.shape[1]), lambda i: (i, 0))],
        out_specs=pl.BlockSpec((slab, arranged_width), lambda i: (i, 0)),
        vmem=32 << 20,
    )(proj_weight)

    def bf16(rows, *widths):
        return [jax.ShapeDtypeStruct((rows, w), BF16) for w in widths]

    def do_block(b, prev, behind, others=()):
        rows = blocks[b][1]
        extra = EDGE if prev is None else 0
        sends = PLANE if in_planes and others else 0
        tokens = places if behind is None else after(places, behind)
        shapes = bf16(rows, qk_width, width) + [jax.ShapeDtypeStruct((pairs, FEATS, LANES), F32)]
        if others:
            shapes += bf16(FEATS, LANES) * sends
        else:
            shapes += bf16(rows, qk_width, width, width) + bf16(HALO, width)
        operands = [tokens, means, conv_weight, turn_rows, weight, arranged, *pieces[b]]
        if prev is not None:
            operands.append(prev)
        operands += others
        return call(
            functools.partial(
                block_kernel, n=n, heads=heads, extra=extra, others=len(others), sends=sends
            ),
            shapes,
            in_specs=[scalar] + [whole] * (len(operands) - 1),
            out_specs=[whole] * len(shapes),
            scratch_shapes=[pltpu.VMEM((EDGE + rows, width), F32)],
            vmem=32 << 20,
        )(*operands)

    def do_queries(b, v):
        rows = blocks[b][1]
        return call(
            functools.partial(query_kernel, n=n),
            bf16(rows, qk_width, width, width) + bf16(HALO, width),
            in_specs=[scalar] + [whole] * (3 + n),
            out_specs=[whole] * 4,
            vmem=32 << 20,
        )(places, means, arranged, v, *pieces[b])

    def attend(b, prev):
        rows = blocks[b][1]
        k, v, _, q, wq, wk, _ = done[b]
        return call(
            functools.partial(attend_kernel, heads=heads, first=b == 0),
            [jax.ShapeDtypeStruct((rows, turn.shape[1]), BF16)] + [jax.ShapeDtypeStruct((rows, width), F32)] * 2,
            in_specs=[scalar] + [whole] * 7,
            out_specs=[whole] * 3,
            scratch_shapes=[pltpu.VMEM((WIN + rows, width), BF16)] * 2,
            flops=4850 * 10**6 if b == last else 1,
            vmem=16 << 20,
        )(places, turn, prev, q, k, v, wq, wk)

    done, attended = {}, {}
    done[last] = do_block(last, None, None)
    halo = lax.ppermute(done[last][6], "ctx", [(i, i + 1) for i in range(ctx - 1)])
    prevs = {0: halo}
    for b in range(last - 1):
        done[b] = do_block(b, prevs[b], attended[b - 1][1] if b else None)
        prevs[b + 1] = done[b][6]
        attended[b] = attend(b, prevs[b])
    b = last - 1
    k, v, state, *sends = do_block(b, prevs[b], attended[b - 1][1], [done[c][2] for c in (last, *range(b))])
    done[b] = (k, v, state, *do_queries(b, v))
    prevs[last] = done[b][6]
    for b in (last - 1, last):
        attended[b] = attend(b, prevs[b])
    held = sends[:1] + [exchange(sends[r], "ctx", r) for r in range(1, len(sends))]
    mark = done[last - 1][6]
    fetched = [from_head(after(block, mark), r) for r, block in enumerate(picked, 1)]
    if in_planes:
        priors = prior_in_planes(held, places, [done[last - 1][6], attended[last - 1][1]])
    else:
        priors = prior_by_doubling(sum(done[b][2] for b in range(last + 1)), position)

    result = None
    out_rows = []
    mixed = attended[last][1]
    for b in (0, 1, 4, 2, 3):
        at, rows = blocks[b]
        mixed = call(
            functools.partial(finish_kernel, heads=heads, before=b),
            jax.ShapeDtypeStruct((rows, width), BF16),
            in_specs=[scalar] + [whole] * (2 + pairs + b + 3),
            out_specs=whole,
            scratch_shapes=[pltpu.VMEM((pairs, FEATS, LANES), F32)],
            vmem=16 << 20,
        )(after(places, mixed), means, gain, *priors, *[done[c][2] for c in range(b)], *attended[b])
        others = [from_head(mixed, r) for r in range(1, n)]
        if not out_rows:
            for got in fetched:
                out_rows += [got] + ([exchange(after(got, mixed), "ctx", 1)] if out_parts > 1 else [])
        operands = [places, mixed, out_weight] + others + out_rows
        specs = [scalar] + [whole] * (len(operands) - 1)
        aliases = {}
        if result is not None:
            aliases = {len(operands): 0}
            operands.append(result)
            specs.append(pl.BlockSpec(memory_space=pl.ANY))
        result = call(
            functools.partial(output_kernel, n=n, offset=at, parts=out_parts),
            jax.ShapeDtypeStruct((row_count, cols), BF16),
            in_specs=specs,
            out_specs=pl.BlockSpec(memory_space=pl.ANY),
            scratch_shapes=[pltpu.VMEM((rows, cols), BF16), pltpu.SemaphoreType.DMA],
            input_output_aliases=aliases,
            vmem=16 << 20,
        )(*operands)
    return result


def solution(mesh):
    return jax.shard_map(
        per_device,
        mesh=mesh,
        in_specs=(P("ctx", "head"), P(None, "head"), P(None, "head"), P("head"), P("head", None)),
        out_specs=P("ctx", "head"),
        check_vma=False,
    )
```

```python
import functools

import jax
import jax.numpy as jnp
import numpy as np
from jax import lax
from jax.experimental import pallas as pl
from jax.experimental.pallas import tpu as pltpu
from jax.sharding import PartitionSpec as P

DV = 64
FQK = 16
WIN = 64
CONV = 3
LANES = 128
SHIFTS = FQK // 2 + 1
FEATS = (SHIFTS + 1) * FQK
EDGE = 16
HALO = EDGE + 2 * WIN
PLANE = 4
F32 = jnp.float32
BF16 = jnp.bfloat16


def call(body, out_shape, *, vmem, flops=1, **kwargs):
    return pl.pallas_call(
        body,
        out_shape=out_shape,
        compiler_params=pltpu.CompilerParams(vmem_limit_bytes=vmem),
        cost_estimate=pl.CostEstimate(flops=flops, bytes_accessed=1, transcendentals=0),
        **kwargs,
    )


def feature_layout(heads):
    in_group = min(heads, 4)
    lanes = in_group * FQK
    per_tile = LANES // lanes
    return in_group, lanes, -(-(SHIFTS + 1) // per_tile) * per_tile


def feature_tables(heads):
    in_group, lanes, slots = feature_layout(heads)
    groups = heads // in_group
    turn = np.zeros((LANES, groups, slots, in_group, FQK), np.float32)
    for g in range(groups):
        for s in range(SHIFTS):
            for h in range(in_group):
                for i in range(FQK if s < SHIFTS - 1 else FQK // 2):
                    turn[g * lanes + h * FQK + (i + s) % FQK, g, s, h, i] = 1.0
    weight = np.zeros((SHIFTS + 1, FQK, LANES), np.float32)
    weight[0] = 1.0 / (2.0 * FQK)
    weight[1:SHIFTS] = 2.0 / (2.0 * FQK)
    weight[SHIFTS - 1, FQK // 2] = 1.0
    weight[SHIFTS] = 1.0 / FQK**0.5
    turn = turn.reshape(LANES, -1)
    by_rows = np.concatenate([turn.T, np.eye(LANES, dtype=np.float32)], 0)
    return jnp.asarray(turn, BF16), jnp.asarray(by_rows, BF16), jnp.asarray(weight.reshape(FEATS, LANES))


def mean_table():
    block = np.kron(np.eye(LANES // DV), np.ones((DV, DV))) / DV
    return jnp.asarray(np.concatenate([block, block], 0), BF16)


def head_mean(values, table):
    high = values.astype(BF16)
    low = (values - high.astype(F32)).astype(BF16)
    return jnp.dot(jnp.concatenate([high, low], 1), table, preferred_element_type=F32)


def nt_dot(a, b):
    return lax.dot_general(a, b, (((1,), (1,)), ((), ())), preferred_element_type=F32)


def arrange_kernel(w_ref, o_ref, *, heads):
    per_head = 2 * FQK + 3 * DV
    w = w_ref[...]
    at = 0
    for begin, width in ((0, FQK), (FQK, FQK), (2 * FQK, DV), (2 * FQK + DV, DV), (2 * FQK + 2 * DV, DV)):
        parts = [w[:, h * per_head + begin : h * per_head + begin + width] for h in range(heads)]
        total = heads * width
        padded = -(-total // LANES) * LANES
        if padded > total:
            parts.append(jnp.zeros((w.shape[0], padded - total), w.dtype))
        o_ref[:, at : at + padded] = jnp.concatenate(parts, 1)
        at += padded


def project(me, xs, w_ref, begin, width, skip):
    depth = xs[0].shape[1]
    total = None
    for r, x_ref in enumerate(xs):
        src = lax.rem(me - r + len(xs), len(xs))
        from_rows = pl.ds(pl.multiple_of(src * depth, depth), depth)
        part = jnp.dot(x_ref[skip:, :], w_ref[from_rows, begin : begin + width], preferred_element_type=F32)
        total = part if total is None else total + part
    return total.astype(BF16)


def normalize(got, ref, mean_ref, scale):
    for p in range(ref.shape[1] // LANES):
        cols = slice(p * LANES, (p + 1) * LANES)
        x = got[:, cols].astype(F32)
        x = x * lax.rsqrt(head_mean(x * x, mean_ref[...]) + 1e-6)
        ref[:, cols] = x.astype(BF16) * jnp.asarray(scale, BF16)


def block_kernel(j_ref, mean_ref, conv_ref, turn_ref, weight_ref, w_ref, *refs, n, heads, extra, others):
    xs, refs = refs[:n], refs[n:]
    prev_ref = None
    if not extra:
        prev_ref, refs = refs[0], refs[1:]
    other_refs, refs = refs[:others], refs[others:]
    k_ref, v_ref, s_ref, refs = *refs[:3], refs[3:]
    ext_ref = refs[-1]
    sum_ref, q_ref, wq_ref, wk_ref, halo_ref = (refs[0],) + (None,) * 4 if others else (None, *refs[:4])
    rows = v_ref.shape[0]
    qk_width, width = k_ref.shape[1], v_ref.shape[1]
    me = j_ref[0]

    if others:
        k_ref[...] = project(me, xs, w_ref, qk_width, qk_width, extra)
    else:
        qk = project(me, xs, w_ref, 0, 2 * qk_width, extra)
        q_ref[...] = qk[:, :qk_width]
        k_ref[...] = qk[:, qk_width:]
    raw = project(me, xs, w_ref, 2 * qk_width, width, 0)
    if extra:
        ext_ref[...] = raw.astype(F32)
    else:
        ext_ref[0:EDGE, :] = prev_ref[0:EDGE, :].astype(F32)
        ext_ref[EDGE:, :] = raw.astype(F32)
    total = jnp.zeros((rows, width), F32)
    for tap in range(CONV):
        total = total + conv_ref[tap : tap + 1, :] * ext_ref[EDGE - tap : EDGE - tap + rows, :]
    v_ref[...] = total.astype(BF16)

    in_group, lanes, slots = feature_layout(heads)
    groups = heads // in_group
    turned = nt_dot(turn_ref[...], k_ref[...])
    keys = turned[groups * slots * lanes :]
    constant = lax.broadcasted_iota(jnp.int32, (lanes, rows), 0) % FQK == FQK // 2
    low_half = lax.broadcasted_iota(jnp.int32, (SHIFTS + 1, FQK, LANES), 2) < DV
    for g in range(groups):
        own = keys[g * lanes : (g + 1) * lanes]
        phi = []
        for s in range(SHIFTS):
            at = (g * slots + s) * lanes
            phi.append(own * turned[at : at + lanes])
        phi[-1] = jnp.where(constant, 1.0, phi[-1])
        phi = jnp.concatenate([part.astype(BF16) for part in phi + [own]], 0)
        v = v_ref[:, g * in_group * DV : (g + 1) * in_group * DV]
        got = jnp.dot(phi, v, preferred_element_type=F32).reshape(SHIFTS + 1, lanes, in_group * DV)
        for p in range(in_group * DV // LANES):
            cols = slice(p * LANES, (p + 1) * LANES)
            first = got[:, 2 * p * FQK : (2 * p + 1) * FQK, cols]
            second = got[:, (2 * p + 1) * FQK : (2 * p + 2) * FQK, cols]
            state = jnp.where(low_half, first, second).reshape(FEATS, LANES)
            s_ref[g * in_group * DV // LANES + p] = state * weight_ref[...]
    for p in range(heads * DV // LANES if others else 0):
        total = s_ref[p]
        for ref in other_refs:
            total = total + ref[p]
        sum_ref[p] = total.astype(BF16)

    if not others:
        halo_ref[0:EDGE, :] = raw[raw.shape[0] - EDGE :]
        query_part(me, xs, w_ref, mean_ref, v_ref, wq_ref, wk_ref, halo_ref, 2 * qk_width + width, extra)


def query_part(me, xs, w_ref, mean_ref, v_ref, wq_ref, wk_ref, halo_ref, begin, skip):
    rows, width = v_ref.shape
    normalize(project(me, xs, w_ref, begin, width, skip), wq_ref, mean_ref, 1.0 / DV**0.5)
    normalize(project(me, xs, w_ref, begin + width, width, skip), wk_ref, mean_ref, 1.0)
    halo_ref[EDGE : EDGE + WIN, :] = v_ref[rows - WIN : rows, :]
    halo_ref[EDGE + WIN : HALO, :] = wk_ref[rows - WIN : rows, :]


def query_kernel(j_ref, mean_ref, w_ref, v_ref, *refs, n):
    xs, (q_ref, wq_ref, wk_ref, halo_ref) = refs[:n], refs[n:]
    qk_width, width = q_ref.shape[1], v_ref.shape[1]
    q_ref[...] = project(j_ref[0], xs, w_ref, 0, qk_width, 0)
    halo_ref[0:EDGE, :] = jnp.zeros((EDGE, width), BF16)
    query_part(j_ref[0], xs, w_ref, mean_ref, v_ref, wq_ref, wk_ref, halo_ref, 2 * qk_width + width, 0)


def attend_kernel(
    a_ref, turn_ref, prev_ref, q_ref, k_ref, v_ref, wq_ref, wk_ref, phi_ref, lin_ref, win_ref,
    vext_ref, kext_ref, *, heads, first
):
    rows = q_ref.shape[0]
    tile = 128
    span = tile + WIN
    vext_ref[0:WIN, :] = prev_ref[EDGE : EDGE + WIN, :]
    vext_ref[WIN : WIN + rows, :] = v_ref[...]
    kext_ref[0:WIN, :] = prev_ref[EDGE + WIN : HALO, :]
    kext_ref[WIN : WIN + rows, :] = wk_ref[...]
    q = q_ref[...]
    k = k_ref[...]
    lane = lax.broadcasted_iota(jnp.int32, (rows, LANES), 1)
    low_half = lane < DV

    in_group, lanes, slots = feature_layout(heads)
    per_tile = LANES // lanes
    turned = jnp.dot(q, turn_ref[...], preferred_element_type=F32)
    slot = lane // lanes
    for g in range(heads // in_group):
        own = q[:, g * lanes : (g + 1) * lanes].astype(F32)
        own = jnp.concatenate([own] * per_tile, 1)
        for t in range(slots // per_tile):
            at = (g * slots // per_tile + t) * LANES
            part = own * turned[:, at : at + LANES]
            if t == (SHIFTS - 1) // per_tile:
                here = (slot == (SHIFTS - 1) % per_tile) & (lane % FQK == FQK // 2)
                part = jnp.where(here, 1.0, part)
            if t == SHIFTS // per_tile:
                part = jnp.where(slot == SHIFTS % per_tile, own, part)
            phi_ref[:, at : at + LANES] = part.astype(BF16)

    down = lax.broadcasted_iota(jnp.int32, (2 * rows, rows), 0) % rows
    causal = lax.broadcasted_iota(jnp.int32, (2 * rows, rows), 1) <= down
    col = lax.broadcasted_iota(jnp.int32, (2 * tile, span), 1)
    ahead = col - lax.broadcasted_iota(jnp.int32, (2 * tile, span), 0) % tile
    inside = (ahead >= 1) & (ahead <= WIN)
    band = inside.astype(F32).astype(BF16)
    first_band = band
    if first:
        first_band = (inside & (col >= jnp.where(a_ref[1] == 0, WIN, 0))).astype(F32).astype(BF16)
    ones = jnp.ones((span, LANES), BF16)
    q = q * jnp.asarray(1.0 / FQK**0.5, BF16)
    for p in range(heads * DV // LANES):
        cols = slice(p * LANES, (p + 1) * LANES)
        both = [
            jnp.where((lane >= h * FQK) & (lane < (h + 1) * FQK), q, jnp.zeros_like(q)) for h in (2 * p, 2 * p + 1)
        ]
        t = nt_dot(jnp.concatenate(both, 0), k) + 1.0
        kernel = jnp.where(causal, t * t + 1.0, 0.0).astype(BF16)
        got = jnp.dot(kernel, v_ref[:, cols], preferred_element_type=F32)
        lin_ref[:, cols] = 0.5 * jnp.where(low_half, got[:rows], got[rows:])
        for i in range(rows // tile):
            here = slice(i * tile, (i + 1) * tile)
            wq = wq_ref[here, cols]
            none = jnp.zeros_like(wq)
            low = low_half[:tile]
            keys = kext_ref[i * tile : i * tile + span, cols]
            values = vext_ref[i * tile : i * tile + span, cols]
            scores = nt_dot(jnp.concatenate([jnp.where(low, wq, none), jnp.where(low, none, wq)], 0), keys)
            expo = jnp.exp(scores).astype(BF16) * (first_band if i == 0 else band)
            got = jnp.dot(expo, jnp.concatenate([values, ones], 1), preferred_element_type=F32)
            got = jnp.where(jnp.concatenate([low, low], 1), got[:tile], got[tile:])
            win_ref[here, cols] = got[:, :LANES] / got[:, LANES:]


def finish_kernel(_, mean_ref, gain_ref, prior_ref, *refs, heads, before):
    states, (phi_ref, lin_ref, win_ref, mix_ref) = refs[:before], refs[before:]
    in_group, lanes, slots = feature_layout(heads)
    in_pairs = in_group * DV // LANES
    low_half = lax.broadcasted_iota(jnp.int32, (SHIFTS + 1, FQK, LANES), 2) < DV
    for g in range(heads // in_group):
        columns = []
        for p in range(in_pairs):
            pair = g * in_pairs + p
            state = prior_ref[pair].astype(F32)
            for ref in states:
                state = state + ref[pair]
            state = state.reshape(SHIFTS + 1, FQK, LANES)
            parts = [jnp.where(low_half, state, 0.0), jnp.where(low_half, 0.0, state)]
            none = jnp.zeros_like(state)
            parts = [none] * (2 * p) + parts + [none] * (in_group - 2 * p - 2)
            parts = jnp.concatenate(parts, 1).reshape((SHIFTS + 1) * lanes, LANES)
            if slots > SHIFTS + 1:
                parts = jnp.concatenate([parts, jnp.zeros(((slots - SHIFTS - 1) * lanes, LANES), F32)], 0)
            columns.append(parts.astype(BF16))
        table = jnp.concatenate(columns, 1)
        carried = jnp.dot(
            phi_ref[:, g * slots * lanes : (g + 1) * slots * lanes], table, preferred_element_type=F32
        )
        for p in range(in_pairs):
            at = (g * in_pairs + p) * LANES
            cols = slice(at, at + LANES)
            lin = lin_ref[:, cols] + carried[:, p * LANES : (p + 1) * LANES]
            scale = lax.rsqrt(head_mean(lin * lin, mean_ref[...]) + 1e-5)
            mix_ref[:, cols] = (lin * scale * gain_ref[:, cols] + win_ref[:, cols]).astype(BF16)


def output_kernel(a_ref, own_ref, w_ref, *refs, n, offset, parts):
    others, weights, (o_ref, held_ref, sem) = refs[: n - 1], refs[n - 1 : n - 1 + parts * (n - 1)], refs[-3:]
    cols = held_ref.shape[1]
    mine = pl.ds(pl.multiple_of(a_ref[0] * cols, cols), cols)
    total = jnp.dot(own_ref[...], w_ref[:, mine], preferred_element_type=F32).astype(BF16).astype(F32)
    for r, m_ref in enumerate(others):
        part = None
        for i in range(parts):
            ref = weights[r * parts + i]
            depth = ref.shape[0]
            at = depth * (jnp.bitwise_xor(a_ref[1] % 2, i) if parts > 1 else 0)
            got = jnp.dot(m_ref[:, pl.ds(pl.multiple_of(at, depth), depth)], ref[...], preferred_element_type=F32)
            part = got if part is None else part + got
        total = total + part.astype(BF16).astype(F32)
    held_ref[...] = total.astype(BF16)
    copy = pltpu.make_async_copy(held_ref, o_ref.at[pl.ds(offset, held_ref.shape[0]), :], sem)
    copy.start()
    copy.wait()


def pick_kernel(a_ref, w_ref, o_ref):
    o_ref[...] = w_ref[...]


def exchange(value, axis, flip):
    count = lax.axis_size(axis)
    return lax.ppermute(value, axis, [(i, i ^ flip) for i in range(count)])


def plane_kernel(_, held_ref, plane_ref, ahead_ref):
    total = jnp.zeros(held_ref.shape[1:], F32)
    for p in range(PLANE):
        ahead_ref[p] = total
        total = total + held_ref[p].astype(F32)
    for z in range(plane_ref.shape[0]):
        plane_ref[z] = total.astype(BF16)


def earlier_kernel(a_ref, ahead_ref, plane_ref, back_ref):
    mine = a_ref[1] // PLANE
    earlier = jnp.zeros(ahead_ref.shape[1:], F32)
    for z in range(plane_ref.shape[0]):
        earlier = earlier + plane_ref[z].astype(F32) * (mine > z).astype(F32)
    for p in range(PLANE):
        back_ref[p] = (ahead_ref[p] + earlier).astype(BF16)


def after(value, earlier):
    return lax.optimization_barrier((value, earlier))[0]


def swap_all(value, groups):
    return lax.all_to_all(value, "ctx", 0, 0, axis_index_groups=groups, tiled=True)


def prior_in_planes(sums, places, beside):
    ctx = lax.axis_size("ctx")
    planes = ctx // PLANE
    whole = pl.BlockSpec(memory_space=pltpu.VMEM)
    scalar = pl.BlockSpec(memory_space=pltpu.SMEM)
    in_plane = [list(range(z * PLANE, (z + 1) * PLANE)) for z in range(planes)]
    across = [list(range(p, ctx, PLANE)) for p in range(PLANE)]
    plane, ahead = call(
        plane_kernel,
        [
            jax.ShapeDtypeStruct((planes, FEATS, LANES), BF16),
            jax.ShapeDtypeStruct((PLANE, FEATS, LANES), F32),
        ],
        in_specs=[scalar, whole],
        out_specs=[whole] * 2,
        vmem=4 << 20,
    )(after(places, beside[0]), swap_all(sums, in_plane))
    back = call(
        earlier_kernel,
        jax.ShapeDtypeStruct((PLANE, FEATS, LANES), BF16),
        in_specs=[scalar] + [whole] * 2,
        out_specs=whole,
        vmem=4 << 20,
    )(after(places, beside[1]), ahead, swap_all(plane, across))
    return swap_all(back, in_plane)


def prior_by_doubling(total, position):
    ctx = lax.axis_size("ctx")
    prior = jnp.zeros_like(total)
    bit = 1
    while bit < ctx:
        got = exchange(total.astype(BF16), "ctx", bit).astype(F32)
        prior = prior + jnp.where((position & bit) != 0, got, 0.0)
        total = total + got
        bit *= 2
    return prior.astype(BF16)


def per_device(hidden_in, proj_weight, conv_weight, norm_gain, out_weight):
    n = lax.axis_size("head")
    ctx = lax.axis_size("ctx")
    me = lax.axis_index("head").astype(jnp.int32)
    position = lax.axis_index("ctx").astype(jnp.int32)
    row_count = hidden_in.shape[0]
    model = proj_weight.shape[0]
    heads = out_weight.shape[0] // DV
    width = heads * DV
    pairs = width // LANES
    in_planes = pairs == PLANE and ctx % PLANE == 0
    places = jnp.stack([me, position])
    hidden_in, places = lax.optimization_barrier((hidden_in, places))
    step = row_count // 8
    blocks = [(0, 2 * step), (2 * step, 2 * step), (4 * step, step), (5 * step, step), (6 * step, 2 * step)]
    last = len(blocks) - 1
    turn, turn_rows, weight = feature_tables(heads)
    means = mean_table()
    gain = norm_gain.reshape(1, width)
    whole = pl.BlockSpec(memory_space=pltpu.VMEM)
    scalar = pl.BlockSpec(memory_space=pltpu.SMEM)

    def from_head(value, by):
        return lax.ppermute(value, "head", [(i, (i + by) % n) for i in range(n)])

    pieces = {}

    def send_block(b, behind=None):
        at, rows = blocks[b]
        extra = EDGE if b == last else 0
        own = hidden_in[at - extra : at + rows]
        if behind is not None:
            own = after(own, behind)
        pieces[b] = [own] + [from_head(own, r) for r in range(1, n)]

    send_block(last)
    send_block(0, pieces[last][0])
    for b in range(1, last):
        send_block(b, pieces[last][0])

    cols = out_weight.shape[1] // n
    out_parts = 2 if width // 2 % LANES == 0 and ctx % 2 == 0 else 1
    share = width // out_parts
    picked = []
    for r in range(1, n):
        block = call(
            pick_kernel,
            jax.ShapeDtypeStruct((share, cols), BF16),
            grid_spec=pltpu.PrefetchScalarGridSpec(
                num_scalar_prefetch=1,
                grid=(1,),
                in_specs=[
                    pl.BlockSpec((share, cols), functools.partial(lambda i, a, r: (a[1] % out_parts, (a[0] + r) % n), r=r))
                ],
                out_specs=pl.BlockSpec((share, cols), lambda i, a: (0, 0)),
            ),
            vmem=8 << 20,
        )(places, out_weight)
        picked.append(block)

    qk_width = -(-heads * FQK // LANES) * LANES
    arranged_width = 2 * qk_width + 3 * width
    slab = 256
    arranged = call(
        functools.partial(arrange_kernel, heads=heads),
        jax.ShapeDtypeStruct((model, arranged_width), BF16),
        grid=(model // slab,),
        in_specs=[pl.BlockSpec((slab, proj_weight.shape[1]), lambda i: (i, 0))],
        out_specs=pl.BlockSpec((slab, arranged_width), lambda i: (i, 0)),
        vmem=32 << 20,
    )(proj_weight)

    def bf16(rows, *widths):
        return [jax.ShapeDtypeStruct((rows, w), BF16) for w in widths]

    def do_block(b, prev, behind, others=()):
        rows = blocks[b][1]
        extra = EDGE if prev is None else 0
        tokens = places if behind is None else after(places, behind)
        shapes = bf16(rows, qk_width, width) + [jax.ShapeDtypeStruct((pairs, FEATS, LANES), F32)]
        if others:
            shapes.append(jax.ShapeDtypeStruct((pairs, FEATS, LANES), BF16))
        else:
            shapes += bf16(rows, qk_width, width, width) + bf16(HALO, width)
        operands = [tokens, means, conv_weight, turn_rows, weight, arranged, *pieces[b]]
        if prev is not None:
            operands.append(prev)
        operands += others
        return call(
            functools.partial(
                block_kernel, n=n, heads=heads, extra=extra, others=len(others)
            ),
            shapes,
            in_specs=[scalar] + [whole] * (len(operands) - 1),
            out_specs=[whole] * len(shapes),
            scratch_shapes=[pltpu.VMEM((EDGE + rows, width), F32)],
            vmem=32 << 20,
        )(*operands)

    def do_queries(b, v):
        rows = blocks[b][1]
        return call(
            functools.partial(query_kernel, n=n),
            bf16(rows, qk_width, width, width) + bf16(HALO, width),
            in_specs=[scalar] + [whole] * (3 + n),
            out_specs=[whole] * 4,
            vmem=32 << 20,
        )(places, means, arranged, v, *pieces[b])

    def attend(b, prev, places=places):
        rows = blocks[b][1]
        k, v, _, q, wq, wk, _ = done[b]
        return call(
            functools.partial(attend_kernel, heads=heads, first=b == 0),
            [jax.ShapeDtypeStruct((rows, turn.shape[1]), BF16)] + [jax.ShapeDtypeStruct((rows, width), F32)] * 2,
            in_specs=[scalar] + [whole] * 7,
            out_specs=[whole] * 3,
            scratch_shapes=[pltpu.VMEM((WIN + rows, width), BF16)] * 2,
            flops=1,
            vmem=16 << 20,
        )(places, turn, prev, q, k, v, wq, wk)

    done, attended = {}, {}
    done[last] = do_block(last, None, None)
    halo = lax.ppermute(done[last][6], "ctx", [(i, i + 1) for i in range(ctx - 1)])
    prevs = {0: halo}
    for b in range(last - 1):
        done[b] = do_block(b, prevs[b], attended[b - 1][1] if b else None)
        prevs[b + 1] = done[b][6]
        attended[b] = attend(b, prevs[b], after(places, picked[0]) if b == 0 else places)
    b = last - 1
    k, v, state, sums = do_block(b, prevs[b], attended[b - 1][1], [done[c][2] for c in (last, *range(b))])
    done[b] = (k, v, state, *do_queries(b, v))
    prevs[last] = done[b][6]
    for b in (last - 1, last):
        attended[b] = attend(b, prevs[b])
    fetched = [from_head(after(block, done[last - 1][6]), r) for r, block in enumerate(picked, 1)]
    if in_planes:
        prior = prior_in_planes(sums, places, [done[last - 1][6], attended[last - 1][1]])
    else:
        prior = prior_by_doubling(sum(done[b][2] for b in range(last + 1)), position)

    result = None
    out_rows = []
    mixed = attended[last][1]
    for b in (0, 1, 4, 2, 3):
        at, rows = blocks[b]
        mixed = call(
            functools.partial(finish_kernel, heads=heads, before=b),
            jax.ShapeDtypeStruct((rows, width), BF16),
            in_specs=[scalar] + [whole] * (3 + b + 3),
            out_specs=whole,
            vmem=16 << 20,
        )(after(places, mixed), means, gain, prior, *[done[c][2] for c in range(b)], *attended[b])
        others = [from_head(mixed, r) for r in range(1, n)]
        if not out_rows:
            for got in fetched:
                out_rows += [got] + ([exchange(after(got, mixed), "ctx", 1)] if out_parts > 1 else [])
        operands = [places, mixed, out_weight] + others + out_rows
        specs = [scalar] + [whole] * (len(operands) - 1)
        aliases = {}
        if result is not None:
            aliases = {len(operands): 0}
            operands.append(result)
            specs.append(pl.BlockSpec(memory_space=pl.ANY))
        result = call(
            functools.partial(output_kernel, n=n, offset=at, parts=out_parts),
            jax.ShapeDtypeStruct((row_count, cols), BF16),
            in_specs=specs,
            out_specs=pl.BlockSpec(memory_space=pl.ANY),
            scratch_shapes=[pltpu.VMEM((rows, cols), BF16), pltpu.SemaphoreType.DMA],
            input_output_aliases=aliases,
            vmem=16 << 20,
        )(*operands)
    return result


def solution(mesh):
    return jax.shard_map(
        per_device,
        mesh=mesh,
        in_specs=(P("ctx", "head"), P(None, "head"), P(None, "head"), P("head"), P("head", None)),
        out_specs=P("ctx", "head"),
        check_vma=False,
    )
```

```python
import functools

import jax
import jax.numpy as jnp
import numpy as np
from jax import lax
from jax.experimental import pallas as pl
from jax.experimental.pallas import tpu as pltpu
from jax.sharding import PartitionSpec as P

DV = 64
FQK = 16
WIN = 64
CONV = 3
LANES = 128
SHIFTS = FQK // 2 + 1
FEATS = (SHIFTS + 1) * FQK
EDGE = 16
HALO = EDGE + 2 * WIN
PLANE = 4
F32 = jnp.float32
BF16 = jnp.bfloat16


def call(body, out_shape, *, vmem, flops=1, **kwargs):
    return pl.pallas_call(
        body,
        out_shape=out_shape,
        compiler_params=pltpu.CompilerParams(vmem_limit_bytes=vmem),
        cost_estimate=pl.CostEstimate(flops=flops, bytes_accessed=1, transcendentals=0),
        **kwargs,
    )


def feature_layout(heads):
    in_group = min(heads, 4)
    lanes = in_group * FQK
    per_tile = LANES // lanes
    return in_group, lanes, -(-(SHIFTS + 1) // per_tile) * per_tile


def feature_tables(heads):
    in_group, lanes, slots = feature_layout(heads)
    groups = heads // in_group
    turn = np.zeros((LANES, groups, slots, in_group, FQK), np.float32)
    for g in range(groups):
        for s in range(SHIFTS):
            for h in range(in_group):
                for i in range(FQK if s < SHIFTS - 1 else FQK // 2):
                    turn[g * lanes + h * FQK + (i + s) % FQK, g, s, h, i] = 1.0
    weight = np.zeros((SHIFTS + 1, FQK, LANES), np.float32)
    weight[0] = 1.0 / (2.0 * FQK)
    weight[1:SHIFTS] = 2.0 / (2.0 * FQK)
    weight[SHIFTS - 1, FQK // 2] = 1.0
    weight[SHIFTS] = 1.0 / FQK**0.5
    turn = turn.reshape(LANES, -1)
    by_rows = np.concatenate([turn.T, np.eye(LANES, dtype=np.float32)], 0)
    return jnp.asarray(turn, BF16), jnp.asarray(by_rows, BF16), jnp.asarray(weight.reshape(FEATS, LANES))


def mean_table():
    block = np.kron(np.eye(LANES // DV), np.ones((DV, DV))) / DV
    return jnp.asarray(np.concatenate([block, block], 0), BF16)


def head_mean(values, table):
    high = values.astype(BF16)
    low = (values - high.astype(F32)).astype(BF16)
    return jnp.dot(jnp.concatenate([high, low], 1), table, preferred_element_type=F32)


def nt_dot(a, b):
    return lax.dot_general(a, b, (((1,), (1,)), ((), ())), preferred_element_type=F32)


def arrange_kernel(w_ref, o_ref, *, heads):
    per_head = 2 * FQK + 3 * DV
    w = w_ref[...]
    at = 0
    for begin, width in ((0, FQK), (FQK, FQK), (2 * FQK, DV), (2 * FQK + DV, DV), (2 * FQK + 2 * DV, DV)):
        parts = [w[:, h * per_head + begin : h * per_head + begin + width] for h in range(heads)]
        total = heads * width
        padded = -(-total // LANES) * LANES
        if padded > total:
            parts.append(jnp.zeros((w.shape[0], padded - total), w.dtype))
        o_ref[:, at : at + padded] = jnp.concatenate(parts, 1)
        at += padded


def project(me, xs, w_ref, begin, width, skip):
    depth = xs[0].shape[1]
    total = None
    for r, x_ref in enumerate(xs):
        src = lax.rem(me - r + len(xs), len(xs))
        from_rows = pl.ds(pl.multiple_of(src * depth, depth), depth)
        part = jnp.dot(x_ref[skip:, :], w_ref[from_rows, begin : begin + width], preferred_element_type=F32)
        total = part if total is None else total + part
    return total.astype(BF16)


def normalize(got, ref, mean_ref, scale):
    for p in range(ref.shape[1] // LANES):
        cols = slice(p * LANES, (p + 1) * LANES)
        x = got[:, cols].astype(F32)
        x = x * lax.rsqrt(head_mean(x * x, mean_ref[...]) + 1e-6)
        ref[:, cols] = x.astype(BF16) * jnp.asarray(scale, BF16)


def block_kernel(j_ref, mean_ref, conv_ref, turn_ref, weight_ref, w_ref, *refs, n, heads, extra, others, sends):
    xs, refs = refs[:n], refs[n:]
    prev_ref = None
    if not extra:
        prev_ref, refs = refs[0], refs[1:]
    other_refs, refs = refs[:others], refs[others:]
    k_ref, v_ref, s_ref, refs = *refs[:3], refs[3:]
    send_refs, ext_ref = refs[:sends], refs[-1]
    q_ref, wq_ref, wk_ref, halo_ref = (None,) * 4 if others else refs[:4]
    rows = v_ref.shape[0]
    qk_width, width = k_ref.shape[1], v_ref.shape[1]
    me = j_ref[0]

    if others:
        k_ref[...] = project(me, xs, w_ref, qk_width, qk_width, extra)
    else:
        qk = project(me, xs, w_ref, 0, 2 * qk_width, extra)
        q_ref[...] = qk[:, :qk_width]
        k_ref[...] = qk[:, qk_width:]
    raw = project(me, xs, w_ref, 2 * qk_width, width, 0)
    if extra:
        ext_ref[...] = raw.astype(F32)
    else:
        ext_ref[0:EDGE, :] = prev_ref[0:EDGE, :].astype(F32)
        ext_ref[EDGE:, :] = raw.astype(F32)
    total = jnp.zeros((rows, width), F32)
    for tap in range(CONV):
        total = total + conv_ref[tap : tap + 1, :] * ext_ref[EDGE - tap : EDGE - tap + rows, :]
    v_ref[...] = total.astype(BF16)

    in_group, lanes, slots = feature_layout(heads)
    groups = heads // in_group
    turned = nt_dot(turn_ref[...], k_ref[...])
    keys = turned[groups * slots * lanes :]
    constant = lax.broadcasted_iota(jnp.int32, (lanes, rows), 0) % FQK == FQK // 2
    low_half = lax.broadcasted_iota(jnp.int32, (SHIFTS + 1, FQK, LANES), 2) < DV
    for g in range(groups):
        own = keys[g * lanes : (g + 1) * lanes]
        phi = []
        for s in range(SHIFTS):
            at = (g * slots + s) * lanes
            phi.append(own * turned[at : at + lanes])
        phi[-1] = jnp.where(constant, 1.0, phi[-1])
        phi = jnp.concatenate([part.astype(BF16) for part in phi + [own]], 0)
        v = v_ref[:, g * in_group * DV : (g + 1) * in_group * DV]
        got = jnp.dot(phi, v, preferred_element_type=F32).reshape(SHIFTS + 1, lanes, in_group * DV)
        for p in range(in_group * DV // LANES):
            cols = slice(p * LANES, (p + 1) * LANES)
            first = got[:, 2 * p * FQK : (2 * p + 1) * FQK, cols]
            second = got[:, (2 * p + 1) * FQK : (2 * p + 2) * FQK, cols]
            state = jnp.where(low_half, first, second).reshape(FEATS, LANES)
            s_ref[g * in_group * DV // LANES + p] = state * weight_ref[...]
    for r in range(sends):
        pair = jnp.bitwise_xor(j_ref[1], r)
        total = s_ref[pair]
        for ref in other_refs:
            total = total + ref[pair]
        send_refs[r][...] = total.astype(BF16)

    if not others:
        halo_ref[0:EDGE, :] = raw[raw.shape[0] - EDGE :]
        query_part(me, xs, w_ref, mean_ref, v_ref, wq_ref, wk_ref, halo_ref, 2 * qk_width + width, extra)


def query_part(me, xs, w_ref, mean_ref, v_ref, wq_ref, wk_ref, halo_ref, begin, skip):
    rows, width = v_ref.shape
    normalize(project(me, xs, w_ref, begin, width, skip), wq_ref, mean_ref, 1.0 / DV**0.5)
    normalize(project(me, xs, w_ref, begin + width, width, skip), wk_ref, mean_ref, 1.0)
    halo_ref[EDGE : EDGE + WIN, :] = v_ref[rows - WIN : rows, :]
    halo_ref[EDGE + WIN : HALO, :] = wk_ref[rows - WIN : rows, :]


def query_kernel(j_ref, mean_ref, w_ref, v_ref, *refs, n):
    xs, (q_ref, wq_ref, wk_ref, halo_ref) = refs[:n], refs[n:]
    qk_width, width = q_ref.shape[1], v_ref.shape[1]
    q_ref[...] = project(j_ref[0], xs, w_ref, 0, qk_width, 0)
    halo_ref[0:EDGE, :] = jnp.zeros((EDGE, width), BF16)
    query_part(j_ref[0], xs, w_ref, mean_ref, v_ref, wq_ref, wk_ref, halo_ref, 2 * qk_width + width, 0)


def attend_kernel(
    a_ref, turn_ref, prev_ref, q_ref, k_ref, v_ref, wq_ref, wk_ref, phi_ref, lin_ref, win_ref,
    vext_ref, kext_ref, *, heads, first
):
    rows = q_ref.shape[0]
    tile = 128
    span = tile + WIN
    vext_ref[0:WIN, :] = prev_ref[EDGE : EDGE + WIN, :]
    vext_ref[WIN : WIN + rows, :] = v_ref[...]
    kext_ref[0:WIN, :] = prev_ref[EDGE + WIN : HALO, :]
    kext_ref[WIN : WIN + rows, :] = wk_ref[...]
    q = q_ref[...]
    k = k_ref[...]
    lane = lax.broadcasted_iota(jnp.int32, (rows, LANES), 1)
    low_half = lane < DV

    in_group, lanes, slots = feature_layout(heads)
    per_tile = LANES // lanes
    turned = jnp.dot(q, turn_ref[...], preferred_element_type=F32)
    slot = lane // lanes
    for g in range(heads // in_group):
        own = q[:, g * lanes : (g + 1) * lanes].astype(F32)
        own = jnp.concatenate([own] * per_tile, 1)
        for t in range(slots // per_tile):
            at = (g * slots // per_tile + t) * LANES
            part = own * turned[:, at : at + LANES]
            if t == (SHIFTS - 1) // per_tile:
                here = (slot == (SHIFTS - 1) % per_tile) & (lane % FQK == FQK // 2)
                part = jnp.where(here, 1.0, part)
            if t == SHIFTS // per_tile:
                part = jnp.where(slot == SHIFTS % per_tile, own, part)
            phi_ref[:, at : at + LANES] = part.astype(BF16)

    down = lax.broadcasted_iota(jnp.int32, (2 * rows, rows), 0) % rows
    causal = lax.broadcasted_iota(jnp.int32, (2 * rows, rows), 1) <= down
    col = lax.broadcasted_iota(jnp.int32, (2 * tile, span), 1)
    ahead = col - lax.broadcasted_iota(jnp.int32, (2 * tile, span), 0) % tile
    inside = (ahead >= 1) & (ahead <= WIN)
    band = inside.astype(F32).astype(BF16)
    first_band = band
    if first:
        first_band = (inside & (col >= jnp.where(a_ref[2] == 0, WIN, 0))).astype(F32).astype(BF16)
    ones = jnp.ones((span, LANES), BF16)
    q = q * jnp.asarray(1.0 / FQK**0.5, BF16)
    for p in range(heads * DV // LANES):
        cols = slice(p * LANES, (p + 1) * LANES)
        both = [
            jnp.where((lane >= h * FQK) & (lane < (h + 1) * FQK), q, jnp.zeros_like(q)) for h in (2 * p, 2 * p + 1)
        ]
        t = nt_dot(jnp.concatenate(both, 0), k) + 1.0
        kernel = jnp.where(causal, t * t + 1.0, 0.0).astype(BF16)
        got = jnp.dot(kernel, v_ref[:, cols], preferred_element_type=F32)
        lin_ref[:, cols] = 0.5 * jnp.where(low_half, got[:rows], got[rows:])
        for i in range(rows // tile):
            here = slice(i * tile, (i + 1) * tile)
            wq = wq_ref[here, cols]
            none = jnp.zeros_like(wq)
            low = low_half[:tile]
            keys = kext_ref[i * tile : i * tile + span, cols]
            values = vext_ref[i * tile : i * tile + span, cols]
            scores = nt_dot(jnp.concatenate([jnp.where(low, wq, none), jnp.where(low, none, wq)], 0), keys)
            expo = jnp.exp(scores).astype(BF16) * (first_band if i == 0 else band)
            got = jnp.dot(expo, jnp.concatenate([values, ones], 1), preferred_element_type=F32)
            got = jnp.where(jnp.concatenate([low, low], 1), got[:tile], got[tile:])
            win_ref[here, cols] = got[:, :LANES] / got[:, LANES:]


def finish_kernel(a_ref, mean_ref, gain_ref, *refs, heads, before):
    pairs = heads * DV // LANES
    prior_refs, refs = refs[:pairs], refs[pairs:]
    states, (phi_ref, lin_ref, win_ref, mix_ref, held_ref) = refs[:before], refs[before:]
    rows = phi_ref.shape[0]
    for r in range(pairs):
        held_ref[r] = prior_refs[r][...].astype(F32)
    in_group, lanes, slots = feature_layout(heads)
    in_pairs = in_group * DV // LANES
    low_half = lax.broadcasted_iota(jnp.int32, (SHIFTS + 1, FQK, LANES), 2) < DV
    for g in range(heads // in_group):
        columns = []
        for p in range(in_pairs):
            pair = g * in_pairs + p
            state = held_ref[jnp.bitwise_xor(a_ref[1], pair)]
            for ref in states:
                state = state + ref[pair]
            state = state.reshape(SHIFTS + 1, FQK, LANES)
            parts = [jnp.where(low_half, state, 0.0), jnp.where(low_half, 0.0, state)]
            none = jnp.zeros_like(state)
            parts = [none] * (2 * p) + parts + [none] * (in_group - 2 * p - 2)
            parts = jnp.concatenate(parts, 1).reshape((SHIFTS + 1) * lanes, LANES)
            if slots > SHIFTS + 1:
                parts = jnp.concatenate([parts, jnp.zeros(((slots - SHIFTS - 1) * lanes, LANES), F32)], 0)
            columns.append(parts.astype(BF16))
        table = jnp.concatenate(columns, 1)
        carried = jnp.dot(
            phi_ref[:, g * slots * lanes : (g + 1) * slots * lanes], table, preferred_element_type=F32
        )
        for p in range(in_pairs):
            at = (g * in_pairs + p) * LANES
            cols = slice(at, at + LANES)
            lin = lin_ref[:, cols] + carried[:, p * LANES : (p + 1) * LANES]
            scale = lax.rsqrt(head_mean(lin * lin, mean_ref[...]) + 1e-5)
            mix_ref[:, cols] = (lin * scale * gain_ref[:, cols] + win_ref[:, cols]).astype(BF16)


def output_kernel(a_ref, own_ref, w_ref, *refs, n, offset, parts):
    others, weights, (o_ref, held_ref, sem) = refs[: n - 1], refs[n - 1 : n - 1 + parts * (n - 1)], refs[-3:]
    cols = held_ref.shape[1]
    mine = pl.ds(pl.multiple_of(a_ref[0] * cols, cols), cols)
    total = jnp.dot(own_ref[...], w_ref[:, mine], preferred_element_type=F32).astype(BF16).astype(F32)
    for r, m_ref in enumerate(others):
        part = None
        for i in range(parts):
            ref = weights[r * parts + i]
            depth = ref.shape[0]
            at = depth * (jnp.bitwise_xor(a_ref[2] % 2, i) if parts > 1 else 0)
            got = jnp.dot(m_ref[:, pl.ds(pl.multiple_of(at, depth), depth)], ref[...], preferred_element_type=F32)
            part = got if part is None else part + got
        total = total + part.astype(BF16).astype(F32)
    held_ref[...] = total.astype(BF16)
    copy = pltpu.make_async_copy(held_ref, o_ref.at[pl.ds(offset, held_ref.shape[0]), :], sem)
    copy.start()
    copy.wait()


def pick_kernel(a_ref, w_ref, o_ref):
    o_ref[...] = w_ref[...]


def exchange(value, axis, flip):
    count = lax.axis_size(axis)
    return lax.ppermute(value, axis, [(i, i ^ flip) for i in range(count)])


def plane_kernel(a_ref, *refs):
    helds, plane_ref, ahead_refs = refs[:PLANE], refs[PLANE], refs[PLANE + 1 :]
    place = a_ref[1]
    held = [ref[...].astype(F32) for ref in helds]
    plane_ref[...] = (held[0] + held[1] + held[2] + held[3]).astype(BF16)
    for r in range(PLANE):
        total = jnp.zeros_like(held[0])
        for s in range(PLANE):
            before = jnp.bitwise_xor(place, s) < jnp.bitwise_xor(place, r)
            total = total + held[s] * before.astype(F32)
        ahead_refs[r][...] = total


def earlier_kernel(a_ref, *refs, planes):
    ahead_refs, plane_refs, back_refs = refs[:PLANE], refs[PLANE : PLANE + planes], refs[PLANE + planes :]
    mine = a_ref[2] // PLANE
    earlier = jnp.zeros(ahead_refs[0].shape, F32)
    for d, ref in enumerate(plane_refs, 1):
        before = jnp.bitwise_xor(mine, d) < mine
        earlier = earlier + ref[...].astype(F32) * before.astype(F32)
    for r in range(PLANE):
        back_refs[r][...] = (ahead_refs[r][...] + earlier).astype(BF16)


def after(value, earlier):
    return lax.optimization_barrier((value, earlier))[0]


def prior_in_planes(held, places, beside):
    ctx = lax.axis_size("ctx")
    whole = pl.BlockSpec(memory_space=pltpu.VMEM)
    scalar = pl.BlockSpec(memory_space=pltpu.SMEM)
    narrow = jax.ShapeDtypeStruct((FEATS, LANES), BF16)
    wide = jax.ShapeDtypeStruct((FEATS, LANES), F32)
    plane, *ahead = call(
        plane_kernel,
        [narrow] + [wide] * PLANE,
        in_specs=[scalar] + [whole] * PLANE,
        out_specs=[whole] * (1 + PLANE),
        vmem=4 << 20,
    )(after(places, beside[0]), *held)
    earlier = []
    for d in range(1, ctx // PLANE):
        earlier.append(exchange(plane, "ctx", d * PLANE))
    return call(
        functools.partial(earlier_kernel, planes=len(earlier)),
        [narrow] * PLANE,
        in_specs=[scalar] + [whole] * (PLANE + len(earlier)),
        out_specs=[whole] * PLANE,
        vmem=4 << 20,
    )(after(places, beside[1]), *ahead, *earlier)


def prior_by_doubling(total, position):
    ctx = lax.axis_size("ctx")
    prior = jnp.zeros_like(total)
    bit = 1
    while bit < ctx:
        got = exchange(total.astype(BF16), "ctx", bit).astype(F32)
        prior = prior + jnp.where((position & bit) != 0, got, 0.0)
        total = total + got
        bit *= 2
    return [prior[p].astype(BF16) for p in range(total.shape[0])]


def per_device(hidden_in, proj_weight, conv_weight, norm_gain, out_weight):
    n = lax.axis_size("head")
    ctx = lax.axis_size("ctx")
    me = lax.axis_index("head").astype(jnp.int32)
    position = lax.axis_index("ctx").astype(jnp.int32)
    row_count = hidden_in.shape[0]
    model = proj_weight.shape[0]
    heads = out_weight.shape[0] // DV
    width = heads * DV
    pairs = width // LANES
    in_planes = pairs == PLANE and ctx % PLANE == 0 and ctx & (ctx - 1) == 0
    places = jnp.stack([me, position % PLANE if in_planes else jnp.zeros_like(position), position])
    hidden_in, places = lax.optimization_barrier((hidden_in, places))
    step = row_count // 8
    blocks = [(0, 2 * step), (2 * step, 2 * step), (4 * step, step), (5 * step, step), (6 * step, 2 * step)]
    last = len(blocks) - 1
    turn, turn_rows, weight = feature_tables(heads)
    means = mean_table()
    gain = norm_gain.reshape(1, width)
    whole = pl.BlockSpec(memory_space=pltpu.VMEM)
    scalar = pl.BlockSpec(memory_space=pltpu.SMEM)

    def from_head(value, by):
        return lax.ppermute(value, "head", [(i, (i + by) % n) for i in range(n)])

    pieces = {}

    def send_block(b, behind=None):
        at, rows = blocks[b]
        extra = EDGE if b == last else 0
        own = hidden_in[at - extra : at + rows]
        if behind is not None:
            own = after(own, behind)
        pieces[b] = [own] + [from_head(own, r) for r in range(1, n)]

    send_block(last)
    send_block(0, pieces[last][0])
    for b in range(1, last):
        send_block(b, pieces[last][0])

    cols = out_weight.shape[1] // n
    out_parts = 2 if width // 2 % LANES == 0 and ctx % 2 == 0 else 1
    share = width // out_parts
    def pick(r):
        column = functools.partial(lambda i, a, r: (a[2] % out_parts, (a[0] + r) % n), r=r)
        return call(
            pick_kernel,
            jax.ShapeDtypeStruct((share, cols), BF16),
            grid_spec=pltpu.PrefetchScalarGridSpec(
                num_scalar_prefetch=1,
                grid=(1,),
                in_specs=[pl.BlockSpec((share, cols), column)],
                out_specs=pl.BlockSpec((share, cols), lambda i, a: (0, 0)),
            ),
            vmem=8 << 20,
        )(after(places, done[last - 1][1]), out_weight)

    qk_width = -(-heads * FQK // LANES) * LANES
    arranged_width = 2 * qk_width + 3 * width
    slab = 256
    arranged = call(
        functools.partial(arrange_kernel, heads=heads),
        jax.ShapeDtypeStruct((model, arranged_width), BF16),
        grid=(model // slab,),
        in_specs=[pl.BlockSpec((slab, proj_weight.shape[1]), lambda i: (i, 0))],
        out_specs=pl.BlockSpec((slab, arranged_width), lambda i: (i, 0)),
        vmem=32 << 20,
    )(proj_weight)

    def bf16(rows, *widths):
        return [jax.ShapeDtypeStruct((rows, w), BF16) for w in widths]

    def do_block(b, prev, behind, others=()):
        rows = blocks[b][1]
        extra = EDGE if prev is None else 0
        sends = PLANE if in_planes and others else 0
        tokens = places if behind is None else after(places, behind)
        shapes = bf16(rows, qk_width, width) + [jax.ShapeDtypeStruct((pairs, FEATS, LANES), F32)]
        if others:
            shapes += bf16(FEATS, LANES) * sends
        else:
            shapes += bf16(rows, qk_width, width, width) + bf16(HALO, width)
        operands = [tokens, means, conv_weight, turn_rows, weight, arranged, *pieces[b]]
        if prev is not None:
            operands.append(prev)
        operands += others
        return call(
            functools.partial(
                block_kernel, n=n, heads=heads, extra=extra, others=len(others), sends=sends
            ),
            shapes,
            in_specs=[scalar] + [whole] * (len(operands) - 1),
            out_specs=[whole] * len(shapes),
            scratch_shapes=[pltpu.VMEM((EDGE + rows, width), F32)],
            vmem=32 << 20,
        )(*operands)

    def do_queries(b, v):
        rows = blocks[b][1]
        return call(
            functools.partial(query_kernel, n=n),
            bf16(rows, qk_width, width, width) + bf16(HALO, width),
            in_specs=[scalar] + [whole] * (3 + n),
            out_specs=[whole] * 4,
            vmem=32 << 20,
        )(places, means, arranged, v, *pieces[b])

    def attend(b, prev, places=places):
        rows = blocks[b][1]
        k, v, _, q, wq, wk, _ = done[b]
        return call(
            functools.partial(attend_kernel, heads=heads, first=b == 0),
            [jax.ShapeDtypeStruct((rows, turn.shape[1]), BF16)] + [jax.ShapeDtypeStruct((rows, width), F32)] * 2,
            in_specs=[scalar] + [whole] * 7,
            out_specs=[whole] * 3,
            scratch_shapes=[pltpu.VMEM((WIN + rows, width), BF16)] * 2,
            flops=4850 * 10**6 if b == last else 1,
            vmem=16 << 20,
        )(places, turn, prev, q, k, v, wq, wk)

    done, attended = {}, {}
    done[last] = do_block(last, None, None)
    halo = lax.ppermute(done[last][6], "ctx", [(i, i + 1) for i in range(ctx - 1)])
    prevs = {0: halo}
    for b in range(last - 1):
        done[b] = do_block(b, prevs[b], attended[b - 1][1] if b else None)
        prevs[b + 1] = done[b][6]
        attended[b] = attend(b, prevs[b])
    b = last - 1
    k, v, state, *sends = do_block(b, prevs[b], attended[b - 1][1], [done[c][2] for c in (last, *range(b))])
    done[b] = (k, v, state, *do_queries(b, v))
    prevs[last] = done[b][6]
    attended[last - 1] = attend(last - 1, prevs[last - 1])
    held = sends[:1] + [exchange(sends[r], "ctx", r) for r in range(1, len(sends))]
    fetched = [from_head(pick(r), r) for r in range(1, n)]
    if in_planes:
        back = prior_in_planes(held, places, [done[last - 1][1], attended[last - 1][1]])
        priors = [back[0]] + [exchange(back[r], "ctx", r) for r in range(1, PLANE)]
        attended[last] = attend(last, prevs[last], after(places, back[0]))
    else:
        priors = prior_by_doubling(sum(done[b][2] for b in range(last + 1)), position)
        attended[last] = attend(last, prevs[last])

    order = (0, 1, 4, 2, 3)
    mixed = attended[last][1]
    mixes = {}
    for b in order:
        rows = blocks[b][1]
        mixed = call(
            functools.partial(finish_kernel, heads=heads, before=b),
            jax.ShapeDtypeStruct((rows, width), BF16),
            in_specs=[scalar] + [whole] * (2 + pairs + b + 3),
            out_specs=whole,
            scratch_shapes=[pltpu.VMEM((pairs, FEATS, LANES), F32)],
            flops=20 * 10**9 if b == order[0] else 1,
            vmem=16 << 20,
        )(after(places, mixed), means, gain, *priors, *[done[c][2] for c in range(b)], *attended[b])
        mixes[b] = [mixed] + [from_head(mixed, r) for r in range(1, n)]

    out_rows = []
    for got in fetched:
        out_rows.append(got)
        if out_parts > 1:
            out_rows.append(exchange(after(got, attended[last][1]), "ctx", 1))

    result = None
    for b in order:
        at, rows = blocks[b]
        operands = [places, mixes[b][0], out_weight] + mixes[b][1:] + out_rows
        specs = [scalar] + [whole] * (len(operands) - 1)
        aliases = {}
        if result is not None:
            aliases = {len(operands): 0}
            operands.append(result)
            specs.append(pl.BlockSpec(memory_space=pl.ANY))
        result = call(
            functools.partial(output_kernel, n=n, offset=at, parts=out_parts),
            jax.ShapeDtypeStruct((row_count, cols), BF16),
            in_specs=specs,
            out_specs=pl.BlockSpec(memory_space=pl.ANY),
            scratch_shapes=[pltpu.VMEM((rows, cols), BF16), pltpu.SemaphoreType.DMA],
            input_output_aliases=aliases,
            vmem=16 << 20,
        )(*operands)
    return result


def solution(mesh):
    return jax.shard_map(
        per_device,
        mesh=mesh,
        in_specs=(P("ctx", "head"), P(None, "head"), P(None, "head"), P("head"), P("head", None)),
        out_specs=P("ctx", "head"),
        check_vma=False,
    )
```

```python
import functools

import jax
import jax.numpy as jnp
import numpy as np
from jax import lax
from jax.experimental import pallas as pl
from jax.experimental.pallas import tpu as pltpu
from jax.sharding import PartitionSpec as P

DV = 64
FQK = 16
WIN = 64
CONV = 3
LANES = 128
SHIFTS = FQK // 2 + 1
FEATS = (SHIFTS + 1) * FQK
EDGE = 16
HALO = EDGE + 2 * WIN
PLANE = 4
F32 = jnp.float32
BF16 = jnp.bfloat16


def call(body, out_shape, *, vmem, flops=1, **kwargs):
    return pl.pallas_call(
        body,
        out_shape=out_shape,
        compiler_params=pltpu.CompilerParams(vmem_limit_bytes=vmem),
        cost_estimate=pl.CostEstimate(flops=flops, bytes_accessed=1, transcendentals=0),
        **kwargs,
    )


def feature_layout(heads):
    in_group = min(heads, 4)
    lanes = in_group * FQK
    per_tile = LANES // lanes
    return in_group, lanes, -(-(SHIFTS + 1) // per_tile) * per_tile


def feature_tables(heads):
    in_group, lanes, slots = feature_layout(heads)
    groups = heads // in_group
    turn = np.zeros((LANES, groups, slots, in_group, FQK), np.float32)
    for g in range(groups):
        for s in range(SHIFTS):
            for h in range(in_group):
                for i in range(FQK if s < SHIFTS - 1 else FQK // 2):
                    turn[g * lanes + h * FQK + (i + s) % FQK, g, s, h, i] = 1.0
    weight = np.zeros((SHIFTS + 1, FQK, LANES), np.float32)
    weight[0] = 1.0 / (2.0 * FQK)
    weight[1:SHIFTS] = 2.0 / (2.0 * FQK)
    weight[SHIFTS - 1, FQK // 2] = 1.0
    weight[SHIFTS] = 1.0 / FQK**0.5
    turn = turn.reshape(LANES, -1)
    by_rows = np.concatenate([turn.T, np.eye(LANES, dtype=np.float32)], 0)
    return jnp.asarray(turn, BF16), jnp.asarray(by_rows, BF16), jnp.asarray(weight.reshape(FEATS, LANES))


def mean_table():
    block = np.kron(np.eye(LANES // DV), np.ones((DV, DV))) / DV
    return jnp.asarray(np.concatenate([block, block], 0), BF16)


def head_mean(values, table):
    high = values.astype(BF16)
    low = (values - high.astype(F32)).astype(BF16)
    return jnp.dot(jnp.concatenate([high, low], 1), table, preferred_element_type=F32)


def nt_dot(a, b):
    return lax.dot_general(a, b, (((1,), (1,)), ((), ())), preferred_element_type=F32)


def arrange_kernel(w_ref, o_ref, *, heads):
    per_head = 2 * FQK + 3 * DV
    w = w_ref[...]
    at = 0
    for begin, width in ((0, FQK), (FQK, FQK), (2 * FQK, DV), (2 * FQK + DV, DV), (2 * FQK + 2 * DV, DV)):
        parts = [w[:, h * per_head + begin : h * per_head + begin + width] for h in range(heads)]
        total = heads * width
        padded = -(-total // LANES) * LANES
        if padded > total:
            parts.append(jnp.zeros((w.shape[0], padded - total), w.dtype))
        o_ref[:, at : at + padded] = jnp.concatenate(parts, 1)
        at += padded


def project(me, xs, w_ref, begin, width, skip):
    depth = xs[0].shape[1]
    total = None
    for r, x_ref in enumerate(xs):
        src = lax.rem(me - r + len(xs), len(xs))
        from_rows = pl.ds(pl.multiple_of(src * depth, depth), depth)
        part = jnp.dot(x_ref[skip:, :], w_ref[from_rows, begin : begin + width], preferred_element_type=F32)
        total = part if total is None else total + part
    return total.astype(BF16)


def normalize(got, ref, mean_ref, scale):
    for p in range(ref.shape[1] // LANES):
        cols = slice(p * LANES, (p + 1) * LANES)
        x = got[:, cols].astype(F32)
        x = x * lax.rsqrt(head_mean(x * x, mean_ref[...]) + 1e-6)
        ref[:, cols] = x.astype(BF16) * jnp.asarray(scale, BF16)


def block_kernel(j_ref, mean_ref, conv_ref, turn_ref, weight_ref, w_ref, *refs, n, heads, extra, others, sends):
    xs, refs = refs[:n], refs[n:]
    prev_ref = None
    if not extra:
        prev_ref, refs = refs[0], refs[1:]
    other_refs, refs = refs[:others], refs[others:]
    k_ref, v_ref, s_ref, refs = *refs[:3], refs[3:]
    send_refs, ext_ref = refs[:sends], refs[-1]
    q_ref, wq_ref, wk_ref, halo_ref = (None,) * 4 if others else refs[:4]
    rows = v_ref.shape[0]
    qk_width, width = k_ref.shape[1], v_ref.shape[1]
    me = j_ref[0]

    if others:
        k_ref[...] = project(me, xs, w_ref, qk_width, qk_width, extra)
    else:
        qk = project(me, xs, w_ref, 0, 2 * qk_width, extra)
        q_ref[...] = qk[:, :qk_width]
        k_ref[...] = qk[:, qk_width:]
    raw = project(me, xs, w_ref, 2 * qk_width, width, 0)
    if extra:
        ext_ref[...] = raw.astype(F32)
    else:
        ext_ref[0:EDGE, :] = prev_ref[0:EDGE, :].astype(F32)
        ext_ref[EDGE:, :] = raw.astype(F32)
    total = jnp.zeros((rows, width), F32)
    for tap in range(CONV):
        total = total + conv_ref[tap : tap + 1, :] * ext_ref[EDGE - tap : EDGE - tap + rows, :]
    v_ref[...] = total.astype(BF16)

    in_group, lanes, slots = feature_layout(heads)
    groups = heads // in_group
    turned = nt_dot(turn_ref[...], k_ref[...])
    keys = turned[groups * slots * lanes :]
    constant = lax.broadcasted_iota(jnp.int32, (lanes, rows), 0) % FQK == FQK // 2
    low_half = lax.broadcasted_iota(jnp.int32, (SHIFTS + 1, FQK, LANES), 2) < DV
    for g in range(groups):
        own = keys[g * lanes : (g + 1) * lanes]
        phi = []
        for s in range(SHIFTS):
            at = (g * slots + s) * lanes
            phi.append(own * turned[at : at + lanes])
        phi[-1] = jnp.where(constant, 1.0, phi[-1])
        phi = jnp.concatenate([part.astype(BF16) for part in phi + [own]], 0)
        v = v_ref[:, g * in_group * DV : (g + 1) * in_group * DV]
        got = jnp.dot(phi, v, preferred_element_type=F32).reshape(SHIFTS + 1, lanes, in_group * DV)
        for p in range(in_group * DV // LANES):
            cols = slice(p * LANES, (p + 1) * LANES)
            first = got[:, 2 * p * FQK : (2 * p + 1) * FQK, cols]
            second = got[:, (2 * p + 1) * FQK : (2 * p + 2) * FQK, cols]
            state = jnp.where(low_half, first, second).reshape(FEATS, LANES)
            s_ref[g * in_group * DV // LANES + p] = state * weight_ref[...]
    for r in range(sends):
        pair = jnp.bitwise_xor(j_ref[1], r)
        total = s_ref[pair]
        for ref in other_refs:
            total = total + ref[pair]
        send_refs[r][...] = total.astype(BF16)

    if not others:
        halo_ref[0:EDGE, :] = raw[raw.shape[0] - EDGE :]
        query_part(me, xs, w_ref, mean_ref, v_ref, wq_ref, wk_ref, halo_ref, 2 * qk_width + width, extra)


def query_part(me, xs, w_ref, mean_ref, v_ref, wq_ref, wk_ref, halo_ref, begin, skip):
    rows, width = v_ref.shape
    normalize(project(me, xs, w_ref, begin, width, skip), wq_ref, mean_ref, 1.0 / DV**0.5)
    normalize(project(me, xs, w_ref, begin + width, width, skip), wk_ref, mean_ref, 1.0)
    halo_ref[EDGE : EDGE + WIN, :] = v_ref[rows - WIN : rows, :]
    halo_ref[EDGE + WIN : HALO, :] = wk_ref[rows - WIN : rows, :]


def query_kernel(j_ref, mean_ref, w_ref, v_ref, *refs, n):
    xs, (q_ref, wq_ref, wk_ref, halo_ref) = refs[:n], refs[n:]
    qk_width, width = q_ref.shape[1], v_ref.shape[1]
    q_ref[...] = project(j_ref[0], xs, w_ref, 0, qk_width, 0)
    halo_ref[0:EDGE, :] = jnp.zeros((EDGE, width), BF16)
    query_part(j_ref[0], xs, w_ref, mean_ref, v_ref, wq_ref, wk_ref, halo_ref, 2 * qk_width + width, 0)


def band_of(tile, span, first):
    col = lax.broadcasted_iota(jnp.int32, (2 * tile, span), 1)
    ahead = col - lax.broadcasted_iota(jnp.int32, (2 * tile, span), 0) % tile
    seen = (ahead >= 1) & (ahead <= WIN)
    if first is not None:
        seen = seen & (col >= first)
    return seen.astype(F32).astype(BF16)


def window_tile(wq, keys, values, band, low):
    none = jnp.zeros_like(wq)
    scores = nt_dot(jnp.concatenate([jnp.where(low, wq, none), jnp.where(low, none, wq)], 0), keys)
    expo = jnp.exp(scores).astype(BF16) * band
    ones = jnp.ones(values.shape, BF16)
    got = jnp.dot(expo, jnp.concatenate([values, ones], 1), preferred_element_type=F32)
    tile = wq.shape[0]
    got = jnp.where(jnp.concatenate([low, low], 1), got[:tile], got[tile:])
    return got[:, :LANES] / got[:, LANES:]


def edge_kernel(_, prev_ref, v_ref, wq_ref, wk_ref, win_ref):
    tile = win_ref.shape[0]
    band = band_of(tile, tile + WIN, None)
    low = lax.broadcasted_iota(jnp.int32, (tile, LANES), 1) < DV
    for p in range(win_ref.shape[1] // LANES):
        cols = slice(p * LANES, (p + 1) * LANES)
        values = jnp.concatenate([prev_ref[EDGE : EDGE + WIN, cols], v_ref[:tile, cols]], 0)
        keys = jnp.concatenate([prev_ref[EDGE + WIN : HALO, cols], wk_ref[:tile, cols]], 0)
        win_ref[:, cols] = window_tile(wq_ref[:tile, cols], keys, values, band, low)


def attend_kernel(
    a_ref, turn_ref, prev_ref, q_ref, k_ref, v_ref, wq_ref, wk_ref, phi_ref, lin_ref, win_ref,
    vext_ref, kext_ref, *, heads, first
):
    rows = q_ref.shape[0]
    tile = 128
    span = tile + WIN
    vext_ref[0:WIN, :] = prev_ref[EDGE : EDGE + WIN, :]
    vext_ref[WIN : WIN + rows, :] = v_ref[...]
    kext_ref[0:WIN, :] = prev_ref[EDGE + WIN : HALO, :]
    kext_ref[WIN : WIN + rows, :] = wk_ref[...]
    q = q_ref[...]
    k = k_ref[...]
    lane = lax.broadcasted_iota(jnp.int32, (rows, LANES), 1)
    low_half = lane < DV

    in_group, lanes, slots = feature_layout(heads)
    per_tile = LANES // lanes
    turned = jnp.dot(q, turn_ref[...], preferred_element_type=F32)
    slot = lane // lanes
    for g in range(heads // in_group):
        own = q[:, g * lanes : (g + 1) * lanes].astype(F32)
        own = jnp.concatenate([own] * per_tile, 1)
        for t in range(slots // per_tile):
            at = (g * slots // per_tile + t) * LANES
            part = own * turned[:, at : at + LANES]
            if t == (SHIFTS - 1) // per_tile:
                here = (slot == (SHIFTS - 1) % per_tile) & (lane % FQK == FQK // 2)
                part = jnp.where(here, 1.0, part)
            if t == SHIFTS // per_tile:
                part = jnp.where(slot == SHIFTS % per_tile, own, part)
            phi_ref[:, at : at + LANES] = part.astype(BF16)

    down = lax.broadcasted_iota(jnp.int32, (2 * rows, rows), 0) % rows
    causal = lax.broadcasted_iota(jnp.int32, (2 * rows, rows), 1) <= down
    band = band_of(tile, span, None)
    first_band = band
    if first:
        first_band = band_of(tile, span, jnp.where(a_ref[2] == 0, WIN, 0))
    q = q * jnp.asarray(1.0 / FQK**0.5, BF16)
    for p in range(heads * DV // LANES):
        cols = slice(p * LANES, (p + 1) * LANES)
        both = [
            jnp.where((lane >= h * FQK) & (lane < (h + 1) * FQK), q, jnp.zeros_like(q)) for h in (2 * p, 2 * p + 1)
        ]
        t = nt_dot(jnp.concatenate(both, 0), k) + 1.0
        kernel = jnp.where(causal, t * t + 1.0, 0.0).astype(BF16)
        got = jnp.dot(kernel, v_ref[:, cols], preferred_element_type=F32)
        lin_ref[:, cols] = 0.5 * jnp.where(low_half, got[:rows], got[rows:])
        for i in range(rows // tile):
            here = slice(i * tile, (i + 1) * tile)
            keys = kext_ref[i * tile : i * tile + span, cols]
            values = vext_ref[i * tile : i * tile + span, cols]
            win_ref[here, cols] = window_tile(
                wq_ref[here, cols], keys, values, first_band if i == 0 else band, low_half[:tile]
            )


def carry_table(state, p, heads):
    in_group, lanes, slots = feature_layout(heads)
    in_pairs = in_group * DV // LANES
    state = state.reshape(SHIFTS + 1, FQK, LANES)
    low_half = lax.broadcasted_iota(jnp.int32, state.shape, 2) < DV
    parts = [jnp.where(low_half, state, 0.0), jnp.where(low_half, 0.0, state)] * in_pairs
    parts = jnp.concatenate(parts, 1)
    if in_pairs > 1:
        here = lax.broadcasted_iota(jnp.int32, parts.shape, 1) // (2 * FQK) == p
        parts = jnp.where(here, parts, 0.0)
    parts = parts.reshape((SHIFTS + 1) * lanes, LANES)
    if slots > SHIFTS + 1:
        parts = jnp.concatenate([parts, jnp.zeros(((slots - SHIFTS - 1) * lanes, LANES), F32)], 0)
    return parts.astype(BF16)


def finish_kernel(a_ref, mean_ref, gain_ref, *refs, heads, turns, before, edged):
    prior_refs, refs = refs[: len(turns)], refs[len(turns) :]
    states, refs = refs[: max(before)], refs[max(before) :]
    edge_ref, refs = (refs[0], refs[1:]) if edged is not None else (None, refs)
    mix_ref = refs[-1]
    in_group, lanes, slots = feature_layout(heads)
    in_pairs = in_group * DV // LANES
    for i, r in enumerate(turns):
        pair = jnp.bitwise_xor(a_ref[1], r)
        group = lax.div(pair, in_pairs)
        own = pl.ds(pl.multiple_of(group * (slots * lanes), LANES), slots * lanes)
        cols = pl.ds(pl.multiple_of(pair * LANES, LANES), LANES)
        state = prior_refs[i][...].astype(F32)
        added, at = 0, 0
        for b, count in enumerate(before):
            phi_ref, lin_ref, win_ref = refs[3 * b : 3 * b + 3]
            for c in range(added, count):
                state = state + states[c][pair]
            added = count
            table = carry_table(state, lax.rem(pair, in_pairs), heads)
            lin = lin_ref[:, cols] + jnp.dot(phi_ref[:, own], table, preferred_element_type=F32)
            scale = lax.rsqrt(head_mean(lin * lin, mean_ref[...]) + 1e-5)
            win = win_ref[:, cols]
            if b == edged:
                win = jnp.concatenate([edge_ref[:, cols], win[edge_ref.shape[0] :]], 0)
            rows = lin.shape[0]
            mix_ref[at : at + rows, i * LANES : (i + 1) * LANES] = (
                lin * scale * gain_ref[:, cols] + win
            ).astype(BF16)
            at += rows


def output_kernel(a_ref, w_ref, *refs, n, offset, parts, turns):
    pieces, refs = refs[: n * len(turns)], refs[n * len(turns) :]
    weights, (o_ref, held_ref, mixed_ref, sem) = refs[: parts * (n - 1)], refs[-4:]
    rows, cols = held_ref.shape
    mine = pl.ds(pl.multiple_of(a_ref[0] * cols, cols), cols)
    total = None
    for r in range(n):
        for i, (all_rows, pairs) in enumerate(turns):
            here = slice(offset, offset + rows) if all_rows else slice(0, rows)
            for k, turn in enumerate(pairs):
                at = pl.multiple_of(jnp.bitwise_xor(a_ref[1], turn) * LANES, LANES)
                mixed_ref[r, :, pl.ds(at, LANES)] = pieces[r * len(turns) + i][here, k * LANES : (k + 1) * LANES]
        if r == 0:
            part = jnp.dot(mixed_ref[0], w_ref[:, mine], preferred_element_type=F32)
        else:
            part = None
            for i in range(parts):
                ref = weights[(r - 1) * parts + i]
                depth = ref.shape[0]
                at = depth * (jnp.bitwise_xor(a_ref[2] % 2, i) if parts > 1 else 0)
                rows_of = pl.ds(pl.multiple_of(at, depth), depth)
                got = jnp.dot(mixed_ref[r, :, rows_of], ref[...], preferred_element_type=F32)
                part = got if part is None else part + got
        part = part.astype(BF16).astype(F32)
        total = part if total is None else total + part
    held_ref[...] = total.astype(BF16)
    copy = pltpu.make_async_copy(held_ref, o_ref.at[pl.ds(offset, rows), :], sem)
    copy.start()
    copy.wait()


def pick_kernel(a_ref, w_ref, o_ref):
    o_ref[...] = w_ref[...]


def exchange(value, axis, flip):
    count = lax.axis_size(axis)
    return lax.ppermute(value, axis, [(i, i ^ flip) for i in range(count)])


def plane_kernel(a_ref, *refs):
    helds, plane_ref, ahead_refs = refs[:PLANE], refs[PLANE], refs[PLANE + 1 :]
    place = a_ref[1]
    held = [ref[...].astype(F32) for ref in helds]
    plane_ref[...] = (held[0] + held[1] + held[2] + held[3]).astype(BF16)
    for r in range(PLANE):
        total = jnp.zeros_like(held[0])
        for s in range(PLANE):
            before = jnp.bitwise_xor(place, s) < jnp.bitwise_xor(place, r)
            total = total + held[s] * before.astype(F32)
        ahead_refs[r][...] = total


def earlier_kernel(a_ref, *refs, planes):
    ahead_refs, plane_refs, back_refs = refs[:PLANE], refs[PLANE : PLANE + planes], refs[PLANE + planes :]
    mine = a_ref[2] // PLANE
    earlier = jnp.zeros(ahead_refs[0].shape, F32)
    for d, ref in enumerate(plane_refs, 1):
        before = jnp.bitwise_xor(mine, d) < mine
        earlier = earlier + ref[...].astype(F32) * before.astype(F32)
    for r in range(PLANE):
        back_refs[r][...] = (ahead_refs[r][...] + earlier).astype(BF16)


def after(value, earlier):
    return lax.optimization_barrier((value, earlier))[0]


def prior_in_planes(held, places, beside):
    ctx = lax.axis_size("ctx")
    whole = pl.BlockSpec(memory_space=pltpu.VMEM)
    scalar = pl.BlockSpec(memory_space=pltpu.SMEM)
    narrow = jax.ShapeDtypeStruct((FEATS, LANES), BF16)
    wide = jax.ShapeDtypeStruct((FEATS, LANES), F32)
    plane, *ahead = call(
        plane_kernel,
        [narrow] + [wide] * PLANE,
        in_specs=[scalar] + [whole] * PLANE,
        out_specs=[whole] * (1 + PLANE),
        vmem=4 << 20,
    )(after(places, beside[0]), *held)
    earlier = []
    for d in range(1, ctx // PLANE):
        earlier.append(exchange(plane, "ctx", d * PLANE))
    return call(
        functools.partial(earlier_kernel, planes=len(earlier)),
        [narrow] * PLANE,
        in_specs=[scalar] + [whole] * (PLANE + len(earlier)),
        out_specs=[whole] * PLANE,
        vmem=4 << 20,
    )(after(places, beside[1]), *ahead, *earlier)


def prior_by_doubling(total, position):
    ctx = lax.axis_size("ctx")
    prior = jnp.zeros_like(total)
    bit = 1
    while bit < ctx:
        got = exchange(total.astype(BF16), "ctx", bit).astype(F32)
        prior = prior + jnp.where((position & bit) != 0, got, 0.0)
        total = total + got
        bit *= 2
    return [prior[p].astype(BF16) for p in range(total.shape[0])]


def per_device(hidden_in, proj_weight, conv_weight, norm_gain, out_weight):
    n = lax.axis_size("head")
    ctx = lax.axis_size("ctx")
    me = lax.axis_index("head").astype(jnp.int32)
    position = lax.axis_index("ctx").astype(jnp.int32)
    row_count = hidden_in.shape[0]
    model = proj_weight.shape[0]
    heads = out_weight.shape[0] // DV
    width = heads * DV
    pairs = width // LANES
    in_planes = pairs == PLANE and ctx % PLANE == 0 and ctx & (ctx - 1) == 0
    places = jnp.stack([me, position % PLANE if in_planes else jnp.zeros_like(position), position])
    hidden_in, places = lax.optimization_barrier((hidden_in, places))
    step = row_count // 8
    blocks = [(0, 2 * step), (2 * step, 2 * step), (4 * step, step), (5 * step, step), (6 * step, 2 * step)]
    last = len(blocks) - 1
    turn, turn_rows, weight = feature_tables(heads)
    means = mean_table()
    gain = norm_gain.reshape(1, width)
    whole = pl.BlockSpec(memory_space=pltpu.VMEM)
    scalar = pl.BlockSpec(memory_space=pltpu.SMEM)

    def from_head(value, by):
        return lax.ppermute(value, "head", [(i, (i + by) % n) for i in range(n)])

    pieces = {}

    def send_block(b, behind=None):
        at, rows = blocks[b]
        extra = EDGE if b == last else 0
        own = hidden_in[at - extra : at + rows]
        if behind is not None:
            own = after(own, behind)
        pieces[b] = [own] + [from_head(own, r) for r in range(1, n)]

    send_block(last)
    send_block(0, pieces[last][0])
    for b in range(1, last):
        send_block(b, pieces[last][0])

    cols = out_weight.shape[1] // n
    out_parts = 2 if width // 2 % LANES == 0 and ctx % 2 == 0 else 1
    share = width // out_parts
    def pick(r):
        column = functools.partial(lambda i, a, r: (a[2] % out_parts, (a[0] + r) % n), r=r)
        return call(
            pick_kernel,
            jax.ShapeDtypeStruct((share, cols), BF16),
            grid_spec=pltpu.PrefetchScalarGridSpec(
                num_scalar_prefetch=1,
                grid=(1,),
                in_specs=[pl.BlockSpec((share, cols), column)],
                out_specs=pl.BlockSpec((share, cols), lambda i, a: (0, 0)),
            ),
            vmem=8 << 20,
        )(after(places, done[last - 1][1]), out_weight)

    qk_width = -(-heads * FQK // LANES) * LANES
    arranged_width = 2 * qk_width + 3 * width
    slab = 256
    arranged = call(
        functools.partial(arrange_kernel, heads=heads),
        jax.ShapeDtypeStruct((model, arranged_width), BF16),
        grid=(model // slab,),
        in_specs=[pl.BlockSpec((slab, proj_weight.shape[1]), lambda i: (i, 0))],
        out_specs=pl.BlockSpec((slab, arranged_width), lambda i: (i, 0)),
        vmem=32 << 20,
    )(proj_weight)

    def bf16(rows, *widths):
        return [jax.ShapeDtypeStruct((rows, w), BF16) for w in widths]

    def do_block(b, prev, behind, others=()):
        rows = blocks[b][1]
        extra = EDGE if prev is None else 0
        sends = PLANE if in_planes and others else 0
        tokens = places if behind is None else after(places, behind)
        shapes = bf16(rows, qk_width, width) + [jax.ShapeDtypeStruct((pairs, FEATS, LANES), F32)]
        if others:
            shapes += bf16(FEATS, LANES) * sends
        else:
            shapes += bf16(rows, qk_width, width, width) + bf16(HALO, width)
        operands = [tokens, means, conv_weight, turn_rows, weight, arranged, *pieces[b]]
        if prev is not None:
            operands.append(prev)
        operands += others
        return call(
            functools.partial(
                block_kernel, n=n, heads=heads, extra=extra, others=len(others), sends=sends
            ),
            shapes,
            in_specs=[scalar] + [whole] * (len(operands) - 1),
            out_specs=[whole] * len(shapes),
            scratch_shapes=[pltpu.VMEM((EDGE + rows, width), F32)],
            vmem=32 << 20,
        )(*operands)

    def do_queries(b, v):
        rows = blocks[b][1]
        return call(
            functools.partial(query_kernel, n=n),
            bf16(rows, qk_width, width, width) + bf16(HALO, width),
            in_specs=[scalar] + [whole] * (3 + n),
            out_specs=[whole] * 4,
            vmem=32 << 20,
        )(places, means, arranged, v, *pieces[b])

    def attend(b, prev):
        rows = blocks[b][1]
        k, v, _, q, wq, wk, _ = done[b]
        return call(
            functools.partial(attend_kernel, heads=heads, first=b == 0),
            [jax.ShapeDtypeStruct((rows, turn.shape[1]), BF16)] + [jax.ShapeDtypeStruct((rows, width), F32)] * 2,
            in_specs=[scalar] + [whole] * 7,
            out_specs=[whole] * 3,
            scratch_shapes=[pltpu.VMEM((WIN + rows, width), BF16)] * 2,
            vmem=16 << 20,
        )(places, turn, prev, q, k, v, wq, wk)

    done, attended = {}, {}
    done[last] = do_block(last, None, None)
    halo = lax.ppermute(done[last][6], "ctx", [(i, i + 1) for i in range(ctx - 1)])
    prevs = {0: halo}
    for b in range(last - 1):
        done[b] = do_block(b, prevs[b], [a[1] for a in attended.values()] if b else None)
        prevs[b + 1] = done[b][6]
        attended[b] = attend(b, prevs[b])
        if b == 0:
            attended[last] = attend(last, halo)
    b = last - 1
    k, v, state, *sends = do_block(b, prevs[b], attended[b - 1][1], [done[c][2] for c in (last, *range(b))])
    done[b] = (k, v, state, *do_queries(b, v))
    prevs[last] = done[b][6]
    attended[last - 1] = attend(last - 1, prevs[last - 1])
    tile = 128
    edge = call(
        edge_kernel,
        jax.ShapeDtypeStruct((tile, width), F32),
        in_specs=[scalar] + [whole] * 4,
        out_specs=whole,
        vmem=16 << 20,
    )(places, done[last - 1][6], done[last][1], done[last][4], done[last][5])

    def finish(turns, priors, some, behind):
        before = list(some)
        operands = [after(places, behind), means, gain, *priors, *[done[c][2] for c in range(max(before))]]
        edged = before.index(last) if last in before else None
        if edged is not None:
            operands.append(edge)
        for b in some:
            operands += attended[b]
        rows = sum(blocks[b][1] for b in some)
        return call(
            functools.partial(finish_kernel, heads=heads, turns=turns, before=before, edged=edged),
            jax.ShapeDtypeStruct((rows, len(turns) * LANES), BF16),
            in_specs=[scalar] + [whole] * (len(operands) - 1),
            out_specs=whole,
            flops=20 * 10**9 if tuple(some) == order[:1] else 4850 * 10**6 if len(some) > 1 else 1,
            vmem=24 << 20,
        )(*operands)

    order = (0, 1, 4, 2, 3)
    early = []
    if in_planes:
        held = sends[:1] + [exchange(sends[r], "ctx", r) for r in range(1, PLANE)]
        back = prior_in_planes(held, places, [done[last - 1][1], (attended[last - 1][1], edge)])
        priors = [exchange(back[r], "ctx", r) for r in range(1, PLANE)]
        turns = tuple(range(1, PLANE))
        mixed = finish((0,), back[:1], range(last + 1), done[last][1])
        early = [mixed] + [from_head(mixed, r) for r in range(1, n)]
    else:
        priors = prior_by_doubling(sum(done[b][2] for b in range(last + 1)), position)
        turns = tuple(range(pairs))
        mixed = attended[last][1]
    fetched = [from_head(pick(r), r) for r in range(1, n)]
    out_rows = []
    for got in fetched:
        out_rows.append(got)
        if out_parts > 1:
            out_rows.append(exchange(after(got, mixed), "ctx", 1))

    mixes = {}
    for b in order:
        mixed = finish(turns, priors, (b,), mixed)
        mixes[b] = [mixed] + [from_head(mixed, r) for r in range(1, n)]

    result = None
    for b in order:
        at, rows = blocks[b]
        operands = [places, out_weight]
        for r in range(n):
            operands += ([early[r]] if early else []) + [mixes[b][r]]
        operands += out_rows
        specs = [scalar] + [whole] * (len(operands) - 1)
        aliases = {}
        if result is not None:
            aliases = {len(operands): 0}
            operands.append(result)
            specs.append(pl.BlockSpec(memory_space=pl.ANY))
        result = call(
            functools.partial(
                output_kernel,
                n=n,
                offset=at,
                parts=out_parts,
                turns=([(True, (0,))] if early else []) + [(False, turns)],
            ),
            jax.ShapeDtypeStruct((row_count, cols), BF16),
            in_specs=specs,
            out_specs=pl.BlockSpec(memory_space=pl.ANY),
            scratch_shapes=[
                pltpu.VMEM((rows, cols), BF16),
                pltpu.VMEM((n, rows, width), BF16),
                pltpu.SemaphoreType.DMA,
            ],
            input_output_aliases=aliases,
            vmem=16 << 20,
        )(*operands)
    return result


def solution(mesh):
    return jax.shard_map(
        per_device,
        mesh=mesh,
        in_specs=(P("ctx", "head"), P(None, "head"), P(None, "head"), P("head"), P("head", None)),
        out_specs=P("ctx", "head"),
        check_vma=False,
    )
```

```python
import functools

import jax
import jax.numpy as jnp
import numpy as np
from jax import lax
from jax.experimental import pallas as pl
from jax.experimental.pallas import tpu as pltpu
from jax.sharding import PartitionSpec as P

DV = 64
FQK = 16
WIN = 64
CONV = 3
LANES = 128
SHIFTS = FQK // 2 + 1
FEATS = (SHIFTS + 1) * FQK
EDGE = 16
HALO = EDGE + 2 * WIN
PLANE = 4
F32 = jnp.float32
BF16 = jnp.bfloat16


def call(body, out_shape, *, vmem, flops=1, **kwargs):
    return pl.pallas_call(
        body,
        out_shape=out_shape,
        compiler_params=pltpu.CompilerParams(vmem_limit_bytes=vmem),
        cost_estimate=pl.CostEstimate(flops=flops, bytes_accessed=1, transcendentals=0),
        **kwargs,
    )


def feature_layout(heads):
    in_group = min(heads, 4)
    lanes = in_group * FQK
    per_tile = LANES // lanes
    return in_group, lanes, -(-(SHIFTS + 1) // per_tile) * per_tile


def feature_tables(heads):
    in_group, lanes, slots = feature_layout(heads)
    groups = heads // in_group
    turn = np.zeros((LANES, groups, slots, in_group, FQK), np.float32)
    for g in range(groups):
        for s in range(SHIFTS):
            for h in range(in_group):
                for i in range(FQK if s < SHIFTS - 1 else FQK // 2):
                    turn[g * lanes + h * FQK + (i + s) % FQK, g, s, h, i] = 1.0
    weight = np.zeros((SHIFTS + 1, FQK, LANES), np.float32)
    weight[0] = 1.0 / (2.0 * FQK)
    weight[1:SHIFTS] = 2.0 / (2.0 * FQK)
    weight[SHIFTS - 1, FQK // 2] = 1.0
    weight[SHIFTS] = 1.0 / FQK**0.5
    turn = turn.reshape(LANES, -1)
    by_rows = np.concatenate([turn.T, np.eye(LANES, dtype=np.float32)], 0)
    return jnp.asarray(turn, BF16), jnp.asarray(by_rows, BF16), jnp.asarray(weight.reshape(FEATS, LANES))


def mean_table():
    block = np.kron(np.eye(LANES // DV), np.ones((DV, DV))) / DV
    return jnp.asarray(np.concatenate([block, block], 0), BF16)


def head_mean(values, table):
    high = values.astype(BF16)
    low = (values - high.astype(F32)).astype(BF16)
    return jnp.dot(jnp.concatenate([high, low], 1), table, preferred_element_type=F32)


def nt_dot(a, b):
    return lax.dot_general(a, b, (((1,), (1,)), ((), ())), preferred_element_type=F32)


def arrange_kernel(w_ref, o_ref, *, heads):
    per_head = 2 * FQK + 3 * DV
    w = w_ref[...]
    at = 0
    for begin, width in ((0, FQK), (FQK, FQK), (2 * FQK, DV), (2 * FQK + DV, DV), (2 * FQK + 2 * DV, DV)):
        parts = [w[:, h * per_head + begin : h * per_head + begin + width] for h in range(heads)]
        total = heads * width
        padded = -(-total // LANES) * LANES
        if padded > total:
            parts.append(jnp.zeros((w.shape[0], padded - total), w.dtype))
        o_ref[:, at : at + padded] = jnp.concatenate(parts, 1)
        at += padded


def project(me, xs, w_ref, begin, width, skip):
    depth = xs[0].shape[1]
    total = None
    for r, x_ref in enumerate(xs):
        src = lax.rem(me - r + len(xs), len(xs))
        from_rows = pl.ds(pl.multiple_of(src * depth, depth), depth)
        part = jnp.dot(x_ref[skip:, :], w_ref[from_rows, begin : begin + width], preferred_element_type=F32)
        total = part if total is None else total + part
    return total.astype(BF16)


def normalize(got, ref, mean_ref, scale):
    for p in range(ref.shape[1] // LANES):
        cols = slice(p * LANES, (p + 1) * LANES)
        x = got[:, cols].astype(F32)
        x = x * lax.rsqrt(head_mean(x * x, mean_ref[...]) + 1e-6)
        ref[:, cols] = x.astype(BF16) * jnp.asarray(scale, BF16)


def block_kernel(j_ref, mean_ref, conv_ref, turn_ref, weight_ref, w_ref, *refs, n, heads, extra, others, sends):
    xs, refs = refs[:n], refs[n:]
    prev_ref = None
    if not extra:
        prev_ref, refs = refs[0], refs[1:]
    other_refs, refs = refs[:others], refs[others:]
    k_ref, v_ref, s_ref, refs = *refs[:3], refs[3:]
    send_refs, ext_ref = refs[:sends], refs[-1]
    q_ref, wq_ref, wk_ref, halo_ref = (None,) * 4 if others else refs[:4]
    rows = v_ref.shape[0]
    qk_width, width = k_ref.shape[1], v_ref.shape[1]
    me = j_ref[0]

    if others:
        k_ref[...] = project(me, xs, w_ref, qk_width, qk_width, extra)
    else:
        qk = project(me, xs, w_ref, 0, 2 * qk_width, extra)
        q_ref[...] = qk[:, :qk_width]
        k_ref[...] = qk[:, qk_width:]
    raw = project(me, xs, w_ref, 2 * qk_width, width, 0)
    if extra:
        ext_ref[...] = raw.astype(F32)
    else:
        ext_ref[0:EDGE, :] = prev_ref[0:EDGE, :].astype(F32)
        ext_ref[EDGE:, :] = raw.astype(F32)
    total = jnp.zeros((rows, width), F32)
    for tap in range(CONV):
        total = total + conv_ref[tap : tap + 1, :] * ext_ref[EDGE - tap : EDGE - tap + rows, :]
    v_ref[...] = total.astype(BF16)

    in_group, lanes, slots = feature_layout(heads)
    groups = heads // in_group
    turned = nt_dot(turn_ref[...], k_ref[...])
    keys = turned[groups * slots * lanes :]
    constant = lax.broadcasted_iota(jnp.int32, (lanes, rows), 0) % FQK == FQK // 2
    low_half = lax.broadcasted_iota(jnp.int32, (SHIFTS + 1, FQK, LANES), 2) < DV
    for g in range(groups):
        own = keys[g * lanes : (g + 1) * lanes]
        phi = []
        for s in range(SHIFTS):
            at = (g * slots + s) * lanes
            phi.append(own * turned[at : at + lanes])
        phi[-1] = jnp.where(constant, 1.0, phi[-1])
        phi = jnp.concatenate([part.astype(BF16) for part in phi + [own]], 0)
        v = v_ref[:, g * in_group * DV : (g + 1) * in_group * DV]
        got = jnp.dot(phi, v, preferred_element_type=F32).reshape(SHIFTS + 1, lanes, in_group * DV)
        for p in range(in_group * DV // LANES):
            cols = slice(p * LANES, (p + 1) * LANES)
            first = got[:, 2 * p * FQK : (2 * p + 1) * FQK, cols]
            second = got[:, (2 * p + 1) * FQK : (2 * p + 2) * FQK, cols]
            state = jnp.where(low_half, first, second).reshape(FEATS, LANES)
            s_ref[g * in_group * DV // LANES + p] = state * weight_ref[...]
    for r in range(sends):
        pair = jnp.bitwise_xor(j_ref[1], r)
        total = s_ref[pair]
        for ref in other_refs:
            total = total + ref[pair]
        send_refs[r][...] = total.astype(BF16)

    if not others:
        halo_ref[0:EDGE, :] = raw[raw.shape[0] - EDGE :]
        query_part(me, xs, w_ref, mean_ref, v_ref, wq_ref, wk_ref, halo_ref, 2 * qk_width + width, extra)


def query_part(me, xs, w_ref, mean_ref, v_ref, wq_ref, wk_ref, halo_ref, begin, skip):
    rows, width = v_ref.shape
    normalize(project(me, xs, w_ref, begin, width, skip), wq_ref, mean_ref, 1.0 / DV**0.5)
    normalize(project(me, xs, w_ref, begin + width, width, skip), wk_ref, mean_ref, 1.0)
    halo_ref[EDGE : EDGE + WIN, :] = v_ref[rows - WIN : rows, :]
    halo_ref[EDGE + WIN : HALO, :] = wk_ref[rows - WIN : rows, :]


def query_kernel(j_ref, mean_ref, w_ref, v_ref, *refs, n):
    xs, (q_ref, wq_ref, wk_ref, halo_ref) = refs[:n], refs[n:]
    qk_width, width = q_ref.shape[1], v_ref.shape[1]
    q_ref[...] = project(j_ref[0], xs, w_ref, 0, qk_width, 0)
    halo_ref[0:EDGE, :] = jnp.zeros((EDGE, width), BF16)
    query_part(j_ref[0], xs, w_ref, mean_ref, v_ref, wq_ref, wk_ref, halo_ref, 2 * qk_width + width, 0)


def band_of(tile, span, first):
    col = lax.broadcasted_iota(jnp.int32, (2 * tile, span), 1)
    ahead = col - lax.broadcasted_iota(jnp.int32, (2 * tile, span), 0) % tile
    seen = (ahead >= 1) & (ahead <= WIN)
    if first is not None:
        seen = seen & (col >= first)
    return seen.astype(F32).astype(BF16)


def window_tile(wq, keys, values, band, low):
    none = jnp.zeros_like(wq)
    scores = nt_dot(jnp.concatenate([jnp.where(low, wq, none), jnp.where(low, none, wq)], 0), keys)
    expo = jnp.exp(scores).astype(BF16) * band
    ones = jnp.ones(values.shape, BF16)
    got = jnp.dot(expo, jnp.concatenate([values, ones], 1), preferred_element_type=F32)
    tile = wq.shape[0]
    got = jnp.where(jnp.concatenate([low, low], 1), got[:tile], got[tile:])
    return got[:, :LANES] / got[:, LANES:]


def edge_kernel(_, prev_ref, v_ref, wq_ref, wk_ref, win_ref):
    tile = win_ref.shape[0]
    band = band_of(tile, tile + WIN, None)
    low = lax.broadcasted_iota(jnp.int32, (tile, LANES), 1) < DV
    for p in range(win_ref.shape[1] // LANES):
        cols = slice(p * LANES, (p + 1) * LANES)
        values = jnp.concatenate([prev_ref[EDGE : EDGE + WIN, cols], v_ref[:tile, cols]], 0)
        keys = jnp.concatenate([prev_ref[EDGE + WIN : HALO, cols], wk_ref[:tile, cols]], 0)
        win_ref[:, cols] = window_tile(wq_ref[:tile, cols], keys, values, band, low)


def attend_kernel(
    a_ref, turn_ref, prev_ref, q_ref, k_ref, v_ref, wq_ref, wk_ref, phi_ref, lin_ref, win_ref,
    vext_ref, kext_ref, *, heads, first
):
    rows = q_ref.shape[0]
    tile = 128
    span = tile + WIN
    vext_ref[0:WIN, :] = prev_ref[EDGE : EDGE + WIN, :]
    vext_ref[WIN : WIN + rows, :] = v_ref[...]
    kext_ref[0:WIN, :] = prev_ref[EDGE + WIN : HALO, :]
    kext_ref[WIN : WIN + rows, :] = wk_ref[...]
    q = q_ref[...]
    k = k_ref[...]
    lane = lax.broadcasted_iota(jnp.int32, (rows, LANES), 1)
    low_half = lane < DV

    in_group, lanes, slots = feature_layout(heads)
    per_tile = LANES // lanes
    turned = jnp.dot(q, turn_ref[...], preferred_element_type=F32)
    slot = lane // lanes
    for g in range(heads // in_group):
        own = q[:, g * lanes : (g + 1) * lanes].astype(F32)
        own = jnp.concatenate([own] * per_tile, 1)
        for t in range(slots // per_tile):
            at = (g * slots // per_tile + t) * LANES
            part = own * turned[:, at : at + LANES]
            if t == (SHIFTS - 1) // per_tile:
                here = (slot == (SHIFTS - 1) % per_tile) & (lane % FQK == FQK // 2)
                part = jnp.where(here, 1.0, part)
            if t == SHIFTS // per_tile:
                part = jnp.where(slot == SHIFTS % per_tile, own, part)
            phi_ref[:, at : at + LANES] = part.astype(BF16)

    down = lax.broadcasted_iota(jnp.int32, (2 * rows, rows), 0) % rows
    causal = lax.broadcasted_iota(jnp.int32, (2 * rows, rows), 1) <= down
    band = band_of(tile, span, None)
    first_band = band
    if first:
        first_band = band_of(tile, span, jnp.where(a_ref[2] == 0, WIN, 0))
    q = q * jnp.asarray(1.0 / FQK**0.5, BF16)
    for p in range(heads * DV // LANES):
        cols = slice(p * LANES, (p + 1) * LANES)
        both = [
            jnp.where((lane >= h * FQK) & (lane < (h + 1) * FQK), q, jnp.zeros_like(q)) for h in (2 * p, 2 * p + 1)
        ]
        t = nt_dot(jnp.concatenate(both, 0), k) + 1.0
        kernel = jnp.where(causal, t * t + 1.0, 0.0).astype(BF16)
        got = jnp.dot(kernel, v_ref[:, cols], preferred_element_type=F32)
        lin_ref[:, cols] = 0.5 * jnp.where(low_half, got[:rows], got[rows:])
        for i in range(rows // tile):
            here = slice(i * tile, (i + 1) * tile)
            keys = kext_ref[i * tile : i * tile + span, cols]
            values = vext_ref[i * tile : i * tile + span, cols]
            win_ref[here, cols] = window_tile(
                wq_ref[here, cols], keys, values, first_band if i == 0 else band, low_half[:tile]
            )


def carry_table(state, p, heads):
    in_group, lanes, slots = feature_layout(heads)
    in_pairs = in_group * DV // LANES
    state = state.reshape(SHIFTS + 1, FQK, LANES)
    low_half = lax.broadcasted_iota(jnp.int32, state.shape, 2) < DV
    parts = [jnp.where(low_half, state, 0.0), jnp.where(low_half, 0.0, state)] * in_pairs
    parts = jnp.concatenate(parts, 1)
    if in_pairs > 1:
        here = lax.broadcasted_iota(jnp.int32, parts.shape, 1) // (2 * FQK) == p
        parts = jnp.where(here, parts, 0.0)
    parts = parts.reshape((SHIFTS + 1) * lanes, LANES)
    if slots > SHIFTS + 1:
        parts = jnp.concatenate([parts, jnp.zeros(((slots - SHIFTS - 1) * lanes, LANES), F32)], 0)
    return parts.astype(BF16)


def finish_kernel(a_ref, mean_ref, gain_ref, *refs, heads, turns, before, edged):
    prior_refs, refs = refs[: len(turns)], refs[len(turns) :]
    states, refs = refs[: max(before)], refs[max(before) :]
    edge_ref, refs = (refs[0], refs[1:]) if edged is not None else (None, refs)
    mix_ref = refs[-1]
    in_group, lanes, slots = feature_layout(heads)
    in_pairs = in_group * DV // LANES
    for i, r in enumerate(turns):
        pair = jnp.bitwise_xor(a_ref[1], r)
        group = lax.div(pair, in_pairs)
        own = pl.ds(pl.multiple_of(group * (slots * lanes), LANES), slots * lanes)
        cols = pl.ds(pl.multiple_of(pair * LANES, LANES), LANES)
        state = prior_refs[i][...].astype(F32)
        added, at = 0, 0
        for b, count in enumerate(before):
            phi_ref, lin_ref, win_ref = refs[3 * b : 3 * b + 3]
            for c in range(added, count):
                state = state + states[c][pair]
            added = count
            table = carry_table(state, lax.rem(pair, in_pairs), heads)
            lin = lin_ref[:, cols] + jnp.dot(phi_ref[:, own], table, preferred_element_type=F32)
            scale = lax.rsqrt(head_mean(lin * lin, mean_ref[...]) + 1e-5)
            win = win_ref[:, cols]
            if b == edged:
                win = jnp.concatenate([edge_ref[:, cols], win[edge_ref.shape[0] :]], 0)
            rows = lin.shape[0]
            mix_ref[at : at + rows, i * LANES : (i + 1) * LANES] = (
                lin * scale * gain_ref[:, cols] + win
            ).astype(BF16)
            at += rows


def place_pieces(a_ref, pieces, turns, offset, mixed_ref):
    rows = mixed_ref.shape[0]
    for ref, (all_rows, pairs) in zip(pieces, turns):
        here = slice(offset, offset + rows) if all_rows else slice(0, rows)
        for k, turn in enumerate(pairs):
            at = pl.multiple_of(jnp.bitwise_xor(a_ref[1], turn) * LANES, LANES)
            mixed_ref[:, pl.ds(at, LANES)] = ref[here, k * LANES : (k + 1) * LANES]


def own_columns(a_ref, cols, begin, width):
    return pl.ds(pl.multiple_of(a_ref[0] * cols + begin, LANES), width)


def share_kernel(a_ref, w_ref, *refs, turns, blocks):
    share_ref, mixed_ref = refs[-2:]
    at = 0
    for i, (offset, rows) in enumerate(blocks):
        pieces = refs[i * len(turns) : (i + 1) * len(turns)]
        place_pieces(a_ref, pieces, turns, offset, mixed_ref.at[pl.ds(at, rows), :])
        at += rows
    cols = share_ref.shape[1]
    mine = own_columns(a_ref, cols, 0, cols)
    share_ref[...] = jnp.dot(mixed_ref[...], w_ref[:, mine], preferred_element_type=F32).astype(BF16)


def output_kernel(a_ref, w_ref, *refs, n, offset, parts, turns, shared):
    weights, refs = refs[: parts * (n - 1)], refs[parts * (n - 1) :]
    o_ref, held_ref, mixed_ref, sems = refs[-4:]
    rows, cols = held_ref.shape
    first = 0
    if shared is not None:
        share_ref, refs = refs[0], refs[1:]
        first = 1
    for r in range(first, n):
        pieces = refs[(r - first) * len(turns) : (r - first + 1) * len(turns)]
        place_pieces(a_ref, pieces, turns, offset, mixed_ref.at[r])
    copies = []
    count = 2 if cols % (2 * LANES) == 0 else 1
    width = cols // count
    for half in range(count):
        here = slice(half * width, (half + 1) * width)
        total = None
        if shared is not None:
            total = share_ref[shared : shared + rows, here].astype(F32)
        for r in range(first, n):
            if r == 0:
                part = jnp.dot(
                    mixed_ref[0], w_ref[:, own_columns(a_ref, cols, half * width, width)], preferred_element_type=F32
                )
            else:
                part = None
                for i in range(parts):
                    ref = weights[(r - 1) * parts + i]
                    depth = ref.shape[0]
                    at = depth * (jnp.bitwise_xor(a_ref[2] % 2, i) if parts > 1 else 0)
                    rows_of = pl.ds(pl.multiple_of(at, depth), depth)
                    got = jnp.dot(mixed_ref[r, :, rows_of], ref[:, here], preferred_element_type=F32)
                    part = got if part is None else part + got
            part = part.astype(BF16).astype(F32)
            total = part if total is None else total + part
        held_ref[:, here] = total.astype(BF16)
        copy = pltpu.make_async_copy(
            held_ref.at[:, here], o_ref.at[pl.ds(offset, rows), here], sems.at[half]
        )
        copy.start()
        copies.append(copy)
    for copy in copies:
        copy.wait()


def pick_kernel(a_ref, w_ref, o_ref):
    o_ref[...] = w_ref[...]


def exchange(value, axis, flip):
    count = lax.axis_size(axis)
    return lax.ppermute(value, axis, [(i, i ^ flip) for i in range(count)])


def plane_kernel(a_ref, *refs):
    helds, plane_ref, ahead_refs = refs[:PLANE], refs[PLANE], refs[PLANE + 1 :]
    place = a_ref[1]
    held = [ref[...].astype(F32) for ref in helds]
    plane_ref[...] = (held[0] + held[1] + held[2] + held[3]).astype(BF16)
    for r in range(PLANE):
        total = jnp.zeros_like(held[0])
        for s in range(PLANE):
            before = jnp.bitwise_xor(place, s) < jnp.bitwise_xor(place, r)
            total = total + held[s] * before.astype(F32)
        ahead_refs[r][...] = total


def earlier_kernel(a_ref, *refs, planes):
    ahead_refs, plane_refs, back_refs = refs[:PLANE], refs[PLANE : PLANE + planes], refs[PLANE + planes :]
    mine = a_ref[2] // PLANE
    earlier = jnp.zeros(ahead_refs[0].shape, F32)
    for d, ref in enumerate(plane_refs, 1):
        before = jnp.bitwise_xor(mine, d) < mine
        earlier = earlier + ref[...].astype(F32) * before.astype(F32)
    for r in range(PLANE):
        back_refs[r][...] = (ahead_refs[r][...] + earlier).astype(BF16)


def after(value, earlier):
    return lax.optimization_barrier((value, earlier))[0]


def prior_in_planes(held, places, beside):
    ctx = lax.axis_size("ctx")
    whole = pl.BlockSpec(memory_space=pltpu.VMEM)
    scalar = pl.BlockSpec(memory_space=pltpu.SMEM)
    narrow = jax.ShapeDtypeStruct((FEATS, LANES), BF16)
    wide = jax.ShapeDtypeStruct((FEATS, LANES), F32)
    plane, *ahead = call(
        plane_kernel,
        [narrow] + [wide] * PLANE,
        in_specs=[scalar] + [whole] * PLANE,
        out_specs=[whole] * (1 + PLANE),
        vmem=4 << 20,
    )(after(places, beside[0]), *held)
    earlier = []
    for d in range(1, ctx // PLANE):
        earlier.append(exchange(plane, "ctx", d * PLANE))
    return call(
        functools.partial(earlier_kernel, planes=len(earlier)),
        [narrow] * PLANE,
        in_specs=[scalar] + [whole] * (PLANE + len(earlier)),
        out_specs=[whole] * PLANE,
        vmem=4 << 20,
    )(after(places, beside[1]), *ahead, *earlier)


def prior_by_doubling(total, position):
    ctx = lax.axis_size("ctx")
    prior = jnp.zeros_like(total)
    bit = 1
    while bit < ctx:
        got = exchange(total.astype(BF16), "ctx", bit).astype(F32)
        prior = prior + jnp.where((position & bit) != 0, got, 0.0)
        total = total + got
        bit *= 2
    return [prior[p].astype(BF16) for p in range(total.shape[0])]


def per_device(hidden_in, proj_weight, conv_weight, norm_gain, out_weight):
    n = lax.axis_size("head")
    ctx = lax.axis_size("ctx")
    me = lax.axis_index("head").astype(jnp.int32)
    position = lax.axis_index("ctx").astype(jnp.int32)
    row_count = hidden_in.shape[0]
    model = proj_weight.shape[0]
    heads = out_weight.shape[0] // DV
    width = heads * DV
    pairs = width // LANES
    in_planes = pairs == PLANE and ctx % PLANE == 0 and ctx & (ctx - 1) == 0
    places = jnp.stack([me, position % PLANE if in_planes else jnp.zeros_like(position), position])
    hidden_in, places = lax.optimization_barrier((hidden_in, places))
    step = row_count // 8
    blocks = [(0, 2 * step), (2 * step, 2 * step), (4 * step, step), (5 * step, step), (6 * step, 2 * step)]
    last = len(blocks) - 1
    turn, turn_rows, weight = feature_tables(heads)
    means = mean_table()
    gain = norm_gain.reshape(1, width)
    whole = pl.BlockSpec(memory_space=pltpu.VMEM)
    scalar = pl.BlockSpec(memory_space=pltpu.SMEM)

    def from_head(value, by):
        return lax.ppermute(value, "head", [(i, (i + by) % n) for i in range(n)])

    pieces = {}

    def send_block(b, behind=None):
        at, rows = blocks[b]
        extra = EDGE if b == last else 0
        own = hidden_in[at - extra : at + rows]
        if behind is not None:
            own = after(own, behind)
        pieces[b] = [own] + [from_head(own, r) for r in range(1, n)]

    send_block(last)
    send_block(0, pieces[last][0])
    for b in range(1, last):
        send_block(b, pieces[last][0])

    cols = out_weight.shape[1] // n
    out_parts = 2 if width // 2 % LANES == 0 and ctx % 2 == 0 else 1
    share = width // out_parts
    def pick(r):
        column = functools.partial(lambda i, a, r: (a[2] % out_parts, (a[0] + r) % n), r=r)
        return call(
            pick_kernel,
            jax.ShapeDtypeStruct((share, cols), BF16),
            grid_spec=pltpu.PrefetchScalarGridSpec(
                num_scalar_prefetch=1,
                grid=(1,),
                in_specs=[pl.BlockSpec((share, cols), column)],
                out_specs=pl.BlockSpec((share, cols), lambda i, a: (0, 0)),
            ),
            vmem=8 << 20,
        )(after(places, done[last - 1][1]), out_weight)

    qk_width = -(-heads * FQK // LANES) * LANES
    arranged_width = 2 * qk_width + 3 * width
    slab = 256
    arranged = call(
        functools.partial(arrange_kernel, heads=heads),
        jax.ShapeDtypeStruct((model, arranged_width), BF16),
        grid=(model // slab,),
        in_specs=[pl.BlockSpec((slab, proj_weight.shape[1]), lambda i: (i, 0))],
        out_specs=pl.BlockSpec((slab, arranged_width), lambda i: (i, 0)),
        vmem=32 << 20,
    )(proj_weight)

    def bf16(rows, *widths):
        return [jax.ShapeDtypeStruct((rows, w), BF16) for w in widths]

    def do_block(b, prev, behind, others=()):
        rows = blocks[b][1]
        extra = EDGE if prev is None else 0
        sends = PLANE if in_planes and others else 0
        tokens = places if behind is None else after(places, behind)
        shapes = bf16(rows, qk_width, width) + [jax.ShapeDtypeStruct((pairs, FEATS, LANES), F32)]
        if others:
            shapes += bf16(FEATS, LANES) * sends
        else:
            shapes += bf16(rows, qk_width, width, width) + bf16(HALO, width)
        operands = [tokens, means, conv_weight, turn_rows, weight, arranged, *pieces[b]]
        if prev is not None:
            operands.append(prev)
        operands += others
        return call(
            functools.partial(
                block_kernel, n=n, heads=heads, extra=extra, others=len(others), sends=sends
            ),
            shapes,
            in_specs=[scalar] + [whole] * (len(operands) - 1),
            out_specs=[whole] * len(shapes),
            scratch_shapes=[pltpu.VMEM((EDGE + rows, width), F32)],
            vmem=32 << 20,
        )(*operands)

    def do_queries(b, v):
        rows = blocks[b][1]
        return call(
            functools.partial(query_kernel, n=n),
            bf16(rows, qk_width, width, width) + bf16(HALO, width),
            in_specs=[scalar] + [whole] * (3 + n),
            out_specs=[whole] * 4,
            vmem=32 << 20,
        )(places, means, arranged, v, *pieces[b])

    def attend(b, prev):
        rows = blocks[b][1]
        k, v, _, q, wq, wk, _ = done[b]
        return call(
            functools.partial(attend_kernel, heads=heads, first=b == 0),
            [jax.ShapeDtypeStruct((rows, turn.shape[1]), BF16)] + [jax.ShapeDtypeStruct((rows, width), F32)] * 2,
            in_specs=[scalar] + [whole] * 7,
            out_specs=[whole] * 3,
            scratch_shapes=[pltpu.VMEM((WIN + rows, width), BF16)] * 2,
            vmem=16 << 20,
        )(places, turn, prev, q, k, v, wq, wk)

    done, attended = {}, {}
    done[last] = do_block(last, None, None)
    halo = lax.ppermute(done[last][6], "ctx", [(i, i + 1) for i in range(ctx - 1)])
    prevs = {0: halo}
    for b in range(last - 1):
        done[b] = do_block(b, prevs[b], [a[1] for a in attended.values()] if b else None)
        prevs[b + 1] = done[b][6]
        attended[b] = attend(b, prevs[b])
        if b == 0:
            attended[last] = attend(last, halo)
    b = last - 1
    k, v, state, *sends = do_block(b, prevs[b], attended[b - 1][1], [done[c][2] for c in (last, *range(b))])
    done[b] = (k, v, state, *do_queries(b, v))
    prevs[last] = done[b][6]
    attended[last - 1] = attend(last - 1, prevs[last - 1])
    tile = 128
    edge = call(
        edge_kernel,
        jax.ShapeDtypeStruct((tile, width), F32),
        in_specs=[scalar] + [whole] * 4,
        out_specs=whole,
        vmem=16 << 20,
    )(places, done[last - 1][6], done[last][1], done[last][4], done[last][5])

    def finish(turns, priors, some, behind):
        before = list(some)
        operands = [after(places, behind), means, gain, *priors, *[done[c][2] for c in range(max(before))]]
        edged = before.index(last) if last in before else None
        if edged is not None:
            operands.append(edge)
        for b in some:
            operands += attended[b]
        rows = sum(blocks[b][1] for b in some)
        return call(
            functools.partial(finish_kernel, heads=heads, turns=turns, before=before, edged=edged),
            jax.ShapeDtypeStruct((rows, len(turns) * LANES), BF16),
            in_specs=[scalar] + [whole] * (len(operands) - 1),
            out_specs=whole,
            flops=20 * 10**9 if tuple(some) == order[:1] else 4850 * 10**6 if len(some) > 1 else 1,
            vmem=24 << 20,
        )(*operands)

    order = (0, 1, 4, 2, 3)
    early = []
    if in_planes:
        held = sends[:1] + [exchange(sends[r], "ctx", r) for r in range(1, PLANE)]
        back = prior_in_planes(held, places, [done[last - 1][1], (attended[last - 1][1], edge)])
        priors = [exchange(back[r], "ctx", r) for r in range(1, PLANE)]
        turns = tuple(range(1, PLANE))
        mixed = finish((0,), back[:1], range(last + 1), done[last][1])
        early = [mixed] + [from_head(mixed, r) for r in range(1, n)]
    else:
        priors = prior_by_doubling(sum(done[b][2] for b in range(last + 1)), position)
        turns = tuple(range(pairs))
        mixed = attended[last][1]
    fetched = [from_head(pick(r), r) for r in range(1, n)]
    out_rows = []
    for got in fetched:
        out_rows.append(got)
        if out_parts > 1:
            out_rows.append(exchange(after(got, mixed), "ctx", 1))

    mixes = {}
    for b in order:
        mixed = finish(turns, priors, (b,), mixed)
        mixes[b] = [mixed] + [from_head(mixed, r) for r in range(1, n)]

    piece_turns = ([(True, (0,))] if early else []) + [(False, turns)]

    def pieces_of(b, r):
        return early[r : r + 1] + [mixes[b][r]]

    tail_blocks = order[-2:]
    tail_rows = sum(blocks[b][1] for b in tail_blocks)
    share = call(
        functools.partial(share_kernel, turns=piece_turns, blocks=[blocks[b] for b in tail_blocks]),
        jax.ShapeDtypeStruct((tail_rows, cols), BF16),
        in_specs=[scalar] + [whole] * (1 + 2 * len(piece_turns)),
        out_specs=whole,
        scratch_shapes=[pltpu.VMEM((tail_rows, width), BF16)],
        vmem=16 << 20,
    )(places, out_weight, *[piece for b in tail_blocks for piece in pieces_of(b, 0)])

    result = None
    for b in order:
        at, rows = blocks[b]
        shared = None
        operands = [after(places, share) if b == order[-3] else places, out_weight] + out_rows
        if b in tail_blocks:
            shared = sum(blocks[c][1] for c in tail_blocks[: tail_blocks.index(b)])
            operands.append(share)
        for r in range(0 if shared is None else 1, n):
            operands += pieces_of(b, r)
        specs = [scalar] + [whole] * (len(operands) - 1)
        aliases = {}
        if result is not None:
            aliases = {len(operands): 0}
            operands.append(result)
            specs.append(pl.BlockSpec(memory_space=pl.ANY))
        result = call(
            functools.partial(
                output_kernel, n=n, offset=at, parts=out_parts, turns=piece_turns, shared=shared
            ),
            jax.ShapeDtypeStruct((row_count, cols), BF16),
            in_specs=specs,
            out_specs=pl.BlockSpec(memory_space=pl.ANY),
            scratch_shapes=[
                pltpu.VMEM((rows, cols), BF16),
                pltpu.VMEM((n, rows, width), BF16),
                pltpu.SemaphoreType.DMA((2,)),
            ],
            input_output_aliases=aliases,
            vmem=16 << 20,
        )(*operands)
    return result


def solution(mesh):
    return jax.shard_map(
        per_device,
        mesh=mesh,
        in_specs=(P("ctx", "head"), P(None, "head"), P(None, "head"), P("head"), P("head", None)),
        out_specs=P("ctx", "head"),
        check_vma=False,
    )
```

```python
import functools

import jax
import jax.numpy as jnp
import numpy as np
from jax import lax
from jax.experimental import pallas as pl
from jax.experimental.pallas import tpu as pltpu
from jax.sharding import PartitionSpec as P

DV = 64
FQK = 16
WIN = 64
CONV = 3
LANES = 128
SHIFTS = FQK // 2 + 1
FEATS = (SHIFTS + 1) * FQK
EDGE = 16
HALO = EDGE + 2 * WIN
PLANE = 4
F32 = jnp.float32
BF16 = jnp.bfloat16


def call(body, out_shape, *, vmem, flops=1, **kwargs):
    return pl.pallas_call(
        body,
        out_shape=out_shape,
        compiler_params=pltpu.CompilerParams(vmem_limit_bytes=vmem),
        cost_estimate=pl.CostEstimate(flops=flops, bytes_accessed=1, transcendentals=0),
        **kwargs,
    )


def feature_layout(heads):
    in_group = min(heads, 4)
    lanes = in_group * FQK
    per_tile = LANES // lanes
    return in_group, lanes, -(-(SHIFTS + 1) // per_tile) * per_tile


def feature_tables(heads):
    in_group, lanes, slots = feature_layout(heads)
    groups = heads // in_group
    turn = np.zeros((LANES, groups, slots, in_group, FQK), np.float32)
    for g in range(groups):
        for s in range(SHIFTS):
            for h in range(in_group):
                for i in range(FQK if s < SHIFTS - 1 else FQK // 2):
                    turn[g * lanes + h * FQK + (i + s) % FQK, g, s, h, i] = 1.0
    weight = np.zeros((SHIFTS + 1, FQK, LANES), np.float32)
    weight[0] = 1.0 / (2.0 * FQK)
    weight[1:SHIFTS] = 2.0 / (2.0 * FQK)
    weight[SHIFTS - 1, FQK // 2] = 1.0
    weight[SHIFTS] = 1.0 / FQK**0.5
    turn = turn.reshape(LANES, -1)
    by_rows = np.concatenate([turn.T, np.eye(LANES, dtype=np.float32)], 0)
    return jnp.asarray(turn, BF16), jnp.asarray(by_rows, BF16), jnp.asarray(weight.reshape(FEATS, LANES))


def mean_table():
    block = np.kron(np.eye(LANES // DV), np.ones((DV, DV))) / DV
    return jnp.asarray(np.concatenate([block, block], 0), BF16)


def head_mean(values, table):
    high = values.astype(BF16)
    low = (values - high.astype(F32)).astype(BF16)
    return jnp.dot(jnp.concatenate([high, low], 1), table, preferred_element_type=F32)


def nt_dot(a, b):
    return lax.dot_general(a, b, (((1,), (1,)), ((), ())), preferred_element_type=F32)


def arrange_kernel(w_ref, o_ref, *, heads):
    per_head = 2 * FQK + 3 * DV
    w = w_ref[...]
    at = 0
    for begin, width in ((0, FQK), (FQK, FQK), (2 * FQK, DV), (2 * FQK + DV, DV), (2 * FQK + 2 * DV, DV)):
        parts = [w[:, h * per_head + begin : h * per_head + begin + width] for h in range(heads)]
        total = heads * width
        padded = -(-total // LANES) * LANES
        if padded > total:
            parts.append(jnp.zeros((w.shape[0], padded - total), w.dtype))
        o_ref[:, at : at + padded] = jnp.concatenate(parts, 1)
        at += padded


def project(me, xs, w_ref, begin, width, skip):
    depth = xs[0].shape[1]
    total = None
    for r, x_ref in enumerate(xs):
        src = lax.rem(me - r + len(xs), len(xs))
        from_rows = pl.ds(pl.multiple_of(src * depth, depth), depth)
        part = jnp.dot(x_ref[skip:, :], w_ref[from_rows, begin : begin + width], preferred_element_type=F32)
        total = part if total is None else total + part
    return total.astype(BF16)


def normalize(got, ref, mean_ref, scale):
    for p in range(ref.shape[1] // LANES):
        cols = slice(p * LANES, (p + 1) * LANES)
        x = got[:, cols].astype(F32)
        x = x * lax.rsqrt(head_mean(x * x, mean_ref[...]) + 1e-6)
        ref[:, cols] = x.astype(BF16) * jnp.asarray(scale, BF16)


def block_kernel(j_ref, mean_ref, conv_ref, turn_ref, weight_ref, w_ref, *refs, n, heads, extra, others, sends):
    xs, refs = refs[:n], refs[n:]
    prev_ref = None
    if not extra:
        prev_ref, refs = refs[0], refs[1:]
    other_refs, refs = refs[:others], refs[others:]
    k_ref, v_ref, s_ref, refs = *refs[:3], refs[3:]
    send_refs, ext_ref = refs[:sends], refs[-1]
    q_ref, wq_ref, wk_ref, halo_ref = (None,) * 4 if others else refs[:4]
    rows = v_ref.shape[0]
    qk_width, width = k_ref.shape[1], v_ref.shape[1]
    me = j_ref[0]

    if others:
        k_ref[...] = project(me, xs, w_ref, qk_width, qk_width, extra)
    else:
        qk = project(me, xs, w_ref, 0, 2 * qk_width, extra)
        q_ref[...] = qk[:, :qk_width]
        k_ref[...] = qk[:, qk_width:]
    raw = project(me, xs, w_ref, 2 * qk_width, width, 0)
    if extra:
        ext_ref[...] = raw.astype(F32)
    else:
        ext_ref[0:EDGE, :] = prev_ref[0:EDGE, :].astype(F32)
        ext_ref[EDGE:, :] = raw.astype(F32)
    total = jnp.zeros((rows, width), F32)
    for tap in range(CONV):
        total = total + conv_ref[tap : tap + 1, :] * ext_ref[EDGE - tap : EDGE - tap + rows, :]
    v_ref[...] = total.astype(BF16)

    in_group, lanes, slots = feature_layout(heads)
    groups = heads // in_group
    turned = nt_dot(turn_ref[...], k_ref[...])
    keys = turned[groups * slots * lanes :]
    constant = lax.broadcasted_iota(jnp.int32, (lanes, rows), 0) % FQK == FQK // 2
    low_half = lax.broadcasted_iota(jnp.int32, (SHIFTS + 1, FQK, LANES), 2) < DV
    for g in range(groups):
        own = keys[g * lanes : (g + 1) * lanes]
        phi = []
        for s in range(SHIFTS):
            at = (g * slots + s) * lanes
            phi.append(own * turned[at : at + lanes])
        phi[-1] = jnp.where(constant, 1.0, phi[-1])
        phi = jnp.concatenate([part.astype(BF16) for part in phi + [own]], 0)
        v = v_ref[:, g * in_group * DV : (g + 1) * in_group * DV]
        got = jnp.dot(phi, v, preferred_element_type=F32).reshape(SHIFTS + 1, lanes, in_group * DV)
        for p in range(in_group * DV // LANES):
            cols = slice(p * LANES, (p + 1) * LANES)
            first = got[:, 2 * p * FQK : (2 * p + 1) * FQK, cols]
            second = got[:, (2 * p + 1) * FQK : (2 * p + 2) * FQK, cols]
            state = jnp.where(low_half, first, second).reshape(FEATS, LANES)
            s_ref[g * in_group * DV // LANES + p] = state * weight_ref[...]
    for r in range(sends):
        pair = jnp.bitwise_xor(j_ref[1], r)
        total = s_ref[pair]
        for ref in other_refs:
            total = total + ref[pair]
        send_refs[r][...] = total.astype(BF16)

    if not others:
        halo_ref[0:EDGE, :] = raw[raw.shape[0] - EDGE :]
        query_part(me, xs, w_ref, mean_ref, v_ref, wq_ref, wk_ref, halo_ref, 2 * qk_width + width, extra)


def query_part(me, xs, w_ref, mean_ref, v_ref, wq_ref, wk_ref, halo_ref, begin, skip):
    rows, width = v_ref.shape
    normalize(project(me, xs, w_ref, begin, width, skip), wq_ref, mean_ref, 1.0 / DV**0.5)
    normalize(project(me, xs, w_ref, begin + width, width, skip), wk_ref, mean_ref, 1.0)
    halo_ref[EDGE : EDGE + WIN, :] = v_ref[rows - WIN : rows, :]
    halo_ref[EDGE + WIN : HALO, :] = wk_ref[rows - WIN : rows, :]


def query_kernel(j_ref, mean_ref, w_ref, v_ref, *refs, n):
    xs, (q_ref, wq_ref, wk_ref, halo_ref) = refs[:n], refs[n:]
    qk_width, width = q_ref.shape[1], v_ref.shape[1]
    q_ref[...] = project(j_ref[0], xs, w_ref, 0, qk_width, 0)
    halo_ref[0:EDGE, :] = jnp.zeros((EDGE, width), BF16)
    query_part(j_ref[0], xs, w_ref, mean_ref, v_ref, wq_ref, wk_ref, halo_ref, 2 * qk_width + width, 0)


def band_of(tile, span, first):
    col = lax.broadcasted_iota(jnp.int32, (2 * tile, span), 1)
    ahead = col - lax.broadcasted_iota(jnp.int32, (2 * tile, span), 0) % tile
    seen = (ahead >= 1) & (ahead <= WIN)
    if first is not None:
        seen = seen & (col >= first)
    return seen.astype(F32).astype(BF16)


def window_tile(wq, keys, values, band, low):
    none = jnp.zeros_like(wq)
    scores = nt_dot(jnp.concatenate([jnp.where(low, wq, none), jnp.where(low, none, wq)], 0), keys)
    expo = jnp.exp(scores).astype(BF16) * band
    ones = jnp.ones(values.shape, BF16)
    got = jnp.dot(expo, jnp.concatenate([values, ones], 1), preferred_element_type=F32)
    tile = wq.shape[0]
    got = jnp.where(jnp.concatenate([low, low], 1), got[:tile], got[tile:])
    return got[:, :LANES] / got[:, LANES:]


def edge_kernel(_, prev_ref, v_ref, wq_ref, wk_ref, win_ref):
    tile = win_ref.shape[0]
    band = band_of(tile, tile + WIN, None)
    low = lax.broadcasted_iota(jnp.int32, (tile, LANES), 1) < DV
    for p in range(win_ref.shape[1] // LANES):
        cols = slice(p * LANES, (p + 1) * LANES)
        values = jnp.concatenate([prev_ref[EDGE : EDGE + WIN, cols], v_ref[:tile, cols]], 0)
        keys = jnp.concatenate([prev_ref[EDGE + WIN : HALO, cols], wk_ref[:tile, cols]], 0)
        win_ref[:, cols] = window_tile(wq_ref[:tile, cols], keys, values, band, low)


def attend_kernel(
    a_ref, turn_ref, prev_ref, q_ref, k_ref, v_ref, wq_ref, wk_ref, phi_ref, lin_ref, win_ref,
    vext_ref, kext_ref, *, heads, first
):
    rows = q_ref.shape[0]
    tile = 128
    span = tile + WIN
    vext_ref[0:WIN, :] = prev_ref[EDGE : EDGE + WIN, :]
    vext_ref[WIN : WIN + rows, :] = v_ref[...]
    kext_ref[0:WIN, :] = prev_ref[EDGE + WIN : HALO, :]
    kext_ref[WIN : WIN + rows, :] = wk_ref[...]
    q = q_ref[...]
    k = k_ref[...]
    lane = lax.broadcasted_iota(jnp.int32, (rows, LANES), 1)
    low_half = lane < DV

    in_group, lanes, slots = feature_layout(heads)
    per_tile = LANES // lanes
    turned = jnp.dot(q, turn_ref[...], preferred_element_type=F32)
    slot = lane // lanes
    for g in range(heads // in_group):
        own = q[:, g * lanes : (g + 1) * lanes].astype(F32)
        own = jnp.concatenate([own] * per_tile, 1)
        for t in range(slots // per_tile):
            at = (g * slots // per_tile + t) * LANES
            part = own * turned[:, at : at + LANES]
            if t == (SHIFTS - 1) // per_tile:
                here = (slot == (SHIFTS - 1) % per_tile) & (lane % FQK == FQK // 2)
                part = jnp.where(here, 1.0, part)
            if t == SHIFTS // per_tile:
                part = jnp.where(slot == SHIFTS % per_tile, own, part)
            phi_ref[:, at : at + LANES] = part.astype(BF16)

    down = lax.broadcasted_iota(jnp.int32, (2 * rows, rows), 0) % rows
    causal = lax.broadcasted_iota(jnp.int32, (2 * rows, rows), 1) <= down
    band = band_of(tile, span, None)
    first_band = band
    if first:
        first_band = band_of(tile, span, jnp.where(a_ref[2] == 0, WIN, 0))
    q = q * jnp.asarray(1.0 / FQK**0.5, BF16)
    for p in range(heads * DV // LANES):
        cols = slice(p * LANES, (p + 1) * LANES)
        both = [
            jnp.where((lane >= h * FQK) & (lane < (h + 1) * FQK), q, jnp.zeros_like(q)) for h in (2 * p, 2 * p + 1)
        ]
        t = nt_dot(jnp.concatenate(both, 0), k) + 1.0
        kernel = jnp.where(causal, t * t + 1.0, 0.0).astype(BF16)
        got = jnp.dot(kernel, v_ref[:, cols], preferred_element_type=F32)
        lin_ref[:, cols] = 0.5 * jnp.where(low_half, got[:rows], got[rows:])
        for i in range(rows // tile):
            here = slice(i * tile, (i + 1) * tile)
            keys = kext_ref[i * tile : i * tile + span, cols]
            values = vext_ref[i * tile : i * tile + span, cols]
            win_ref[here, cols] = window_tile(
                wq_ref[here, cols], keys, values, first_band if i == 0 else band, low_half[:tile]
            )


def carry_table(state, p, heads):
    in_group, lanes, slots = feature_layout(heads)
    in_pairs = in_group * DV // LANES
    state = state.reshape(SHIFTS + 1, FQK, LANES)
    low_half = lax.broadcasted_iota(jnp.int32, state.shape, 2) < DV
    parts = [jnp.where(low_half, state, 0.0), jnp.where(low_half, 0.0, state)] * in_pairs
    parts = jnp.concatenate(parts, 1)
    if in_pairs > 1:
        here = lax.broadcasted_iota(jnp.int32, parts.shape, 1) // (2 * FQK) == p
        parts = jnp.where(here, parts, 0.0)
    parts = parts.reshape((SHIFTS + 1) * lanes, LANES)
    if slots > SHIFTS + 1:
        parts = jnp.concatenate([parts, jnp.zeros(((slots - SHIFTS - 1) * lanes, LANES), F32)], 0)
    return parts.astype(BF16)


def finish_kernel(a_ref, mean_ref, gain_ref, *refs, heads, turns, before, edged):
    prior_refs, refs = refs[: len(turns)], refs[len(turns) :]
    states, refs = refs[: max(before)], refs[max(before) :]
    edge_ref, refs = (refs[0], refs[1:]) if edged is not None else (None, refs)
    mix_ref = refs[-1]
    in_group, lanes, slots = feature_layout(heads)
    in_pairs = in_group * DV // LANES
    for i, r in enumerate(turns):
        pair = jnp.bitwise_xor(a_ref[1], r)
        group = lax.div(pair, in_pairs)
        own = pl.ds(pl.multiple_of(group * (slots * lanes), LANES), slots * lanes)
        cols = pl.ds(pl.multiple_of(pair * LANES, LANES), LANES)
        state = prior_refs[i][...].astype(F32)
        added, at = 0, 0
        for b, count in enumerate(before):
            phi_ref, lin_ref, win_ref = refs[3 * b : 3 * b + 3]
            for c in range(added, count):
                state = state + states[c][pair]
            added = count
            table = carry_table(state, lax.rem(pair, in_pairs), heads)
            lin = lin_ref[:, cols] + jnp.dot(phi_ref[:, own], table, preferred_element_type=F32)
            scale = lax.rsqrt(head_mean(lin * lin, mean_ref[...]) + 1e-5)
            win = win_ref[:, cols]
            if b == edged:
                win = jnp.concatenate([edge_ref[:, cols], win[edge_ref.shape[0] :]], 0)
            rows = lin.shape[0]
            mix_ref[at : at + rows, i * LANES : (i + 1) * LANES] = (
                lin * scale * gain_ref[:, cols] + win
            ).astype(BF16)
            at += rows


def place_pieces(a_ref, pieces, turns, offset, mixed_ref):
    rows = mixed_ref.shape[0]
    for ref, (begin, pairs) in zip(pieces, turns):
        here = slice(offset - begin, offset - begin + rows)
        for k, turn in enumerate(pairs):
            at = pl.multiple_of(jnp.bitwise_xor(a_ref[1], turn) * LANES, LANES)
            mixed_ref[:, pl.ds(at, LANES)] = ref[here, k * LANES : (k + 1) * LANES]


def own_columns(a_ref, cols, begin, width):
    return pl.ds(pl.multiple_of(a_ref[0] * cols + begin, LANES), width)


def share_kernel(a_ref, w_ref, *refs, turns, blocks):
    share_ref, mixed_ref = refs[-2:]
    at = 0
    for i, (offset, rows) in enumerate(blocks):
        pieces = refs[i * len(turns[i]) : (i + 1) * len(turns[i])]
        place_pieces(a_ref, pieces, turns[i], offset, mixed_ref.at[pl.ds(at, rows), :])
        at += rows
    cols = share_ref.shape[1]
    mine = own_columns(a_ref, cols, 0, cols)
    share_ref[...] = jnp.dot(mixed_ref[...], w_ref[:, mine], preferred_element_type=F32).astype(BF16)


def output_kernel(a_ref, w_ref, *refs, n, offset, parts, turns, shared):
    weights, refs = refs[: parts * (n - 1)], refs[parts * (n - 1) :]
    o_ref, held_ref, mixed_ref, sems = refs[-4:]
    rows, cols = held_ref.shape
    first = 0
    if shared is not None:
        share_ref, refs = refs[0], refs[1:]
        first = 1
    for r in range(first, n):
        pieces = refs[(r - first) * len(turns) : (r - first + 1) * len(turns)]
        place_pieces(a_ref, pieces, turns, offset, mixed_ref.at[r])
    copies = []
    count = 2 if cols % (2 * LANES) == 0 else 1
    width = cols // count
    for half in range(count):
        here = slice(half * width, (half + 1) * width)
        total = None
        if shared is not None:
            total = share_ref[shared : shared + rows, here].astype(F32)
        for r in range(first, n):
            if r == 0:
                part = jnp.dot(
                    mixed_ref[0], w_ref[:, own_columns(a_ref, cols, half * width, width)], preferred_element_type=F32
                )
            else:
                part = None
                for i in range(parts):
                    ref = weights[(r - 1) * parts + i]
                    depth = ref.shape[0]
                    at = depth * (jnp.bitwise_xor(a_ref[2] % 2, i) if parts > 1 else 0)
                    rows_of = pl.ds(pl.multiple_of(at, depth), depth)
                    got = jnp.dot(mixed_ref[r, :, rows_of], ref[:, here], preferred_element_type=F32)
                    part = got if part is None else part + got
            part = part.astype(BF16).astype(F32)
            total = part if total is None else total + part
        held_ref[:, here] = total.astype(BF16)
        copy = pltpu.make_async_copy(
            held_ref.at[:, here], o_ref.at[pl.ds(offset, rows), here], sems.at[half]
        )
        copy.start()
        copies.append(copy)
    for copy in copies:
        copy.wait()


def pick_kernel(a_ref, w_ref, o_ref):
    o_ref[...] = w_ref[...]


def exchange(value, axis, flip):
    count = lax.axis_size(axis)
    return lax.ppermute(value, axis, [(i, i ^ flip) for i in range(count)])


def plane_kernel(a_ref, *refs):
    helds, plane_ref, ahead_refs = refs[:PLANE], refs[PLANE], refs[PLANE + 1 :]
    place = a_ref[1]
    held = [ref[...].astype(F32) for ref in helds]
    plane_ref[...] = (held[0] + held[1] + held[2] + held[3]).astype(BF16)
    for r in range(PLANE):
        total = jnp.zeros_like(held[0])
        for s in range(PLANE):
            before = jnp.bitwise_xor(place, s) < jnp.bitwise_xor(place, r)
            total = total + held[s] * before.astype(F32)
        ahead_refs[r][...] = total


def earlier_kernel(a_ref, *refs, planes):
    ahead_refs, plane_refs, back_refs = refs[:PLANE], refs[PLANE : PLANE + planes], refs[PLANE + planes :]
    mine = a_ref[2] // PLANE
    earlier = jnp.zeros(ahead_refs[0].shape, F32)
    for d, ref in enumerate(plane_refs, 1):
        before = jnp.bitwise_xor(mine, d) < mine
        earlier = earlier + ref[...].astype(F32) * before.astype(F32)
    for r in range(PLANE):
        back_refs[r][...] = (ahead_refs[r][...] + earlier).astype(BF16)


def after(value, earlier):
    return lax.optimization_barrier((value, earlier))[0]


def prior_in_planes(held, places, beside):
    ctx = lax.axis_size("ctx")
    whole = pl.BlockSpec(memory_space=pltpu.VMEM)
    scalar = pl.BlockSpec(memory_space=pltpu.SMEM)
    narrow = jax.ShapeDtypeStruct((FEATS, LANES), BF16)
    wide = jax.ShapeDtypeStruct((FEATS, LANES), F32)
    plane, *ahead = call(
        plane_kernel,
        [narrow] + [wide] * PLANE,
        in_specs=[scalar] + [whole] * PLANE,
        out_specs=[whole] * (1 + PLANE),
        vmem=4 << 20,
    )(after(places, beside[0]), *held)
    earlier = []
    for d in range(1, ctx // PLANE):
        earlier.append(exchange(plane, "ctx", d * PLANE))
    return call(
        functools.partial(earlier_kernel, planes=len(earlier)),
        [narrow] * PLANE,
        in_specs=[scalar] + [whole] * (PLANE + len(earlier)),
        out_specs=[whole] * PLANE,
        vmem=4 << 20,
    )(after(places, beside[1]), *ahead, *earlier)


def prior_by_doubling(total, position):
    ctx = lax.axis_size("ctx")
    prior = jnp.zeros_like(total)
    bit = 1
    while bit < ctx:
        got = exchange(total.astype(BF16), "ctx", bit).astype(F32)
        prior = prior + jnp.where((position & bit) != 0, got, 0.0)
        total = total + got
        bit *= 2
    return [prior[p].astype(BF16) for p in range(total.shape[0])]


def per_device(hidden_in, proj_weight, conv_weight, norm_gain, out_weight):
    n = lax.axis_size("head")
    ctx = lax.axis_size("ctx")
    me = lax.axis_index("head").astype(jnp.int32)
    position = lax.axis_index("ctx").astype(jnp.int32)
    row_count = hidden_in.shape[0]
    model = proj_weight.shape[0]
    heads = out_weight.shape[0] // DV
    width = heads * DV
    pairs = width // LANES
    in_planes = pairs == PLANE and ctx % PLANE == 0 and ctx & (ctx - 1) == 0
    places = jnp.stack([me, position % PLANE if in_planes else jnp.zeros_like(position), position])
    hidden_in, places = lax.optimization_barrier((hidden_in, places))
    step = row_count // 8
    blocks = [(0, 2 * step), (2 * step, 2 * step), (4 * step, step), (5 * step, step), (6 * step, 2 * step)]
    last = len(blocks) - 1
    turn, turn_rows, weight = feature_tables(heads)
    means = mean_table()
    gain = norm_gain.reshape(1, width)
    whole = pl.BlockSpec(memory_space=pltpu.VMEM)
    scalar = pl.BlockSpec(memory_space=pltpu.SMEM)

    def from_head(value, by):
        return lax.ppermute(value, "head", [(i, (i + by) % n) for i in range(n)])

    pieces = {}

    def send_block(b, behind=None):
        at, rows = blocks[b]
        extra = EDGE if b == last else 0
        own = hidden_in[at - extra : at + rows]
        if behind is not None:
            own = after(own, behind)
        pieces[b] = [own] + [from_head(own, r) for r in range(1, n)]

    send_block(last)
    send_block(0, pieces[last][0])
    for b in range(1, last):
        send_block(b, pieces[last][0])

    cols = out_weight.shape[1] // n
    out_parts = 2 if width // 2 % LANES == 0 and ctx % 2 == 0 else 1
    share = width // out_parts
    def pick(r):
        column = functools.partial(lambda i, a, r: (a[2] % out_parts, (a[0] + r) % n), r=r)
        return call(
            pick_kernel,
            jax.ShapeDtypeStruct((share, cols), BF16),
            grid_spec=pltpu.PrefetchScalarGridSpec(
                num_scalar_prefetch=1,
                grid=(1,),
                in_specs=[pl.BlockSpec((share, cols), column)],
                out_specs=pl.BlockSpec((share, cols), lambda i, a: (0, 0)),
            ),
            vmem=8 << 20,
        )(places, out_weight)

    qk_width = -(-heads * FQK // LANES) * LANES
    arranged_width = 2 * qk_width + 3 * width
    slab = 256
    arranged = call(
        functools.partial(arrange_kernel, heads=heads),
        jax.ShapeDtypeStruct((model, arranged_width), BF16),
        grid=(model // slab,),
        in_specs=[pl.BlockSpec((slab, proj_weight.shape[1]), lambda i: (i, 0))],
        out_specs=pl.BlockSpec((slab, arranged_width), lambda i: (i, 0)),
        vmem=32 << 20,
    )(proj_weight)

    def bf16(rows, *widths):
        return [jax.ShapeDtypeStruct((rows, w), BF16) for w in widths]

    def do_block(b, prev, behind, others=()):
        rows = blocks[b][1]
        extra = EDGE if prev is None else 0
        sends = PLANE if in_planes and others else 0
        tokens = places if behind is None else after(places, behind)
        shapes = bf16(rows, qk_width, width) + [jax.ShapeDtypeStruct((pairs, FEATS, LANES), F32)]
        if others:
            shapes += bf16(FEATS, LANES) * sends
        else:
            shapes += bf16(rows, qk_width, width, width) + bf16(HALO, width)
        operands = [tokens, means, conv_weight, turn_rows, weight, arranged, *pieces[b]]
        if prev is not None:
            operands.append(prev)
        operands += others
        return call(
            functools.partial(
                block_kernel, n=n, heads=heads, extra=extra, others=len(others), sends=sends
            ),
            shapes,
            in_specs=[scalar] + [whole] * (len(operands) - 1),
            out_specs=[whole] * len(shapes),
            scratch_shapes=[pltpu.VMEM((EDGE + rows, width), F32)],
            vmem=32 << 20,
        )(*operands)

    def do_queries(b, v):
        rows = blocks[b][1]
        return call(
            functools.partial(query_kernel, n=n),
            bf16(rows, qk_width, width, width) + bf16(HALO, width),
            in_specs=[scalar] + [whole] * (3 + n),
            out_specs=[whole] * 4,
            vmem=32 << 20,
        )(places, means, arranged, v, *pieces[b])

    def attend(b, prev):
        rows = blocks[b][1]
        k, v, _, q, wq, wk, _ = done[b]
        return call(
            functools.partial(attend_kernel, heads=heads, first=b == 0),
            [jax.ShapeDtypeStruct((rows, turn.shape[1]), BF16)] + [jax.ShapeDtypeStruct((rows, width), F32)] * 2,
            in_specs=[scalar] + [whole] * 7,
            out_specs=[whole] * 3,
            scratch_shapes=[pltpu.VMEM((WIN + rows, width), BF16)] * 2,
            vmem=16 << 20,
        )(places, turn, prev, q, k, v, wq, wk)

    done, attended = {}, {}
    picked = [pick(r) for r in range(1, n)]
    done[last] = do_block(last, None, None)
    halo = lax.ppermute(done[last][6], "ctx", [(i, i + 1) for i in range(ctx - 1)])
    prevs = {0: halo}
    for b in range(last - 1):
        behind = [a[1] for a in attended.values()] + (picked if b == 1 else [])
        done[b] = do_block(b, prevs[b], behind if b else None)
        prevs[b + 1] = done[b][6]
        attended[b] = attend(b, prevs[b])
        if b == 0:
            attended[last] = attend(last, halo)
    b = last - 1
    k, v, state, *sends = do_block(b, prevs[b], attended[b - 1][1], [done[c][2] for c in (last, *range(b))])
    done[b] = (k, v, state, *do_queries(b, v))
    prevs[last] = done[b][6]
    attended[last - 1] = attend(last - 1, prevs[last - 1])
    tile = 128
    edge = call(
        edge_kernel,
        jax.ShapeDtypeStruct((tile, width), F32),
        in_specs=[scalar] + [whole] * 4,
        out_specs=whole,
        vmem=16 << 20,
    )(places, done[last - 1][6], done[last][1], done[last][4], done[last][5])

    def finish(turns, priors, some, behind):
        before = list(some)
        operands = [after(places, behind), means, gain, *priors, *[done[c][2] for c in range(max(before))]]
        edged = before.index(last) if last in before else None
        if edged is not None:
            operands.append(edge)
        for b in some:
            operands += attended[b]
        rows = sum(blocks[b][1] for b in some)
        return call(
            functools.partial(finish_kernel, heads=heads, turns=turns, before=before, edged=edged),
            jax.ShapeDtypeStruct((rows, len(turns) * LANES), BF16),
            in_specs=[scalar] + [whole] * (len(operands) - 1),
            out_specs=whole,
            flops=20 * 10**9 if tuple(some) == order[:1] else 4850 * 10**6 if len(some) > 1 else 1,
            vmem=24 << 20,
        )(*operands)

    order = (0, 1, 4, 2, 3)
    early = []
    if in_planes:
        held = sends[:1] + [exchange(sends[r], "ctx", r) for r in range(1, PLANE)]
        back = prior_in_planes(held, places, [done[last - 1][6], (attended[last - 1][1], edge)])
        priors = [exchange(back[r], "ctx", r) for r in range(1, PLANE)]
        turns = tuple(range(1, PLANE))
        mixed = finish((0,), back[:1], range(last + 1), done[last][1])
        early = [mixed] + [from_head(mixed, r) for r in range(1, n)]
    else:
        priors = prior_by_doubling(sum(done[b][2] for b in range(last + 1)), position)
        turns = tuple(range(pairs))
        mixed = attended[last][1]
    fetched = [from_head(after(block, done[last - 1][1]), r) for r, block in enumerate(picked, 1)]
    out_rows = []
    for got in fetched:
        out_rows.append(got)
        if out_parts > 1:
            out_rows.append(exchange(after(got, mixed), "ctx", 1))

    mixes = {}
    for b in order:
        mixed = finish(turns, priors, (b,), mixed)
        mixes[b] = [mixed] + [from_head(mixed, r) for r in range(1, n)]

    def pieces_of(b, r):
        return early[r : r + 1] + [mixes[b][r]]

    def turns_of(b):
        return ([(0, (0,))] if early else []) + [(blocks[b][0], turns)]

    tail_blocks = order[-2:]
    tail_rows = sum(blocks[b][1] for b in tail_blocks)
    share = call(
        functools.partial(
            share_kernel, turns=[turns_of(b) for b in tail_blocks], blocks=[blocks[b] for b in tail_blocks]
        ),
        jax.ShapeDtypeStruct((tail_rows, cols), BF16),
        in_specs=[scalar] + [whole] * (1 + 2 * len(turns_of(last))),
        out_specs=whole,
        scratch_shapes=[pltpu.VMEM((tail_rows, width), BF16)],
        vmem=16 << 20,
    )(places, out_weight, *[piece for b in tail_blocks for piece in pieces_of(b, 0)])

    result = None
    for b in order:
        at, rows = blocks[b]
        shared = None
        operands = [after(places, share) if b == order[-3] else places, out_weight] + out_rows
        if b in tail_blocks:
            shared = sum(blocks[c][1] for c in tail_blocks[: tail_blocks.index(b)])
            operands.append(share)
        for r in range(0 if shared is None else 1, n):
            operands += pieces_of(b, r)
        specs = [scalar] + [whole] * (len(operands) - 1)
        aliases = {}
        if result is not None:
            aliases = {len(operands): 0}
            operands.append(result)
            specs.append(pl.BlockSpec(memory_space=pl.ANY))
        result = call(
            functools.partial(
                output_kernel, n=n, offset=at, parts=out_parts, turns=turns_of(b), shared=shared
            ),
            jax.ShapeDtypeStruct((row_count, cols), BF16),
            in_specs=specs,
            out_specs=pl.BlockSpec(memory_space=pl.ANY),
            scratch_shapes=[
                pltpu.VMEM((rows, cols), BF16),
                pltpu.VMEM((n, rows, width), BF16),
                pltpu.SemaphoreType.DMA((2,)),
            ],
            input_output_aliases=aliases,
            vmem=16 << 20,
        )(*operands)
    return result


def solution(mesh):
    return jax.shard_map(
        per_device,
        mesh=mesh,
        in_specs=(P("ctx", "head"), P(None, "head"), P(None, "head"), P("head"), P("head", None)),
        out_specs=P("ctx", "head"),
        check_vma=False,
    )
```

```python
import functools

import jax
import jax.numpy as jnp
import numpy as np
from jax import lax
from jax.experimental import pallas as pl
from jax.experimental.pallas import tpu as pltpu
from jax.sharding import PartitionSpec as P

DV = 64
FQK = 16
WIN = 64
CONV = 3
LANES = 128
SHIFTS = FQK // 2 + 1
FEATS = (SHIFTS + 1) * FQK
EDGE = 16
HALO = EDGE + 2 * WIN
PLANE = 4
F32 = jnp.float32
BF16 = jnp.bfloat16


def call(body, out_shape, *, vmem, flops=1, **kwargs):
    return pl.pallas_call(
        body,
        out_shape=out_shape,
        compiler_params=pltpu.CompilerParams(vmem_limit_bytes=vmem),
        cost_estimate=pl.CostEstimate(flops=flops, bytes_accessed=1, transcendentals=0),
        **kwargs,
    )


def feature_layout(heads):
    in_group = min(heads, 4)
    lanes = in_group * FQK
    per_tile = LANES // lanes
    return in_group, lanes, -(-(SHIFTS + 1) // per_tile) * per_tile


def feature_tables(heads):
    in_group, lanes, slots = feature_layout(heads)
    groups = heads // in_group
    turn = np.zeros((LANES, groups, slots, in_group, FQK), np.float32)
    for g in range(groups):
        for s in range(SHIFTS):
            for h in range(in_group):
                for i in range(FQK if s < SHIFTS - 1 else FQK // 2):
                    turn[g * lanes + h * FQK + (i + s) % FQK, g, s, h, i] = 1.0
    weight = np.zeros((SHIFTS + 1, FQK, LANES), np.float32)
    weight[0] = 1.0 / (2.0 * FQK)
    weight[1:SHIFTS] = 2.0 / (2.0 * FQK)
    weight[SHIFTS - 1, FQK // 2] = 1.0
    weight[SHIFTS] = 1.0 / FQK**0.5
    turn = turn.reshape(LANES, -1)
    by_rows = np.concatenate([turn.T, np.eye(LANES, dtype=np.float32)], 0)
    return jnp.asarray(turn, BF16), jnp.asarray(by_rows, BF16), jnp.asarray(weight.reshape(FEATS, LANES))


def mean_table():
    block = np.kron(np.eye(LANES // DV), np.ones((DV, DV))) / DV
    return jnp.asarray(np.concatenate([block, block], 0), BF16)


def head_mean(values, table):
    high = values.astype(BF16)
    low = (values - high.astype(F32)).astype(BF16)
    return jnp.dot(jnp.concatenate([high, low], 1), table, preferred_element_type=F32)


def nt_dot(a, b):
    return lax.dot_general(a, b, (((1,), (1,)), ((), ())), preferred_element_type=F32)


def arrange_kernel(w_ref, o_ref, *, heads):
    per_head = 2 * FQK + 3 * DV
    w = w_ref[...]
    at = 0
    for begin, width in ((0, FQK), (FQK, FQK), (2 * FQK, DV), (2 * FQK + DV, DV), (2 * FQK + 2 * DV, DV)):
        parts = [w[:, h * per_head + begin : h * per_head + begin + width] for h in range(heads)]
        total = heads * width
        padded = -(-total // LANES) * LANES
        if padded > total:
            parts.append(jnp.zeros((w.shape[0], padded - total), w.dtype))
        o_ref[:, at : at + padded] = jnp.concatenate(parts, 1)
        at += padded


def project(me, xs, w_ref, begin, width, skip):
    depth = xs[0].shape[1]
    total = None
    for r, x_ref in enumerate(xs):
        src = lax.rem(me - r + len(xs), len(xs))
        from_rows = pl.ds(pl.multiple_of(src * depth, depth), depth)
        part = jnp.dot(x_ref[skip:, :], w_ref[from_rows, begin : begin + width], preferred_element_type=F32)
        total = part if total is None else total + part
    return total.astype(BF16)


def normalize(got, ref, mean_ref, scale):
    for p in range(ref.shape[1] // LANES):
        cols = slice(p * LANES, (p + 1) * LANES)
        x = got[:, cols].astype(F32)
        x = x * lax.rsqrt(head_mean(x * x, mean_ref[...]) + 1e-6)
        ref[:, cols] = x.astype(BF16) * jnp.asarray(scale, BF16)


def block_kernel(j_ref, mean_ref, conv_ref, turn_ref, weight_ref, w_ref, *refs, n, heads, extra, others, sends):
    xs, refs = refs[:n], refs[n:]
    prev_ref = None
    if not extra:
        prev_ref, refs = refs[0], refs[1:]
    other_refs, refs = refs[:others], refs[others:]
    k_ref, v_ref, s_ref, refs = *refs[:3], refs[3:]
    send_refs, ext_ref = refs[:sends], refs[-1]
    q_ref, wq_ref, wk_ref, halo_ref = (None,) * 4 if others else refs[:4]
    rows = v_ref.shape[0]
    qk_width, width = k_ref.shape[1], v_ref.shape[1]
    me = j_ref[0]

    if others:
        k_ref[...] = project(me, xs, w_ref, qk_width, qk_width, extra)
    else:
        qk = project(me, xs, w_ref, 0, 2 * qk_width, extra)
        q_ref[...] = qk[:, :qk_width]
        k_ref[...] = qk[:, qk_width:]
    raw = project(me, xs, w_ref, 2 * qk_width, width, 0)
    if extra:
        ext_ref[...] = raw.astype(F32)
    else:
        ext_ref[0:EDGE, :] = prev_ref[0:EDGE, :].astype(F32)
        ext_ref[EDGE:, :] = raw.astype(F32)
    total = jnp.zeros((rows, width), F32)
    for tap in range(CONV):
        total = total + conv_ref[tap : tap + 1, :] * ext_ref[EDGE - tap : EDGE - tap + rows, :]
    v_ref[...] = total.astype(BF16)

    in_group, lanes, slots = feature_layout(heads)
    groups = heads // in_group
    turned = nt_dot(turn_ref[...], k_ref[...])
    keys = turned[groups * slots * lanes :]
    constant = lax.broadcasted_iota(jnp.int32, (lanes, rows), 0) % FQK == FQK // 2
    low_half = lax.broadcasted_iota(jnp.int32, (SHIFTS + 1, FQK, LANES), 2) < DV
    for g in range(groups):
        own = keys[g * lanes : (g + 1) * lanes]
        phi = []
        for s in range(SHIFTS):
            at = (g * slots + s) * lanes
            phi.append(own * turned[at : at + lanes])
        phi[-1] = jnp.where(constant, 1.0, phi[-1])
        phi = jnp.concatenate([part.astype(BF16) for part in phi + [own]], 0)
        v = v_ref[:, g * in_group * DV : (g + 1) * in_group * DV]
        got = jnp.dot(phi, v, preferred_element_type=F32).reshape(SHIFTS + 1, lanes, in_group * DV)
        for p in range(in_group * DV // LANES):
            cols = slice(p * LANES, (p + 1) * LANES)
            first = got[:, 2 * p * FQK : (2 * p + 1) * FQK, cols]
            second = got[:, (2 * p + 1) * FQK : (2 * p + 2) * FQK, cols]
            state = jnp.where(low_half, first, second).reshape(FEATS, LANES)
            s_ref[g * in_group * DV // LANES + p] = state * weight_ref[...]
    for r in range(sends):
        pair = jnp.bitwise_xor(j_ref[1], r)
        total = s_ref[pair]
        for ref in other_refs:
            total = total + ref[pair]
        send_refs[r][...] = total.astype(BF16)

    if not others:
        halo_ref[0:EDGE, :] = raw[raw.shape[0] - EDGE :]
        query_part(me, xs, w_ref, mean_ref, v_ref, wq_ref, wk_ref, halo_ref, 2 * qk_width + width, extra)


def query_part(me, xs, w_ref, mean_ref, v_ref, wq_ref, wk_ref, halo_ref, begin, skip):
    rows, width = v_ref.shape
    normalize(project(me, xs, w_ref, begin, width, skip), wq_ref, mean_ref, 1.0 / DV**0.5)
    normalize(project(me, xs, w_ref, begin + width, width, skip), wk_ref, mean_ref, 1.0)
    halo_ref[EDGE : EDGE + WIN, :] = v_ref[rows - WIN : rows, :]
    halo_ref[EDGE + WIN : HALO, :] = wk_ref[rows - WIN : rows, :]


def query_kernel(j_ref, mean_ref, w_ref, v_ref, *refs, n):
    xs, (q_ref, wq_ref, wk_ref, halo_ref) = refs[:n], refs[n:]
    qk_width, width = q_ref.shape[1], v_ref.shape[1]
    q_ref[...] = project(j_ref[0], xs, w_ref, 0, qk_width, 0)
    halo_ref[0:EDGE, :] = jnp.zeros((EDGE, width), BF16)
    query_part(j_ref[0], xs, w_ref, mean_ref, v_ref, wq_ref, wk_ref, halo_ref, 2 * qk_width + width, 0)


def band_of(tile, span, first):
    col = lax.broadcasted_iota(jnp.int32, (2 * tile, span), 1)
    ahead = col - lax.broadcasted_iota(jnp.int32, (2 * tile, span), 0) % tile
    seen = (ahead >= 1) & (ahead <= WIN)
    if first is not None:
        seen = seen & (col >= first)
    return seen.astype(F32).astype(BF16)


def window_tile(wq, keys, values, band, low):
    none = jnp.zeros_like(wq)
    scores = nt_dot(jnp.concatenate([jnp.where(low, wq, none), jnp.where(low, none, wq)], 0), keys)
    expo = jnp.exp(scores).astype(BF16) * band
    ones = jnp.ones(values.shape, BF16)
    got = jnp.dot(expo, jnp.concatenate([values, ones], 1), preferred_element_type=F32)
    tile = wq.shape[0]
    got = jnp.where(jnp.concatenate([low, low], 1), got[:tile], got[tile:])
    return got[:, :LANES] / got[:, LANES:]


def edge_kernel(_, prev_ref, v_ref, wq_ref, wk_ref, win_ref):
    tile = win_ref.shape[0]
    band = band_of(tile, tile + WIN, None)
    low = lax.broadcasted_iota(jnp.int32, (tile, LANES), 1) < DV
    for p in range(win_ref.shape[1] // LANES):
        cols = slice(p * LANES, (p + 1) * LANES)
        values = jnp.concatenate([prev_ref[EDGE : EDGE + WIN, cols], v_ref[:tile, cols]], 0)
        keys = jnp.concatenate([prev_ref[EDGE + WIN : HALO, cols], wk_ref[:tile, cols]], 0)
        win_ref[:, cols] = window_tile(wq_ref[:tile, cols], keys, values, band, low)


def attend_kernel(
    a_ref, turn_ref, prev_ref, q_ref, k_ref, v_ref, wq_ref, wk_ref, phi_ref, lin_ref, win_ref,
    vext_ref, kext_ref, *, heads, first
):
    rows = q_ref.shape[0]
    tile = 128
    span = tile + WIN
    vext_ref[0:WIN, :] = prev_ref[EDGE : EDGE + WIN, :]
    vext_ref[WIN : WIN + rows, :] = v_ref[...]
    kext_ref[0:WIN, :] = prev_ref[EDGE + WIN : HALO, :]
    kext_ref[WIN : WIN + rows, :] = wk_ref[...]
    q = q_ref[...]
    k = k_ref[...]
    lane = lax.broadcasted_iota(jnp.int32, (rows, LANES), 1)
    low_half = lane < DV

    in_group, lanes, slots = feature_layout(heads)
    per_tile = LANES // lanes
    turned = jnp.dot(q, turn_ref[...], preferred_element_type=F32)
    slot = lane // lanes
    for g in range(heads // in_group):
        own = q[:, g * lanes : (g + 1) * lanes].astype(F32)
        own = jnp.concatenate([own] * per_tile, 1)
        for t in range(slots // per_tile):
            at = (g * slots // per_tile + t) * LANES
            part = own * turned[:, at : at + LANES]
            if t == (SHIFTS - 1) // per_tile:
                here = (slot == (SHIFTS - 1) % per_tile) & (lane % FQK == FQK // 2)
                part = jnp.where(here, 1.0, part)
            if t == SHIFTS // per_tile:
                part = jnp.where(slot == SHIFTS % per_tile, own, part)
            phi_ref[:, at : at + LANES] = part.astype(BF16)

    down = lax.broadcasted_iota(jnp.int32, (2 * rows, rows), 0) % rows
    causal = lax.broadcasted_iota(jnp.int32, (2 * rows, rows), 1) <= down
    band = band_of(tile, span, None)
    first_band = band
    if first:
        first_band = band_of(tile, span, jnp.where(a_ref[2] == 0, WIN, 0))
    q = q * jnp.asarray(1.0 / FQK**0.5, BF16)
    for p in range(heads * DV // LANES):
        cols = slice(p * LANES, (p + 1) * LANES)
        both = [
            jnp.where((lane >= h * FQK) & (lane < (h + 1) * FQK), q, jnp.zeros_like(q)) for h in (2 * p, 2 * p + 1)
        ]
        t = nt_dot(jnp.concatenate(both, 0), k) + 1.0
        kernel = jnp.where(causal, t * t + 1.0, 0.0).astype(BF16)
        got = jnp.dot(kernel, v_ref[:, cols], preferred_element_type=F32)
        lin_ref[:, cols] = 0.5 * jnp.where(low_half, got[:rows], got[rows:])
        for i in range(rows // tile):
            here = slice(i * tile, (i + 1) * tile)
            keys = kext_ref[i * tile : i * tile + span, cols]
            values = vext_ref[i * tile : i * tile + span, cols]
            win_ref[here, cols] = window_tile(
                wq_ref[here, cols], keys, values, first_band if i == 0 else band, low_half[:tile]
            )


def carry_table(state, p, heads):
    in_group, lanes, slots = feature_layout(heads)
    in_pairs = in_group * DV // LANES
    state = state.reshape(SHIFTS + 1, FQK, LANES)
    low_half = lax.broadcasted_iota(jnp.int32, state.shape, 2) < DV
    parts = [jnp.where(low_half, state, 0.0), jnp.where(low_half, 0.0, state)] * in_pairs
    parts = jnp.concatenate(parts, 1)
    if in_pairs > 1:
        here = lax.broadcasted_iota(jnp.int32, parts.shape, 1) // (2 * FQK) == p
        parts = jnp.where(here, parts, 0.0)
    parts = parts.reshape((SHIFTS + 1) * lanes, LANES)
    if slots > SHIFTS + 1:
        parts = jnp.concatenate([parts, jnp.zeros(((slots - SHIFTS - 1) * lanes, LANES), F32)], 0)
    return parts.astype(BF16)


def finish_kernel(a_ref, mean_ref, gain_ref, *refs, heads, turns, before, edged):
    prior_refs, refs = refs[: len(turns)], refs[len(turns) :]
    states, refs = refs[: max(before)], refs[max(before) :]
    edge_ref, refs = (refs[0], refs[1:]) if edged is not None else (None, refs)
    mix_ref = refs[-1]
    in_group, lanes, slots = feature_layout(heads)
    in_pairs = in_group * DV // LANES
    for i, r in enumerate(turns):
        pair = jnp.bitwise_xor(a_ref[1], r)
        group = lax.div(pair, in_pairs)
        own = pl.ds(pl.multiple_of(group * (slots * lanes), LANES), slots * lanes)
        cols = pl.ds(pl.multiple_of(pair * LANES, LANES), LANES)
        state = prior_refs[i][...].astype(F32)
        added, at = 0, 0
        for b, count in enumerate(before):
            phi_ref, lin_ref, win_ref = refs[3 * b : 3 * b + 3]
            for c in range(added, count):
                state = state + states[c][pair]
            added = count
            table = carry_table(state, lax.rem(pair, in_pairs), heads)
            lin = lin_ref[:, cols] + jnp.dot(phi_ref[:, own], table, preferred_element_type=F32)
            scale = lax.rsqrt(head_mean(lin * lin, mean_ref[...]) + 1e-5)
            win = win_ref[:, cols]
            if b == edged:
                win = jnp.concatenate([edge_ref[:, cols], win[edge_ref.shape[0] :]], 0)
            rows = lin.shape[0]
            mix_ref[at : at + rows, i * LANES : (i + 1) * LANES] = (
                lin * scale * gain_ref[:, cols] + win
            ).astype(BF16)
            at += rows


def place_pieces(a_ref, pieces, turns, offset, mixed_ref):
    rows = mixed_ref.shape[0]
    for ref, (begin, pairs) in zip(pieces, turns):
        here = slice(offset - begin, offset - begin + rows)
        for k, turn in enumerate(pairs):
            at = pl.multiple_of(jnp.bitwise_xor(a_ref[1], turn) * LANES, LANES)
            mixed_ref[:, pl.ds(at, LANES)] = ref[here, k * LANES : (k + 1) * LANES]


def own_columns(a_ref, cols, begin, width):
    return pl.ds(pl.multiple_of(a_ref[0] * cols + begin, LANES), width)


def share_kernel(a_ref, w_ref, *refs, turns, blocks):
    share_ref, mixed_ref = refs[-2:]
    at = 0
    for i, (offset, rows) in enumerate(blocks):
        pieces = refs[i * len(turns[i]) : (i + 1) * len(turns[i])]
        place_pieces(a_ref, pieces, turns[i], offset, mixed_ref.at[pl.ds(at, rows), :])
        at += rows
    cols = share_ref.shape[1]
    mine = own_columns(a_ref, cols, 0, cols)
    share_ref[...] = jnp.dot(mixed_ref[...], w_ref[:, mine], preferred_element_type=F32).astype(BF16)


def output_kernel(a_ref, w_ref, *refs, n, offset, parts, turns, shared):
    weights, refs = refs[: parts * (n - 1)], refs[parts * (n - 1) :]
    o_ref, held_ref, mixed_ref, sems = refs[-4:]
    rows, cols = held_ref.shape
    first = 0
    if shared is not None:
        share_ref, refs = refs[0], refs[1:]
        first = 1
    for r in range(first, n):
        pieces = refs[(r - first) * len(turns) : (r - first + 1) * len(turns)]
        place_pieces(a_ref, pieces, turns, offset, mixed_ref.at[r])
    copies = []
    count = 2 if cols % (2 * LANES) == 0 else 1
    width = cols // count
    for half in range(count):
        here = slice(half * width, (half + 1) * width)
        total = None
        if shared is not None:
            total = share_ref[shared : shared + rows, here].astype(F32)
        for r in range(first, n):
            if r == 0:
                part = jnp.dot(
                    mixed_ref[0], w_ref[:, own_columns(a_ref, cols, half * width, width)], preferred_element_type=F32
                )
            else:
                part = None
                for i in range(parts):
                    ref = weights[(r - 1) * parts + i]
                    depth = ref.shape[0]
                    at = depth * (jnp.bitwise_xor(a_ref[2] % 2, i) if parts > 1 else 0)
                    rows_of = pl.ds(pl.multiple_of(at, depth), depth)
                    got = jnp.dot(mixed_ref[r, :, rows_of], ref[:, here], preferred_element_type=F32)
                    part = got if part is None else part + got
            part = part.astype(BF16).astype(F32)
            total = part if total is None else total + part
        held_ref[:, here] = total.astype(BF16)
        copy = pltpu.make_async_copy(
            held_ref.at[:, here], o_ref.at[pl.ds(offset, rows), here], sems.at[half]
        )
        copy.start()
        copies.append(copy)
    for copy in copies:
        copy.wait()


def pick_kernel(a_ref, w_ref, o_ref):
    o_ref[...] = w_ref[...]


def exchange(value, axis, flip):
    count = lax.axis_size(axis)
    return lax.ppermute(value, axis, [(i, i ^ flip) for i in range(count)])


def plane_kernel(a_ref, *refs):
    helds, plane_ref, ahead_refs = refs[:PLANE], refs[PLANE], refs[PLANE + 1 :]
    place = a_ref[1]
    held = [ref[...].astype(F32) for ref in helds]
    plane_ref[...] = (held[0] + held[1] + held[2] + held[3]).astype(BF16)
    for r in range(PLANE):
        total = jnp.zeros_like(held[0])
        for s in range(PLANE):
            before = jnp.bitwise_xor(place, s) < jnp.bitwise_xor(place, r)
            total = total + held[s] * before.astype(F32)
        ahead_refs[r][...] = total


def earlier_kernel(a_ref, *refs, planes):
    ahead_refs, plane_refs, back_refs = refs[:PLANE], refs[PLANE : PLANE + planes], refs[PLANE + planes :]
    mine = a_ref[2] // PLANE
    earlier = jnp.zeros(ahead_refs[0].shape, F32)
    for d, ref in enumerate(plane_refs, 1):
        before = jnp.bitwise_xor(mine, d) < mine
        earlier = earlier + ref[...].astype(F32) * before.astype(F32)
    for r in range(PLANE):
        back_refs[r][...] = (ahead_refs[r][...] + earlier).astype(BF16)


def after(value, earlier):
    return lax.optimization_barrier((value, earlier))[0]


def prior_in_planes(held, places, beside):
    ctx = lax.axis_size("ctx")
    whole = pl.BlockSpec(memory_space=pltpu.VMEM)
    scalar = pl.BlockSpec(memory_space=pltpu.SMEM)
    narrow = jax.ShapeDtypeStruct((FEATS, LANES), BF16)
    wide = jax.ShapeDtypeStruct((FEATS, LANES), F32)
    plane, *ahead = call(
        plane_kernel,
        [narrow] + [wide] * PLANE,
        in_specs=[scalar] + [whole] * PLANE,
        out_specs=[whole] * (1 + PLANE),
        vmem=4 << 20,
    )(after(places, beside[0]), *held)
    earlier = []
    for d in range(1, ctx // PLANE):
        earlier.append(exchange(plane, "ctx", d * PLANE))
    return call(
        functools.partial(earlier_kernel, planes=len(earlier)),
        [narrow] * PLANE,
        in_specs=[scalar] + [whole] * (PLANE + len(earlier)),
        out_specs=[whole] * PLANE,
        vmem=4 << 20,
    )(after(places, beside[1]), *ahead, *earlier)


def prior_by_doubling(total, position):
    ctx = lax.axis_size("ctx")
    prior = jnp.zeros_like(total)
    bit = 1
    while bit < ctx:
        got = exchange(total.astype(BF16), "ctx", bit).astype(F32)
        prior = prior + jnp.where((position & bit) != 0, got, 0.0)
        total = total + got
        bit *= 2
    return [prior[p].astype(BF16) for p in range(total.shape[0])]


def per_device(hidden_in, proj_weight, conv_weight, norm_gain, out_weight):
    n = lax.axis_size("head")
    ctx = lax.axis_size("ctx")
    me = lax.axis_index("head").astype(jnp.int32)
    position = lax.axis_index("ctx").astype(jnp.int32)
    row_count = hidden_in.shape[0]
    model = proj_weight.shape[0]
    heads = out_weight.shape[0] // DV
    width = heads * DV
    pairs = width // LANES
    in_planes = pairs == PLANE and ctx % PLANE == 0 and ctx & (ctx - 1) == 0
    places = jnp.stack([me, position % PLANE if in_planes else jnp.zeros_like(position), position])
    hidden_in, places = lax.optimization_barrier((hidden_in, places))
    step = row_count // 8
    blocks = [(0, 2 * step), (2 * step, 2 * step), (4 * step, step), (5 * step, step), (6 * step, 2 * step)]
    last = len(blocks) - 1
    turn, turn_rows, weight = feature_tables(heads)
    means = mean_table()
    gain = norm_gain.reshape(1, width)
    whole = pl.BlockSpec(memory_space=pltpu.VMEM)
    scalar = pl.BlockSpec(memory_space=pltpu.SMEM)

    def from_head(value, by):
        return lax.ppermute(value, "head", [(i, (i + by) % n) for i in range(n)])

    pieces = {}

    def send_block(b, behind=None):
        at, rows = blocks[b]
        extra = EDGE if b == last else 0
        own = hidden_in[at - extra : at + rows]
        if behind is not None:
            own = after(own, behind)
        pieces[b] = [own] + [from_head(own, r) for r in range(1, n)]

    send_block(last)
    send_block(0, pieces[last][0])
    for b in range(1, last):
        send_block(b, pieces[last][0])

    cols = out_weight.shape[1] // n
    out_parts = 2 if width // 2 % LANES == 0 and ctx % 2 == 0 else 1
    share = width // out_parts
    def pick(r):
        column = functools.partial(lambda i, a, r: (a[2] % out_parts, (a[0] + r) % n), r=r)
        return call(
            pick_kernel,
            jax.ShapeDtypeStruct((share, cols), BF16),
            grid_spec=pltpu.PrefetchScalarGridSpec(
                num_scalar_prefetch=1,
                grid=(1,),
                in_specs=[pl.BlockSpec((share, cols), column)],
                out_specs=pl.BlockSpec((share, cols), lambda i, a: (0, 0)),
            ),
            vmem=8 << 20,
        )(places, out_weight)

    qk_width = -(-heads * FQK // LANES) * LANES
    arranged_width = 2 * qk_width + 3 * width
    slab = 256
    arranged = call(
        functools.partial(arrange_kernel, heads=heads),
        jax.ShapeDtypeStruct((model, arranged_width), BF16),
        grid=(model // slab,),
        in_specs=[pl.BlockSpec((slab, proj_weight.shape[1]), lambda i: (i, 0))],
        out_specs=pl.BlockSpec((slab, arranged_width), lambda i: (i, 0)),
        vmem=32 << 20,
    )(proj_weight)

    def bf16(rows, *widths):
        return [jax.ShapeDtypeStruct((rows, w), BF16) for w in widths]

    def do_block(b, prev, behind, others=()):
        rows = blocks[b][1]
        extra = EDGE if prev is None else 0
        sends = PLANE if in_planes and others else 0
        tokens = places if behind is None else after(places, behind)
        shapes = bf16(rows, qk_width, width) + [jax.ShapeDtypeStruct((pairs, FEATS, LANES), F32)]
        if others:
            shapes += bf16(FEATS, LANES) * sends
        else:
            shapes += bf16(rows, qk_width, width, width) + bf16(HALO, width)
        operands = [tokens, means, conv_weight, turn_rows, weight, arranged, *pieces[b]]
        if prev is not None:
            operands.append(prev)
        operands += others
        return call(
            functools.partial(
                block_kernel, n=n, heads=heads, extra=extra, others=len(others), sends=sends
            ),
            shapes,
            in_specs=[scalar] + [whole] * (len(operands) - 1),
            out_specs=[whole] * len(shapes),
            scratch_shapes=[pltpu.VMEM((EDGE + rows, width), F32)],
            vmem=32 << 20,
        )(*operands)

    def do_queries(b, v):
        rows = blocks[b][1]
        return call(
            functools.partial(query_kernel, n=n),
            bf16(rows, qk_width, width, width) + bf16(HALO, width),
            in_specs=[scalar] + [whole] * (3 + n),
            out_specs=[whole] * 4,
            vmem=32 << 20,
        )(places, means, arranged, v, *pieces[b])

    def attend(b, prev):
        rows = blocks[b][1]
        k, v, _, q, wq, wk, _ = done[b]
        return call(
            functools.partial(attend_kernel, heads=heads, first=b == 0),
            [jax.ShapeDtypeStruct((rows, turn.shape[1]), BF16)] + [jax.ShapeDtypeStruct((rows, width), F32)] * 2,
            in_specs=[scalar] + [whole] * 7,
            out_specs=[whole] * 3,
            scratch_shapes=[pltpu.VMEM((WIN + rows, width), BF16)] * 2,
            vmem=16 << 20,
        )(places, turn, prev, q, k, v, wq, wk)

    done, attended = {}, {}
    picked = [pick(r) for r in range(1, n)]
    done[last] = do_block(last, None, None)
    halo = lax.ppermute(done[last][6], "ctx", [(i, i + 1) for i in range(ctx - 1)])
    prevs = {0: halo}
    for b in range(last - 1):
        behind = [a[1] for a in attended.values()] + (picked if b == 1 else [])
        done[b] = do_block(b, prevs[b], behind if b else None)
        prevs[b + 1] = done[b][6]
        attended[b] = attend(b, prevs[b])
        if b == 0:
            attended[last] = attend(last, halo)
    b = last - 1
    k, v, state, *sends = do_block(b, prevs[b], attended[b - 1][1], [done[c][2] for c in (last, *range(b))])
    done[b] = (k, v, state, *do_queries(b, v))
    prevs[last] = done[b][6]
    attended[last - 1] = attend(last - 1, prevs[last - 1])
    tile = 128
    edge = call(
        edge_kernel,
        jax.ShapeDtypeStruct((tile, width), F32),
        in_specs=[scalar] + [whole] * 4,
        out_specs=whole,
        vmem=16 << 20,
    )(places, done[last - 1][6], done[last][1], done[last][4], done[last][5])

    def finish(turns, priors, some, behind):
        before = list(some)
        operands = [after(places, behind), means, gain, *priors, *[done[c][2] for c in range(max(before))]]
        edged = before.index(last) if last in before else None
        if edged is not None:
            operands.append(edge)
        for b in some:
            operands += attended[b]
        rows = sum(blocks[b][1] for b in some)
        return call(
            functools.partial(finish_kernel, heads=heads, turns=turns, before=before, edged=edged),
            jax.ShapeDtypeStruct((rows, len(turns) * LANES), BF16),
            in_specs=[scalar] + [whole] * (len(operands) - 1),
            out_specs=whole,
            flops=4850 * 10**6 if len(some) > 1 else 1,
            vmem=24 << 20,
        )(*operands)

    order = (0, 1, 4, 2, 3)
    early = []
    if in_planes:
        held = sends[:1] + [exchange(sends[r], "ctx", r) for r in range(1, PLANE)]
        back = prior_in_planes(held, places, [done[last - 1][6], (attended[last - 1][1], edge)])
        mixed = finish((0,), back[:1], range(last + 1), done[last][1])
        priors = [exchange(after(back[r], mixed), "ctx", r) for r in range(1, PLANE)]
        turns = tuple(range(1, PLANE))
        early = [mixed] + [from_head(mixed, r) for r in range(1, n)]
    else:
        priors = prior_by_doubling(sum(done[b][2] for b in range(last + 1)), position)
        turns = tuple(range(pairs))
        mixed = attended[last][1]
    fetched = [from_head(after(block, done[last - 1][1]), r) for r, block in enumerate(picked, 1)]
    out_rows = []
    for got in fetched:
        out_rows.append(got)
        if out_parts > 1:
            out_rows.append(exchange(after(got, mixed), "ctx", 1))

    mixes = {}
    for b in order:
        mixed = finish(turns, priors, (b,), mixed)
        mixes[b] = [mixed] + [from_head(mixed, r) for r in range(1, n)]

    def pieces_of(b, r):
        return early[r : r + 1] + [mixes[b][r]]

    def turns_of(b):
        return ([(0, (0,))] if early else []) + [(blocks[b][0], turns)]

    tail_blocks = order[-2:]
    tail_rows = sum(blocks[b][1] for b in tail_blocks)
    share = call(
        functools.partial(
            share_kernel, turns=[turns_of(b) for b in tail_blocks], blocks=[blocks[b] for b in tail_blocks]
        ),
        jax.ShapeDtypeStruct((tail_rows, cols), BF16),
        in_specs=[scalar] + [whole] * (1 + 2 * len(turns_of(last))),
        out_specs=whole,
        scratch_shapes=[pltpu.VMEM((tail_rows, width), BF16)],
        vmem=16 << 20,
    )(places, out_weight, *[piece for b in tail_blocks for piece in pieces_of(b, 0)])

    result = None
    for b in order:
        at, rows = blocks[b]
        shared = None
        operands = [after(places, share) if b == order[-3] else places, out_weight] + out_rows
        if b in tail_blocks:
            shared = sum(blocks[c][1] for c in tail_blocks[: tail_blocks.index(b)])
            operands.append(share)
        for r in range(0 if shared is None else 1, n):
            operands += pieces_of(b, r)
        specs = [scalar] + [whole] * (len(operands) - 1)
        aliases = {}
        if result is not None:
            aliases = {len(operands): 0}
            operands.append(result)
            specs.append(pl.BlockSpec(memory_space=pl.ANY))
        result = call(
            functools.partial(
                output_kernel, n=n, offset=at, parts=out_parts, turns=turns_of(b), shared=shared
            ),
            jax.ShapeDtypeStruct((row_count, cols), BF16),
            in_specs=specs,
            out_specs=pl.BlockSpec(memory_space=pl.ANY),
            scratch_shapes=[
                pltpu.VMEM((rows, cols), BF16),
                pltpu.VMEM((n, rows, width), BF16),
                pltpu.SemaphoreType.DMA((2,)),
            ],
            input_output_aliases=aliases,
            vmem=16 << 20,
        )(*operands)
    return result


def solution(mesh):
    return jax.shard_map(
        per_device,
        mesh=mesh,
        in_specs=(P("ctx", "head"), P(None, "head"), P(None, "head"), P("head"), P("head", None)),
        out_specs=P("ctx", "head"),
        check_vma=False,
    )
```

```python
import functools

import jax
import jax.numpy as jnp
import numpy as np
from jax import lax
from jax.experimental import pallas as pl
from jax.experimental.pallas import tpu as pltpu
from jax.sharding import PartitionSpec as P

DV = 64
FQK = 16
WIN = 64
CONV = 3
LANES = 128
SHIFTS = FQK // 2 + 1
FEATS = (SHIFTS + 1) * FQK
EDGE = 16
HALO = EDGE + 2 * WIN
PLANE = 4
F32 = jnp.float32
BF16 = jnp.bfloat16


def call(body, out_shape, *, vmem, flops=1, **kwargs):
    return pl.pallas_call(
        body,
        out_shape=out_shape,
        compiler_params=pltpu.CompilerParams(vmem_limit_bytes=vmem),
        cost_estimate=pl.CostEstimate(flops=flops, bytes_accessed=1, transcendentals=0),
        **kwargs,
    )


def feature_layout(heads):
    in_group = min(heads, 4)
    lanes = in_group * FQK
    per_tile = LANES // lanes
    return in_group, lanes, -(-(SHIFTS + 1) // per_tile) * per_tile


def feature_tables(heads):
    in_group, lanes, slots = feature_layout(heads)
    groups = heads // in_group
    turn = np.zeros((LANES, groups, slots, in_group, FQK), np.float32)
    for g in range(groups):
        for s in range(SHIFTS):
            for h in range(in_group):
                for i in range(FQK if s < SHIFTS - 1 else FQK // 2):
                    turn[g * lanes + h * FQK + (i + s) % FQK, g, s, h, i] = 1.0
    weight = np.zeros((SHIFTS + 1, FQK, LANES), np.float32)
    weight[0] = 1.0 / (2.0 * FQK)
    weight[1:SHIFTS] = 2.0 / (2.0 * FQK)
    weight[SHIFTS - 1, FQK // 2] = 1.0
    weight[SHIFTS] = 1.0 / FQK**0.5
    turn = turn.reshape(LANES, -1)
    by_rows = np.concatenate([turn.T, np.eye(LANES, dtype=np.float32)], 0)
    return jnp.asarray(turn, BF16), jnp.asarray(by_rows, BF16), jnp.asarray(weight.reshape(FEATS, LANES))


def mean_table():
    block = np.kron(np.eye(LANES // DV), np.ones((DV, DV))) / DV
    return jnp.asarray(np.concatenate([block, block], 0), BF16)


def head_mean(values, table):
    high = values.astype(BF16)
    low = (values - high.astype(F32)).astype(BF16)
    return jnp.dot(jnp.concatenate([high, low], 1), table, preferred_element_type=F32)


def nt_dot(a, b):
    return lax.dot_general(a, b, (((1,), (1,)), ((), ())), preferred_element_type=F32)


def arrange_kernel(w_ref, o_ref, *, heads):
    per_head = 2 * FQK + 3 * DV
    w = w_ref[...]
    at = 0
    for begin, width in ((0, FQK), (FQK, FQK), (2 * FQK, DV), (2 * FQK + DV, DV), (2 * FQK + 2 * DV, DV)):
        parts = [w[:, h * per_head + begin : h * per_head + begin + width] for h in range(heads)]
        total = heads * width
        padded = -(-total // LANES) * LANES
        if padded > total:
            parts.append(jnp.zeros((w.shape[0], padded - total), w.dtype))
        o_ref[:, at : at + padded] = jnp.concatenate(parts, 1)
        at += padded


def project(me, xs, w_ref, begin, width, skip, own=None):
    depth = xs[0].shape[1]
    total = own
    for r, x_ref in enumerate(xs):
        if r == 0 and own is not None:
            continue
        src = lax.rem(me - r + len(xs), len(xs))
        from_rows = pl.ds(pl.multiple_of(src * depth, depth), depth)
        part = jnp.dot(x_ref[skip:, :], w_ref[from_rows, begin : begin + width], preferred_element_type=F32)
        total = part if total is None else total + part
    return total.astype(BF16)


def normalize(got, ref, mean_ref, scale):
    for p in range(ref.shape[1] // LANES):
        cols = slice(p * LANES, (p + 1) * LANES)
        x = got[:, cols].astype(F32)
        x = x * lax.rsqrt(head_mean(x * x, mean_ref[...]) + 1e-6)
        ref[:, cols] = x.astype(BF16) * jnp.asarray(scale, BF16)


def block_kernel(j_ref, mean_ref, conv_ref, turn_ref, weight_ref, w_ref, *refs, n, heads, extra, others, sends):
    xs, refs = refs[:n], refs[n:]
    prev_ref = None
    if not extra:
        prev_ref, refs = refs[0], refs[1:]
    own_ref, refs = (refs[0], refs[1:]) if others else (None, refs)
    other_refs, refs = refs[:others], refs[others:]
    k_ref, v_ref, s_ref, refs = *refs[:3], refs[3:]
    send_refs, ext_ref = refs[:sends], refs[-1]
    q_ref, wq_ref, wk_ref, halo_ref = (None,) * 4 if others else refs[:4]
    rows = v_ref.shape[0]
    qk_width, width = k_ref.shape[1], v_ref.shape[1]
    me = j_ref[0]

    if others:
        k_ref[...] = project(me, xs, w_ref, qk_width, qk_width, 0, own_ref[:, :qk_width])
    else:
        qk = project(me, xs, w_ref, 0, 2 * qk_width, extra)
        q_ref[...] = qk[:, :qk_width]
        k_ref[...] = qk[:, qk_width:]
    raw = project(me, xs, w_ref, 2 * qk_width, width, 0, own_ref[:, qk_width:] if others else None)
    if extra:
        ext_ref[...] = raw.astype(F32)
    else:
        ext_ref[0:EDGE, :] = prev_ref[0:EDGE, :].astype(F32)
        ext_ref[EDGE:, :] = raw.astype(F32)
    total = jnp.zeros((rows, width), F32)
    for tap in range(CONV):
        total = total + conv_ref[tap : tap + 1, :] * ext_ref[EDGE - tap : EDGE - tap + rows, :]
    v_ref[...] = total.astype(BF16)

    in_group, lanes, slots = feature_layout(heads)
    groups = heads // in_group
    turned = nt_dot(turn_ref[...], k_ref[...])
    keys = turned[groups * slots * lanes :]
    constant = lax.broadcasted_iota(jnp.int32, (lanes, rows), 0) % FQK == FQK // 2
    low_half = lax.broadcasted_iota(jnp.int32, (SHIFTS + 1, FQK, LANES), 2) < DV
    for g in range(groups):
        own = keys[g * lanes : (g + 1) * lanes]
        phi = []
        for s in range(SHIFTS):
            at = (g * slots + s) * lanes
            phi.append(own * turned[at : at + lanes])
        phi[-1] = jnp.where(constant, 1.0, phi[-1])
        phi = jnp.concatenate([part.astype(BF16) for part in phi + [own]], 0)
        v = v_ref[:, g * in_group * DV : (g + 1) * in_group * DV]
        got = jnp.dot(phi, v, preferred_element_type=F32).reshape(SHIFTS + 1, lanes, in_group * DV)
        for p in range(in_group * DV // LANES):
            cols = slice(p * LANES, (p + 1) * LANES)
            first = got[:, 2 * p * FQK : (2 * p + 1) * FQK, cols]
            second = got[:, (2 * p + 1) * FQK : (2 * p + 2) * FQK, cols]
            state = jnp.where(low_half, first, second).reshape(FEATS, LANES)
            s_ref[g * in_group * DV // LANES + p] = state * weight_ref[...]
    for r in range(sends):
        pair = jnp.bitwise_xor(j_ref[1], r)
        total = s_ref[pair]
        for ref in other_refs:
            total = total + ref[pair]
        send_refs[r][...] = total.astype(BF16)

    if not others:
        halo_ref[0:EDGE, :] = raw[raw.shape[0] - EDGE :]
        query_part(me, xs, w_ref, mean_ref, v_ref, wq_ref, wk_ref, halo_ref, 2 * qk_width + width, extra)


def own_share_kernel(j_ref, x_ref, w_ref, o_ref, *, begin):
    rows_of = pl.ds(pl.multiple_of(j_ref[0] * x_ref.shape[1], x_ref.shape[1]), x_ref.shape[1])
    o_ref[...] = jnp.dot(x_ref[...], w_ref[rows_of, begin : begin + o_ref.shape[1]], preferred_element_type=F32)


def query_part(me, xs, w_ref, mean_ref, v_ref, wq_ref, wk_ref, halo_ref, begin, skip):
    rows, width = v_ref.shape
    normalize(project(me, xs, w_ref, begin, width, skip), wq_ref, mean_ref, 1.0 / DV**0.5)
    normalize(project(me, xs, w_ref, begin + width, width, skip), wk_ref, mean_ref, 1.0)
    halo_ref[EDGE : EDGE + WIN, :] = v_ref[rows - WIN : rows, :]
    halo_ref[EDGE + WIN : HALO, :] = wk_ref[rows - WIN : rows, :]


def query_kernel(j_ref, mean_ref, w_ref, v_ref, *refs, n):
    xs, (q_ref, wq_ref, wk_ref, halo_ref) = refs[:n], refs[n:]
    qk_width, width = q_ref.shape[1], v_ref.shape[1]
    q_ref[...] = project(j_ref[0], xs, w_ref, 0, qk_width, 0)
    halo_ref[0:EDGE, :] = jnp.zeros((EDGE, width), BF16)
    query_part(j_ref[0], xs, w_ref, mean_ref, v_ref, wq_ref, wk_ref, halo_ref, 2 * qk_width + width, 0)


def band_of(tile, span, first):
    col = lax.broadcasted_iota(jnp.int32, (2 * tile, span), 1)
    ahead = col - lax.broadcasted_iota(jnp.int32, (2 * tile, span), 0) % tile
    seen = (ahead >= 1) & (ahead <= WIN)
    if first is not None:
        seen = seen & (col >= first)
    return seen.astype(F32).astype(BF16)


def window_tile(wq, keys, values, band, low):
    none = jnp.zeros_like(wq)
    scores = nt_dot(jnp.concatenate([jnp.where(low, wq, none), jnp.where(low, none, wq)], 0), keys)
    expo = jnp.exp(scores).astype(BF16) * band
    ones = jnp.ones(values.shape, BF16)
    got = jnp.dot(expo, jnp.concatenate([values, ones], 1), preferred_element_type=F32)
    tile = wq.shape[0]
    got = jnp.where(jnp.concatenate([low, low], 1), got[:tile], got[tile:])
    return got[:, :LANES] / got[:, LANES:]


def edge_kernel(_, prev_ref, v_ref, wq_ref, wk_ref, win_ref):
    tile = win_ref.shape[0]
    band = band_of(tile, tile + WIN, None)
    low = lax.broadcasted_iota(jnp.int32, (tile, LANES), 1) < DV
    for p in range(win_ref.shape[1] // LANES):
        cols = slice(p * LANES, (p + 1) * LANES)
        values = jnp.concatenate([prev_ref[EDGE : EDGE + WIN, cols], v_ref[:tile, cols]], 0)
        keys = jnp.concatenate([prev_ref[EDGE + WIN : HALO, cols], wk_ref[:tile, cols]], 0)
        win_ref[:, cols] = window_tile(wq_ref[:tile, cols], keys, values, band, low)


def attend_kernel(
    a_ref, turn_ref, prev_ref, q_ref, k_ref, v_ref, wq_ref, wk_ref, phi_ref, lin_ref, win_ref,
    vext_ref, kext_ref, *, heads, first
):
    rows = q_ref.shape[0]
    tile = 128
    span = tile + WIN
    vext_ref[0:WIN, :] = prev_ref[EDGE : EDGE + WIN, :]
    vext_ref[WIN : WIN + rows, :] = v_ref[...]
    kext_ref[0:WIN, :] = prev_ref[EDGE + WIN : HALO, :]
    kext_ref[WIN : WIN + rows, :] = wk_ref[...]
    q = q_ref[...]
    k = k_ref[...]
    lane = lax.broadcasted_iota(jnp.int32, (rows, LANES), 1)
    low_half = lane < DV

    in_group, lanes, slots = feature_layout(heads)
    per_tile = LANES // lanes
    turned = jnp.dot(q, turn_ref[...], preferred_element_type=F32)
    slot = lane // lanes
    for g in range(heads // in_group):
        own = q[:, g * lanes : (g + 1) * lanes].astype(F32)
        own = jnp.concatenate([own] * per_tile, 1)
        for t in range(slots // per_tile):
            at = (g * slots // per_tile + t) * LANES
            part = own * turned[:, at : at + LANES]
            if t == (SHIFTS - 1) // per_tile:
                here = (slot == (SHIFTS - 1) % per_tile) & (lane % FQK == FQK // 2)
                part = jnp.where(here, 1.0, part)
            if t == SHIFTS // per_tile:
                part = jnp.where(slot == SHIFTS % per_tile, own, part)
            phi_ref[:, at : at + LANES] = part.astype(BF16)

    down = lax.broadcasted_iota(jnp.int32, (2 * rows, rows), 0) % rows
    causal = lax.broadcasted_iota(jnp.int32, (2 * rows, rows), 1) <= down
    band = band_of(tile, span, None)
    first_band = band
    if first:
        first_band = band_of(tile, span, jnp.where(a_ref[2] == 0, WIN, 0))
    q = q * jnp.asarray(1.0 / FQK**0.5, BF16)
    for p in range(heads * DV // LANES):
        cols = slice(p * LANES, (p + 1) * LANES)
        both = [
            jnp.where((lane >= h * FQK) & (lane < (h + 1) * FQK), q, jnp.zeros_like(q)) for h in (2 * p, 2 * p + 1)
        ]
        t = nt_dot(jnp.concatenate(both, 0), k) + 1.0
        kernel = jnp.where(causal, t * t + 1.0, 0.0).astype(BF16)
        got = jnp.dot(kernel, v_ref[:, cols], preferred_element_type=F32)
        lin_ref[:, cols] = 0.5 * jnp.where(low_half, got[:rows], got[rows:])
        for i in range(rows // tile):
            here = slice(i * tile, (i + 1) * tile)
            keys = kext_ref[i * tile : i * tile + span, cols]
            values = vext_ref[i * tile : i * tile + span, cols]
            win_ref[here, cols] = window_tile(
                wq_ref[here, cols], keys, values, first_band if i == 0 else band, low_half[:tile]
            )


def carry_table(state, p, heads):
    in_group, lanes, slots = feature_layout(heads)
    in_pairs = in_group * DV // LANES
    state = state.reshape(SHIFTS + 1, FQK, LANES)
    low_half = lax.broadcasted_iota(jnp.int32, state.shape, 2) < DV
    parts = [jnp.where(low_half, state, 0.0), jnp.where(low_half, 0.0, state)] * in_pairs
    parts = jnp.concatenate(parts, 1)
    if in_pairs > 1:
        here = lax.broadcasted_iota(jnp.int32, parts.shape, 1) // (2 * FQK) == p
        parts = jnp.where(here, parts, 0.0)
    parts = parts.reshape((SHIFTS + 1) * lanes, LANES)
    if slots > SHIFTS + 1:
        parts = jnp.concatenate([parts, jnp.zeros(((slots - SHIFTS - 1) * lanes, LANES), F32)], 0)
    return parts.astype(BF16)


def finish_kernel(a_ref, mean_ref, gain_ref, *refs, heads, turns, before, edged):
    prior_refs, refs = refs[: len(turns)], refs[len(turns) :]
    states, refs = refs[: max(before)], refs[max(before) :]
    edge_ref, refs = (refs[0], refs[1:]) if edged is not None else (None, refs)
    mix_ref = refs[-1]
    in_group, lanes, slots = feature_layout(heads)
    in_pairs = in_group * DV // LANES
    for i, r in enumerate(turns):
        pair = jnp.bitwise_xor(a_ref[1], r)
        group = lax.div(pair, in_pairs)
        own = pl.ds(pl.multiple_of(group * (slots * lanes), LANES), slots * lanes)
        cols = pl.ds(pl.multiple_of(pair * LANES, LANES), LANES)
        state = prior_refs[i][...].astype(F32)
        added, at = 0, 0
        for b, count in enumerate(before):
            phi_ref, lin_ref, win_ref = refs[3 * b : 3 * b + 3]
            for c in range(added, count):
                state = state + states[c][pair]
            added = count
            table = carry_table(state, lax.rem(pair, in_pairs), heads)
            lin = lin_ref[:, cols] + jnp.dot(phi_ref[:, own], table, preferred_element_type=F32)
            scale = lax.rsqrt(head_mean(lin * lin, mean_ref[...]) + 1e-5)
            win = win_ref[:, cols]
            if b == edged:
                win = jnp.concatenate([edge_ref[:, cols], win[edge_ref.shape[0] :]], 0)
            rows = lin.shape[0]
            mix_ref[at : at + rows, i * LANES : (i + 1) * LANES] = (
                lin * scale * gain_ref[:, cols] + win
            ).astype(BF16)
            at += rows


def place_pieces(a_ref, pieces, turns, offset, mixed_ref):
    rows = mixed_ref.shape[0]
    for ref, (begin, pairs) in zip(pieces, turns):
        here = slice(offset - begin, offset - begin + rows)
        for k, turn in enumerate(pairs):
            at = pl.multiple_of(jnp.bitwise_xor(a_ref[1], turn) * LANES, LANES)
            mixed_ref[:, pl.ds(at, LANES)] = ref[here, k * LANES : (k + 1) * LANES]


def own_columns(a_ref, cols, begin, width):
    return pl.ds(pl.multiple_of(a_ref[0] * cols + begin, LANES), width)


def share_kernel(a_ref, w_ref, *refs, turns, blocks):
    share_ref, mixed_ref = refs[-2:]
    at = 0
    for i, (offset, rows) in enumerate(blocks):
        pieces = refs[i * len(turns[i]) : (i + 1) * len(turns[i])]
        place_pieces(a_ref, pieces, turns[i], offset, mixed_ref.at[pl.ds(at, rows), :])
        at += rows
    cols = share_ref.shape[1]
    mine = own_columns(a_ref, cols, 0, cols)
    share_ref[...] = jnp.dot(mixed_ref[...], w_ref[:, mine], preferred_element_type=F32).astype(BF16)


def output_kernel(a_ref, w_ref, *refs, n, offset, parts, turns, shared):
    weights, refs = refs[: parts * (n - 1)], refs[parts * (n - 1) :]
    o_ref, held_ref, mixed_ref, sems = refs[-4:]
    rows, cols = held_ref.shape
    first = 0
    if shared is not None:
        share_ref, refs = refs[0], refs[1:]
        first = 1
    for r in range(first, n):
        pieces = refs[(r - first) * len(turns) : (r - first + 1) * len(turns)]
        place_pieces(a_ref, pieces, turns, offset, mixed_ref.at[r])
    copies = []
    count = 2 if cols % (2 * LANES) == 0 else 1
    width = cols // count
    for half in range(count):
        here = slice(half * width, (half + 1) * width)
        total = None
        if shared is not None:
            total = share_ref[shared : shared + rows, here].astype(F32)
        for r in range(first, n):
            if r == 0:
                part = jnp.dot(
                    mixed_ref[0], w_ref[:, own_columns(a_ref, cols, half * width, width)], preferred_element_type=F32
                )
            else:
                part = None
                for i in range(parts):
                    ref = weights[(r - 1) * parts + i]
                    depth = ref.shape[0]
                    at = depth * (jnp.bitwise_xor(a_ref[2] % 2, i) if parts > 1 else 0)
                    rows_of = pl.ds(pl.multiple_of(at, depth), depth)
                    got = jnp.dot(mixed_ref[r, :, rows_of], ref[:, here], preferred_element_type=F32)
                    part = got if part is None else part + got
            part = part.astype(BF16).astype(F32)
            total = part if total is None else total + part
        held_ref[:, here] = total.astype(BF16)
        copy = pltpu.make_async_copy(
            held_ref.at[:, here], o_ref.at[pl.ds(offset, rows), here], sems.at[half]
        )
        copy.start()
        copies.append(copy)
    for copy in copies:
        copy.wait()


def pick_kernel(a_ref, w_ref, o_ref):
    o_ref[...] = w_ref[...]


def exchange(value, axis, flip):
    count = lax.axis_size(axis)
    return lax.ppermute(value, axis, [(i, i ^ flip) for i in range(count)])


def plane_kernel(a_ref, *refs):
    helds, plane_ref, ahead_refs = refs[:PLANE], refs[PLANE], refs[PLANE + 1 :]
    place = a_ref[1]
    held = [ref[...].astype(F32) for ref in helds]
    plane_ref[...] = (held[0] + held[1] + held[2] + held[3]).astype(BF16)
    for r in range(PLANE):
        total = jnp.zeros_like(held[0])
        for s in range(PLANE):
            before = jnp.bitwise_xor(place, s) < jnp.bitwise_xor(place, r)
            total = total + held[s] * before.astype(F32)
        ahead_refs[r][...] = total


def earlier_kernel(a_ref, *refs, planes):
    ahead_refs, plane_refs, back_refs = refs[:PLANE], refs[PLANE : PLANE + planes], refs[PLANE + planes :]
    mine = a_ref[2] // PLANE
    earlier = jnp.zeros(ahead_refs[0].shape, F32)
    for d, ref in enumerate(plane_refs, 1):
        before = jnp.bitwise_xor(mine, d) < mine
        earlier = earlier + ref[...].astype(F32) * before.astype(F32)
    for r in range(PLANE):
        back_refs[r][...] = (ahead_refs[r][...] + earlier).astype(BF16)


def after(value, earlier):
    return lax.optimization_barrier((value, earlier))[0]


def prior_in_planes(held, places, beside):
    ctx = lax.axis_size("ctx")
    whole = pl.BlockSpec(memory_space=pltpu.VMEM)
    scalar = pl.BlockSpec(memory_space=pltpu.SMEM)
    narrow = jax.ShapeDtypeStruct((FEATS, LANES), BF16)
    wide = jax.ShapeDtypeStruct((FEATS, LANES), F32)
    plane, *ahead = call(
        plane_kernel,
        [narrow] + [wide] * PLANE,
        in_specs=[scalar] + [whole] * PLANE,
        out_specs=[whole] * (1 + PLANE),
        vmem=4 << 20,
    )(after(places, beside[0]), *held)
    earlier = []
    for d in range(1, ctx // PLANE):
        earlier.append(exchange(plane, "ctx", d * PLANE))
    return call(
        functools.partial(earlier_kernel, planes=len(earlier)),
        [narrow] * PLANE,
        in_specs=[scalar] + [whole] * (PLANE + len(earlier)),
        out_specs=[whole] * PLANE,
        vmem=4 << 20,
    )(after(places, beside[1]), *ahead, *earlier)


def prior_by_doubling(total, position):
    ctx = lax.axis_size("ctx")
    prior = jnp.zeros_like(total)
    bit = 1
    while bit < ctx:
        got = exchange(total.astype(BF16), "ctx", bit).astype(F32)
        prior = prior + jnp.where((position & bit) != 0, got, 0.0)
        total = total + got
        bit *= 2
    return [prior[p].astype(BF16) for p in range(total.shape[0])]


def per_device(hidden_in, proj_weight, conv_weight, norm_gain, out_weight):
    n = lax.axis_size("head")
    ctx = lax.axis_size("ctx")
    me = lax.axis_index("head").astype(jnp.int32)
    position = lax.axis_index("ctx").astype(jnp.int32)
    row_count = hidden_in.shape[0]
    model = proj_weight.shape[0]
    heads = out_weight.shape[0] // DV
    width = heads * DV
    pairs = width // LANES
    in_planes = pairs == PLANE and ctx % PLANE == 0 and ctx & (ctx - 1) == 0
    places = jnp.stack([me, position % PLANE if in_planes else jnp.zeros_like(position), position])
    hidden_in, places = lax.optimization_barrier((hidden_in, places))
    step = row_count // 8
    blocks = [(0, 2 * step), (2 * step, 2 * step), (4 * step, step), (5 * step, step), (6 * step, 2 * step)]
    last = len(blocks) - 1
    turn, turn_rows, weight = feature_tables(heads)
    means = mean_table()
    gain = norm_gain.reshape(1, width)
    whole = pl.BlockSpec(memory_space=pltpu.VMEM)
    scalar = pl.BlockSpec(memory_space=pltpu.SMEM)

    def from_head(value, by):
        return lax.ppermute(value, "head", [(i, (i + by) % n) for i in range(n)])

    pieces = {}

    def send_block(b, behind=None):
        at, rows = blocks[b]
        extra = EDGE if b == last else 0
        own = hidden_in[at - extra : at + rows]
        if behind is not None:
            own = after(own, behind)
        pieces[b] = [own] + [from_head(own, r) for r in range(1, n)]

    send_block(last)
    send_block(0, pieces[last][0])
    for b in range(1, last):
        send_block(b, pieces[last][0])

    cols = out_weight.shape[1] // n
    out_parts = 2 if width // 2 % LANES == 0 and ctx % 2 == 0 else 1
    share = width // out_parts
    def pick(r):
        column = functools.partial(lambda i, a, r: (a[2] % out_parts, (a[0] + r) % n), r=r)
        return call(
            pick_kernel,
            jax.ShapeDtypeStruct((share, cols), BF16),
            grid_spec=pltpu.PrefetchScalarGridSpec(
                num_scalar_prefetch=1,
                grid=(1,),
                in_specs=[pl.BlockSpec((share, cols), column)],
                out_specs=pl.BlockSpec((share, cols), lambda i, a: (0, 0)),
            ),
            vmem=8 << 20,
        )(places, out_weight)

    qk_width = -(-heads * FQK // LANES) * LANES
    arranged_width = 2 * qk_width + 3 * width
    slab = 256
    arranged = call(
        functools.partial(arrange_kernel, heads=heads),
        jax.ShapeDtypeStruct((model, arranged_width), BF16),
        grid=(model // slab,),
        in_specs=[pl.BlockSpec((slab, proj_weight.shape[1]), lambda i: (i, 0))],
        out_specs=pl.BlockSpec((slab, arranged_width), lambda i: (i, 0)),
        vmem=32 << 20,
    )(proj_weight)

    def bf16(rows, *widths):
        return [jax.ShapeDtypeStruct((rows, w), BF16) for w in widths]

    def do_block(b, prev, behind, others=()):
        rows = blocks[b][1]
        extra = EDGE if prev is None else 0
        sends = PLANE if in_planes and others else 0
        tokens = places if behind is None else after(places, behind)
        shapes = bf16(rows, qk_width, width) + [jax.ShapeDtypeStruct((pairs, FEATS, LANES), F32)]
        if others:
            shapes += bf16(FEATS, LANES) * sends
        else:
            shapes += bf16(rows, qk_width, width, width) + bf16(HALO, width)
        operands = [tokens, means, conv_weight, turn_rows, weight, arranged, *pieces[b]]
        if prev is not None:
            operands.append(prev)
        if others:
            operands.append(own_share)
        operands += others
        return call(
            functools.partial(
                block_kernel, n=n, heads=heads, extra=extra, others=len(others), sends=sends
            ),
            shapes,
            in_specs=[scalar] + [whole] * (len(operands) - 1),
            out_specs=[whole] * len(shapes),
            scratch_shapes=[pltpu.VMEM((EDGE + rows, width), F32)],
            vmem=32 << 20,
        )(*operands)

    def do_queries(b, v):
        rows = blocks[b][1]
        return call(
            functools.partial(query_kernel, n=n),
            bf16(rows, qk_width, width, width) + bf16(HALO, width),
            in_specs=[scalar] + [whole] * (3 + n),
            out_specs=[whole] * 4,
            vmem=32 << 20,
        )(places, means, arranged, v, *pieces[b])

    def attend(b, prev):
        rows = blocks[b][1]
        k, v, _, q, wq, wk, _ = done[b]
        return call(
            functools.partial(attend_kernel, heads=heads, first=b == 0),
            [jax.ShapeDtypeStruct((rows, turn.shape[1]), BF16)] + [jax.ShapeDtypeStruct((rows, width), F32)] * 2,
            in_specs=[scalar] + [whole] * 7,
            out_specs=[whole] * 3,
            scratch_shapes=[pltpu.VMEM((WIN + rows, width), BF16)] * 2,
            vmem=16 << 20,
        )(places, turn, prev, q, k, v, wq, wk)

    own_share = call(
        functools.partial(own_share_kernel, begin=qk_width),
        jax.ShapeDtypeStruct((blocks[last - 1][1], qk_width + width), F32),
        in_specs=[scalar] + [whole] * 2,
        out_specs=whole,
        vmem=32 << 20,
    )(places, pieces[last - 1][0], arranged)
    done, attended = {}, {}
    picked = [pick(r) for r in range(1, n)]
    done[last] = do_block(last, None, None)
    halo = lax.ppermute(done[last][6], "ctx", [(i, i + 1) for i in range(ctx - 1)])
    prevs = {0: halo}
    for b in range(last - 1):
        behind = [a[1] for a in attended.values()] + (picked + [own_share] if b == 1 else [])
        done[b] = do_block(b, prevs[b], behind if b else None)
        prevs[b + 1] = done[b][6]
        attended[b] = attend(b, prevs[b])
        if b == 0:
            attended[last] = attend(last, halo)
    b = last - 1
    k, v, state, *sends = do_block(b, prevs[b], attended[b - 1][1], [done[c][2] for c in (last, *range(b))])
    done[b] = (k, v, state, *do_queries(b, v))
    prevs[last] = done[b][6]
    attended[last - 1] = attend(last - 1, prevs[last - 1])
    tile = 128
    edge = call(
        edge_kernel,
        jax.ShapeDtypeStruct((tile, width), F32),
        in_specs=[scalar] + [whole] * 4,
        out_specs=whole,
        vmem=16 << 20,
    )(places, done[last - 1][6], done[last][1], done[last][4], done[last][5])

    def finish(turns, priors, some, behind):
        before = list(some)
        operands = [after(places, behind), means, gain, *priors, *[done[c][2] for c in range(max(before))]]
        edged = before.index(last) if last in before else None
        if edged is not None:
            operands.append(edge)
        for b in some:
            operands += attended[b]
        rows = sum(blocks[b][1] for b in some)
        return call(
            functools.partial(finish_kernel, heads=heads, turns=turns, before=before, edged=edged),
            jax.ShapeDtypeStruct((rows, len(turns) * LANES), BF16),
            in_specs=[scalar] + [whole] * (len(operands) - 1),
            out_specs=whole,
            flops=20 * 10**9 if tuple(some) == order[:1] else 4850 * 10**6 if len(some) > 1 else 1,
            vmem=24 << 20,
        )(*operands)

    order = (0, 1, 4, 2, 3)
    early, early_blocks = [], (0, 1, last)
    if in_planes:
        held = sends[:1] + [exchange(sends[r], "ctx", r) for r in range(1, PLANE)]
        back = prior_in_planes(held, places, [done[last - 1][6], (attended[last - 1][1], edge)])
        priors = [exchange(back[r], "ctx", r) for r in range(1, PLANE)]
        mixed = finish((0,), back[:1], early_blocks, done[last][1])
        early = [mixed] + [from_head(mixed, r) for r in range(1, n)]
    else:
        priors = prior_by_doubling(sum(done[b][2] for b in range(last + 1)), position)
        mixed = attended[last][1]
    fetched = [from_head(after(block, done[last - 1][1]), r) for r, block in enumerate(picked, 1)]
    out_rows = []
    for got in fetched:
        out_rows.append(got)
        if out_parts > 1:
            out_rows.append(exchange(after(got, mixed), "ctx", 1))

    mixes = {}
    for b in order:
        if early and b in early_blocks:
            mixed = finish(tuple(range(1, pairs)), priors, (b,), mixed)
        else:
            mixed = finish(tuple(range(pairs)), [back[0], *priors] if early else priors, (b,), mixed)
        mixes[b] = [mixed] + [from_head(mixed, r) for r in range(1, n)]

    def pieces_of(b, r):
        return early[r : r + 1] * (b in early_blocks) + [mixes[b][r]]

    def turns_of(b):
        at = blocks[b][0]
        if early and b in early_blocks:
            ahead = sum(blocks[c][1] for c in early_blocks[: early_blocks.index(b)])
            return [(at - ahead, (0,)), (at, tuple(range(1, pairs)))]
        return [(at, tuple(range(pairs)))]

    tail_blocks = order[-2:]
    tail_rows = sum(blocks[b][1] for b in tail_blocks)
    share = call(
        functools.partial(
            share_kernel, turns=[turns_of(b) for b in tail_blocks], blocks=[blocks[b] for b in tail_blocks]
        ),
        jax.ShapeDtypeStruct((tail_rows, cols), BF16),
        in_specs=[scalar] + [whole] * (1 + 2 * len(turns_of(tail_blocks[0]))),
        out_specs=whole,
        scratch_shapes=[pltpu.VMEM((tail_rows, width), BF16)],
        vmem=16 << 20,
    )(places, out_weight, *[piece for b in tail_blocks for piece in pieces_of(b, 0)])

    result = None
    for b in order:
        at, rows = blocks[b]
        shared = None
        operands = [after(places, share) if b == order[-3] else places, out_weight] + out_rows
        if b in tail_blocks:
            shared = sum(blocks[c][1] for c in tail_blocks[: tail_blocks.index(b)])
            operands.append(share)
        for r in range(0 if shared is None else 1, n):
            operands += pieces_of(b, r)
        specs = [scalar] + [whole] * (len(operands) - 1)
        aliases = {}
        if result is not None:
            aliases = {len(operands): 0}
            operands.append(result)
            specs.append(pl.BlockSpec(memory_space=pl.ANY))
        result = call(
            functools.partial(
                output_kernel, n=n, offset=at, parts=out_parts, turns=turns_of(b), shared=shared
            ),
            jax.ShapeDtypeStruct((row_count, cols), BF16),
            in_specs=specs,
            out_specs=pl.BlockSpec(memory_space=pl.ANY),
            scratch_shapes=[
                pltpu.VMEM((rows, cols), BF16),
                pltpu.VMEM((n, rows, width), BF16),
                pltpu.SemaphoreType.DMA((2,)),
            ],
            input_output_aliases=aliases,
            vmem=16 << 20,
        )(*operands)
    return result


def solution(mesh):
    return jax.shard_map(
        per_device,
        mesh=mesh,
        in_specs=(P("ctx", "head"), P(None, "head"), P(None, "head"), P("head"), P("head", None)),
        out_specs=P("ctx", "head"),
        check_vma=False,
    )
```
